32 devices in a mesh: stream: 4 (over y, core), cross: 8 (over z, x).
Axes of the slice: x: 2, y: 2, z: 4, core: 2. Of those that a mesh axis runs over, the one named last changes fastest.
Arguments:
- pressure: float32 [96, 64, 128], P('stream', 'cross'), may hold values from -6 to 6
- geo_diag: float32 [3, 96, 64, 128], P(None, 'stream', 'cross'), may hold values from 0.004 to 0.04
- geo_off: float32 [3, 96, 64, 128], P(None, 'stream', 'cross'), may hold values from -0.008 to 0.008
- modes_first: float32 [12, 10, 10], P('stream'), may hold values from -2 to 2
- modes_second: float32 [8, 10, 10], P('cross'), may hold values from -2 to 2
- modes_third: float32 [16, 10, 10], replicated, may hold values from -2 to 2
- eigen_first: float32 [12, 10], P('stream'), may hold values from 0.3 to 3
- eigen_second: float32 [8, 10], P('cross'), may hold values from 0.3 to 3
- eigen_third: float32 [16, 10], replicated, may hold values from 0.3 to 3
Outputs:
- operator_out: float32 [96, 64, 128], P('stream', 'cross')
- preconditioned: float32 [96, 64, 128], P('stream', 'cross')
The draws below stay inside these ranges and needn't reach their ends.
All inputs are finite; a program needn't handle non-finite values.
Results may differ from the reference program's by a relative error of at most 0.00013.
Values sent between devices are 32-bit elements; how exact they have to be, the bound alone decides.
No kernel may reach another device: no remote copies, remote signals or barrier semaphores. Data moves between devices by JAX's collectives and lax.ppermute only.
A program may use at most 64 MiB of HBM per device.

```python
import math
import jax
import jax.numpy as jnp
import numpy as np
from jax import lax

N1 = 8
M = 10
EZ = 16
EX = 12
EY = 8
PX = 96
PY = 64
PZ = 128


def shard_levels(rng, dims, cuts, smallest, top_value):
    gain, own = 1.0, jax.random.fold_in(rng, 6)
    for position, shards_of in cuts:
        draws = jnp.exp(jax.random.uniform(jax.random.fold_in(own, position), (shards_of,), jnp.float32, smallest / len(cuts), top_value / len(cuts)))
        gain = gain * jnp.repeat(draws, dims[position] // shards_of).reshape([-1 if axis == position else 1 for axis in range(len(dims))])
    return gain


def scatter_about(own_key, dims, width, limit, pieces=(), kind=jnp.bfloat16):
    level = shard_levels(own_key, dims, pieces, -0.22, 0.18) if pieces else 1.0
    array = jax.random.normal(own_key, dims, jnp.float32) * width * level
    return jnp.minimum(jnp.maximum(array, -limit), limit).astype(kind)


def setup_inputs(seed: int = 0) -> dict:
    key_of = jax.random.split(jax.random.key(seed), 10)
    return {
        "pressure": scatter_about(key_of[0], (PX, PY, PZ), 1.0, 6.0, ((0, 4), (1, 8)), jnp.float32),
        "geo_diag": jnp.clip(jnp.exp(math.log(0.04) - 2.30258502 * jax.random.uniform(key_of[1], (3, PX, PY, PZ), jnp.float32) ** shard_levels(key_of[1], (3, PX, PY, PZ), ((1, 4), (2, 8)), -0.2, 0.2)), 0.004, 0.04),
        "geo_off": jnp.clip(jax.random.uniform(key_of[2], (3, PX, PY, PZ), jnp.float32, -0.008, 0.008) * shard_levels(key_of[2], (3, PX, PY, PZ), ((1, 4), (2, 8)), -0.4, 0.0), -0.008, 0.008),
        "modes_first": scatter_about(key_of[3], (EX, M, M), M ** -0.5, 2.0, ((0, 4),), jnp.float32),
        "modes_second": scatter_about(key_of[4], (EY, M, M), M ** -0.5, 2.0, ((0, 8),), jnp.float32),
        "modes_third": scatter_about(key_of[5], (EZ, M, M), M ** -0.5, 2.0, (), jnp.float32),
        "eigen_first": jnp.clip(jnp.exp(math.log(3.0) - 2.3025851 * jax.random.uniform(key_of[6], (EX, M), jnp.float32) ** shard_levels(key_of[6], (EX, M), ((0, 4),), -0.2, 0.2)), 0.3, 3.0),
        "eigen_second": jnp.clip(jnp.exp(math.log(3.0) - 2.3025851 * jax.random.uniform(key_of[7], (EY, M), jnp.float32) ** shard_levels(key_of[7], (EY, M), ((0, 8),), -0.2, 0.2)), 0.3, 3.0),
        "eigen_third": jnp.clip(jnp.exp(jax.random.uniform(key_of[8], (EZ, M), jnp.float32, math.log(0.3), math.log(3.0))), 0.3, 3.0),
    }


HIGHEST = lax.Precision.HIGHEST


def legendre_values(nodes, degree):
    table = np.zeros((nodes.shape[0], degree + 1))
    table[:, 0] = 1.0
    table[:, 1] = nodes
    for order in range(2, degree + 1):
        table[:, order] = ((2 * order - 1) * nodes * table[:, order - 1] - (order - 1) * table[:, order - 2]) / order
    return table


def derivative_table(points):
    degree = points - 1
    nodes = np.cos(np.pi * np.arange(points) / degree)
    for sweep in range(100):
        table = legendre_values(nodes, degree)
        nodes = nodes - (nodes * table[:, degree] - table[:, degree - 1]) / (points * table[:, degree])
    gll_nodes = nodes[::-1]
    legendre_at = legendre_values(gll_nodes, degree)[:, degree]
    diff_table = np.zeros((points, points))
    for first_index in range(points):
        for second_index in range(points):
            if first_index != second_index:
                diff_table[first_index, second_index] = legendre_at[first_index] / (
                    legendre_at[second_index] * (gll_nodes[first_index] - gll_nodes[second_index]))
    diff_table[0, 0] = -degree * (degree + 1) / 4.0
    diff_table[degree, degree] = degree * (degree + 1) / 4.0
    return diff_table


def group_size(blocks):
    return 16 if blocks % 16 == 0 else blocks


def along_first(source, matrix):
    nodes_count = matrix.shape[0]
    blocks = source.shape[0] // nodes_count
    shaped = source.reshape(blocks, nodes_count, source.shape[1], source.shape[2])
    result = jnp.einsum('ij,ajyz->aiyz', matrix, shaped, precision=HIGHEST)
    return result.reshape(source.shape)


def along_second(source, matrix):
    nodes_count = matrix.shape[0]
    blocks = source.shape[1] // nodes_count
    shaped = source.reshape(source.shape[0], blocks, nodes_count, source.shape[2])
    result = jnp.einsum('ij,xbjz->xbiz', matrix, shaped, precision=HIGHEST)
    return result.reshape(source.shape)


def along_third(source, matrix):
    nodes_count = matrix.shape[0]
    blocks = source.shape[2] // nodes_count
    grouped = group_size(blocks)
    kron_matrix = jnp.kron(jnp.eye(grouped, dtype=jnp.float32), matrix)
    shaped = source.reshape(source.shape[0], source.shape[1], blocks // grouped, grouped * nodes_count)
    result = jnp.einsum('xybl,kl->xybk', shaped, kron_matrix, precision=HIGHEST)
    return result.reshape(source.shape)


def modal_first(source, modes, backward):
    blocks = modes.shape[0]
    extent = modes.shape[1]
    shaped = source.reshape(blocks, extent, source.shape[1], source.shape[2])
    if backward:
        result = jnp.einsum('amp,apyz->amyz', modes, shaped, precision=HIGHEST)
    else:
        result = jnp.einsum('amp,amyz->apyz', modes, shaped, precision=HIGHEST)
    return result.reshape(source.shape)


def modal_second(source, modes, backward):
    blocks = modes.shape[0]
    extent = modes.shape[1]
    shaped = source.reshape(source.shape[0], blocks, extent, source.shape[2])
    if backward:
        result = jnp.einsum('bmp,xbpz->xbmz', modes, shaped, precision=HIGHEST)
    else:
        result = jnp.einsum('bmp,xbmz->xbpz', modes, shaped, precision=HIGHEST)
    return result.reshape(source.shape)


def modal_third(source, modes, backward):
    blocks = modes.shape[0]
    extent = modes.shape[1]
    grouped = group_size(blocks)
    identity = jnp.eye(grouped, dtype=jnp.float32)
    kron_modes = jnp.einsum('gh,bgmp->bgmhp', identity, modes.reshape(blocks // grouped, grouped, extent, extent),
                            precision=HIGHEST).reshape(blocks // grouped, grouped * extent, grouped * extent)
    shaped = source.reshape(source.shape[0], source.shape[1], blocks // grouped, grouped * extent)
    if backward:
        result = jnp.einsum('xybp,bmp->xybm', shaped, kron_modes, precision=HIGHEST)
    else:
        result = jnp.einsum('xybm,bmp->xybp', shaped, kron_modes, precision=HIGHEST)
    return result.reshape(source.shape)


def local_laplacian(pressure, geo_diag, geo_off, diff_matrix):
    grad_first = along_first(pressure, diff_matrix)
    grad_second = along_second(pressure, diff_matrix)
    grad_third = along_third(pressure, diff_matrix)
    flux_first = geo_diag[0] * grad_first + geo_off[0] * grad_second + geo_off[1] * grad_third
    flux_second = geo_off[0] * grad_first + geo_diag[1] * grad_second + geo_off[2] * grad_third
    flux_third = geo_off[1] * grad_first + geo_off[2] * grad_second + geo_diag[2] * grad_third
    transposed = diff_matrix.T
    return (along_first(flux_first, transposed) + along_second(flux_second, transposed)
            + along_third(flux_third, transposed))


def owner_sum_axis(source, dimension, offset, nodes_count):
    length = source.shape[dimension]
    broadcast_shape = [1] * source.ndim
    broadcast_shape[dimension] = length
    local_node = ((jnp.arange(length, dtype=jnp.int32) - offset) % nodes_count).reshape(broadcast_shape)
    zero_slab = jnp.zeros_like(lax.slice_in_dim(source, 0, 1, axis=dimension))
    previous = jnp.concatenate([zero_slab, lax.slice_in_dim(source, 0, length - 1, axis=dimension)], axis=dimension)
    following = jnp.concatenate([lax.slice_in_dim(source, 1, length, axis=dimension), zero_slab], axis=dimension)
    return (source + jnp.where(local_node == 0, previous, 0.0)
            + jnp.where(local_node == nodes_count - 1, following, 0.0))


def owner_sum(source, offset, nodes_count):
    summed = owner_sum_axis(source, 0, offset, nodes_count)
    summed = owner_sum_axis(summed, 1, offset, nodes_count)
    return owner_sum_axis(summed, 2, 0, nodes_count)


def with_blocks(section, dimension, blocks, extent):
    new_shape = list(section.shape)
    new_shape[dimension:dimension + 1] = [blocks, extent]
    return section.reshape(new_shape)


def extend_axis(padded, dimension, blocks, nodes_count):
    extent_all = blocks * nodes_count
    left_part = lax.slice_in_dim(padded, 0, extent_all, stride=nodes_count, axis=dimension)
    middle = lax.slice_in_dim(padded, 2, extent_all + 2, axis=dimension)
    right_part = lax.slice_in_dim(padded, nodes_count + 3, extent_all + 4, stride=nodes_count, axis=dimension)
    joined = jnp.concatenate([with_blocks(left_part, dimension, blocks, 1),
                              with_blocks(middle, dimension, blocks, nodes_count),
                              with_blocks(right_part, dimension, blocks, 1)], axis=dimension + 1)
    new_shape = list(padded.shape)
    new_shape[dimension] = blocks * (nodes_count + 2)
    return joined.reshape(new_shape)


def restrict_axis(source, dimension, blocks, extent):
    shaped = with_blocks(source, dimension, blocks, extent)
    kept_part = lax.slice_in_dim(shaped, 1, extent - 1, axis=dimension + 1)
    new_shape = list(source.shape)
    new_shape[dimension] = blocks * (extent - 2)
    return kept_part.reshape(new_shape)


def fast_solve(extended, modes_first, modes_second, modes_third, eigen_first, eigen_second, eigen_third):
    spectral = modal_first(extended, modes_first, False)
    spectral = modal_second(spectral, modes_second, False)
    spectral = modal_third(spectral, modes_third, False)
    denominator = eigen_first.reshape(-1, 1, 1) + eigen_second.reshape(1, -1, 1) + eigen_third.reshape(1, 1, -1)
    spectral = spectral / denominator
    solved = modal_first(spectral, modes_first, True)
    solved = modal_second(solved, modes_second, True)
    return modal_third(solved, modes_third, True)


def reference(pressure, geo_diag, geo_off, modes_first, modes_second, modes_third, eigen_first, eigen_second,
              eigen_third):
    diff_matrix = jnp.asarray(derivative_table(N1), dtype=jnp.float32)
    local_product = local_laplacian(pressure, geo_diag, geo_off, diff_matrix)
    operator_out = owner_sum(local_product, 0, N1)
    padded = jnp.pad(operator_out, 2)
    extended = extend_axis(padded, 0, EX, N1)
    extended = extend_axis(extended, 1, EY, N1)
    extended = extend_axis(extended, 2, EZ, N1)
    solved = fast_solve(extended, modes_first, modes_second, modes_third, eigen_first, eigen_second, eigen_third)
    restricted = restrict_axis(solved, 0, EX, N1 + 2)
    restricted = restrict_axis(restricted, 1, EY, N1 + 2)
    restricted = restrict_axis(restricted, 2, EZ, N1 + 2)
    preconditioned = owner_sum(restricted, 0, N1)
    return (operator_out, preconditioned)
```

```python
import functools

import jax
import jax.numpy as jnp
import numpy as np
from jax import lax
from jax.experimental import pallas as pl
from jax.experimental.pallas import tpu as pltpu
from jax.sharding import PartitionSpec as P

N1 = 8
F32 = jnp.float32
BF16 = jnp.bfloat16
HIGHEST = lax.Precision.HIGHEST
VMEM = pl.BlockSpec(memory_space=pltpu.VMEM)


def legendre_values(nodes, degree):
    table = np.zeros((nodes.shape[0], degree + 1))
    table[:, 0] = 1.0
    table[:, 1] = nodes
    for order in range(2, degree + 1):
        table[:, order] = (
            (2 * order - 1) * nodes * table[:, order - 1] - (order - 1) * table[:, order - 2]
        ) / order
    return table


def derivative_table(points):
    degree = points - 1
    nodes = np.cos(np.pi * np.arange(points) / degree)
    for sweep in range(100):
        table = legendre_values(nodes, degree)
        nodes = nodes - (nodes * table[:, degree] - table[:, degree - 1]) / (
            points * table[:, degree]
        )
    gll_nodes = nodes[::-1]
    legendre_at = legendre_values(gll_nodes, degree)[:, degree]
    diff_table = np.zeros((points, points))
    for first_index in range(points):
        for second_index in range(points):
            if first_index != second_index:
                diff_table[first_index, second_index] = legendre_at[first_index] / (
                    legendre_at[second_index] * (gll_nodes[first_index] - gll_nodes[second_index])
                )
    diff_table[0, 0] = -degree * (degree + 1) / 4.0
    diff_table[degree, degree] = degree * (degree + 1) / 4.0
    return diff_table


def halves(table):
    table = np.asarray(table, np.float32)
    high = table.astype(jnp.bfloat16)
    return high, (table - high.astype(np.float32)).astype(jnp.bfloat16)


def operator_tables(blocks):
    diff = derivative_table(N1).astype(np.float32)
    eye = np.eye(N1, dtype=np.float32)
    both = np.concatenate([np.kron(diff, eye), np.kron(eye, diff)])
    third = np.kron(np.eye(blocks, dtype=np.float32), diff.T)
    high, low = halves(both)
    grad = np.concatenate([high, high, low], 1)
    high, low = halves(both.T)
    back = np.concatenate([high, high, low], 1)
    high, low = halves(third)
    third_grad = np.concatenate([high, low, high], 0)
    high, low = halves(third.T)
    third_back = np.concatenate([high, low, high], 0)
    return grad, third_grad, back, third_back


def third_tables(blocks, modes):
    length = blocks * N1
    gather = np.zeros((length, modes, blocks), np.float32)
    for c in range(blocks):
        for o in range(N1):
            gather[c * N1 + o, o + 1, c] = 1
        if c > 0:
            gather[c * N1 - 1, 1, c] = 1
            gather[c * N1 - 2, 0, c] = 1
        if c < blocks - 1:
            gather[(c + 1) * N1, N1, c] = 1
            gather[(c + 1) * N1 + 1, N1 + 1, c] = 1
    inner = gather.copy()
    inner[:, 0] = 0
    inner[:, -1] = 0
    gather = gather.reshape(length, modes * blocks)
    inner = inner.reshape(length, modes * blocks)
    spread = np.tile(np.eye(modes, dtype=np.float32), (1, blocks))
    own = np.kron(np.eye(blocks, dtype=np.float32), np.ones((1, modes), np.float32))
    return gather.astype(jnp.bfloat16), inner.T.astype(jnp.bfloat16), spread, np.tile(own, (modes, 1)), own


def round_up(count, unit):
    return -(-count // unit) * unit


def box_tables(modes):
    pad = round_up(modes, 16)
    pairs = round_up(modes * modes, 16)
    pick_p = np.zeros((pairs, pad), np.float32)
    pick_q = np.zeros((pairs, pad), np.float32)
    for p in range(modes):
        for q in range(modes):
            pick_p[p * modes + q, p] = 1
            pick_q[p * modes + q, q] = 1
    layers = N1 + 4
    node_of = [0] + [1 + i for i in range(N1)] + [modes - 1]
    node_of = [0, 1] + [1 + i for i in range(N1)] + [N1, N1 + 1]
    own_m = np.zeros((pad, layers * N1), np.float32)
    own_n = np.zeros((pad, layers * N1), np.float32)
    for l in range(layers):
        for y in range(N1):
            own_m[node_of[l], l * N1 + y] = 1
            own_n[y + 1, l * N1 + y] = 1
    kinds = [0, 1, N1, N1 + 1]
    rim_m = np.zeros((pad, 4 * 16), np.float32)
    rim_n = np.zeros((pad, 4 * 16), np.float32)
    for k in range(4):
        for l in range(layers):
            rim_m[node_of[l], k * 16 + l] = 1
            rim_n[kinds[k], k * 16 + l] = 1
    lay_m = np.concatenate([own_m] * 3 + [rim_m] * 3, 1)
    lay_n = np.concatenate([own_n] * 3 + [rim_n] * 3, 1)
    row_m = np.zeros((N1 * N1, pad), np.float32)
    row_n = np.zeros((N1 * N1, pad), np.float32)
    for i in range(N1):
        for y in range(N1):
            row_m[i * N1 + y, i + 1] = 1
            row_n[i * N1 + y, y + 1] = 1
    wide = lambda t: np.concatenate([t] * 3, 1).astype(jnp.bfloat16)
    return dict(
        pick_p=pick_p,
        pick_q=pick_q,
        pick_p3=wide(pick_p),
        pick_q3=wide(pick_q),
        lay_m=lay_m,
        lay_n=lay_n,
        row_m3=wide(row_m),
        row_n3=wide(row_n),
        pick_pt=np.concatenate([pick_p.T] * 3, 1),
        pick_qt=np.concatenate([pick_q.T] * 3, 1),
    )


def dot(left, right, dims=((1,), (0,)), precision=None):
    return lax.dot_general(
        left, right, (dims, ((), ())), precision=precision, preferred_element_type=F32
    )


def split(value):
    high = value.astype(BF16)
    return high, (value - high.astype(F32)).astype(BF16)


def split3(value):
    high = value.astype(BF16)
    rest = value - high.astype(F32)
    mid = rest.astype(BF16)
    return high, mid, (rest - mid.astype(F32)).astype(BF16)


def stacked(value):
    high, low = split(value)
    return jnp.concatenate([high, low, high], 0)


def abreast(value):
    high, low = split(value)
    return jnp.concatenate([high, high, low], 1)


def even(index):
    return lax.rem(index, 2) == 0


def local_kernel(
    p_ref, gd_ref, go_ref, mf_ref, ef_ref, grad_ref, third_ref, back_ref, third_back_ref,
    lp_ref, near_ref, far_ref,
):
    layers, rows, width = p_ref.shape
    first_blocks = layers // N1
    box = N1 * rows
    modes = mf_ref.shape[0]
    halo = modes * rows
    p_all = p_ref[...].reshape(layers * rows, width)
    third = dot(abreast(p_all), third_ref[...])
    for a in range(first_blocks):
        here = slice(a * box, (a + 1) * box)
        grads = dot(grad_ref[...], stacked(p_all[here]))
        one, two, three = grads[:box], grads[box:], third[here]
        g = [
            gd_ref[k, a * N1 : (a + 1) * N1].reshape(box, width) for k in range(3)
        ] + [go_ref[k, a * N1 : (a + 1) * N1].reshape(box, width) for k in range(3)]
        flux_one = g[0] * one + g[3] * two + g[4] * three
        flux_two = g[3] * one + g[1] * two + g[5] * three
        flux_three = g[4] * one + g[5] * two + g[2] * three
        lp_ref[here, :] = dot(
            back_ref[...], stacked(jnp.concatenate([flux_one, flux_two], 0))
        ) + dot(abreast(flux_three), third_back_ref[...])
    forward = even(lax.axis_index("stream"))
    last = layers * rows - halo
    for ref, up in ((near_ref, forward), (far_ref, jnp.logical_not(forward))):
        start = pl.multiple_of(jnp.where(up, last, 0), 8)
        ref[:halo, :] = lp_ref[pl.ds(start, halo), :]
        ref[halo:, :] = jnp.zeros((ref.shape[0] - halo, width), F32)
        ref[halo : halo + modes, :modes] = jnp.where(
            up, mf_ref[:, first_blocks - 1, :], mf_ref[:, 0, :]
        )
        ref[halo + 16 : halo + 17, :modes] = jnp.where(
            up, ef_ref[first_blocks - 1 : first_blocks, :], ef_ref[0:1, :]
        )


def from_sides(near, far, axis):
    index = lax.axis_index(axis)
    is_even = even(index)
    before = jnp.where(is_even, far, near)
    after = jnp.where(is_even, near, far)
    before = jnp.where(index == 0, 0.0, before)
    after = jnp.where(index == lax.axis_size(axis) - 1, 0.0, after)
    return before, after


def rows_kernel(lp_ref, near_ref, far_ref, out_near_ref, out_far_ref):
    rows = N1
    layers = lp_ref.shape[0] // rows
    halo = 10
    padded = out_near_ref.shape[0] // 2
    tail = padded - layers - 2 * halo
    width = lp_ref.shape[1]
    found = {}
    for k in (0, 1, rows - 2, rows - 1):
        before, after = from_sides(
            near_ref[pl.ds(k, halo, stride=rows), :], far_ref[pl.ds(k, halo, stride=rows), :], "stream"
        )
        found[k] = (before, lp_ref[pl.ds(k, layers, stride=rows), :], after)
    up = even(lax.axis_index("cross"))
    for ref, high in ((out_near_ref, up), (out_far_ref, jnp.logical_not(up))):
        for slot in range(2):
            base = slot * padded
            parts = [
                jnp.where(high, one, two) for one, two in zip(found[rows - 2 + slot], found[slot])
            ]
            ref[base : base + halo, :] = parts[0]
            ref[base + halo : base + halo + layers, :] = parts[1]
            ref[base + halo + layers : base + 2 * halo + layers, :] = parts[2]
            if tail:
                ref[base + 2 * halo + layers : base + padded, :] = jnp.zeros((tail, width), F32)


def third_kernel(mt_ref, e3_ref, gather_ref, inner_ref, spread_ref, own_ref, own_row_ref, w_ref, wbh_ref, wbl_ref, e3_row_ref):
    kron = dot(mt_ref[...], spread_ref[...], precision=HIGHEST) * own_ref[...]
    parts = split3(kron)
    table = sum(dot(gather_ref[...], part) for part in parts)
    high, low = split(table)
    w_ref[...] = jnp.concatenate([high, low, high], 0)
    table = sum(dot(part, inner_ref[...], ((0,), (0,))) for part in parts)
    high, low = split(table)
    wbh_ref[...] = high
    wbl_ref[...] = low
    e3_row_ref[...] = jnp.sum(
        dot(e3_ref[...], spread_ref[...], precision=HIGHEST) * own_row_ref[...], 0, keepdims=True
    )


def columns_kernel(
    lp_ref, near_ref, far_ref, mf_ref, ef_ref, ms_ref, es_ref, e3_row_ref, w_ref,
    pick_p_ref, pick_q_ref, pick_p3_ref, pick_q3_ref, lay_m_ref, lay_n_ref, row_m3_ref, row_n3_ref,
    pick_pt_ref, pick_qt_ref,
    v_ref, rim_ref, rec_ref, b_ref,
    pad_ref, stack_ref,
):
    rows = N1
    modes = ms_ref.shape[0]
    halo = modes * rows
    own_rows = lp_ref.shape[0]
    first_blocks = own_rows // (N1 * rows)
    pairs = pick_p_ref.shape[0]
    pad = pick_p_ref.shape[1]
    kin = (N1 + 4) * rows
    near, far = near_ref[...], far_ref[...]
    before, after = from_sides(near, far, "stream")
    odd = jnp.logical_not(even(lax.axis_index("stream")))
    stack_ref[:halo, :] = before[:halo]
    stack_ref[halo : halo + own_rows, :] = lp_ref[...]
    stack_ref[halo + own_rows :, :] = after[:halo]
    u = dot(abreast(stack_ref[...]), w_ref[...])

    pad_ref[...] = jnp.zeros_like(pad_ref)
    for a in range(first_blocks):
        pad_ref[a, :modes, :modes] = mf_ref[:, a, :]
    pad_ref[first_blocks, :modes, :modes] = ms_ref[...]
    mode_list = [before[halo : halo + pad, :pad]]
    mode_list += [pad_ref[a] for a in range(first_blocks)]
    mode_list += [after[halo : halo + pad, :pad]]
    second = pad_ref[first_blocks]
    pad_ref[first_blocks, 0:1, :modes] = es_ref[...]
    pad_ref[first_blocks, 1 : 1 + first_blocks, :modes] = ef_ref[...]
    edge_near, edge_far = near[halo + 16 : halo + 17, :pad], far[halo + 16 : halo + 17, :pad]
    eigen_list = [jnp.where(odd, edge_near, edge_far)]
    eigen_list += [pad_ref[first_blocks, 1 + a : 2 + a, :] for a in range(first_blocks)]
    eigen_list += [jnp.where(odd, edge_far, edge_near)]
    second_eigen = pad_ref[first_blocks, 0:1, :]

    lane = lax.broadcasted_iota(jnp.int32, (1, lay_m_ref.shape[1]), 1)
    low_lane = ((lane >= 2 * kin) & (lane < 3 * kin)) | (lane >= 3 * kin + 128)
    back_lane = lax.broadcasted_iota(jnp.int32, (1, pick_pt_ref.shape[1]), 1) >= 2 * pairs

    def spread_columns(table, lay_ref, pick_ref):
        parts = split3(dot(table, lay_ref[...], ((0,), (0,)), HIGHEST))
        return dot(pick_ref[...], jnp.concatenate(parts, 0))

    def spread_rows(table, pick_ref, row_ref):
        parts = split3(dot(table, pick_ref[...], precision=HIGHEST))
        return dot(row_ref[...], jnp.concatenate(parts, 0))

    def halves_by_lane(value, low):
        high = value.astype(BF16).astype(F32)
        return jnp.where(low, value - high, high).astype(BF16)

    second_columns = spread_columns(second, lay_n_ref, pick_q3_ref)
    second_rows = spread_rows(second, pick_qt_ref, row_n3_ref)
    second_sum = jnp.sum(pick_q_ref[...] * second_eigen, 1, keepdims=True)
    for a, (table, eigen) in enumerate(zip(mode_list, eigen_list)):
        columns = halves_by_lane(
            spread_columns(table, lay_m_ref, pick_p3_ref) * second_columns, low_lane
        )
        rim_ref[a] = columns[:, 3 * kin :]
        b_ref[a] = halves_by_lane(
            spread_rows(table, pick_pt_ref, row_m3_ref) * second_rows, back_lane
        )
        total = jnp.sum(pick_p_ref[...] * eigen, 1, keepdims=True) + second_sum
        rec_ref[a] = 1.0 / (total + e3_row_ref[...])
        begin = a * N1 * rows
        v_ref[a] = dot(columns[:, : 3 * kin], stacked(u[begin : begin + kin]))


def solve_kernel(near_ref, far_ref, w_ref, wbh_ref, wbl_ref, v_ref, rim_ref, rec_ref, b_ref, r_ref, out_near_ref, out_far_ref):
    rows = N1
    columns = v_ref.shape[0]
    padded = near_ref.shape[0] // 2
    box = N1 * rows
    before, after = from_sides(near_ref[...], far_ref[...], "cross")
    u = dot(abreast(jnp.concatenate([before, after], 0)), w_ref[...])
    parts = []
    for a in range(columns):
        rim = jnp.concatenate(
            [u[k * padded + a * N1 : k * padded + a * N1 + 16] for k in range(4)], 0
        )
        spectral = (v_ref[a] + dot(rim_ref[a], stacked(rim))) * rec_ref[a]
        if a == 0:
            parts.append(dot(b_ref[a, box - 16 : box], stacked(spectral))[16 - rows :])
        elif a == columns - 1:
            parts.append(dot(b_ref[a, :16], stacked(spectral))[:rows])
        else:
            parts.append(dot(b_ref[a], stacked(spectral)))
    high, low = split(jnp.concatenate(parts, 0))
    solved = dot(high, wbh_ref[...]) + dot(high, wbl_ref[...]) + dot(low, wbh_ref[...])
    for a in range(columns - 2):
        base = rows + a * box
        top, bottom = solved[base : base + rows], solved[base + box - rows : base + box]
        r_ref[a * box : a * box + rows, :] = top + solved[base - rows : base]
        r_ref[a * box + rows : (a + 1) * box - rows, :] = solved[base + rows : base + box - rows]
        r_ref[(a + 1) * box - rows : (a + 1) * box, :] = bottom + solved[base + box : base + box + rows]
    layers = r_ref.shape[0] // rows
    low_row = r_ref[pl.ds(0, layers, stride=rows), :]
    high_row = r_ref[pl.ds(rows - 1, layers, stride=rows), :]
    up = even(lax.axis_index("cross"))
    out_near_ref[...] = jnp.where(up, high_row, low_row)
    out_far_ref[...] = jnp.where(up, low_row, high_row)


def operator_kernel(lp_ref, s_near_ref, s_far_ref, c_near_ref, c_far_ref, out_ref, acc_ref):
    rows = N1
    total_rows, width = lp_ref.shape
    layers = total_rows // rows
    halo = 10
    padded = c_near_ref.shape[0] // 2
    before, after = from_sides(s_near_ref[: halo * rows, :], s_far_ref[: halo * rows, :], "stream")
    left, right = from_sides(c_near_ref[...], c_far_ref[...], "cross")
    acc_ref[...] = jnp.zeros_like(acc_ref)
    acc_ref[: layers * rows, :] = lp_ref[...]
    pads = (layers + 2) * rows
    stack = jnp.concatenate([before[(halo - 1) * rows :], lp_ref[...], after[:rows]], 0)
    acc_ref[...] = stack
    low = acc_ref[pl.ds(0, layers + 2, stride=rows), :]
    high = acc_ref[pl.ds(rows - 1, layers + 2, stride=rows), :]
    acc_ref[pl.ds(0, layers + 2, stride=rows), :] = (
        low + left[padded + halo - 1 : padded + halo + layers + 1]
    )
    acc_ref[pl.ds(rows - 1, layers + 2, stride=rows), :] = (
        high + right[halo - 1 : halo + layers + 1]
    )
    box = N1 * rows
    lane = lax.broadcasted_iota(jnp.int32, (1, width), 1)
    first = (lax.rem(lane, N1) == 0) & (lane > 0)
    final = (lax.rem(lane, N1) == N1 - 1) & (lane < width - 1)
    for a in range(layers // N1):
        base = rows + a * box
        for i in range(N1):
            at = base + i * rows
            value = acc_ref[at : at + rows, :]
            if i == 0:
                value = value + acc_ref[at - rows : at, :]
            if i == N1 - 1:
                value = value + acc_ref[at + rows : at + 2 * rows, :]
            value = (
                value
                + jnp.where(first, pltpu.roll(value, 1, 1), 0.0)
                + jnp.where(final, pltpu.roll(value, width - 1, 1), 0.0)
            )
            out_ref[a * N1 + i] = value


def add_kernel(r_ref, near_ref, far_ref, out_ref, acc_ref):
    rows = N1
    layers = r_ref.shape[0] // rows
    before, after = from_sides(near_ref[...], far_ref[...], "cross")
    acc_ref[...] = r_ref[...]
    low = pl.ds(0, layers, stride=rows)
    high = pl.ds(rows - 1, layers, stride=rows)
    acc_ref[low, :] = acc_ref[low, :] + before
    acc_ref[high, :] = acc_ref[high, :] + after
    out_ref[...] = acc_ref[...].reshape(out_ref.shape)


def shape(*dims, dtype=F32):
    return jax.ShapeDtypeStruct(dims, dtype)


def call(kernel, name, out, *args, scratch=(), out_specs=None, flops=1000000):
    single = isinstance(out, jax.ShapeDtypeStruct)
    return pl.pallas_call(
        kernel,
        out_shape=out,
        in_specs=[VMEM] * len(args),
        out_specs=out_specs if out_specs is not None else (VMEM if single else [VMEM] * len(out)),
        scratch_shapes=list(scratch),
        cost_estimate=pl.CostEstimate(flops=flops, bytes_accessed=flops, transcendentals=0),
        name=name,
    )(*args)


def swaps(axis):
    count = lax.axis_size(axis)
    near = [(i, i ^ 1) for i in range(count)]
    far = [(i, (i - 1) % count if i % 2 == 0 else (i + 1) % count) for i in range(count)]
    return near, far


def swap_stream(near, far):
    first, second = swaps("stream")
    far = lax.ppermute(far, "stream", second)
    near = lax.ppermute(near, "stream", first)
    return near, far


def swap_cross(near, far):
    count, streams = lax.axis_size("cross"), lax.axis_size("stream")
    first, second = swaps("cross")
    pairs = []
    for s in range(streams):
        for i, j in second:
            wrapped = {i, j} == {0, count - 1}
            pairs.append((s * count + i, (s ^ 1) * count + i if wrapped else s * count + j))
    far = lax.ppermute(far, ("stream", "cross"), pairs)
    near = lax.ppermute(near, "cross", first)
    return near, far


def shards(
    pressure, geo_diag, geo_off, modes_first, modes_second, modes_third, eigen_first, eigen_second,
    eigen_third,
):
    layers, rows, width = pressure.shape
    modes = modes_first.shape[1]
    if rows != N1 or modes != N1 + 2 or lax.axis_size("stream") % 2 or lax.axis_size("cross") % 2:
        raise ValueError("unsupported sizes")
    first_blocks, third_blocks = layers // N1, width // N1
    columns = first_blocks + 2
    halo = modes * rows
    box = N1 * rows
    padded = (first_blocks + 3) * N1
    wide = third_blocks * modes

    grad, third_grad, back, third_back = operator_tables(third_blocks)
    gather, inner, spread, own, own_row = third_tables(third_blocks, modes)
    tables = box_tables(modes)
    pairs, pad = tables["pick_p"].shape
    rim_width = 3 * 64

    mf = jnp.transpose(modes_first, (1, 0, 2))
    ms = modes_second[0]
    mt = jnp.transpose(modes_third, (1, 0, 2)).reshape(modes * third_blocks, modes)

    lp, s_near, s_far = call(
        local_kernel, "local_product",
        [shape(layers * rows, width), shape(halo + 24, width), shape(halo + 24, width)],
        pressure, geo_diag, geo_off, mf, eigen_first, grad, third_grad, back, third_back,
    )
    s_near, s_far = swap_stream(s_near, s_far)
    w, wbh, wbl, e3_row = call(
        third_kernel, "third_modes",
        [
            shape(3 * width, wide, dtype=BF16), shape(wide, width, dtype=BF16),
            shape(wide, width, dtype=BF16), shape(1, wide),
        ],
        mt, eigen_third, gather, inner, spread, own, own_row,
    )
    c_near, c_far = call(
        rows_kernel, "rows_to_send",
        [shape(2 * padded, width), shape(2 * padded, width)],
        lp, s_near, s_far,
    )
    c_near, c_far = swap_cross(c_near, c_far)
    v, rim, rec, b = call(
        columns_kernel, "own_part",
        [
            shape(columns, pairs, wide), shape(columns, pairs, rim_width, dtype=BF16),
            shape(columns, pairs, wide), shape(columns, box, 3 * pairs, dtype=BF16),
        ],
        lp, s_near, s_far, mf, eigen_first, ms, eigen_second, e3_row, w,
        *[tables[k] for k in (
            "pick_p", "pick_q", "pick_p3", "pick_q3", "lay_m", "lay_n", "row_m3", "row_n3", "pick_pt", "pick_qt",
        )],
        scratch=[
            pltpu.VMEM((first_blocks + 1, pad, pad), F32),
            pltpu.VMEM((layers * rows + 2 * halo, width), F32),
        ],
    )
    restricted, f_near, f_far = call(
        solve_kernel, "solve",
        [shape(layers * rows, width), shape(layers, width), shape(layers, width)],
        c_near, c_far, w, wbh, wbl, v, rim, rec, b,
    )
    f_near, f_far = swap_cross(f_near, f_far)
    whole = pl.BlockSpec((layers, rows, width), lambda: (0, 0, 0))
    operator_out = call(
        operator_kernel, "operator_out", shape(layers, rows, width),
        lp, s_near, s_far, c_near, c_far, out_specs=whole,
        scratch=[pltpu.VMEM(((layers + 2) * rows, width), F32)],
    )
    preconditioned = call(
        add_kernel, "preconditioned", shape(layers, rows, width), restricted, f_near, f_far, out_specs=whole,
        scratch=[pltpu.VMEM((layers * rows, width), F32)],
    )
    return (operator_out, preconditioned)


def solution(mesh):
    in_specs = (
        P("stream", "cross", None),
        P(None, "stream", "cross", None),
        P(None, "stream", "cross", None),
        P("stream", None, None),
        P("cross", None, None),
        P(),
        P("stream", None),
        P("cross", None),
        P(),
    )
    out_specs = (P("stream", "cross", None), P("stream", "cross", None))
    return jax.shard_map(shards, mesh=mesh, in_specs=in_specs, out_specs=out_specs, check_vma=False)
```

```python
import functools

import jax
import jax.numpy as jnp
import numpy as np
from jax import lax
from jax.experimental import pallas as pl
from jax.experimental.pallas import tpu as pltpu
from jax.sharding import PartitionSpec as P

N1 = 8
F32 = jnp.float32
BF16 = jnp.bfloat16
HIGHEST = lax.Precision.HIGHEST
VMEM_LIMIT = 16 * 2**20
VMEM = pl.BlockSpec(memory_space=pltpu.VMEM)


def legendre_values(nodes, degree):
    table = np.zeros((nodes.shape[0], degree + 1))
    table[:, 0] = 1.0
    table[:, 1] = nodes
    for order in range(2, degree + 1):
        table[:, order] = (
            (2 * order - 1) * nodes * table[:, order - 1] - (order - 1) * table[:, order - 2]
        ) / order
    return table


def derivative_table(points):
    degree = points - 1
    nodes = np.cos(np.pi * np.arange(points) / degree)
    for sweep in range(100):
        table = legendre_values(nodes, degree)
        nodes = nodes - (nodes * table[:, degree] - table[:, degree - 1]) / (
            points * table[:, degree]
        )
    gll_nodes = nodes[::-1]
    legendre_at = legendre_values(gll_nodes, degree)[:, degree]
    diff_table = np.zeros((points, points))
    for first_index in range(points):
        for second_index in range(points):
            if first_index != second_index:
                diff_table[first_index, second_index] = legendre_at[first_index] / (
                    legendre_at[second_index] * (gll_nodes[first_index] - gll_nodes[second_index])
                )
    diff_table[0, 0] = -degree * (degree + 1) / 4.0
    diff_table[degree, degree] = degree * (degree + 1) / 4.0
    return diff_table


def halves(table):
    table = np.asarray(table, np.float32)
    high = table.astype(jnp.bfloat16)
    return high, (table - high.astype(np.float32)).astype(jnp.bfloat16)


def operator_tables(blocks):
    diff = derivative_table(N1).astype(np.float32)
    eye = np.eye(N1, dtype=np.float32)
    both = np.concatenate([np.kron(diff, eye), np.kron(eye, diff)])
    third = np.kron(np.eye(blocks, dtype=np.float32), diff.T)
    high, low = halves(both)
    grad = np.concatenate([high, high, low], 1)
    high, low = halves(both.T)
    back = np.concatenate([high, high, low], 1)
    high, low = halves(third)
    third_grad = np.concatenate([high, low, high], 0)
    high, low = halves(third.T)
    third_back = np.concatenate([high, low, high], 0)
    return grad, third_grad, back, third_back


def third_tables(blocks, modes):
    length = blocks * N1
    gather = np.zeros((length, modes, blocks), np.float32)
    for c in range(blocks):
        for o in range(N1):
            gather[c * N1 + o, o + 1, c] = 1
        if c > 0:
            gather[c * N1 - 1, 1, c] = 1
            gather[c * N1 - 2, 0, c] = 1
        if c < blocks - 1:
            gather[(c + 1) * N1, N1, c] = 1
            gather[(c + 1) * N1 + 1, N1 + 1, c] = 1
    inner = gather.copy()
    inner[:, 0] = 0
    inner[:, -1] = 0
    gather = gather.reshape(length, modes * blocks)
    inner = inner.reshape(length, modes * blocks)
    spread = np.tile(np.eye(modes, dtype=np.float32), (1, blocks))
    own = np.kron(np.eye(blocks, dtype=np.float32), np.ones((1, modes), np.float32))
    return gather.astype(jnp.bfloat16), inner.T.astype(jnp.bfloat16), spread, np.tile(own, (modes, 1)), own


def round_up(count, unit):
    return -(-count // unit) * unit


def box_tables(modes):
    pad = round_up(modes, 16)
    pairs = round_up(modes * modes, 16)
    pick_p = np.zeros((pairs, pad), np.float32)
    pick_q = np.zeros((pairs, pad), np.float32)
    for p in range(modes):
        for q in range(modes):
            pick_p[p * modes + q, p] = 1
            pick_q[p * modes + q, q] = 1
    layers = N1 + 4
    node_of = [0, 1] + [1 + i for i in range(N1)] + [N1, N1 + 1]
    own_m = np.zeros((pad, layers * N1), np.float32)
    own_n = np.zeros((pad, layers * N1), np.float32)
    for l in range(layers):
        for y in range(N1):
            own_m[node_of[l], l * N1 + y] = 1
            own_n[y + 1, l * N1 + y] = 1
    kinds = [0, 1, N1, N1 + 1]
    rim_m = np.zeros((pad, 4 * 16), np.float32)
    rim_n = np.zeros((pad, 4 * 16), np.float32)
    for k in range(4):
        for l in range(layers):
            rim_m[node_of[l], k * 16 + l] = 1
            rim_n[kinds[k], k * 16 + l] = 1
    lay_m = np.concatenate([own_m] * 3 + [rim_m] * 3, 1)
    lay_n = np.concatenate([own_n] * 3 + [rim_n] * 3, 1)
    row_m = np.zeros((N1 * N1, pad), np.float32)
    row_n = np.zeros((N1 * N1, pad), np.float32)
    for i in range(N1):
        for y in range(N1):
            row_m[i * N1 + y, i + 1] = 1
            row_n[i * N1 + y, y + 1] = 1
    wide = lambda t: np.concatenate([t] * 3, 1).astype(jnp.bfloat16)
    return dict(
        pick_p=pick_p,
        pick_q=pick_q,
        pick_p3=wide(pick_p),
        pick_q3=wide(pick_q),
        lay_m=np.concatenate([lay_m] * 3, 0).astype(jnp.bfloat16),
        lay_n=np.concatenate([lay_n] * 3, 0).astype(jnp.bfloat16),
        row_m3=wide(row_m),
        row_n3=wide(row_n),
        pick_pt=wide(pick_p.T),
        pick_qt=wide(pick_q.T),
    )


def dot(left, right, dims=((1,), (0,)), precision=None):
    return lax.dot_general(
        left, right, (dims, ((), ())), precision=precision, preferred_element_type=F32
    )


def split(value):
    high = value.astype(BF16)
    return high, (value - high.astype(F32)).astype(BF16)


def split3(value):
    high = value.astype(BF16)
    rest = value - high.astype(F32)
    mid = rest.astype(BF16)
    return high, mid, (rest - mid.astype(F32)).astype(BF16)


def stacked(value):
    high, low = split(value)
    return jnp.concatenate([high, low, high], 0)


def abreast(value):
    high, low = split(value)
    return jnp.concatenate([high, high, low], 1)


def even(index):
    return lax.rem(index, 2) == 0


def local_kernel(*refs):
    count = 9
    sources, outs, scratch = refs[:count], refs[count : count + 3], refs[count + 3 :]
    lp_ref, near_ref, far_ref = outs
    p_ref, gd_ref, go_ref, mf_ref, ef_ref, grad_ref, third_ref, back_ref, third_back_ref = scratch[:count]
    copies = [
        pltpu.make_async_copy(source, target, scratch[count].at[k])
        for k, (source, target) in enumerate(zip(sources, scratch))
    ]
    for k in (0, 6, 5, 1, 2, 7, 8, 3, 4):
        copies[k].start()
    layers, rows, width = p_ref.shape
    for k in (0, 6, 5):
        copies[k].wait()
    first_blocks = layers // N1
    box = N1 * rows
    modes = mf_ref.shape[0]
    halo = modes * rows
    p_all = p_ref[...].reshape(layers * rows, width)
    third = dot(abreast(p_all), third_ref[...])
    grads = [
        dot(grad_ref[...], stacked(p_all[a * box : (a + 1) * box])) for a in range(first_blocks)
    ]
    for k in (1, 2, 7, 8):
        copies[k].wait()
    for a in range(first_blocks):
        here = slice(a * box, (a + 1) * box)
        one, two, three = grads[a][:box], grads[a][box:], third[here]
        g = [
            gd_ref[k, a * N1 : (a + 1) * N1].reshape(box, width) for k in range(3)
        ] + [go_ref[k, a * N1 : (a + 1) * N1].reshape(box, width) for k in range(3)]
        flux_one = g[0] * one + g[3] * two + g[4] * three
        flux_two = g[3] * one + g[1] * two + g[5] * three
        flux_three = g[4] * one + g[5] * two + g[2] * three
        lp_ref[here, :] = dot(
            back_ref[...], stacked(jnp.concatenate([flux_one, flux_two], 0))
        ) + dot(abreast(flux_three), third_back_ref[...])
    for k in (3, 4):
        copies[k].wait()
    forward = even(lax.axis_index("stream"))
    last = layers * rows - halo
    for ref, up in ((near_ref, forward), (far_ref, jnp.logical_not(forward))):
        start = pl.multiple_of(jnp.where(up, last, 0), 8)
        ref[:halo, :] = lp_ref[pl.ds(start, halo), :]
        ref[halo:, :] = jnp.zeros((ref.shape[0] - halo, width), F32)
        ref[halo : halo + modes, :modes] = jnp.where(
            up, mf_ref[:, first_blocks - 1, :], mf_ref[:, 0, :]
        )
        ref[halo + 16 : halo + 17, :modes] = jnp.where(
            up, ef_ref[first_blocks - 1 : first_blocks, :], ef_ref[0:1, :]
        )


def from_sides(near, far, axis):
    index = lax.axis_index(axis)
    is_even = even(index)
    before = jnp.where(is_even, far, near)
    after = jnp.where(is_even, near, far)
    before = jnp.where(index == 0, 0.0, before)
    after = jnp.where(index == lax.axis_size(axis) - 1, 0.0, after)
    return before, after


def rows_kernel(lp_ref, near_ref, far_ref, done_ref, out_near_ref, out_far_ref):
    rows = N1
    layers = lp_ref.shape[0] // rows
    halo = 10
    padded = out_near_ref.shape[0] // 2
    tail = padded - layers - 2 * halo
    width = lp_ref.shape[1]
    found = {}
    for k in (0, 1, rows - 2, rows - 1):
        before, after = from_sides(
            near_ref[pl.ds(k, halo, stride=rows), :], far_ref[pl.ds(k, halo, stride=rows), :], "stream"
        )
        found[k] = (before, lp_ref[pl.ds(k, layers, stride=rows), :], after)
    up = even(lax.axis_index("cross"))
    for ref, high in ((out_near_ref, up), (out_far_ref, jnp.logical_not(up))):
        for slot in range(2):
            base = slot * padded
            parts = [
                jnp.where(high, one, two) for one, two in zip(found[rows - 2 + slot], found[slot])
            ]
            ref[base : base + halo, :] = parts[0]
            ref[base + halo : base + halo + layers, :] = parts[1]
            ref[base + halo + layers : base + 2 * halo + layers, :] = parts[2]
            if tail:
                ref[base + 2 * halo + layers : base + padded, :] = jnp.zeros((tail, width), F32)


def spread_columns(parts, lay_ref, pick_ref):
    table = dot(parts, lay_ref[...], ((0,), (0,)))
    return dot(pick_ref[...], jnp.concatenate(split3(table), 0))


def spread_rows(parts, pick_ref, row_ref):
    pad = parts.shape[0] // 3
    table = sum(dot(parts[k * pad : (k + 1) * pad], pick_ref[...]) for k in range(3))
    return dot(row_ref[...], jnp.concatenate(split3(table), 0))


def halves_by_lane(value, low):
    high = value.astype(BF16).astype(F32)
    return jnp.where(low, value - high, high).astype(BF16)


def low_lanes(columns_ref, rows_ref, kin):
    wide, pairs = columns_ref.shape[1], rows_ref.shape[1] // 3
    lane = lax.broadcasted_iota(jnp.int32, (1, wide), 1)
    rim = (wide - 3 * kin) // 3
    low = ((lane >= 2 * kin) & (lane < 3 * kin)) | (lane >= 3 * kin + 2 * rim)
    return low, lax.broadcasted_iota(jnp.int32, (1, 3 * pairs), 1) >= 2 * pairs


def modes_kernel(
    mt_ref, e3_ref, gather_ref, inner_ref, spread_ref, own_ref, own_row_ref,
    mf_ref, ef_ref, ms_ref, es_ref,
    pick_p_ref, pick_q_ref, pick_p3_ref, pick_q3_ref, lay_m_ref, lay_n_ref, row_m3_ref, row_n3_ref, pick_pt_ref, pick_qt_ref,
    w_ref, wbh_ref, wbl_ref, e3_row_ref, own_columns_ref, own_rim_ref, b_ref, rec_ref, second_columns_ref, second_rows_ref,
    second_sum_ref,
    pad_ref,
):
    spread = spread_ref[...].astype(BF16)
    parts = [
        (dot(part, spread) * own_ref[...]).astype(BF16) for part in split3(mt_ref[...])
    ]
    table = sum(dot(gather_ref[...], part) for part in parts)
    high, low = split(table)
    w_ref[...] = jnp.concatenate([high, low, high], 0)
    table = sum(dot(part, inner_ref[...], ((0,), (0,))) for part in parts)
    high, low = split(table)
    wbh_ref[...] = high
    wbl_ref[...] = low
    e3_row = jnp.sum(
        sum(dot(part, spread) for part in split3(e3_ref[...])) * own_row_ref[...], 0, keepdims=True
    )
    e3_row_ref[...] = e3_row

    modes = ms_ref.shape[0]
    first_blocks = rec_ref.shape[0]
    pad_ref[...] = jnp.zeros_like(pad_ref)
    for a in range(first_blocks):
        pad_ref[a, :modes, :modes] = mf_ref[:, a, :]
        pad_ref[first_blocks + 1, a : a + 1, :modes] = ef_ref[a : a + 1, :]
    pad_ref[first_blocks, :modes, :modes] = ms_ref[...]
    pad_ref[first_blocks + 1, first_blocks : first_blocks + 1, :modes] = es_ref[...]
    eigen = pad_ref[first_blocks + 1]
    kin = own_columns_ref.shape[2] // 3
    low, back_low = low_lanes(lay_m_ref, pick_pt_ref, kin)
    second = jnp.concatenate(split3(pad_ref[first_blocks]), 0)
    second_columns = spread_columns(second, lay_n_ref, pick_q3_ref)
    second_rows = spread_rows(second, pick_qt_ref, row_n3_ref)
    second_sum = jnp.sum(pick_q_ref[...] * eigen[first_blocks : first_blocks + 1], 1, keepdims=True)
    second_columns_ref[...] = second_columns
    second_rows_ref[...] = second_rows
    second_sum_ref[...] = second_sum
    for a in range(first_blocks):
        first = jnp.concatenate(split3(pad_ref[a]), 0)
        columns = halves_by_lane(spread_columns(first, lay_m_ref, pick_p3_ref) * second_columns, low)
        own_columns_ref[a] = columns[:, : 3 * kin]
        own_rim_ref[a] = columns[:, 3 * kin :]
        b_ref[a] = halves_by_lane(spread_rows(first, pick_pt_ref, row_m3_ref) * second_rows, back_low)
        total = jnp.sum(pick_p_ref[...] * eigen[a : a + 1], 1, keepdims=True) + second_sum
        rec_ref[a] = 1.0 / (total + e3_row)


def columns_kernel(
    lp_ref, near_ref, far_ref, w_ref, e3_row_ref, own_columns_ref, second_columns_ref, second_rows_ref, second_sum_ref,
    pick_p_ref, pick_p3_ref, lay_m_ref, row_m3_ref, pick_pt_ref,
    v_ref, side_rim_ref, side_b_ref, side_rec_ref,
    stack_ref,
):
    rows = N1
    halo = (N1 + 2) * rows
    own_rows = lp_ref.shape[0]
    first_blocks = own_columns_ref.shape[0]
    pad = pick_p_ref.shape[1]
    kin = own_columns_ref.shape[2] // 3
    box = N1 * rows
    near, far = near_ref[...], far_ref[...]
    before, after = from_sides(near, far, "stream")
    odd = jnp.logical_not(even(lax.axis_index("stream")))
    stack_ref[:halo, :] = before[:halo]
    stack_ref[halo : halo + own_rows, :] = lp_ref[...]
    stack_ref[halo + own_rows :, :] = after[:halo]
    u = dot(abreast(stack_ref[...]), w_ref[...])
    edge_near, edge_far = near[halo + 16 : halo + 17, :pad], far[halo + 16 : halo + 17, :pad]
    low, back_low = low_lanes(lay_m_ref, pick_pt_ref, kin)
    sides = (
        (0, before, jnp.where(odd, edge_near, edge_far), slice(box - 16, box), 0),
        (1, after, jnp.where(odd, edge_far, edge_near), slice(0, 16), first_blocks + 1),
    )
    for side, source, eigen, last_rows, place in sides:
        first = jnp.concatenate(split3(source[halo : halo + pad, :pad]), 0)
        columns = halves_by_lane(
            spread_columns(first, lay_m_ref, pick_p3_ref) * second_columns_ref[...], low
        )
        side_rim_ref[side] = columns[:, 3 * kin :]
        side_b_ref[side] = halves_by_lane(
            spread_rows(first, pick_pt_ref, row_m3_ref[last_rows]) * second_rows_ref[last_rows], back_low
        )
        total = jnp.sum(pick_p_ref[...] * eigen, 1, keepdims=True) + second_sum_ref[...]
        side_rec_ref[side] = 1.0 / (total + e3_row_ref[...])
        begin = place * box
        v_ref[place] = dot(columns[:, : 3 * kin], stacked(u[begin : begin + kin]))
    for a in range(first_blocks):
        begin = (a + 1) * box
        v_ref[a + 1] = dot(own_columns_ref[a], stacked(u[begin : begin + kin]))


def solve_kernel(
    near_ref, far_ref, w_ref, wbh_ref, wbl_ref, v_ref, own_rim_ref, own_rec_ref, own_b_ref, side_rim_ref, side_rec_ref,
    side_b_ref, r_ref, out_near_ref, out_far_ref,
):
    rows = N1
    columns = v_ref.shape[0]
    padded = near_ref.shape[0] // 2
    box = N1 * rows
    before, after = from_sides(near_ref[...], far_ref[...], "cross")
    u = dot(abreast(jnp.concatenate([before, after], 0)), w_ref[...])
    parts = []
    for a in range(columns):
        rim = jnp.concatenate(
            [u[k * padded + a * N1 : k * padded + a * N1 + 16] for k in range(4)], 0
        )
        if a in (0, columns - 1):
            rim_ref, rec_ref, b_ref, at = side_rim_ref, side_rec_ref, side_b_ref, min(a, 1)
        else:
            rim_ref, rec_ref, b_ref, at = own_rim_ref, own_rec_ref, own_b_ref, a - 1
        spectral = (v_ref[a] + dot(rim_ref[at], stacked(rim))) * rec_ref[at]
        solved = dot(b_ref[at], stacked(spectral))
        if a == 0:
            solved = solved[16 - rows :]
        elif a == columns - 1:
            solved = solved[:rows]
        parts.append(solved)
    high, low = split(jnp.concatenate(parts, 0))
    solved = dot(high, wbh_ref[...]) + dot(high, wbl_ref[...]) + dot(low, wbh_ref[...])
    for a in range(columns - 2):
        base = rows + a * box
        top, bottom = solved[base : base + rows], solved[base + box - rows : base + box]
        r_ref[a * box : a * box + rows, :] = top + solved[base - rows : base]
        r_ref[a * box + rows : (a + 1) * box - rows, :] = solved[base + rows : base + box - rows]
        r_ref[(a + 1) * box - rows : (a + 1) * box, :] = bottom + solved[base + box : base + box + rows]
    layers = r_ref.shape[0] // rows
    low_row = r_ref[pl.ds(0, layers, stride=rows), :]
    high_row = r_ref[pl.ds(rows - 1, layers, stride=rows), :]
    up = even(lax.axis_index("cross"))
    out_near_ref[...] = jnp.where(up, high_row, low_row)
    out_far_ref[...] = jnp.where(up, low_row, high_row)


def operator_kernel(lp_ref, s_near_ref, s_far_ref, c_near_ref, c_far_ref, out_ref, acc_ref):
    rows = N1
    total_rows, width = lp_ref.shape
    layers = total_rows // rows
    halo = 10
    padded = c_near_ref.shape[0] // 2
    before, after = from_sides(s_near_ref[: halo * rows, :], s_far_ref[: halo * rows, :], "stream")
    left, right = from_sides(c_near_ref[...], c_far_ref[...], "cross")
    stack = jnp.concatenate([before[(halo - 1) * rows :], lp_ref[...], after[:rows]], 0)
    acc_ref[...] = stack
    low = acc_ref[pl.ds(0, layers + 2, stride=rows), :]
    high = acc_ref[pl.ds(rows - 1, layers + 2, stride=rows), :]
    acc_ref[pl.ds(0, layers + 2, stride=rows), :] = (
        low + left[padded + halo - 1 : padded + halo + layers + 1]
    )
    acc_ref[pl.ds(rows - 1, layers + 2, stride=rows), :] = (
        high + right[halo - 1 : halo + layers + 1]
    )
    box = N1 * rows
    lane = lax.broadcasted_iota(jnp.int32, (1, width), 1)
    first = (lax.rem(lane, N1) == 0) & (lane > 0)
    final = (lax.rem(lane, N1) == N1 - 1) & (lane < width - 1)
    for a in range(layers // N1):
        base = rows + a * box
        for i in range(N1):
            at = base + i * rows
            value = acc_ref[at : at + rows, :]
            if i == 0:
                value = value + acc_ref[at - rows : at, :]
            if i == N1 - 1:
                value = value + acc_ref[at + rows : at + 2 * rows, :]
            value = (
                value
                + jnp.where(first, pltpu.roll(value, 1, 1), 0.0)
                + jnp.where(final, pltpu.roll(value, width - 1, 1), 0.0)
            )
            out_ref[a * N1 + i] = value


def add_kernel(r_ref, near_ref, far_ref, out_ref, acc_ref):
    rows = N1
    layers = r_ref.shape[0] // rows
    before, after = from_sides(near_ref[...], far_ref[...], "cross")
    acc_ref[...] = r_ref[...]
    low = pl.ds(0, layers, stride=rows)
    high = pl.ds(rows - 1, layers, stride=rows)
    acc_ref[low, :] = acc_ref[low, :] + before
    acc_ref[high, :] = acc_ref[high, :] + after
    out_ref[...] = acc_ref[...].reshape(out_ref.shape)


def shape(*dims, dtype=F32):
    return pltpu.VMEM(dims, dtype)


def call(kernel, name, out, *args, scratch=(), out_specs=None, flops=1000000, place=pltpu.VMEM):
    single = not isinstance(out, list)
    args = [pltpu.with_memory_space_constraint(x, place) for x in args]
    return pl.pallas_call(
        kernel,
        out_shape=out,
        in_specs=[pl.BlockSpec(memory_space=place)] * len(args),
        out_specs=out_specs if out_specs is not None else (VMEM if single else [VMEM] * len(out)),
        scratch_shapes=list(scratch),
        compiler_params=pltpu.CompilerParams(vmem_limit_bytes=VMEM_LIMIT),
        cost_estimate=pl.CostEstimate(flops=flops, bytes_accessed=flops, transcendentals=0),
        name=name,
    )(*args)


def swaps(axis):
    count = lax.axis_size(axis)
    near = [(i, i ^ 1) for i in range(count)]
    far = [(i, (i - 1) % count if i % 2 == 0 else (i + 1) % count) for i in range(count)]
    return near, far


def swap_stream(near, far):
    first, second = swaps("stream")
    near = lax.ppermute(near, "stream", first)
    far = lax.ppermute(far, "stream", second)
    return near, far


def swap_cross(near, far):
    count, streams = lax.axis_size("cross"), lax.axis_size("stream")
    first, second = swaps("cross")
    pairs = []
    for s in range(streams):
        for i, j in second:
            wrapped = {i, j} == {0, count - 1}
            pairs.append((s * count + i, (s ^ 1) * count + i if wrapped else s * count + j))
    near = lax.ppermute(near, "cross", first)
    far = lax.ppermute(far, ("stream", "cross"), pairs)
    return near, far


def shards(
    pressure, geo_diag, geo_off, modes_first, modes_second, modes_third, eigen_first, eigen_second,
    eigen_third,
):
    layers, rows, width = pressure.shape
    modes = modes_first.shape[1]
    if rows != N1 or modes != N1 + 2 or lax.axis_size("stream") % 2 or lax.axis_size("cross") % 2:
        raise ValueError("unsupported sizes")
    first_blocks, third_blocks = layers // N1, width // N1
    columns = first_blocks + 2
    halo = modes * rows
    box = N1 * rows
    padded = (first_blocks + 3) * N1
    wide = third_blocks * modes

    grad, third_grad, back, third_back = operator_tables(third_blocks)
    gather, inner, spread, own, own_row = third_tables(third_blocks, modes)
    tables = box_tables(modes)
    pairs, pad = tables["pick_p"].shape

    mf = jnp.transpose(modes_first, (1, 0, 2))
    ms = modes_second[0]
    mt = jnp.transpose(modes_third, (1, 0, 2)).reshape(modes * third_blocks, modes)

    inputs = [
        jnp.asarray(x)
        for x in (pressure, geo_diag, geo_off, mf, eigen_first, grad, third_grad, back, third_back)
    ]
    lp, s_near, s_far = call(
        local_kernel, "local_product",
        [shape(layers * rows, width), shape(halo + 24, width), shape(halo + 24, width)],
        *inputs, place=pltpu.HBM,
        scratch=[pltpu.VMEM(x.shape, x.dtype) for x in inputs] + [pltpu.SemaphoreType.DMA((len(inputs),))],
    )
    s_near, s_far = swap_stream(s_near, s_far)
    kin, rim_width = 3 * (N1 + 4) * rows, 3 * 64
    w, wbh, wbl, e3_row, own_columns, own_rim, own_b, own_rec, second_columns, second_rows, second_sum = call(
        modes_kernel, "mode_tables",
        [
            shape(3 * width, wide, dtype=BF16), shape(wide, width, dtype=BF16),
            shape(wide, width, dtype=BF16), shape(1, wide),
            shape(first_blocks, pairs, kin, dtype=BF16), shape(first_blocks, pairs, rim_width, dtype=BF16),
            shape(first_blocks, box, 3 * pairs, dtype=BF16), shape(first_blocks, pairs, wide),
            shape(pairs, kin + rim_width), shape(box, 3 * pairs), shape(pairs, 1),
        ],
        mt, eigen_third, gather, inner, spread, own, own_row, mf, eigen_first, ms, eigen_second,
        *[tables[k] for k in (
            "pick_p", "pick_q", "pick_p3", "pick_q3", "lay_m", "lay_n", "row_m3", "row_n3", "pick_pt", "pick_qt",
        )],
        scratch=[pltpu.VMEM((first_blocks + 2, pad, pad), F32)],
    )
    c_near, c_far = call(
        rows_kernel, "rows_to_send",
        [shape(2 * padded, width), shape(2 * padded, width)],
        lp, s_near, s_far, e3_row,
    )
    c_near, c_far = swap_cross(c_near, c_far)
    v, side_rim, side_b, side_rec = call(
        columns_kernel, "own_part",
        [
            shape(columns, pairs, wide), shape(2, pairs, rim_width, dtype=BF16),
            shape(2, 16, 3 * pairs, dtype=BF16), shape(2, pairs, wide),
        ],
        lp, s_near, s_far, w, e3_row, own_columns, second_columns, second_rows, second_sum,
        *[tables[k] for k in ("pick_p", "pick_p3", "lay_m", "row_m3", "pick_pt")],
        scratch=[pltpu.VMEM((layers * rows + 2 * halo, width), F32)],
    )
    restricted, f_near, f_far = call(
        solve_kernel, "solve",
        [shape(layers * rows, width), shape(layers, width), shape(layers, width)],
        c_near, c_far, w, wbh, wbl, v, own_rim, own_rec, own_b, side_rim, side_rec, side_b,
    )
    f_near, f_far = swap_cross(f_near, f_far)
    whole = pl.BlockSpec((layers, rows, width), lambda: (0, 0, 0))
    operator_out = call(
        operator_kernel, "operator_out", jax.ShapeDtypeStruct(pressure.shape, F32),
        lp, s_near, s_far, c_near, c_far, out_specs=whole,
        scratch=[pltpu.VMEM(((layers + 2) * rows, width), F32)],
    )
    preconditioned = call(
        add_kernel, "preconditioned", jax.ShapeDtypeStruct(pressure.shape, F32), restricted, f_near, f_far, out_specs=whole,
        scratch=[pltpu.VMEM((layers * rows, width), F32)],
    )
    return (operator_out, preconditioned)


def solution(mesh):
    in_specs = (
        P("stream", "cross", None),
        P(None, "stream", "cross", None),
        P(None, "stream", "cross", None),
        P("stream", None, None),
        P("cross", None, None),
        P(),
        P("stream", None),
        P("cross", None),
        P(),
    )
    out_specs = (P("stream", "cross", None), P("stream", "cross", None))
    return jax.shard_map(shards, mesh=mesh, in_specs=in_specs, out_specs=out_specs, check_vma=False)
```

```python
import functools

import jax
import jax.numpy as jnp
import numpy as np
from jax import lax
from jax.experimental import pallas as pl
from jax.experimental.pallas import tpu as pltpu
from jax.sharding import PartitionSpec as P

N1 = 8
F32 = jnp.float32
BF16 = jnp.bfloat16
HIGHEST = lax.Precision.HIGHEST
VMEM_LIMIT = 16 * 2**20
VMEM = pl.BlockSpec(memory_space=pltpu.VMEM)


def legendre_values(nodes, degree):
    table = np.zeros((nodes.shape[0], degree + 1))
    table[:, 0] = 1.0
    table[:, 1] = nodes
    for order in range(2, degree + 1):
        table[:, order] = (
            (2 * order - 1) * nodes * table[:, order - 1] - (order - 1) * table[:, order - 2]
        ) / order
    return table


def derivative_table(points):
    degree = points - 1
    nodes = np.cos(np.pi * np.arange(points) / degree)
    for sweep in range(100):
        table = legendre_values(nodes, degree)
        nodes = nodes - (nodes * table[:, degree] - table[:, degree - 1]) / (
            points * table[:, degree]
        )
    gll_nodes = nodes[::-1]
    legendre_at = legendre_values(gll_nodes, degree)[:, degree]
    diff_table = np.zeros((points, points))
    for first_index in range(points):
        for second_index in range(points):
            if first_index != second_index:
                diff_table[first_index, second_index] = legendre_at[first_index] / (
                    legendre_at[second_index] * (gll_nodes[first_index] - gll_nodes[second_index])
                )
    diff_table[0, 0] = -degree * (degree + 1) / 4.0
    diff_table[degree, degree] = degree * (degree + 1) / 4.0
    return diff_table


def halves(table):
    table = np.asarray(table, np.float32)
    high = table.astype(jnp.bfloat16)
    return high, (table - high.astype(np.float32)).astype(jnp.bfloat16)


def operator_tables(blocks):
    diff = derivative_table(N1).astype(np.float32)
    eye = np.eye(N1, dtype=np.float32)
    both = np.concatenate([np.kron(diff, eye), np.kron(eye, diff)])
    third = np.kron(np.eye(blocks, dtype=np.float32), diff.T)
    high, low = halves(both)
    grad = np.concatenate([high, high, low], 1)
    high, low = halves(both.T)
    back = np.concatenate([high, high, low], 1)
    high, low = halves(third)
    third_grad = np.concatenate([high, low, high], 0)
    high, low = halves(third.T)
    third_back = np.concatenate([high, low, high], 0)
    return grad, third_grad, back, third_back


def third_tables(blocks, modes):
    length = blocks * N1
    gather = np.zeros((length, modes, blocks), np.float32)
    for c in range(blocks):
        for o in range(N1):
            gather[c * N1 + o, o + 1, c] = 1
        if c > 0:
            gather[c * N1 - 1, 1, c] = 1
            gather[c * N1 - 2, 0, c] = 1
        if c < blocks - 1:
            gather[(c + 1) * N1, N1, c] = 1
            gather[(c + 1) * N1 + 1, N1 + 1, c] = 1
    inner = gather.copy()
    inner[:, 0] = 0
    inner[:, -1] = 0
    gather = gather.reshape(length, modes * blocks)
    inner = inner.reshape(length, modes * blocks)
    spread = np.tile(np.eye(modes, dtype=np.float32), (1, blocks))
    own = np.kron(np.eye(blocks, dtype=np.float32), np.ones((1, modes), np.float32))
    return gather.astype(jnp.bfloat16), inner.T.astype(jnp.bfloat16), spread, np.tile(own, (modes, 1)), own


def round_up(count, unit):
    return -(-count // unit) * unit


def box_tables(modes):
    pad = round_up(modes, 16)
    pairs = round_up(modes * modes, 16)
    pick_p = np.zeros((pairs, pad), np.float32)
    pick_q = np.zeros((pairs, pad), np.float32)
    for p in range(modes):
        for q in range(modes):
            pick_p[p * modes + q, p] = 1
            pick_q[p * modes + q, q] = 1
    layers = N1 + 4
    node_of = [0, 1] + [1 + i for i in range(N1)] + [N1, N1 + 1]
    own_m = np.zeros((pad, layers * N1), np.float32)
    own_n = np.zeros((pad, layers * N1), np.float32)
    for l in range(layers):
        for y in range(N1):
            own_m[node_of[l], l * N1 + y] = 1
            own_n[y + 1, l * N1 + y] = 1
    kinds = [0, 1, N1, N1 + 1]
    rim_m = np.zeros((pad, 4 * 16), np.float32)
    rim_n = np.zeros((pad, 4 * 16), np.float32)
    for k in range(4):
        for l in range(layers):
            rim_m[node_of[l], k * 16 + l] = 1
            rim_n[kinds[k], k * 16 + l] = 1
    lay_m = np.concatenate([own_m] * 3 + [rim_m] * 3, 1)
    lay_n = np.concatenate([own_n] * 3 + [rim_n] * 3, 1)
    row_m = np.zeros((N1 * N1, pad), np.float32)
    row_n = np.zeros((N1 * N1, pad), np.float32)
    for i in range(N1):
        for y in range(N1):
            row_m[i * N1 + y, i + 1] = 1
            row_n[i * N1 + y, y + 1] = 1
    faces = [i * N1 for i in range(N1)] + [i * N1 + N1 - 1 for i in range(N1)]
    wide = lambda t: np.concatenate([t] * 3, 1).astype(jnp.bfloat16)
    return dict(
        pick_p=pick_p,
        pick_q=pick_q,
        pick_p3=wide(pick_p),
        pick_q3=wide(pick_q),
        lay_m=np.concatenate([lay_m] * 3, 0).astype(jnp.bfloat16),
        lay_n=np.concatenate([lay_n] * 3, 0).astype(jnp.bfloat16),
        row_m3=wide(row_m),
        row_n3=wide(row_n),
        face_m3=wide(row_m[faces]),
        face_n3=wide(row_n[faces]),
        pick_pt=wide(pick_p.T),
        pick_qt=wide(pick_q.T),
    )


def dot(left, right, dims=((1,), (0,)), precision=None):
    return lax.dot_general(
        left, right, (dims, ((), ())), precision=precision, preferred_element_type=F32
    )


def split(value):
    high = value.astype(BF16)
    return high, (value - high.astype(F32)).astype(BF16)


def split3(value):
    high = value.astype(BF16)
    rest = value - high.astype(F32)
    mid = rest.astype(BF16)
    return high, mid, (rest - mid.astype(F32)).astype(BF16)


def stacked(value):
    high, low = split(value)
    return jnp.concatenate([high, low, high], 0)


def abreast(value):
    high, low = split(value)
    return jnp.concatenate([high, high, low], 1)


def even(index):
    return lax.rem(index, 2) == 0


def local_kernel(*refs):
    count = 9
    sources, outs, scratch = refs[:count], refs[count : count + 3], refs[count + 3 :]
    lp_ref, near_ref, far_ref = outs
    p_ref, gd_ref, go_ref, mf_ref, ef_ref, grad_ref, third_ref, back_ref, third_back_ref = scratch[:count]
    copies = [
        pltpu.make_async_copy(source, target, scratch[count].at[k])
        for k, (source, target) in enumerate(zip(sources, scratch))
    ]
    for k in (0, 6, 5, 1, 2, 7, 8, 3, 4):
        copies[k].start()
    layers, rows, width = p_ref.shape
    for k in (0, 6, 5):
        copies[k].wait()
    first_blocks = layers // N1
    box = N1 * rows
    modes = mf_ref.shape[0]
    p_all = p_ref[...].reshape(layers * rows, width)
    third = dot(abreast(p_all), third_ref[...])
    grads = [
        dot(grad_ref[...], stacked(p_all[a * box : (a + 1) * box])) for a in range(first_blocks)
    ]
    for k in (1, 2, 7, 8):
        copies[k].wait()
    for a in range(first_blocks):
        here = slice(a * box, (a + 1) * box)
        one, two, three = grads[a][:box], grads[a][box:], third[here]
        g = [
            gd_ref[k, a * N1 : (a + 1) * N1].reshape(box, width) for k in range(3)
        ] + [go_ref[k, a * N1 : (a + 1) * N1].reshape(box, width) for k in range(3)]
        flux_one = g[0] * one + g[3] * two + g[4] * three
        flux_two = g[3] * one + g[1] * two + g[5] * three
        flux_three = g[4] * one + g[5] * two + g[2] * three
        lp_ref[here, :] = dot(
            back_ref[...], stacked(jnp.concatenate([flux_one, flux_two], 0))
        ) + dot(abreast(flux_three), third_back_ref[...])
    for k in (3, 4):
        copies[k].wait()
    layer = lambda l: slice(l * rows, (l + 1) * rows)
    body = (modes - 1) * rows
    up_layers = [
        (0, rows, lp_ref[layer(layers - modes), :]),
        (rows, 2 * rows, lp_ref[layer(layers - modes + 1), :] + lp_ref[layer(layers - modes + 2), :]),
        (2 * rows, body, lp_ref[(layers - modes + 3) * rows :, :]),
    ]
    down_layers = [
        (0, body - 2 * rows, lp_ref[: (modes - 3) * rows, :]),
        (body - 2 * rows, body - rows, lp_ref[layer(modes - 3), :] + lp_ref[layer(modes - 2), :]),
        (body - rows, body, lp_ref[layer(modes - 1), :]),
    ]
    forward = even(lax.axis_index("stream"))

    def fill(ref, parts, a):
        for begin, end, value in parts:
            ref[begin:end, :] = value
        ref[body:, :] = jnp.zeros((rows, width), F32)
        ref[body:, :modes] = mf_ref[:rows, a, :]
        ref[body : body + modes - rows, 16 : 16 + modes] = mf_ref[rows:, a, :]
        ref[body : body + 1, 32 : 32 + modes] = ef_ref[a : a + 1, :]

    @pl.when(forward)
    def _():
        fill(near_ref, up_layers, first_blocks - 1)
        fill(far_ref, down_layers, 0)

    @pl.when(jnp.logical_not(forward))
    def _():
        fill(near_ref, down_layers, 0)
        fill(far_ref, up_layers, first_blocks - 1)


def from_sides(near, far, axis):
    index = lax.axis_index(axis)
    is_even = even(index)
    before = jnp.where(is_even, far, near)
    after = jnp.where(is_even, near, far)
    before = jnp.where(index == 0, 0.0, before)
    after = jnp.where(index == lax.axis_size(axis) - 1, 0.0, after)
    return before, after


def rows_kernel(lp_ref, near_ref, far_ref, built_ref, out_near_ref, out_far_ref):
    rows = N1
    layers = lp_ref.shape[0] // rows
    halo = N1 + 2
    count = halo - 1
    padded = out_near_ref.shape[0] // 2
    zero = jnp.zeros((1, lp_ref.shape[1]), F32)
    found = {}
    for k in (0, 1, rows - 2, rows - 1):
        before, after = from_sides(
            near_ref[pl.ds(k, count, stride=rows), :], far_ref[pl.ds(k, count, stride=rows), :], "stream"
        )
        found[k] = (before, lp_ref[pl.ds(k, layers, stride=rows), :], after)
    up = even(lax.axis_index("cross"))
    for ref, high in ((out_near_ref, up), (out_far_ref, jnp.logical_not(up))):
        for slot in range(2):
            base = slot * padded
            before, own, after = [
                jnp.where(high, one, two) for one, two in zip(found[rows - 2 + slot], found[slot])
            ]
            ref[base : base + 1, :] = before[:1]
            ref[base + 1 : base + 2, :] = zero
            ref[base + 2 : base + halo, :] = before[1:]
            base += halo
            ref[base : base + layers, :] = own
            base += layers
            ref[base : base + halo - 2, :] = after[: halo - 2]
            ref[base + halo - 2 : base + halo - 1, :] = zero
            ref[base + halo - 1 : base + halo, :] = after[halo - 2 :]


def spread_columns(parts, lay_ref, pick_ref):
    table = dot(parts, lay_ref[...], ((0,), (0,)))
    return dot(pick_ref[...], jnp.concatenate(split3(table), 0))


def spread_rows(parts, pick_ref, row_ref):
    pad = parts.shape[0] // 3
    table = sum(dot(parts[k * pad : (k + 1) * pad], pick_ref[...]) for k in range(3))
    return dot(row_ref[...], jnp.concatenate(split3(table), 0))


def halves_by_lane(value, low):
    high = value.astype(BF16).astype(F32)
    return jnp.where(low, value - high, high).astype(BF16)


def low_lanes(columns_ref, rows_ref, kin):
    wide, pairs = columns_ref.shape[1], rows_ref.shape[1] // 3
    lane = lax.broadcasted_iota(jnp.int32, (1, wide), 1)
    rim = (wide - 3 * kin) // 3
    low = ((lane >= 2 * kin) & (lane < 3 * kin)) | (lane >= 3 * kin + 2 * rim)
    return low, lax.broadcasted_iota(jnp.int32, (1, 3 * pairs), 1) >= 2 * pairs


def third_parts(mt_ref, spread_ref, own_ref):
    spread = spread_ref[...].astype(BF16)
    return [(dot(part, spread) * own_ref[...]).astype(BF16) for part in split3(mt_ref[...])]


def pad_modes(pad_ref, mf_ref, ef_ref, ms_ref, es_ref):
    modes = ms_ref.shape[0]
    first_blocks = pad_ref.shape[0] - 2
    pad_ref[...] = jnp.zeros_like(pad_ref)
    for a in range(first_blocks):
        pad_ref[a, :modes, :modes] = mf_ref[:, a, :]
        pad_ref[first_blocks + 1, a : a + 1, :modes] = ef_ref[a : a + 1, :]
    pad_ref[first_blocks, :modes, :modes] = ms_ref[...]
    pad_ref[first_blocks + 1, first_blocks : first_blocks + 1, :modes] = es_ref[...]


def modes_kernel(
    mt_ref, e3_ref, gather_ref, spread_ref, own_ref, own_row_ref, mf_ref, ef_ref, ms_ref, es_ref,
    pick_p3_ref, pick_q3_ref, lay_m_ref, lay_n_ref, pick_pt_ref,
    w_ref, e3_row_ref, own_columns_ref, own_rim_ref, second_columns_ref, pad_ref,
):
    parts = third_parts(mt_ref, spread_ref, own_ref)
    table = sum(dot(gather_ref[...], part) for part in parts)
    high, low = split(table)
    w_ref[...] = jnp.concatenate([high, low, high], 0)
    spread = spread_ref[...].astype(BF16)
    e3_row_ref[...] = jnp.sum(
        sum(dot(part, spread) for part in split3(e3_ref[...])) * own_row_ref[...], 0, keepdims=True
    )
    first_blocks = own_columns_ref.shape[0]
    pad_modes(pad_ref, mf_ref, ef_ref, ms_ref, es_ref)
    kin = own_columns_ref.shape[2] // 3
    low, _ = low_lanes(lay_m_ref, pick_pt_ref, kin)
    second = jnp.concatenate(split3(pad_ref[first_blocks]), 0)
    second_columns = spread_columns(second, lay_n_ref, pick_q3_ref)
    second_columns_ref[...] = second_columns
    for a in range(first_blocks):
        first = jnp.concatenate(split3(pad_ref[a]), 0)
        columns = halves_by_lane(spread_columns(first, lay_m_ref, pick_p3_ref) * second_columns, low)
        own_columns_ref[a] = columns[:, : 3 * kin]
        own_rim_ref[a] = columns[:, 3 * kin :]


def columns_kernel(
    lp_ref, near_ref, far_ref, w_ref, e3_row_ref, own_columns_ref, second_columns_ref, pad_ref,
    mt_ref, inner_ref, spread_ref, own_ref,
    pick_p_ref, pick_q_ref, pick_p3_ref, lay_m_ref, pick_pt_ref, pick_qt_ref, face_m3_ref, face_n3_ref,
    v_ref, side_rim_ref, rec_ref, face_ref, wbh_ref, wbl_ref,
):
    rows = N1
    halo = (N1 + 2) * rows
    first_blocks = own_columns_ref.shape[0]
    pad = pick_p_ref.shape[1]
    kin = own_columns_ref.shape[2] // 3
    box = N1 * rows
    near, far = near_ref[...], far_ref[...]
    before, after = from_sides(near, far, "stream")
    odd = jnp.logical_not(even(lax.axis_index("stream")))
    body = halo - rows
    zero = jnp.zeros((rows, lp_ref.shape[1]), F32)
    stack = jnp.concatenate(
        [before[:rows], zero, before[rows:body], lp_ref[...], after[: body - rows], zero, after[body - rows : body]], 0
    )
    u = dot(abreast(stack), w_ref[...])
    edge_near, edge_far = near[body : body + 1, 32 : 32 + pad], far[body : body + 1, 32 : 32 + pad]
    low, back_low = low_lanes(lay_m_ref, pick_pt_ref, kin)
    own_eigen = pad_ref[first_blocks + 1]
    firsts = [jnp.concatenate([side[body:, :pad], side[body:, 16 : 16 + pad]], 0) for side in (before, after)]
    firsts = [firsts[0]] + [pad_ref[a] for a in range(first_blocks)] + [firsts[1]]
    eigens = [jnp.where(odd, edge_near, edge_far)] + [own_eigen[a : a + 1] for a in range(first_blocks)]
    eigens += [jnp.where(odd, edge_far, edge_near)]
    second = jnp.concatenate(split3(pad_ref[first_blocks]), 0)
    second_faces = spread_rows(second, pick_qt_ref, face_n3_ref)
    second_sum = jnp.sum(pick_q_ref[...] * own_eigen[first_blocks : first_blocks + 1], 1, keepdims=True)
    for a, (first, eigen) in enumerate(zip(firsts, eigens)):
        first = jnp.concatenate(split3(first), 0)
        if a in (0, first_blocks + 1):
            columns = halves_by_lane(
                spread_columns(first, lay_m_ref, pick_p3_ref) * second_columns_ref[...], low
            )
            side_rim_ref[min(a, 1)] = columns[:, 3 * kin :]
            columns = columns[:, : 3 * kin]
        else:
            columns = own_columns_ref[a - 1]
        begin = a * box
        v_ref[a] = dot(columns, stacked(u[begin : begin + kin]))
        face_ref[a] = halves_by_lane(spread_rows(first, pick_pt_ref, face_m3_ref) * second_faces, back_low)
        total = jnp.sum(pick_p_ref[...] * eigen, 1, keepdims=True) + second_sum
        rec_ref[a] = 1.0 / (total + e3_row_ref[...])
    parts = third_parts(mt_ref, spread_ref, own_ref)
    table = sum(dot(part, inner_ref[...], ((0,), (0,))) for part in parts)
    wbh_ref[...], wbl_ref[...] = split(table)


def spectral_columns(near_ref, far_ref, w_ref, v_ref, own_rim_ref, side_rim_ref, rec_ref):
    columns = v_ref.shape[0]
    padded = near_ref.shape[0] // 2
    before, after = from_sides(near_ref[...], far_ref[...], "cross")
    u = dot(abreast(jnp.concatenate([before, after], 0)), w_ref[...])
    u = jnp.concatenate([u, jnp.zeros((8, u.shape[1]), F32)], 0)
    found = []
    for a in range(columns):
        rim = jnp.concatenate(
            [u[k * padded + a * N1 : k * padded + a * N1 + 16] for k in range(4)], 0
        )
        if a in (0, columns - 1):
            table = side_rim_ref[min(a, 1)]
        else:
            table = own_rim_ref[a - 1]
        found.append((v_ref[a] + dot(table, stacked(rim))) * rec_ref[a])
    return found


def third_back(parts, wbh_ref, wbl_ref):
    high, low = split(jnp.concatenate(parts, 0))
    return dot(high, wbh_ref[...]) + dot(high, wbl_ref[...]) + dot(low, wbh_ref[...])


def faces_kernel(
    near_ref, far_ref, w_ref, v_ref, own_rim_ref, side_rim_ref, rec_ref, wbh_ref, wbl_ref, face_ref,
    out_near_ref, out_far_ref,
):
    rows = N1
    found = spectral_columns(near_ref, far_ref, w_ref, v_ref, own_rim_ref, side_rim_ref, rec_ref)
    columns = len(found)
    parts = [dot(face_ref[a], stacked(found[a])) for a in range(columns)]
    solved = third_back(parts, wbh_ref, wbl_ref)
    row = lax.broadcasted_iota(jnp.int32, (rows, 1), 0)
    up = even(lax.axis_index("cross"))
    for a in range(1, columns - 1):
        sums = []
        for face in range(2):
            base = 16 * a + rows * face
            previous = base - 16 + rows - 1
            after = base + 16
            sums.append(
                solved[base : base + rows]
                + jnp.where(row == 0, solved[previous : previous + 1], 0.0)
                + jnp.where(row == rows - 1, solved[after : after + 1], 0.0)
            )
        here = slice((a - 1) * rows, a * rows)
        out_near_ref[here, :] = jnp.where(up, sums[1], sums[0])
        out_far_ref[here, :] = jnp.where(up, sums[0], sums[1])


def solve_kernel(
    near_ref, far_ref, w_ref, v_ref, own_rim_ref, side_rim_ref, rec_ref, wbh_ref, wbl_ref, s_near_ref, s_far_ref, pad_ref,
    pick_pt_ref, pick_qt_ref, row_m3_ref, row_n3_ref, r_ref,
):
    rows = N1
    box = N1 * rows
    found = spectral_columns(near_ref, far_ref, w_ref, v_ref, own_rim_ref, side_rim_ref, rec_ref)
    columns = len(found)
    pad = pad_ref.shape[1]
    pairs = pick_pt_ref.shape[1] // 3
    low = lax.broadcasted_iota(jnp.int32, (1, 3 * pairs), 1) >= 2 * pairs
    body = (N1 + 1) * rows
    sides = from_sides(s_near_ref[...], s_far_ref[...], "stream")
    sides = [jnp.concatenate([side[body:, :pad], side[body:, 16 : 16 + pad]], 0) for side in sides]
    firsts = [sides[0]] + [pad_ref[a] for a in range(columns - 2)] + [sides[1]]
    second = spread_rows(jnp.concatenate(split3(pad_ref[columns - 2]), 0), pick_qt_ref, row_n3_ref)
    parts = []
    for a, first in enumerate(firsts):
        kept = slice(box - 16, box) if a == 0 else slice(0, 16) if a == columns - 1 else slice(0, box)
        first = jnp.concatenate(split3(first), 0)
        table = halves_by_lane(spread_rows(first, pick_pt_ref, row_m3_ref[kept]) * second[kept], low)
        parts.append(dot(table, stacked(found[a])))
    parts[0] = parts[0][16 - rows :]
    parts[-1] = parts[-1][:rows]
    solved = third_back(parts, wbh_ref, wbl_ref)
    for a in range(columns - 2):
        base = rows + a * box
        top, bottom = solved[base : base + rows], solved[base + box - rows : base + box]
        r_ref[a * box : a * box + rows, :] = top + solved[base - rows : base]
        r_ref[a * box + rows : (a + 1) * box - rows, :] = solved[base + rows : base + box - rows]
        r_ref[(a + 1) * box - rows : (a + 1) * box, :] = bottom + solved[base + box : base + box + rows]


def operator_kernel(lp_ref, s_near_ref, s_far_ref, c_near_ref, c_far_ref, out_ref, acc_ref):
    rows = N1
    total_rows, width = lp_ref.shape
    layers = total_rows // rows
    halo = N1 + 2
    padded = c_near_ref.shape[0] // 2
    body = (halo - 1) * rows
    before, after = from_sides(s_near_ref[...], s_far_ref[...], "stream")
    left, right = from_sides(c_near_ref[...], c_far_ref[...], "cross")
    stack = jnp.concatenate([before[body - rows : body], lp_ref[...], after[:rows]], 0)
    acc_ref[...] = stack
    low = acc_ref[pl.ds(0, layers + 2, stride=rows), :]
    high = acc_ref[pl.ds(rows - 1, layers + 2, stride=rows), :]
    acc_ref[pl.ds(0, layers + 2, stride=rows), :] = (
        low + left[padded + halo - 1 : padded + halo + layers + 1]
    )
    acc_ref[pl.ds(rows - 1, layers + 2, stride=rows), :] = (
        high + right[halo - 1 : halo + layers + 1]
    )
    box = N1 * rows
    lane = lax.broadcasted_iota(jnp.int32, (1, width), 1)
    first = (lax.rem(lane, N1) == 0) & (lane > 0)
    final = (lax.rem(lane, N1) == N1 - 1) & (lane < width - 1)
    for a in range(layers // N1):
        base = rows + a * box
        for i in range(N1):
            at = base + i * rows
            value = acc_ref[at : at + rows, :]
            if i == 0:
                value = value + acc_ref[at - rows : at, :]
            if i == N1 - 1:
                value = value + acc_ref[at + rows : at + 2 * rows, :]
            value = (
                value
                + jnp.where(first, pltpu.roll(value, 1, 1), 0.0)
                + jnp.where(final, pltpu.roll(value, width - 1, 1), 0.0)
            )
            out_ref[a * N1 + i] = value


def add_kernel(r_ref, near_ref, far_ref, out_ref, acc_ref):
    rows = N1
    layers = r_ref.shape[0] // rows
    before, after = from_sides(near_ref[...], far_ref[...], "cross")
    acc_ref[...] = r_ref[...]
    low = pl.ds(0, layers, stride=rows)
    high = pl.ds(rows - 1, layers, stride=rows)
    acc_ref[low, :] = acc_ref[low, :] + before
    acc_ref[high, :] = acc_ref[high, :] + after
    out_ref[...] = acc_ref[...].reshape(out_ref.shape)


def shape(*dims, dtype=F32):
    return pltpu.VMEM(dims, dtype)


def call(kernel, name, out, *args, scratch=(), out_specs=None, flops=1000000, place=pltpu.VMEM):
    single = not isinstance(out, list)
    args = [pltpu.with_memory_space_constraint(x, place) for x in args]
    return pl.pallas_call(
        kernel,
        out_shape=out,
        in_specs=[pl.BlockSpec(memory_space=place)] * len(args),
        out_specs=out_specs if out_specs is not None else (VMEM if single else [VMEM] * len(out)),
        scratch_shapes=list(scratch),
        compiler_params=pltpu.CompilerParams(vmem_limit_bytes=VMEM_LIMIT),
        cost_estimate=pl.CostEstimate(flops=flops, bytes_accessed=flops, transcendentals=0),
        name=name,
    )(*args)


def swaps(axis):
    count = lax.axis_size(axis)
    near = [(i, i ^ 1) for i in range(count)]
    far = [(i, (i - 1) % count if i % 2 == 0 else (i + 1) % count) for i in range(count)]
    return near, far


def swap_stream(near, far):
    first, second = swaps("stream")
    near = lax.ppermute(near, "stream", first)
    far = lax.ppermute(far, "stream", second)
    return near, far


def swap_cross(near, far):
    count, streams = lax.axis_size("cross"), lax.axis_size("stream")
    first, second = swaps("cross")
    pairs = []
    for s in range(streams):
        for i, j in second:
            wrapped = {i, j} == {0, count - 1}
            pairs.append((s * count + i, (s ^ 1) * count + i if wrapped else s * count + j))
    near = lax.ppermute(near, "cross", first)
    far = lax.ppermute(far, ("stream", "cross"), pairs)
    return near, far


def shards(
    pressure, geo_diag, geo_off, modes_first, modes_second, modes_third, eigen_first, eigen_second,
    eigen_third,
):
    layers, rows, width = pressure.shape
    modes = modes_first.shape[1]
    if rows != N1 or modes != N1 + 2 or lax.axis_size("stream") % 2 or lax.axis_size("cross") % 2:
        raise ValueError("unsupported sizes")
    first_blocks, third_blocks = layers // N1, width // N1
    columns = first_blocks + 2
    halo = modes * rows
    box = N1 * rows
    padded = layers + 2 * modes
    wide = third_blocks * modes

    grad, third_grad, back, third_back = operator_tables(third_blocks)
    gather, inner, spread, own, own_row = third_tables(third_blocks, modes)
    tables = box_tables(modes)
    pairs, pad = tables["pick_p"].shape

    mf = jnp.transpose(modes_first, (1, 0, 2))
    ms = modes_second[0]
    mt = jnp.transpose(modes_third, (1, 0, 2)).reshape(modes * third_blocks, modes)

    inputs = [
        jnp.asarray(x)
        for x in (pressure, geo_diag, geo_off, mf, eigen_first, grad, third_grad, back, third_back)
    ]
    lp, s_near, s_far = call(
        local_kernel, "local_product",
        [shape(layers * rows, width), shape(halo, width), shape(halo, width)],
        *inputs, place=pltpu.HBM,
        scratch=[pltpu.VMEM(x.shape, x.dtype) for x in inputs] + [pltpu.SemaphoreType.DMA((len(inputs),))],
    )
    s_near, s_far = swap_stream(s_near, s_far)
    kin, rim_width = 3 * (N1 + 4) * rows, 3 * 64
    w, e3_row, own_columns, own_rim, second_columns, padded_modes = call(
        modes_kernel, "mode_tables",
        [
            shape(3 * width, wide, dtype=BF16), shape(1, wide),
            shape(first_blocks, pairs, kin, dtype=BF16), shape(first_blocks, pairs, rim_width, dtype=BF16),
            shape(pairs, kin + rim_width), shape(first_blocks + 2, pad, pad),
        ],
        mt, eigen_third, gather, spread, own, own_row, mf, eigen_first, ms, eigen_second,
        *[tables[k] for k in ("pick_p3", "pick_q3", "lay_m", "lay_n", "pick_pt")],
    )
    c_near, c_far = call(
        rows_kernel, "rows_to_send",
        [shape(2 * padded, width), shape(2 * padded, width)],
        lp, s_near, s_far, e3_row,
    )
    c_near, c_far = swap_cross(c_near, c_far)
    v, side_rim, rec, face, wbh, wbl = call(
        columns_kernel, "own_part",
        [
            shape(columns, pairs, wide), shape(2, pairs, rim_width, dtype=BF16), shape(columns, pairs, wide),
            shape(columns, 16, 3 * pairs, dtype=BF16), shape(wide, width, dtype=BF16), shape(wide, width, dtype=BF16),
        ],
        lp, s_near, s_far, w, e3_row, own_columns, second_columns, padded_modes, mt, inner, spread, own,
        *[tables[k] for k in (
            "pick_p", "pick_q", "pick_p3", "lay_m", "pick_pt", "pick_qt", "face_m3", "face_n3",
        )],
    )
    box_args = (c_near, c_far, w, v, own_rim, side_rim, rec, wbh, wbl)
    f_near, f_far = call(
        faces_kernel, "faces", [shape(layers, width), shape(layers, width)], *box_args, face,
    )
    f_near, f_far = swap_cross(f_near, f_far)
    restricted = call(
        solve_kernel, "solve", shape(layers * rows, width), *box_args, s_near, s_far, padded_modes,
        *[tables[k] for k in ("pick_pt", "pick_qt", "row_m3", "row_n3")],
    )
    whole = pl.BlockSpec((layers, rows, width), lambda: (0, 0, 0))
    operator_out = call(
        operator_kernel, "operator_out", jax.ShapeDtypeStruct(pressure.shape, F32),
        lp, s_near, s_far, c_near, c_far, out_specs=whole,
        scratch=[pltpu.VMEM(((layers + 2) * rows, width), F32)],
    )
    preconditioned = call(
        add_kernel, "preconditioned", jax.ShapeDtypeStruct(pressure.shape, F32), restricted, f_near, f_far, out_specs=whole,
        scratch=[pltpu.VMEM((layers * rows, width), F32)],
    )
    return (operator_out, preconditioned)


def solution(mesh):
    in_specs = (
        P("stream", "cross", None),
        P(None, "stream", "cross", None),
        P(None, "stream", "cross", None),
        P("stream", None, None),
        P("cross", None, None),
        P(),
        P("stream", None),
        P("cross", None),
        P(),
    )
    out_specs = (P("stream", "cross", None), P("stream", "cross", None))
    return jax.shard_map(shards, mesh=mesh, in_specs=in_specs, out_specs=out_specs, check_vma=False)
```

```python
import functools

import jax
import jax.numpy as jnp
import numpy as np
from jax import lax
from jax.experimental import pallas as pl
from jax.experimental.pallas import tpu as pltpu
from jax.sharding import PartitionSpec as P

N1 = 8
F32 = jnp.float32
BF16 = jnp.bfloat16
HIGHEST = lax.Precision.HIGHEST
VMEM_LIMIT = 16 * 2**20
VMEM = pl.BlockSpec(memory_space=pltpu.VMEM)


def legendre_values(nodes, degree):
    table = np.zeros((nodes.shape[0], degree + 1))
    table[:, 0] = 1.0
    table[:, 1] = nodes
    for order in range(2, degree + 1):
        table[:, order] = (
            (2 * order - 1) * nodes * table[:, order - 1] - (order - 1) * table[:, order - 2]
        ) / order
    return table


def derivative_table(points):
    degree = points - 1
    nodes = np.cos(np.pi * np.arange(points) / degree)
    for sweep in range(100):
        table = legendre_values(nodes, degree)
        nodes = nodes - (nodes * table[:, degree] - table[:, degree - 1]) / (
            points * table[:, degree]
        )
    gll_nodes = nodes[::-1]
    legendre_at = legendre_values(gll_nodes, degree)[:, degree]
    diff_table = np.zeros((points, points))
    for first_index in range(points):
        for second_index in range(points):
            if first_index != second_index:
                diff_table[first_index, second_index] = legendre_at[first_index] / (
                    legendre_at[second_index] * (gll_nodes[first_index] - gll_nodes[second_index])
                )
    diff_table[0, 0] = -degree * (degree + 1) / 4.0
    diff_table[degree, degree] = degree * (degree + 1) / 4.0
    return diff_table


def halves(table):
    table = np.asarray(table, np.float32)
    high = table.astype(jnp.bfloat16)
    return high, (table - high.astype(np.float32)).astype(jnp.bfloat16)


def operator_tables(blocks):
    diff = derivative_table(N1).astype(np.float32)
    eye = np.eye(N1, dtype=np.float32)
    both = np.concatenate([np.kron(diff, eye), np.kron(eye, diff)])
    third = np.kron(np.eye(blocks, dtype=np.float32), diff.T)
    high, low = halves(both)
    grad = np.concatenate([high, high, low], 1)
    high, low = halves(both.T)
    back = np.concatenate([high, high, low], 1)
    high, low = halves(third)
    third_grad = np.concatenate([high, low, high], 0)
    high, low = halves(third.T)
    third_back = np.concatenate([high, low, high], 0)
    return grad, third_grad, back, third_back


def round_up(count, unit):
    return -(-count // unit) * unit


def dot(left, right, dims=((1,), (0,)), precision=None):
    return lax.dot_general(
        left, right, (dims, ((), ())), precision=precision, preferred_element_type=F32
    )


def split(value):
    high = value.astype(BF16)
    return high, (value - high.astype(F32)).astype(BF16)


def split3(value):
    high = value.astype(BF16)
    rest = value - high.astype(F32)
    mid = rest.astype(BF16)
    return high, mid, (rest - mid.astype(F32)).astype(BF16)


def stacked(value):
    high, low = split(value)
    return jnp.concatenate([high, low, high], 0)


def abreast(value):
    high, low = split(value)
    return jnp.concatenate([high, high, low], 1)


def even(index):
    return lax.rem(index, 2) == 0


def local_kernel(*refs):
    count = 9
    sources, outs, scratch = refs[:count], refs[count : count + 5], refs[count + 5 :]
    lp_ref, near_ref, far_ref, mf_ref, ef_ref = outs
    p_ref, gd_ref, go_ref, grad_ref, third_ref, back_ref, third_back_ref, sems = scratch
    targets = (p_ref, gd_ref, go_ref, mf_ref, ef_ref, grad_ref, third_ref, back_ref, third_back_ref)
    copies = [
        pltpu.make_async_copy(source, target, sems.at[k])
        for k, (source, target) in enumerate(zip(sources, targets))
    ]
    for k in (0, 6, 5, 1, 2, 7, 8, 3, 4):
        copies[k].start()
    layers, rows, width = p_ref.shape
    for k in (0, 6, 5):
        copies[k].wait()
    first_blocks = layers // N1
    box = N1 * rows
    modes = mf_ref.shape[0]
    p_all = p_ref[...].reshape(layers * rows, width)
    third = dot(abreast(p_all), third_ref[...])
    grads = [
        dot(grad_ref[...], stacked(p_all[a * box : (a + 1) * box])) for a in range(first_blocks)
    ]
    for k in (1, 2, 7, 8):
        copies[k].wait()
    for a in range(first_blocks):
        here = slice(a * box, (a + 1) * box)
        one, two, three = grads[a][:box], grads[a][box:], third[here]
        g = [
            gd_ref[k, a * N1 : (a + 1) * N1].reshape(box, width) for k in range(3)
        ] + [go_ref[k, a * N1 : (a + 1) * N1].reshape(box, width) for k in range(3)]
        flux_one = g[0] * one + g[3] * two + g[4] * three
        flux_two = g[3] * one + g[1] * two + g[5] * three
        flux_three = g[4] * one + g[5] * two + g[2] * three
        lp_ref[here, :] = dot(
            back_ref[...], stacked(jnp.concatenate([flux_one, flux_two], 0))
        ) + dot(abreast(flux_three), third_back_ref[...])
    for k in (3, 4):
        copies[k].wait()
    layer = lambda l: slice(l * rows, (l + 1) * rows)
    body = (modes - 1) * rows
    up_layers = [
        (0, rows, lp_ref[layer(layers - modes), :]),
        (rows, 2 * rows, lp_ref[layer(layers - modes + 1), :] + lp_ref[layer(layers - modes + 2), :]),
        (2 * rows, body, lp_ref[(layers - modes + 3) * rows :, :]),
    ]
    down_layers = [
        (0, body - 2 * rows, lp_ref[: (modes - 3) * rows, :]),
        (body - 2 * rows, body - rows, lp_ref[layer(modes - 3), :] + lp_ref[layer(modes - 2), :]),
        (body - rows, body, lp_ref[layer(modes - 1), :]),
    ]
    forward = even(lax.axis_index("stream"))

    def fill(ref, parts, a):
        for begin, end, value in parts:
            ref[begin:end, :] = value
        ref[body:, :] = jnp.zeros((rows, width), F32)
        ref[body:, :modes] = mf_ref[:rows, a, :]
        ref[body : body + modes - rows, 16 : 16 + modes] = mf_ref[rows:, a, :]
        ref[body : body + 1, 32 : 32 + modes] = ef_ref[a : a + 1, :]

    @pl.when(forward)
    def _():
        fill(near_ref, up_layers, first_blocks - 1)
        fill(far_ref, down_layers, 0)

    @pl.when(jnp.logical_not(forward))
    def _():
        fill(near_ref, down_layers, 0)
        fill(far_ref, up_layers, first_blocks - 1)


def from_sides(near, far, axis):
    index = lax.axis_index(axis)
    is_even = even(index)
    before = jnp.where(is_even, far, near)
    after = jnp.where(is_even, near, far)
    before = jnp.where(index == 0, 0.0, before)
    after = jnp.where(index == lax.axis_size(axis) - 1, 0.0, after)
    return before, after


def rows_kernel(lp_ref, near_ref, far_ref, built_ref, out_near_ref, out_far_ref):
    rows = N1
    layers = lp_ref.shape[0] // rows
    halo = N1 + 2
    count = halo - 1
    padded = out_near_ref.shape[0] // 2
    zero = jnp.zeros((1, lp_ref.shape[1]), F32)
    found = {}
    for k in (0, 1, rows - 2, rows - 1):
        before, after = from_sides(
            near_ref[pl.ds(k, count, stride=rows), :], far_ref[pl.ds(k, count, stride=rows), :], "stream"
        )
        found[k] = (before, lp_ref[pl.ds(k, layers, stride=rows), :], after)
    up = even(lax.axis_index("cross"))
    for ref, high in ((out_near_ref, up), (out_far_ref, jnp.logical_not(up))):
        for slot in range(2):
            base = slot * padded
            before, own, after = [
                jnp.where(high, one, two) for one, two in zip(found[rows - 2 + slot], found[slot])
            ]
            ref[base : base + 1, :] = before[:1]
            ref[base + 1 : base + 2, :] = zero
            ref[base + 2 : base + halo, :] = before[1:]
            base += halo
            ref[base : base + layers, :] = own
            base += layers
            ref[base : base + halo - 2, :] = after[: halo - 2]
            ref[base + halo - 2 : base + halo - 1, :] = zero
            ref[base + halo - 1 : base + halo, :] = after[halo - 2 :]


def spread_columns(parts, lay, pick):
    table = dot(parts, lay, ((0,), (0,)))
    return dot(pick, jnp.concatenate(split3(table), 0))


def spread_rows(parts, pick, rows):
    pad = parts.shape[0] // 3
    table = sum(dot(parts[k * pad : (k + 1) * pad], pick) for k in range(3))
    return dot(rows, jnp.concatenate(split3(table), 0))


def halves_by_lane(value, low):
    high = value.astype(BF16).astype(F32)
    return jnp.where(low, value - high, high).astype(BF16)


def low_lanes(kin, rim):
    lane = lax.broadcasted_iota(jnp.int32, (1, 3 * (kin + rim)), 1)
    return ((lane >= 2 * kin) & (lane < 3 * kin)) | (lane >= 3 * kin + 2 * rim)


def low_back_lanes(pairs):
    return lax.broadcasted_iota(jnp.int32, (1, 3 * pairs), 1) >= 2 * pairs


def ramps(*dims):
    return [lax.broadcasted_iota(jnp.int32, dims, axis) for axis in range(2)]


def over(value, count):
    quotient = ((value.astype(F32) + 0.5) * (1.0 / count)).astype(jnp.int32)
    return quotient, value - quotient * count


def mask(hit):
    return jnp.where(hit, 1.0, 0.0).astype(BF16)


def spread_table(blocks, modes):
    row, column = ramps(modes, blocks * modes)
    return mask(row == over(column, modes)[1])


def gather_table(blocks, modes):
    row, column = ramps(blocks * N1, modes * blocks)
    node, block = over(column, blocks)
    place = row - block * N1
    hit = (place == node - 1) & (node >= 1) & (node <= N1)
    for n, at in ((0, -2), (1, -1), (N1, N1), (N1 + 1, N1 + 1)):
        hit = hit | ((node == n) & (place == at))
    return mask(hit)


def pick_table(pairs, pad, modes, which):
    row, column = ramps(pairs, 3 * pad)
    return mask(over(row, modes)[which] == over(column, pad)[1])


def pick_rows(pairs, pad, modes, which):
    row, column = ramps(pairs, pad)
    return jnp.where(over(row, modes)[which] == column, 1.0, 0.0)


def back_tables(pairs, pad, modes):
    row, column = ramps(pad, 3 * pairs)
    found = over(over(column, pairs)[1], modes)
    return mask(found[0] == row), mask(found[1] == row)


def box_rows(count, pad):
    row, column = ramps(count, 3 * pad)
    first, second = over(row, N1)
    column = over(column, pad)[1]
    return mask(first + 1 == column), mask(second + 1 == column)


def face_rows(pad):
    row, column = ramps(2 * N1, 3 * pad)
    face, first = over(row, N1)
    column = over(column, pad)[1]
    return mask(first + 1 == column), mask(jnp.where(face == 0, 1, N1) == column)


def inner_table(blocks, modes):
    row, column = ramps(modes * blocks, blocks * N1)
    node, block = over(row, blocks)
    place = column - block * N1
    hit = (place == node - 1) & (node >= 1) & (node <= N1)
    return mask(hit | ((node == 1) & (place == -1)) | ((node == N1) & (place == N1)))


def lay_tables(pad, kin, rim):
    layers = kin // N1
    row, column = ramps(3 * pad, 3 * (kin + rim))
    row = over(row, pad)[1]
    own = column < 3 * kin
    l_own, y = over(over(column, kin)[1], N1)
    kind, l_rim = over(over(jnp.maximum(column - 3 * kin, 0), rim)[1], rim // 4)
    l = jnp.where(own, l_own, l_rim)
    node = jnp.where(l == 0, 0, jnp.where(l == layers - 1, N1 + 1, jnp.clip(l - 1, 1, N1)))
    second = jnp.where(own, y + 1, jnp.where(kind < 2, kind, N1 - 2 + kind))
    inside = l < layers
    return mask(inside & (row == node)), mask(inside & (row == second))


def third_parts(mt_ref, spread):
    rows, modes = mt_ref.shape
    blocks = rows // modes
    row, column = ramps(rows, rows)
    own = over(row, blocks)[1] == over(column, modes)[0]
    return [jnp.where(own, dot(part, spread), 0.0).astype(BF16) for part in split3(mt_ref[...])]


def pad_modes(pad_ref, mf_ref, ms_ref):
    modes = ms_ref.shape[0]
    first_blocks = pad_ref.shape[0] - 1
    pad_ref[...] = jnp.zeros_like(pad_ref)
    for a in range(first_blocks):
        pad_ref[a, :modes, :modes] = mf_ref[:, a, :]
    pad_ref[first_blocks, :modes, :modes] = ms_ref[:, 0, :]


def modes_kernel(
    mt_ref, e3_ref, mf_ref, ef_ref, ms_ref, es_ref,
    w_ref, e3_row_ref, own_columns_ref, own_rim_ref, second_columns_ref, pad_ref, eigen_ref,
):
    blocks, modes = e3_ref.shape
    spread = spread_table(blocks, modes)
    gather = gather_table(blocks, modes)
    table = sum(dot(gather, part) for part in third_parts(mt_ref, spread))
    high, low = split(table)
    w_ref[...] = jnp.concatenate([high, low, high], 0)
    row, column = ramps(blocks, blocks * modes)
    e3_wide = sum(dot(part, spread) for part in split3(e3_ref[...]))
    e3_row_ref[...] = jnp.sum(
        jnp.where(row == over(column, modes)[0], e3_wide, 0.0), 0, keepdims=True
    )
    first_blocks, pairs, kin = own_columns_ref.shape
    kin, rim, pad = kin // 3, own_rim_ref.shape[2] // 3, pad_ref.shape[1]
    pad_modes(pad_ref, mf_ref, ms_ref)
    eigen_ref[...] = jnp.zeros_like(eigen_ref)
    eigen_ref[:first_blocks, :modes] = ef_ref[...]
    eigen_ref[first_blocks : first_blocks + 1, :modes] = es_ref[...]
    lay_m, lay_n = lay_tables(pad, kin, rim)
    low = low_lanes(kin, rim)
    second = jnp.concatenate(split3(pad_ref[first_blocks]), 0)
    second_columns = spread_columns(second, lay_n, pick_table(pairs, pad, modes, 1))
    second_columns_ref[...] = second_columns
    pick = pick_table(pairs, pad, modes, 0)
    for a in range(first_blocks):
        first = jnp.concatenate(split3(pad_ref[a]), 0)
        columns = halves_by_lane(spread_columns(first, lay_m, pick) * second_columns, low)
        own_columns_ref[a] = columns[:, : 3 * kin]
        own_rim_ref[a] = columns[:, 3 * kin :]


def columns_kernel(
    lp_ref, near_ref, far_ref, w_ref, e3_row_ref, own_columns_ref, second_columns_ref, pad_ref,
    eigen_ref, mt_ref, v_ref, side_rim_ref, rec_ref, face_ref, wbh_ref, wbl_ref,
):
    rows = N1
    halo = (N1 + 2) * rows
    first_blocks, pairs, kin = own_columns_ref.shape
    kin, rim, pad, modes = kin // 3, side_rim_ref.shape[2] // 3, pad_ref.shape[1], N1 + 2
    box = N1 * rows
    near, far = near_ref[...], far_ref[...]
    before, after = from_sides(near, far, "stream")
    odd = jnp.logical_not(even(lax.axis_index("stream")))
    body = halo - rows
    zero = jnp.zeros((rows, lp_ref.shape[1]), F32)
    stack = jnp.concatenate(
        [before[:rows], zero, before[rows:body], lp_ref[...], after[: body - rows], zero, after[body - rows : body]], 0
    )
    u = dot(abreast(stack), w_ref[...])
    edge_near, edge_far = near[body : body + 1, 32 : 32 + pad], far[body : body + 1, 32 : 32 + pad]
    low, back_low = low_lanes(kin, rim), low_back_lanes(pairs)
    lay_m, _ = lay_tables(pad, kin, rim)
    pick_p3 = pick_table(pairs, pad, modes, 0)
    pick_p, pick_q = pick_rows(pairs, pad, modes, 0), pick_rows(pairs, pad, modes, 1)
    back_m, back_n = back_tables(pairs, pad, modes)
    face_m, face_n = face_rows(pad)
    own_eigen = eigen_ref[...]
    firsts = [jnp.concatenate([side[body:, :pad], side[body:, 16 : 16 + pad]], 0) for side in (before, after)]
    firsts = [firsts[0]] + [pad_ref[a] for a in range(first_blocks)] + [firsts[1]]
    eigens = [jnp.where(odd, edge_near, edge_far)] + [own_eigen[a : a + 1] for a in range(first_blocks)]
    eigens += [jnp.where(odd, edge_far, edge_near)]
    second = jnp.concatenate(split3(pad_ref[first_blocks]), 0)
    second_faces = spread_rows(second, back_n, face_n)
    second_sum = jnp.sum(pick_q * own_eigen[first_blocks : first_blocks + 1], 1, keepdims=True)
    for a, (first, eigen) in enumerate(zip(firsts, eigens)):
        first = jnp.concatenate(split3(first), 0)
        if a in (0, first_blocks + 1):
            columns = halves_by_lane(
                spread_columns(first, lay_m, pick_p3) * second_columns_ref[...], low
            )
            side_rim_ref[min(a, 1)] = columns[:, 3 * kin :]
            columns = columns[:, : 3 * kin]
        else:
            columns = own_columns_ref[a - 1]
        begin = a * box
        v_ref[a] = dot(columns, stacked(u[begin : begin + kin]))
        face_ref[a] = halves_by_lane(spread_rows(first, back_m, face_m) * second_faces, back_low)
        total = jnp.sum(pick_p * eigen, 1, keepdims=True) + second_sum
        rec_ref[a] = 1.0 / (total + e3_row_ref[...])
    blocks = mt_ref.shape[0] // modes
    inner = inner_table(blocks, modes)
    table = sum(
        dot(part, inner, ((0,), (0,))) for part in third_parts(mt_ref, spread_table(blocks, modes))
    )
    wbh_ref[...], wbl_ref[...] = split(table)


def spectral_columns(near_ref, far_ref, w_ref, v_ref, own_rim_ref, side_rim_ref, rec_ref):
    columns = v_ref.shape[0]
    padded = near_ref.shape[0] // 2
    before, after = from_sides(near_ref[...], far_ref[...], "cross")
    u = dot(abreast(jnp.concatenate([before, after], 0)), w_ref[...])
    u = jnp.concatenate([u, jnp.zeros((8, u.shape[1]), F32)], 0)
    found = []
    for a in range(columns):
        rim = jnp.concatenate(
            [u[k * padded + a * N1 : k * padded + a * N1 + 16] for k in range(4)], 0
        )
        if a in (0, columns - 1):
            table = side_rim_ref[min(a, 1)]
        else:
            table = own_rim_ref[a - 1]
        found.append((v_ref[a] + dot(table, stacked(rim))) * rec_ref[a])
    return found


def third_back(parts, wbh_ref, wbl_ref):
    high, low = split(jnp.concatenate(parts, 0))
    return dot(high, wbh_ref[...]) + dot(high, wbl_ref[...]) + dot(low, wbh_ref[...])


def faces_kernel(
    near_ref, far_ref, w_ref, v_ref, own_rim_ref, side_rim_ref, rec_ref, wbh_ref, wbl_ref, face_ref,
    out_near_ref, out_far_ref,
):
    rows = N1
    found = spectral_columns(near_ref, far_ref, w_ref, v_ref, own_rim_ref, side_rim_ref, rec_ref)
    columns = len(found)
    parts = [dot(face_ref[a], stacked(found[a])) for a in range(columns)]
    solved = third_back(parts, wbh_ref, wbl_ref)
    row = lax.broadcasted_iota(jnp.int32, (rows, 1), 0)
    up = even(lax.axis_index("cross"))
    for a in range(1, columns - 1):
        sums = []
        for face in range(2):
            base = 16 * a + rows * face
            previous = base - 16 + rows - 1
            after = base + 16
            sums.append(
                solved[base : base + rows]
                + jnp.where(row == 0, solved[previous : previous + 1], 0.0)
                + jnp.where(row == rows - 1, solved[after : after + 1], 0.0)
            )
        here = slice((a - 1) * rows, a * rows)
        out_near_ref[here, :] = jnp.where(up, sums[1], sums[0])
        out_far_ref[here, :] = jnp.where(up, sums[0], sums[1])


def solve_kernel(
    near_ref, far_ref, w_ref, v_ref, own_rim_ref, side_rim_ref, rec_ref, wbh_ref, wbl_ref, s_near_ref, s_far_ref, pad_ref, r_ref,
):
    rows = N1
    box = N1 * rows
    found = spectral_columns(near_ref, far_ref, w_ref, v_ref, own_rim_ref, side_rim_ref, rec_ref)
    columns = len(found)
    pad, pairs = pad_ref.shape[1], v_ref.shape[1]
    back_m, back_n = back_tables(pairs, pad, N1 + 2)
    rows_m, rows_n = box_rows(box, pad)
    low = low_back_lanes(pairs)
    body = (N1 + 1) * rows
    sides = from_sides(s_near_ref[...], s_far_ref[...], "stream")
    sides = [jnp.concatenate([side[body:, :pad], side[body:, 16 : 16 + pad]], 0) for side in sides]
    firsts = [sides[0]] + [pad_ref[a] for a in range(columns - 2)] + [sides[1]]
    second = spread_rows(jnp.concatenate(split3(pad_ref[columns - 2]), 0), back_n, rows_n)
    parts = []
    for a, first in enumerate(firsts):
        kept = slice(box - 16, box) if a == 0 else slice(0, 16) if a == columns - 1 else slice(0, box)
        first = jnp.concatenate(split3(first), 0)
        table = halves_by_lane(spread_rows(first, back_m, rows_m[kept]) * second[kept], low)
        parts.append(dot(table, stacked(found[a])))
    parts[0] = parts[0][16 - rows :]
    parts[-1] = parts[-1][:rows]
    solved = third_back(parts, wbh_ref, wbl_ref)
    for a in range(columns - 2):
        base = rows + a * box
        top, bottom = solved[base : base + rows], solved[base + box - rows : base + box]
        r_ref[a * box : a * box + rows, :] = top + solved[base - rows : base]
        r_ref[a * box + rows : (a + 1) * box - rows, :] = solved[base + rows : base + box - rows]
        r_ref[(a + 1) * box - rows : (a + 1) * box, :] = bottom + solved[base + box : base + box + rows]


def operator_kernel(lp_ref, s_near_ref, s_far_ref, c_near_ref, c_far_ref, out_ref, acc_ref):
    rows = N1
    total_rows, width = lp_ref.shape
    layers = total_rows // rows
    halo = N1 + 2
    padded = c_near_ref.shape[0] // 2
    body = (halo - 1) * rows
    before, after = from_sides(s_near_ref[...], s_far_ref[...], "stream")
    left, right = from_sides(c_near_ref[...], c_far_ref[...], "cross")
    stack = jnp.concatenate([before[body - rows : body], lp_ref[...], after[:rows]], 0)
    acc_ref[...] = stack
    low = acc_ref[pl.ds(0, layers + 2, stride=rows), :]
    high = acc_ref[pl.ds(rows - 1, layers + 2, stride=rows), :]
    acc_ref[pl.ds(0, layers + 2, stride=rows), :] = (
        low + left[padded + halo - 1 : padded + halo + layers + 1]
    )
    acc_ref[pl.ds(rows - 1, layers + 2, stride=rows), :] = (
        high + right[halo - 1 : halo + layers + 1]
    )
    box = N1 * rows
    lane = lax.broadcasted_iota(jnp.int32, (1, width), 1)
    first = (lax.rem(lane, N1) == 0) & (lane > 0)
    final = (lax.rem(lane, N1) == N1 - 1) & (lane < width - 1)
    for a in range(layers // N1):
        base = rows + a * box
        for i in range(N1):
            at = base + i * rows
            value = acc_ref[at : at + rows, :]
            if i == 0:
                value = value + acc_ref[at - rows : at, :]
            if i == N1 - 1:
                value = value + acc_ref[at + rows : at + 2 * rows, :]
            value = (
                value
                + jnp.where(first, pltpu.roll(value, 1, 1), 0.0)
                + jnp.where(final, pltpu.roll(value, width - 1, 1), 0.0)
            )
            out_ref[a * N1 + i] = value


def add_kernel(r_ref, near_ref, far_ref, out_ref, acc_ref):
    rows = N1
    layers = r_ref.shape[0] // rows
    before, after = from_sides(near_ref[...], far_ref[...], "cross")
    acc_ref[...] = r_ref[...]
    low = pl.ds(0, layers, stride=rows)
    high = pl.ds(rows - 1, layers, stride=rows)
    acc_ref[low, :] = acc_ref[low, :] + before
    acc_ref[high, :] = acc_ref[high, :] + after
    out_ref[...] = acc_ref[...].reshape(out_ref.shape)


def shape(*dims, dtype=F32):
    return pltpu.VMEM(dims, dtype)


def call(kernel, name, out, *args, scratch=(), out_specs=None, flops=1000000, place=pltpu.VMEM):
    single = not isinstance(out, list)
    args = [pltpu.with_memory_space_constraint(x, place) for x in args]
    return pl.pallas_call(
        kernel,
        out_shape=out,
        in_specs=[pl.BlockSpec(memory_space=place)] * len(args),
        out_specs=out_specs if out_specs is not None else (VMEM if single else [VMEM] * len(out)),
        scratch_shapes=list(scratch),
        compiler_params=pltpu.CompilerParams(vmem_limit_bytes=VMEM_LIMIT),
        cost_estimate=pl.CostEstimate(flops=flops, bytes_accessed=flops, transcendentals=0),
        name=name,
    )(*args)


def swaps(axis):
    count = lax.axis_size(axis)
    near = [(i, i ^ 1) for i in range(count)]
    far = [(i, (i - 1) % count if i % 2 == 0 else (i + 1) % count) for i in range(count)]
    return near, far


def swap_stream(near, far):
    first, second = swaps("stream")
    near = lax.ppermute(near, "stream", first)
    far = lax.ppermute(far, "stream", second)
    return near, far


def swap_cross(near, far):
    count, streams = lax.axis_size("cross"), lax.axis_size("stream")
    first, second = swaps("cross")
    pairs = []
    for s in range(streams):
        for i, j in second:
            wrapped = {i, j} == {0, count - 1}
            pairs.append((s * count + i, (s ^ 1) * count + i if wrapped else s * count + j))
    near = lax.ppermute(near, "cross", first)
    far = lax.ppermute(far, ("stream", "cross"), pairs)
    return near, far


def shards(
    pressure, geo_diag, geo_off, modes_first, modes_second, modes_third, eigen_first, eigen_second,
    eigen_third,
):
    layers, rows, width = pressure.shape
    modes = modes_first.shape[1]
    if rows != N1 or modes != N1 + 2 or lax.axis_size("stream") % 2 or lax.axis_size("cross") % 2:
        raise ValueError("unsupported sizes")
    first_blocks, third_blocks = layers // N1, width // N1
    columns = first_blocks + 2
    halo = modes * rows
    box = N1 * rows
    padded = layers + 2 * modes
    wide = third_blocks * modes

    grad, third_grad, back, third_back = operator_tables(third_blocks)
    pairs, pad = round_up(modes * modes, 16), round_up(modes, 16)

    mf = jnp.transpose(modes_first, (1, 0, 2))
    ms = jnp.transpose(modes_second, (1, 0, 2))
    mt = jnp.transpose(modes_third, (1, 0, 2)).reshape(modes * third_blocks, modes)

    inputs = [
        jnp.asarray(x)
        for x in (pressure, geo_diag, geo_off, mf, eigen_first, grad, third_grad, back, third_back)
    ]
    lp, s_near, s_far, mf, ef = call(
        local_kernel, "local_product",
        [
            shape(layers * rows, width), shape(halo, width), shape(halo, width),
            shape(modes, first_blocks, modes), shape(first_blocks, modes),
        ],
        *inputs, place=pltpu.HBM,
        scratch=[pltpu.VMEM(x.shape, x.dtype) for x in inputs[:3] + inputs[5:]] + [pltpu.SemaphoreType.DMA((len(inputs),))],
    )
    s_near, s_far = swap_stream(s_near, s_far)
    kin, rim_width = 3 * (N1 + 4) * rows, 3 * 64
    w, e3_row, own_columns, own_rim, second_columns, padded_modes, eigen = call(
        modes_kernel, "mode_tables",
        [
            shape(3 * width, wide, dtype=BF16), shape(1, wide),
            shape(first_blocks, pairs, kin, dtype=BF16), shape(first_blocks, pairs, rim_width, dtype=BF16),
            shape(pairs, kin + rim_width), shape(first_blocks + 1, pad, pad), shape(first_blocks + 1, pad),
        ],
        mt, eigen_third, mf, ef, ms, eigen_second,
    )
    c_near, c_far = call(
        rows_kernel, "rows_to_send",
        [shape(2 * padded, width), shape(2 * padded, width)],
        lp, s_near, s_far, e3_row,
    )
    c_near, c_far = swap_cross(c_near, c_far)
    v, side_rim, rec, face, wbh, wbl = call(
        columns_kernel, "own_part",
        [
            shape(columns, pairs, wide), shape(2, pairs, rim_width, dtype=BF16), shape(columns, pairs, wide),
            shape(columns, 16, 3 * pairs, dtype=BF16), shape(wide, width, dtype=BF16), shape(wide, width, dtype=BF16),
        ],
        lp, s_near, s_far, w, e3_row, own_columns, second_columns, padded_modes, eigen, mt,
    )
    box_args = (c_near, c_far, w, v, own_rim, side_rim, rec, wbh, wbl)
    f_near, f_far = call(
        faces_kernel, "faces", [shape(layers, width), shape(layers, width)], *box_args, face,
    )
    f_near, f_far = swap_cross(f_near, f_far)
    restricted = call(
        solve_kernel, "solve", shape(layers * rows, width), *box_args, s_near, s_far, padded_modes,
    )
    whole = pl.BlockSpec((layers, rows, width), lambda: (0, 0, 0))
    operator_out = call(
        operator_kernel, "operator_out", jax.ShapeDtypeStruct(pressure.shape, F32),
        lp, s_near, s_far, c_near, c_far, out_specs=whole,
        scratch=[pltpu.VMEM(((layers + 2) * rows, width), F32)],
    )
    preconditioned = call(
        add_kernel, "preconditioned", jax.ShapeDtypeStruct(pressure.shape, F32), restricted, f_near, f_far, out_specs=whole,
        scratch=[pltpu.VMEM((layers * rows, width), F32)],
    )
    return (operator_out, preconditioned)


def solution(mesh):
    in_specs = (
        P("stream", "cross", None),
        P(None, "stream", "cross", None),
        P(None, "stream", "cross", None),
        P("stream", None, None),
        P("cross", None, None),
        P(),
        P("stream", None),
        P("cross", None),
        P(),
    )
    out_specs = (P("stream", "cross", None), P("stream", "cross", None))
    return jax.shard_map(shards, mesh=mesh, in_specs=in_specs, out_specs=out_specs, check_vma=False)
```

```python
import functools

import jax
import jax.numpy as jnp
import numpy as np
from jax import lax
from jax.experimental import pallas as pl
from jax.experimental.pallas import tpu as pltpu
from jax.sharding import PartitionSpec as P

N1 = 8
F32 = jnp.float32
BF16 = jnp.bfloat16
HIGHEST = lax.Precision.HIGHEST
VMEM_LIMIT = 16 * 2**20
VMEM = pl.BlockSpec(memory_space=pltpu.VMEM)


def legendre_values(nodes, degree):
    table = np.zeros((nodes.shape[0], degree + 1))
    table[:, 0] = 1.0
    table[:, 1] = nodes
    for order in range(2, degree + 1):
        table[:, order] = (
            (2 * order - 1) * nodes * table[:, order - 1] - (order - 1) * table[:, order - 2]
        ) / order
    return table


def derivative_table(points):
    degree = points - 1
    nodes = np.cos(np.pi * np.arange(points) / degree)
    for sweep in range(100):
        table = legendre_values(nodes, degree)
        nodes = nodes - (nodes * table[:, degree] - table[:, degree - 1]) / (
            points * table[:, degree]
        )
    gll_nodes = nodes[::-1]
    legendre_at = legendre_values(gll_nodes, degree)[:, degree]
    diff_table = np.zeros((points, points))
    for first_index in range(points):
        for second_index in range(points):
            if first_index != second_index:
                diff_table[first_index, second_index] = legendre_at[first_index] / (
                    legendre_at[second_index] * (gll_nodes[first_index] - gll_nodes[second_index])
                )
    diff_table[0, 0] = -degree * (degree + 1) / 4.0
    diff_table[degree, degree] = degree * (degree + 1) / 4.0
    return diff_table


def halves(table):
    table = np.asarray(table, np.float32)
    high = table.astype(jnp.bfloat16)
    return high, (table - high.astype(np.float32)).astype(jnp.bfloat16)


def operator_tables(blocks):
    diff = derivative_table(N1).astype(np.float32)
    eye = np.eye(N1, dtype=np.float32)
    both = np.concatenate([np.kron(diff, eye), np.kron(eye, diff)])
    third = np.kron(np.eye(blocks, dtype=np.float32), diff.T)
    high, low = halves(both)
    grad = np.concatenate([high, high, low], 1)
    high, low = halves(both.T)
    back = np.concatenate([high, high, low], 1)
    high, low = halves(third)
    third_grad = np.concatenate([high, low, high], 0)
    high, low = halves(third.T)
    third_back = np.concatenate([high, low, high], 0)
    return grad, third_grad, back, third_back


def round_up(count, unit):
    return -(-count // unit) * unit


def dot(left, right, dims=((1,), (0,)), precision=None):
    return lax.dot_general(
        left, right, (dims, ((), ())), precision=precision, preferred_element_type=F32
    )


def split(value):
    high = value.astype(BF16)
    return high, (value - high.astype(F32)).astype(BF16)


def split3(value):
    high = value.astype(BF16)
    rest = value - high.astype(F32)
    mid = rest.astype(BF16)
    return high, mid, (rest - mid.astype(F32)).astype(BF16)


def stacked(value):
    high, low = split(value)
    return jnp.concatenate([high, low, high], 0)


def abreast(value):
    high, low = split(value)
    return jnp.concatenate([high, high, low], 1)


def even(index):
    return lax.rem(index, 2) == 0


def local_kernel(*refs):
    count = 10
    sources, outs, scratch = refs[:count], refs[count : count + 6], refs[count + 6 :]
    lp_ref, near_ref, far_ref, mf_ref, ef_ref, es_ref = outs
    p_ref, gd_ref, go_ref, grad_ref, third_ref, back_ref, third_back_ref, sems = scratch
    targets = (p_ref, gd_ref, go_ref, mf_ref, ef_ref, grad_ref, third_ref, back_ref, third_back_ref, es_ref)
    copies = [
        pltpu.make_async_copy(source, target, sems.at[k])
        for k, (source, target) in enumerate(zip(sources, targets))
    ]
    for k in (0, 6, 5, 1, 2, 7, 8, 3, 4, 9):
        copies[k].start()
    layers, rows, width = p_ref.shape
    for k in (0, 6, 5):
        copies[k].wait()
    first_blocks = layers // N1
    box = N1 * rows
    modes = mf_ref.shape[0]
    p_all = p_ref[...].reshape(layers * rows, width)
    third = dot(abreast(p_all), third_ref[...])
    grads = [
        dot(grad_ref[...], stacked(p_all[a * box : (a + 1) * box])) for a in range(first_blocks)
    ]
    for k in (1, 2, 7, 8):
        copies[k].wait()
    for a in range(first_blocks):
        here = slice(a * box, (a + 1) * box)
        one, two, three = grads[a][:box], grads[a][box:], third[here]
        g = [
            gd_ref[k, a * N1 : (a + 1) * N1].reshape(box, width) for k in range(3)
        ] + [go_ref[k, a * N1 : (a + 1) * N1].reshape(box, width) for k in range(3)]
        flux_one = g[0] * one + g[3] * two + g[4] * three
        flux_two = g[3] * one + g[1] * two + g[5] * three
        flux_three = g[4] * one + g[5] * two + g[2] * three
        lp_ref[here, :] = dot(
            back_ref[...], stacked(jnp.concatenate([flux_one, flux_two], 0))
        ) + dot(abreast(flux_three), third_back_ref[...])
    for k in (3, 4, 9):
        copies[k].wait()
    layer = lambda l: slice(l * rows, (l + 1) * rows)
    body = (modes - 1) * rows
    up_layers = [
        (0, rows, lp_ref[layer(layers - modes), :]),
        (rows, 2 * rows, lp_ref[layer(layers - modes + 1), :] + lp_ref[layer(layers - modes + 2), :]),
        (2 * rows, body, lp_ref[(layers - modes + 3) * rows :, :]),
    ]
    down_layers = [
        (0, body - 2 * rows, lp_ref[: (modes - 3) * rows, :]),
        (body - 2 * rows, body - rows, lp_ref[layer(modes - 3), :] + lp_ref[layer(modes - 2), :]),
        (body - rows, body, lp_ref[layer(modes - 1), :]),
    ]
    forward = even(lax.axis_index("stream"))

    def fill(ref, parts, a):
        for begin, end, value in parts:
            ref[begin:end, :] = value
        ref[body:, :] = jnp.zeros((rows, width), F32)
        ref[body:, :modes] = mf_ref[:rows, a, :]
        ref[body : body + modes - rows, 16 : 16 + modes] = mf_ref[rows:, a, :]
        ref[body : body + 1, 32 : 32 + modes] = ef_ref[a : a + 1, :]

    @pl.when(forward)
    def _():
        fill(near_ref, up_layers, first_blocks - 1)
        fill(far_ref, down_layers, 0)

    @pl.when(jnp.logical_not(forward))
    def _():
        fill(near_ref, down_layers, 0)
        fill(far_ref, up_layers, first_blocks - 1)


def from_sides(near, far, axis):
    index = lax.axis_index(axis)
    is_even = even(index)
    before = jnp.where(is_even, far, near)
    after = jnp.where(is_even, near, far)
    before = jnp.where(index == 0, 0.0, before)
    after = jnp.where(index == lax.axis_size(axis) - 1, 0.0, after)
    return before, after


def rows_kernel(lp_ref, near_ref, far_ref, built_ref, out_far_ref, out_near_ref):
    rows = N1
    layers = lp_ref.shape[0] // rows
    halo = N1 + 2
    count = halo - 1
    padded = out_near_ref.shape[0] // 2
    zero = jnp.zeros((1, lp_ref.shape[1]), F32)
    found = {}
    for k in (0, 1, rows - 2, rows - 1):
        before, after = from_sides(
            near_ref[pl.ds(k, count, stride=rows), :], far_ref[pl.ds(k, count, stride=rows), :], "stream"
        )
        found[k] = (before, lp_ref[pl.ds(k, layers, stride=rows), :], after)
    up = even(lax.axis_index("cross"))
    for ref, high in ((out_near_ref, up), (out_far_ref, jnp.logical_not(up))):
        for slot in range(2):
            base = slot * padded
            before, own, after = [
                jnp.where(high, one, two) for one, two in zip(found[rows - 2 + slot], found[slot])
            ]
            ref[base : base + 1, :] = before[:1]
            ref[base + 1 : base + 2, :] = zero
            ref[base + 2 : base + halo, :] = before[1:]
            base += halo
            ref[base : base + layers, :] = own
            base += layers
            ref[base : base + halo - 2, :] = after[: halo - 2]
            ref[base + halo - 2 : base + halo - 1, :] = zero
            ref[base + halo - 1 : base + halo, :] = after[halo - 2 :]


def spread_columns(parts, lay, pick):
    table = dot(parts, lay, ((0,), (0,)))
    return dot(pick, jnp.concatenate(split3(table), 0))


def spread_rows(parts, pick, rows):
    pad = parts.shape[0] // 3
    table = sum(dot(parts[k * pad : (k + 1) * pad], pick) for k in range(3))
    return dot(rows, jnp.concatenate(split3(table), 0))


def halves_by_lane(value, low):
    high = value.astype(BF16).astype(F32)
    return jnp.where(low, value - high, high).astype(BF16)


def low_lanes(kin, rim):
    lane = lax.broadcasted_iota(jnp.int32, (1, 3 * (kin + rim)), 1)
    return ((lane >= 2 * kin) & (lane < 3 * kin)) | (lane >= 3 * kin + 2 * rim)


def low_back_lanes(pairs):
    return lax.broadcasted_iota(jnp.int32, (1, 3 * pairs), 1) >= 2 * pairs


def ramps(*dims):
    return [lax.broadcasted_iota(jnp.int32, dims, axis) for axis in range(2)]


def over(value, count):
    quotient = ((value.astype(F32) + 0.5) * (1.0 / count)).astype(jnp.int32)
    return quotient, value - quotient * count


def mask(hit):
    return jnp.where(hit, 1.0, 0.0).astype(BF16)


def spread_table(blocks, modes):
    row, column = ramps(modes, blocks * modes)
    return mask(row == over(column, modes)[1])


def gather_table(blocks, modes):
    row, column = ramps(blocks * N1, modes * blocks)
    node, block = over(column, blocks)
    place = row - block * N1
    hit = (place == node - 1) & (node >= 1) & (node <= N1)
    for n, at in ((0, -2), (1, -1), (N1, N1), (N1 + 1, N1 + 1)):
        hit = hit | ((node == n) & (place == at))
    return mask(hit)


def pick_table(pairs, pad, modes, which):
    row, column = ramps(pairs, 3 * pad)
    return mask(over(row, modes)[which] == over(column, pad)[1])


def pick_rows(pairs, pad, modes, which):
    row, column = ramps(pairs, pad)
    return jnp.where(over(row, modes)[which] == column, 1.0, 0.0)


def back_tables(pairs, pad, modes):
    row, column = ramps(pad, 3 * pairs)
    found = over(over(column, pairs)[1], modes)
    return mask(found[0] == row), mask(found[1] == row)


def box_rows(count, pad):
    row, column = ramps(count, 3 * pad)
    first, second = over(row, N1)
    column = over(column, pad)[1]
    return mask(first + 1 == column), mask(second + 1 == column)


def face_rows(pad):
    row, column = ramps(2 * N1, 3 * pad)
    face, first = over(row, N1)
    column = over(column, pad)[1]
    return mask(first + 1 == column), mask(jnp.where(face == 0, 1, N1) == column)


def inner_table(blocks, modes):
    row, column = ramps(modes * blocks, blocks * N1)
    node, block = over(row, blocks)
    place = column - block * N1
    hit = (place == node - 1) & (node >= 1) & (node <= N1)
    return mask(hit | ((node == 1) & (place == -1)) | ((node == N1) & (place == N1)))


def lay_tables(pad, kin, rim):
    layers = kin // N1
    row, column = ramps(3 * pad, 3 * (kin + rim))
    row = over(row, pad)[1]
    own = column < 3 * kin
    l_own, y = over(over(column, kin)[1], N1)
    kind, l_rim = over(over(jnp.maximum(column - 3 * kin, 0), rim)[1], rim // 4)
    l = jnp.where(own, l_own, l_rim)
    node = jnp.where(l == 0, 0, jnp.where(l == layers - 1, N1 + 1, jnp.clip(l - 1, 1, N1)))
    second = jnp.where(own, y + 1, jnp.where(kind < 2, kind, N1 - 2 + kind))
    inside = l < layers
    return mask(inside & (row == node)), mask(inside & (row == second))


def third_parts(mt_ref, spread):
    rows, modes = mt_ref.shape
    blocks = rows // modes
    row, column = ramps(rows, rows)
    own = over(row, blocks)[1] == over(column, modes)[0]
    return [jnp.where(own, dot(part, spread), 0.0).astype(BF16) for part in split3(mt_ref[...])]


def pad_modes(pad_ref, mf_ref, ms_ref):
    modes = ms_ref.shape[0]
    first_blocks = pad_ref.shape[0] - 1
    pad_ref[...] = jnp.zeros_like(pad_ref)
    for a in range(first_blocks):
        pad_ref[a, :modes, :modes] = mf_ref[:, a, :]
    pad_ref[first_blocks, :modes, :modes] = ms_ref[:, 0, :]


def modes_kernel(
    mt_ref, e3_ref, mf_ref, ef_ref, ms_ref, es_ref,
    w_ref, e3_row_ref, own_columns_ref, own_rim_ref, second_columns_ref, pad_ref, eigen_ref, back_ref,
):
    blocks, modes = e3_ref.shape
    spread = spread_table(blocks, modes)
    gather = gather_table(blocks, modes)
    table = sum(dot(gather, part) for part in third_parts(mt_ref, spread))
    high, low = split(table)
    w_ref[...] = jnp.concatenate([high, low, high], 0)
    row, column = ramps(blocks, blocks * modes)
    e3_wide = sum(dot(part, spread) for part in split3(e3_ref[...]))
    e3_row_ref[...] = jnp.sum(
        jnp.where(row == over(column, modes)[0], e3_wide, 0.0), 0, keepdims=True
    )
    first_blocks, pairs, kin = own_columns_ref.shape
    kin, rim, pad = kin // 3, own_rim_ref.shape[2] // 3, pad_ref.shape[1]
    pad_modes(pad_ref, mf_ref, ms_ref)
    eigen_ref[...] = jnp.zeros_like(eigen_ref)
    eigen_ref[:first_blocks, :modes] = ef_ref[...]
    eigen_ref[first_blocks : first_blocks + 1, :modes] = es_ref[...]
    lay_m, lay_n = lay_tables(pad, kin, rim)
    low = low_lanes(kin, rim)
    second = jnp.concatenate(split3(pad_ref[first_blocks]), 0)
    second_columns = spread_columns(second, lay_n, pick_table(pairs, pad, modes, 1))
    second_columns_ref[...] = second_columns
    pick = pick_table(pairs, pad, modes, 0)
    for a in range(first_blocks):
        first = jnp.concatenate(split3(pad_ref[a]), 0)
        columns = halves_by_lane(spread_columns(first, lay_m, pick) * second_columns, low)
        own_columns_ref[a] = columns[:, : 3 * kin]
        own_rim_ref[a] = columns[:, 3 * kin :]
    box = back_ref.shape[1]
    back_m, back_n = back_tables(pairs, pad, modes)
    rows_m, rows_n = box_rows(box, pad)
    second_rows = spread_rows(second, back_n, rows_n)
    for a in range(first_blocks):
        first = jnp.concatenate(split3(pad_ref[a]), 0)
        back_ref[a] = halves_by_lane(spread_rows(first, back_m, rows_m) * second_rows, low_back_lanes(pairs))


def columns_kernel(
    lp_ref, near_ref, far_ref, w_ref, e3_row_ref, own_columns_ref, second_columns_ref, pad_ref,
    eigen_ref, mt_ref, v_ref, side_rim_ref, rec_ref, face_ref, wbh_ref, wbl_ref,
):
    rows = N1
    halo = (N1 + 2) * rows
    first_blocks, pairs, kin = own_columns_ref.shape
    kin, rim, pad, modes = kin // 3, side_rim_ref.shape[2] // 3, pad_ref.shape[1], N1 + 2
    box = N1 * rows
    near, far = near_ref[...], far_ref[...]
    before, after = from_sides(near, far, "stream")
    odd = jnp.logical_not(even(lax.axis_index("stream")))
    body = halo - rows
    zero = jnp.zeros((rows, lp_ref.shape[1]), F32)
    stack = jnp.concatenate(
        [before[:rows], zero, before[rows:body], lp_ref[...], after[: body - rows], zero, after[body - rows : body]], 0
    )
    u = dot(abreast(stack), w_ref[...])
    edge_near, edge_far = near[body : body + 1, 32 : 32 + pad], far[body : body + 1, 32 : 32 + pad]
    low, back_low = low_lanes(kin, rim), low_back_lanes(pairs)
    lay_m, _ = lay_tables(pad, kin, rim)
    pick_p3 = pick_table(pairs, pad, modes, 0)
    pick_p, pick_q = pick_rows(pairs, pad, modes, 0), pick_rows(pairs, pad, modes, 1)
    back_m, back_n = back_tables(pairs, pad, modes)
    face_m, face_n = face_rows(pad)
    own_eigen = eigen_ref[...]
    firsts = [jnp.concatenate([side[body:, :pad], side[body:, 16 : 16 + pad]], 0) for side in (before, after)]
    firsts = [firsts[0]] + [pad_ref[a] for a in range(first_blocks)] + [firsts[1]]
    eigens = [jnp.where(odd, edge_near, edge_far)] + [own_eigen[a : a + 1] for a in range(first_blocks)]
    eigens += [jnp.where(odd, edge_far, edge_near)]
    second = jnp.concatenate(split3(pad_ref[first_blocks]), 0)
    second_faces = spread_rows(second, back_n, face_n)
    second_sum = jnp.sum(pick_q * own_eigen[first_blocks : first_blocks + 1], 1, keepdims=True)
    for a, (first, eigen) in enumerate(zip(firsts, eigens)):
        first = jnp.concatenate(split3(first), 0)
        if a in (0, first_blocks + 1):
            columns = halves_by_lane(
                spread_columns(first, lay_m, pick_p3) * second_columns_ref[...], low
            )
            side_rim_ref[min(a, 1)] = columns[:, 3 * kin :]
            columns = columns[:, : 3 * kin]
        else:
            columns = own_columns_ref[a - 1]
        begin = a * box
        v_ref[a] = dot(columns, stacked(u[begin : begin + kin]))
        face_ref[a] = halves_by_lane(spread_rows(first, back_m, face_m) * second_faces, back_low)
        total = jnp.sum(pick_p * eigen, 1, keepdims=True) + second_sum
        rec_ref[a] = 1.0 / (total + e3_row_ref[...])
    blocks = mt_ref.shape[0] // modes
    inner = inner_table(blocks, modes)
    table = sum(
        dot(part, inner, ((0,), (0,))) for part in third_parts(mt_ref, spread_table(blocks, modes))
    )
    wbh_ref[...], wbl_ref[...] = split(table)


def spectral_columns(near_ref, far_ref, w_ref, v_ref, own_rim_ref, side_rim_ref, rec_ref):
    columns = v_ref.shape[0]
    padded = near_ref.shape[0] // 2
    before, after = from_sides(near_ref[...], far_ref[...], "cross")
    u = dot(abreast(jnp.concatenate([before, after], 0)), w_ref[...])
    u = jnp.concatenate([u, jnp.zeros((8, u.shape[1]), F32)], 0)
    found = []
    for a in range(columns):
        rim = jnp.concatenate(
            [u[k * padded + a * N1 : k * padded + a * N1 + 16] for k in range(4)], 0
        )
        if a in (0, columns - 1):
            table = side_rim_ref[min(a, 1)]
        else:
            table = own_rim_ref[a - 1]
        found.append((v_ref[a] + dot(table, stacked(rim))) * rec_ref[a])
    return found


def third_back(parts, wbh_ref, wbl_ref):
    high, low = split(jnp.concatenate(parts, 0))
    return dot(high, wbh_ref[...]) + dot(high, wbl_ref[...]) + dot(low, wbh_ref[...])


def faces_kernel(
    far_ref, near_ref, w_ref, v_ref, own_rim_ref, side_rim_ref, rec_ref, wbh_ref, wbl_ref, face_ref,
    out_far_ref, out_near_ref, spectral_ref,
):
    rows = N1
    found = spectral_columns(near_ref, far_ref, w_ref, v_ref, own_rim_ref, side_rim_ref, rec_ref)
    columns = len(found)
    for a in range(columns):
        spectral_ref[a] = found[a]
    parts = [dot(face_ref[a], stacked(found[a])) for a in range(columns)]
    solved = third_back(parts, wbh_ref, wbl_ref)
    row = lax.broadcasted_iota(jnp.int32, (rows, 1), 0)
    up = even(lax.axis_index("cross"))
    for a in range(1, columns - 1):
        sums = []
        for face in range(2):
            base = 16 * a + rows * face
            previous = base - 16 + rows - 1
            after = base + 16
            sums.append(
                solved[base : base + rows]
                + jnp.where(row == 0, solved[previous : previous + 1], 0.0)
                + jnp.where(row == rows - 1, solved[after : after + 1], 0.0)
            )
        here = slice((a - 1) * rows, a * rows)
        out_near_ref[here, :] = jnp.where(up, sums[1], sums[0])
        out_far_ref[here, :] = jnp.where(up, sums[0], sums[1])


def assemble_operator(lp_ref, s_near_ref, s_far_ref, c_near_ref, c_far_ref, out_ref, acc_ref):
    rows = N1
    total_rows, width = lp_ref.shape
    layers = total_rows // rows
    halo = N1 + 2
    padded = c_near_ref.shape[0] // 2
    body = (halo - 1) * rows
    before, after = from_sides(s_near_ref[...], s_far_ref[...], "stream")
    left, right = from_sides(c_near_ref[...], c_far_ref[...], "cross")
    stack = jnp.concatenate([before[body - rows : body], lp_ref[...], after[:rows]], 0)
    acc_ref[...] = stack
    low = acc_ref[pl.ds(0, layers + 2, stride=rows), :]
    high = acc_ref[pl.ds(rows - 1, layers + 2, stride=rows), :]
    acc_ref[pl.ds(0, layers + 2, stride=rows), :] = (
        low + left[padded + halo - 1 : padded + halo + layers + 1]
    )
    acc_ref[pl.ds(rows - 1, layers + 2, stride=rows), :] = (
        high + right[halo - 1 : halo + layers + 1]
    )
    box = N1 * rows
    lane = lax.broadcasted_iota(jnp.int32, (1, width), 1)
    first = (lax.rem(lane, N1) == 0) & (lane > 0)
    final = (lax.rem(lane, N1) == N1 - 1) & (lane < width - 1)
    for a in range(layers // N1):
        base = rows + a * box
        for i in range(N1):
            at = base + i * rows
            value = acc_ref[at : at + rows, :]
            if i == 0:
                value = value + acc_ref[at - rows : at, :]
            if i == N1 - 1:
                value = value + acc_ref[at + rows : at + 2 * rows, :]
            value = (
                value
                + jnp.where(first, pltpu.roll(value, 1, 1), 0.0)
                + jnp.where(final, pltpu.roll(value, width - 1, 1), 0.0)
            )
            out_ref[a * N1 + i] = value


def solve_kernel(
    lp_ref, s_near_ref, s_far_ref, c_far_ref, c_near_ref, spectral_ref, wbh_ref, wbl_ref, pad_ref, back_ref,
    operator_ref, r_ref, out_ref, acc_ref, sem,
):
    assemble_operator(lp_ref, s_near_ref, s_far_ref, c_near_ref, c_far_ref, out_ref, acc_ref)
    copy = pltpu.make_async_copy(out_ref, operator_ref, sem)
    copy.start()
    rows = N1
    box = N1 * rows
    found = [spectral_ref[a] for a in range(spectral_ref.shape[0])]
    columns = len(found)
    pad, pairs = pad_ref.shape[1], spectral_ref.shape[1]
    back_m, back_n = back_tables(pairs, pad, N1 + 2)
    rows_m, rows_n = box_rows(box, pad)
    low = low_back_lanes(pairs)
    body = (N1 + 1) * rows
    sides = from_sides(s_near_ref[...], s_far_ref[...], "stream")
    sides = [jnp.concatenate([side[body:, :pad], side[body:, 16 : 16 + pad]], 0) for side in sides]
    second = jnp.concatenate(split3(pad_ref[columns - 2]), 0)
    parts = [None] * columns
    for a, first, kept in ((0, sides[0], slice(box - 16, box)), (columns - 1, sides[1], slice(0, 16))):
        first = jnp.concatenate(split3(first), 0)
        table = spread_rows(first, back_m, rows_m[kept]) * spread_rows(second, back_n, rows_n[kept])
        parts[a] = dot(halves_by_lane(table, low), stacked(found[a]))
    for a in range(1, columns - 1):
        parts[a] = dot(back_ref[a - 1], stacked(found[a]))
    parts[0] = parts[0][16 - rows :]
    parts[-1] = parts[-1][:rows]
    solved = third_back(parts, wbh_ref, wbl_ref)
    for a in range(columns - 2):
        base = rows + a * box
        top, bottom = solved[base : base + rows], solved[base + box - rows : base + box]
        r_ref[a * box : a * box + rows, :] = top + solved[base - rows : base]
        r_ref[a * box + rows : (a + 1) * box - rows, :] = solved[base + rows : base + box - rows]
        r_ref[(a + 1) * box - rows : (a + 1) * box, :] = bottom + solved[base + box : base + box + rows]
    copy.wait()


def pass_kernel(*refs):
    count = len(refs) // 2
    for source, target in zip(refs[:count], refs[count:]):
        target[...] = source[...]


def add_kernel(r_ref, ahead_ref, far_ref, near_ref, out_ref, acc_ref, sem):
    rows = N1
    near = jnp.where(lax.axis_index("cross") < 2, ahead_ref[...], near_ref[...])
    before, after = from_sides(near, far_ref[...], "cross")
    acc_ref[...] = r_ref[...].reshape(acc_ref.shape)
    acc_ref[:, 0, :] = acc_ref[:, 0, :] + before
    acc_ref[:, rows - 1, :] = acc_ref[:, rows - 1, :] + after
    copy = pltpu.make_async_copy(acc_ref, out_ref, sem)
    copy.start()
    copy.wait()


def shape(*dims, dtype=F32):
    return pltpu.VMEM(dims, dtype)


def call(kernel, name, out, *args, scratch=(), out_specs=None, flops=1000000, place=pltpu.VMEM):
    single = not isinstance(out, list)
    args = [pltpu.with_memory_space_constraint(x, place) for x in args]
    return pl.pallas_call(
        kernel,
        out_shape=out,
        in_specs=[pl.BlockSpec(memory_space=place)] * len(args),
        out_specs=out_specs if out_specs is not None else (VMEM if single else [VMEM] * len(out)),
        scratch_shapes=list(scratch),
        compiler_params=pltpu.CompilerParams(vmem_limit_bytes=VMEM_LIMIT),
        cost_estimate=pl.CostEstimate(flops=flops, bytes_accessed=flops, transcendentals=0),
        name=name,
    )(*args)


def swaps(axis):
    count = lax.axis_size(axis)
    near = [(i, i ^ 1) for i in range(count)]
    far = [(i, (i - 1) % count if i % 2 == 0 else (i + 1) % count) for i in range(count)]
    return near, far


def swap_stream(near, far):
    first, second = swaps("stream")
    near = lax.ppermute(near, "stream", first)
    far = lax.ppermute(far, "stream", second)
    return near, far


def cross_pairs(near, ahead=None):
    count, streams = lax.axis_size("cross"), lax.axis_size("stream")
    pairs = []
    for s in range(streams):
        for i in range(count):
            j = i ^ 1 if near else i - 1 + 2 * (i % 2)
            idle = not 0 <= j < count or (ahead is not None and (i < 2) != ahead)
            pairs.append((s * count + i, (s ^ 1) * count + i if idle else s * count + j))
    return pairs


def swap_cross(near, far):
    axes = ("stream", "cross")
    return lax.ppermute(near, axes, cross_pairs(True)), lax.ppermute(far, axes, cross_pairs(False))


def swap_cross_ahead(near, far):
    axes = ("stream", "cross")
    first = lax.ppermute(near, axes, cross_pairs(True, True))
    far, near = call(pass_kernel, "pass_on", [shape(*far.shape), shape(*near.shape)], far, near)
    return first, lax.ppermute(far, axes, cross_pairs(False)), lax.ppermute(near, axes, cross_pairs(True, False))


def shards(
    pressure, geo_diag, geo_off, modes_first, modes_second, modes_third, eigen_first, eigen_second,
    eigen_third,
):
    layers, rows, width = pressure.shape
    modes = modes_first.shape[1]
    if rows != N1 or modes != N1 + 2 or lax.axis_size("stream") % 2 or lax.axis_size("cross") % 2:
        raise ValueError("unsupported sizes")
    first_blocks, third_blocks = layers // N1, width // N1
    columns = first_blocks + 2
    halo = modes * rows
    box = N1 * rows
    padded = layers + 2 * modes
    wide = third_blocks * modes

    grad, third_grad, back, third_back = operator_tables(third_blocks)
    pairs, pad = round_up(modes * modes, 16), round_up(modes, 16)

    mf = jnp.transpose(modes_first, (1, 0, 2))
    ms = jnp.transpose(modes_second, (1, 0, 2))
    mt = jnp.transpose(modes_third, (1, 0, 2)).reshape(modes * third_blocks, modes)

    inputs = [
        jnp.asarray(x)
        for x in (pressure, geo_diag, geo_off, mf, eigen_first, grad, third_grad, back, third_back, eigen_second)
    ]
    lp, s_near, s_far, mf, ef, es = call(
        local_kernel, "local_product",
        [
            shape(layers * rows, width), shape(halo, width), shape(halo, width),
            shape(modes, first_blocks, modes), shape(first_blocks, modes), shape(1, modes),
        ],
        *inputs, place=pltpu.HBM,
        scratch=[pltpu.VMEM(x.shape, x.dtype) for x in inputs[:3] + inputs[5:9]] + [pltpu.SemaphoreType.DMA((len(inputs),))],
    )
    s_near, s_far = swap_stream(s_near, s_far)
    kin, rim_width = 3 * (N1 + 4) * rows, 3 * 64
    w, e3_row, own_columns, own_rim, second_columns, padded_modes, eigen, own_back = call(
        modes_kernel, "mode_tables",
        [
            shape(3 * width, wide, dtype=BF16), shape(1, wide),
            shape(first_blocks, pairs, kin, dtype=BF16), shape(first_blocks, pairs, rim_width, dtype=BF16),
            shape(pairs, kin + rim_width), shape(first_blocks + 1, pad, pad), shape(first_blocks + 1, pad),
            shape(first_blocks, box, 3 * pairs, dtype=BF16),
        ],
        mt, eigen_third, mf, ef, ms, es,
    )
    c_far, c_near = call(
        rows_kernel, "rows_to_send",
        [shape(2 * padded, width), shape(2 * padded, width)],
        lp, s_near, s_far, e3_row,
    )
    c_near, c_far = swap_cross(c_near, c_far)
    v, side_rim, rec, face, wbh, wbl = call(
        columns_kernel, "own_part",
        [
            shape(columns, pairs, wide), shape(2, pairs, rim_width, dtype=BF16), shape(columns, pairs, wide),
            shape(columns, 16, 3 * pairs, dtype=BF16), shape(wide, width, dtype=BF16), shape(wide, width, dtype=BF16),
        ],
        lp, s_near, s_far, w, e3_row, own_columns, second_columns, padded_modes, eigen, mt,
    )
    f_far, f_near, spectral = call(
        faces_kernel, "faces", [shape(layers, width), shape(layers, width), shape(columns, pairs, wide)],
        c_far, c_near, w, v, own_rim, side_rim, rec, wbh, wbl, face,
    )
    f_ahead, f_far, f_near = swap_cross_ahead(f_near, f_far)
    result = pltpu.HBM(pressure.shape, F32)
    in_hbm = pl.BlockSpec(memory_space=pltpu.HBM)
    operator_out, restricted = call(
        solve_kernel, "solve", [result, shape(layers * rows, width)],
        lp, s_near, s_far, c_far, c_near, spectral, wbh, wbl, padded_modes, own_back, out_specs=[in_hbm, VMEM],
        scratch=[
            pltpu.VMEM(pressure.shape, F32), pltpu.VMEM(((layers + 2) * rows, width), F32), pltpu.SemaphoreType.DMA,
        ],
    )
    preconditioned = call(
        add_kernel, "preconditioned", result, restricted, f_ahead, f_far, f_near, out_specs=in_hbm,
        scratch=[pltpu.VMEM(pressure.shape, F32), pltpu.SemaphoreType.DMA],
    )
    return (operator_out, preconditioned)


def solution(mesh):
    in_specs = (
        P("stream", "cross", None),
        P(None, "stream", "cross", None),
        P(None, "stream", "cross", None),
        P("stream", None, None),
        P("cross", None, None),
        P(),
        P("stream", None),
        P("cross", None),
        P(),
    )
    out_specs = (P("stream", "cross", None), P("stream", "cross", None))
    return jax.shard_map(shards, mesh=mesh, in_specs=in_specs, out_specs=out_specs, check_vma=False)
```

```python
import functools

import jax
import jax.numpy as jnp
import numpy as np
from jax import lax
from jax.experimental import pallas as pl
from jax.experimental.pallas import tpu as pltpu
from jax.sharding import PartitionSpec as P

N1 = 8
F32 = jnp.float32
BF16 = jnp.bfloat16
HIGHEST = lax.Precision.HIGHEST
VMEM_LIMIT = 16 * 2**20
VMEM = pl.BlockSpec(memory_space=pltpu.VMEM)


def legendre_values(nodes, degree):
    table = np.zeros((nodes.shape[0], degree + 1))
    table[:, 0] = 1.0
    table[:, 1] = nodes
    for order in range(2, degree + 1):
        table[:, order] = (
            (2 * order - 1) * nodes * table[:, order - 1] - (order - 1) * table[:, order - 2]
        ) / order
    return table


def derivative_table(points):
    degree = points - 1
    nodes = np.cos(np.pi * np.arange(points) / degree)
    for sweep in range(100):
        table = legendre_values(nodes, degree)
        nodes = nodes - (nodes * table[:, degree] - table[:, degree - 1]) / (
            points * table[:, degree]
        )
    gll_nodes = nodes[::-1]
    legendre_at = legendre_values(gll_nodes, degree)[:, degree]
    diff_table = np.zeros((points, points))
    for first_index in range(points):
        for second_index in range(points):
            if first_index != second_index:
                diff_table[first_index, second_index] = legendre_at[first_index] / (
                    legendre_at[second_index] * (gll_nodes[first_index] - gll_nodes[second_index])
                )
    diff_table[0, 0] = -degree * (degree + 1) / 4.0
    diff_table[degree, degree] = degree * (degree + 1) / 4.0
    return diff_table


def round_up(count, unit):
    return -(-count // unit) * unit


def dot(left, right, dims=((1,), (0,)), precision=None):
    return lax.dot_general(
        left, right, (dims, ((), ())), precision=precision, preferred_element_type=F32
    )


def split(value):
    high = value.astype(BF16)
    return high, (value - high.astype(F32)).astype(BF16)


def split3(value):
    high = value.astype(BF16)
    rest = value - high.astype(F32)
    mid = rest.astype(BF16)
    return high, mid, (rest - mid.astype(F32)).astype(BF16)


def stacked(value):
    high, low = split(value)
    return jnp.concatenate([high, low, high], 0)


def abreast(value):
    high, low = split(value)
    return jnp.concatenate([high, high, low], 1)


def even(index):
    return lax.rem(index, 2) == 0


def diff_parts():
    table = derivative_table(N1).astype(np.float32)
    high = table.astype(jnp.bfloat16).astype(np.float32)
    low = (table - high).astype(jnp.bfloat16).astype(np.float32)
    row, column = ramps(N1, N1)
    place = row * N1 + column
    found = []
    for part in (high, low):
        value = jnp.zeros((N1, N1), F32)
        for k, entry in enumerate(part.reshape(-1)):
            if entry:
                value = jnp.where(place == k, float(entry), value)
        found.append(value.astype(BF16))
    return found


def operator_factors(blocks):
    def kron(part, count, inner, turned):
        row, column = ramps(count, N1)
        quotient, rest = over(row, N1)
        pick = mask((rest if inner else quotient) == column)
        value = dot(pick, part, ((1,), (1 if turned else 0,))).astype(BF16)
        value = dot(value, pick, ((1,), (1,)))
        row, column = ramps(count, count)
        row, column = over(row, N1), over(column, N1)
        same = row[0] == column[0] if inner else row[1] == column[1]
        return jnp.where(same, value, 0.0).astype(BF16)

    parts = diff_parts()
    box = N1 * N1
    high, low = [
        jnp.concatenate([kron(part, box, False, False), kron(part, box, True, False)], 0) for part in parts
    ]
    grad = jnp.concatenate([high, high, low], 1)
    high, low = [
        jnp.concatenate([kron(part, box, False, True), kron(part, box, True, True)], 1) for part in parts
    ]
    back = jnp.concatenate([high, high, low], 1)
    high, low = [kron(part, blocks * N1, True, True) for part in parts]
    third = jnp.concatenate([high, low, high], 0)
    high, low = [kron(part, blocks * N1, True, False) for part in parts]
    return grad, third, back, jnp.concatenate([high, low, high], 0)


def local_kernel(*refs):
    count = 6
    sources, outs, scratch = refs[:count], refs[count : count + 6], refs[count + 6 :]
    lp_ref, near_ref, far_ref, mf_ref, ef_ref, es_ref = outs
    p_ref, gd_ref, go_ref, sems = scratch
    targets = (p_ref, gd_ref, go_ref, mf_ref, ef_ref, es_ref)
    copies = [
        pltpu.make_async_copy(source, target, sems.at[k])
        for k, (source, target) in enumerate(zip(sources, targets))
    ]
    for copy in copies:
        copy.start()
    layers, rows, width = p_ref.shape
    grad, third_grad, back, third_back = operator_factors(width // N1)
    copies[0].wait()
    first_blocks = layers // N1
    box = N1 * rows
    modes = mf_ref.shape[0]
    p_all = p_ref[...].reshape(layers * rows, width)
    third = dot(abreast(p_all), third_grad)
    grads = [
        dot(grad, stacked(p_all[a * box : (a + 1) * box])) for a in range(first_blocks)
    ]
    for k in (1, 2):
        copies[k].wait()
    for a in range(first_blocks):
        here = slice(a * box, (a + 1) * box)
        one, two, three = grads[a][:box], grads[a][box:], third[here]
        g = [
            gd_ref[k, a * N1 : (a + 1) * N1].reshape(box, width) for k in range(3)
        ] + [go_ref[k, a * N1 : (a + 1) * N1].reshape(box, width) for k in range(3)]
        flux_one = g[0] * one + g[3] * two + g[4] * three
        flux_two = g[3] * one + g[1] * two + g[5] * three
        flux_three = g[4] * one + g[5] * two + g[2] * three
        lp_ref[here, :] = dot(
            back, stacked(jnp.concatenate([flux_one, flux_two], 0))
        ) + dot(abreast(flux_three), third_back)
    for k in (3, 4, 5):
        copies[k].wait()
    layer = lambda l: slice(l * rows, (l + 1) * rows)
    body = (modes - 1) * rows
    up_layers = [
        (0, rows, lp_ref[layer(layers - modes), :]),
        (rows, 2 * rows, lp_ref[layer(layers - modes + 1), :] + lp_ref[layer(layers - modes + 2), :]),
        (2 * rows, body, lp_ref[(layers - modes + 3) * rows :, :]),
    ]
    down_layers = [
        (0, body - 2 * rows, lp_ref[: (modes - 3) * rows, :]),
        (body - 2 * rows, body - rows, lp_ref[layer(modes - 3), :] + lp_ref[layer(modes - 2), :]),
        (body - rows, body, lp_ref[layer(modes - 1), :]),
    ]
    forward = even(lax.axis_index("stream"))

    def fill(ref, parts, a):
        for begin, end, value in parts:
            ref[begin:end, :] = value
        ref[body:, :] = jnp.zeros((rows, width), F32)
        ref[body:, :modes] = mf_ref[:rows, a, :]
        ref[body : body + modes - rows, 16 : 16 + modes] = mf_ref[rows:, a, :]
        ref[body : body + 1, 32 : 32 + modes] = ef_ref[a : a + 1, :]

    @pl.when(forward)
    def _():
        fill(near_ref, up_layers, first_blocks - 1)
        fill(far_ref, down_layers, 0)

    @pl.when(jnp.logical_not(forward))
    def _():
        fill(near_ref, down_layers, 0)
        fill(far_ref, up_layers, first_blocks - 1)


def from_sides(near, far, axis):
    index = lax.axis_index(axis)
    is_even = even(index)
    before = jnp.where(is_even, far, near)
    after = jnp.where(is_even, near, far)
    before = jnp.where(index == 0, 0.0, before)
    after = jnp.where(index == lax.axis_size(axis) - 1, 0.0, after)
    return before, after


def rows_kernel(lp_ref, near_ref, far_ref, built_ref, out_far_ref, out_near_ref):
    rows = N1
    layers = lp_ref.shape[0] // rows
    halo = N1 + 2
    count = halo - 1
    padded = out_near_ref.shape[0] // 2
    zero = jnp.zeros((1, lp_ref.shape[1]), F32)
    found = {}
    for k in (0, 1, rows - 2, rows - 1):
        before, after = from_sides(
            near_ref[pl.ds(k, count, stride=rows), :], far_ref[pl.ds(k, count, stride=rows), :], "stream"
        )
        found[k] = (before, lp_ref[pl.ds(k, layers, stride=rows), :], after)
    up = even(lax.axis_index("cross"))
    for ref, high in ((out_near_ref, up), (out_far_ref, jnp.logical_not(up))):
        for slot in range(2):
            base = slot * padded
            before, own, after = [
                jnp.where(high, one, two) for one, two in zip(found[rows - 2 + slot], found[slot])
            ]
            ref[base : base + 1, :] = before[:1]
            ref[base + 1 : base + 2, :] = zero
            ref[base + 2 : base + halo, :] = before[1:]
            base += halo
            ref[base : base + layers, :] = own
            base += layers
            ref[base : base + halo - 2, :] = after[: halo - 2]
            ref[base + halo - 2 : base + halo - 1, :] = zero
            ref[base + halo - 1 : base + halo, :] = after[halo - 2 :]


def spread_columns(parts, lay, pick):
    table = dot(parts, lay, ((0,), (0,)))
    return dot(pick, jnp.concatenate(split3(table), 0))


def spread_rows(parts, pick, rows):
    pad = parts.shape[0] // 3
    table = sum(dot(parts[k * pad : (k + 1) * pad], pick) for k in range(3))
    return dot(rows, jnp.concatenate(split3(table), 0))


def halves_by_lane(value, low):
    high = value.astype(BF16).astype(F32)
    return jnp.where(low, value - high, high).astype(BF16)


def low_lanes(kin, rim):
    lane = lax.broadcasted_iota(jnp.int32, (1, 3 * (kin + rim)), 1)
    return ((lane >= 2 * kin) & (lane < 3 * kin)) | (lane >= 3 * kin + 2 * rim)


def low_back_lanes(pairs):
    return lax.broadcasted_iota(jnp.int32, (1, 3 * pairs), 1) >= 2 * pairs


def ramps(*dims):
    return [lax.broadcasted_iota(jnp.int32, dims, axis) for axis in range(2)]


def over(value, count):
    quotient = ((value.astype(F32) + 0.5) * (1.0 / count)).astype(jnp.int32)
    return quotient, value - quotient * count


def mask(hit):
    return jnp.where(hit, 1.0, 0.0).astype(BF16)


def spread_table(blocks, modes):
    row, column = ramps(modes, blocks * modes)
    return mask(row == over(column, modes)[1])


def gather_table(blocks, modes):
    row, column = ramps(blocks * N1, modes * blocks)
    node, block = over(column, blocks)
    place = row - block * N1
    hit = (place == node - 1) & (node >= 1) & (node <= N1)
    for n, at in ((0, -2), (1, -1), (N1, N1), (N1 + 1, N1 + 1)):
        hit = hit | ((node == n) & (place == at))
    return mask(hit)


def pick_table(pairs, pad, modes, which):
    row, column = ramps(pairs, 3 * pad)
    return mask(over(row, modes)[which] == over(column, pad)[1])


def pick_rows(pairs, pad, modes, which):
    row, column = ramps(pairs, pad)
    return jnp.where(over(row, modes)[which] == column, 1.0, 0.0)


def back_tables(pairs, pad, modes):
    row, column = ramps(pad, 3 * pairs)
    found = over(over(column, pairs)[1], modes)
    return mask(found[0] == row), mask(found[1] == row)


def box_rows(count, pad):
    row, column = ramps(count, 3 * pad)
    first, second = over(row, N1)
    column = over(column, pad)[1]
    return mask(first + 1 == column), mask(second + 1 == column)


def face_rows(pad):
    row, column = ramps(2 * N1, 3 * pad)
    face, first = over(row, N1)
    column = over(column, pad)[1]
    return mask(first + 1 == column), mask(jnp.where(face == 0, 1, N1) == column)


def inner_table(blocks, modes):
    row, column = ramps(modes * blocks, blocks * N1)
    node, block = over(row, blocks)
    place = column - block * N1
    hit = (place == node - 1) & (node >= 1) & (node <= N1)
    return mask(hit | ((node == 1) & (place == -1)) | ((node == N1) & (place == N1)))


def lay_tables(pad, kin, rim):
    layers = kin // N1
    row, column = ramps(3 * pad, 3 * (kin + rim))
    row = over(row, pad)[1]
    own = column < 3 * kin
    l_own, y = over(over(column, kin)[1], N1)
    kind, l_rim = over(over(jnp.maximum(column - 3 * kin, 0), rim)[1], rim // 4)
    l = jnp.where(own, l_own, l_rim)
    node = jnp.where(l == 0, 0, jnp.where(l == layers - 1, N1 + 1, jnp.clip(l - 1, 1, N1)))
    second = jnp.where(own, y + 1, jnp.where(kind < 2, kind, N1 - 2 + kind))
    inside = l < layers
    return mask(inside & (row == node)), mask(inside & (row == second))


def third_parts(mt_ref, spread):
    rows, modes = mt_ref.shape
    blocks = rows // modes
    row, column = ramps(rows, rows)
    own = over(row, blocks)[1] == over(column, modes)[0]
    return [jnp.where(own, dot(part, spread), 0.0).astype(BF16) for part in split3(mt_ref[...])]


def pad_modes(pad_ref, mf_ref, ms_ref):
    modes = ms_ref.shape[0]
    first_blocks = pad_ref.shape[0] - 1
    pad_ref[...] = jnp.zeros_like(pad_ref)
    for a in range(first_blocks):
        pad_ref[a, :modes, :modes] = mf_ref[:, a, :]
    pad_ref[first_blocks, :modes, :modes] = ms_ref[:, 0, :]


def modes_kernel(
    mt_ref, e3_ref, mf_ref, ef_ref, ms_ref, es_ref,
    w_ref, e3_row_ref, own_columns_ref, own_rim_ref, second_columns_ref, pad_ref, eigen_ref, back_ref,
):
    blocks, modes = e3_ref.shape
    spread = spread_table(blocks, modes)
    gather = gather_table(blocks, modes)
    table = sum(dot(gather, part) for part in third_parts(mt_ref, spread))
    high, low = split(table)
    w_ref[...] = jnp.concatenate([high, low, high], 0)
    row, column = ramps(blocks, blocks * modes)
    e3_wide = sum(dot(part, spread) for part in split3(e3_ref[...]))
    e3_row_ref[...] = jnp.sum(
        jnp.where(row == over(column, modes)[0], e3_wide, 0.0), 0, keepdims=True
    )
    first_blocks, pairs, kin = own_columns_ref.shape
    kin, rim, pad = kin // 3, own_rim_ref.shape[2] // 3, pad_ref.shape[1]
    pad_modes(pad_ref, mf_ref, ms_ref)
    eigen_ref[...] = jnp.zeros_like(eigen_ref)
    eigen_ref[:first_blocks, :modes] = ef_ref[...]
    eigen_ref[first_blocks : first_blocks + 1, :modes] = es_ref[...]
    lay_m, lay_n = lay_tables(pad, kin, rim)
    low = low_lanes(kin, rim)
    second = jnp.concatenate(split3(pad_ref[first_blocks]), 0)
    second_columns = spread_columns(second, lay_n, pick_table(pairs, pad, modes, 1))
    second_columns_ref[...] = second_columns
    pick = pick_table(pairs, pad, modes, 0)
    for a in range(first_blocks):
        first = jnp.concatenate(split3(pad_ref[a]), 0)
        columns = halves_by_lane(spread_columns(first, lay_m, pick) * second_columns, low)
        own_columns_ref[a] = columns[:, : 3 * kin]
        own_rim_ref[a] = columns[:, 3 * kin :]
    box = back_ref.shape[1]
    back_m, back_n = back_tables(pairs, pad, modes)
    rows_m, rows_n = box_rows(box, pad)
    second_rows = spread_rows(second, back_n, rows_n)
    for a in range(first_blocks):
        first = jnp.concatenate(split3(pad_ref[a]), 0)
        back_ref[a] = halves_by_lane(spread_rows(first, back_m, rows_m) * second_rows, low_back_lanes(pairs))


def columns_kernel(
    lp_ref, near_ref, far_ref, w_ref, e3_row_ref, own_columns_ref, second_columns_ref, pad_ref,
    eigen_ref, mt_ref, v_ref, side_rim_ref, rec_ref, face_ref, wbh_ref, wbl_ref,
):
    rows = N1
    halo = (N1 + 2) * rows
    first_blocks, pairs, kin = own_columns_ref.shape
    kin, rim, pad, modes = kin // 3, side_rim_ref.shape[2] // 3, pad_ref.shape[1], N1 + 2
    box = N1 * rows
    near, far = near_ref[...], far_ref[...]
    before, after = from_sides(near, far, "stream")
    odd = jnp.logical_not(even(lax.axis_index("stream")))
    body = halo - rows
    zero = jnp.zeros((rows, lp_ref.shape[1]), F32)
    stack = jnp.concatenate(
        [before[:rows], zero, before[rows:body], lp_ref[...], after[: body - rows], zero, after[body - rows : body]], 0
    )
    u = dot(abreast(stack), w_ref[...])
    edge_near, edge_far = near[body : body + 1, 32 : 32 + pad], far[body : body + 1, 32 : 32 + pad]
    low, back_low = low_lanes(kin, rim), low_back_lanes(pairs)
    lay_m, _ = lay_tables(pad, kin, rim)
    pick_p3 = pick_table(pairs, pad, modes, 0)
    pick_p, pick_q = pick_rows(pairs, pad, modes, 0), pick_rows(pairs, pad, modes, 1)
    back_m, back_n = back_tables(pairs, pad, modes)
    face_m, face_n = face_rows(pad)
    own_eigen = eigen_ref[...]
    firsts = [jnp.concatenate([side[body:, :pad], side[body:, 16 : 16 + pad]], 0) for side in (before, after)]
    firsts = [firsts[0]] + [pad_ref[a] for a in range(first_blocks)] + [firsts[1]]
    eigens = [jnp.where(odd, edge_near, edge_far)] + [own_eigen[a : a + 1] for a in range(first_blocks)]
    eigens += [jnp.where(odd, edge_far, edge_near)]
    second = jnp.concatenate(split3(pad_ref[first_blocks]), 0)
    second_faces = spread_rows(second, back_n, face_n)
    second_sum = jnp.sum(pick_q * own_eigen[first_blocks : first_blocks + 1], 1, keepdims=True)
    for a, (first, eigen) in enumerate(zip(firsts, eigens)):
        first = jnp.concatenate(split3(first), 0)
        if a in (0, first_blocks + 1):
            columns = halves_by_lane(
                spread_columns(first, lay_m, pick_p3) * second_columns_ref[...], low
            )
            side_rim_ref[min(a, 1)] = columns[:, 3 * kin :]
            columns = columns[:, : 3 * kin]
        else:
            columns = own_columns_ref[a - 1]
        begin = a * box
        v_ref[a] = dot(columns, stacked(u[begin : begin + kin]))
        face_ref[a] = halves_by_lane(spread_rows(first, back_m, face_m) * second_faces, back_low)
        total = jnp.sum(pick_p * eigen, 1, keepdims=True) + second_sum
        rec_ref[a] = 1.0 / (total + e3_row_ref[...])
    blocks = mt_ref.shape[0] // modes
    inner = inner_table(blocks, modes)
    table = sum(
        dot(part, inner, ((0,), (0,))) for part in third_parts(mt_ref, spread_table(blocks, modes))
    )
    wbh_ref[...], wbl_ref[...] = split(table)


def spectral_columns(near_ref, far_ref, w_ref, v_ref, own_rim_ref, side_rim_ref, rec_ref):
    columns = v_ref.shape[0]
    padded = near_ref.shape[0] // 2
    before, after = from_sides(near_ref[...], far_ref[...], "cross")
    u = dot(abreast(jnp.concatenate([before, after], 0)), w_ref[...])
    u = jnp.concatenate([u, jnp.zeros((8, u.shape[1]), F32)], 0)
    found = []
    for a in range(columns):
        rim = jnp.concatenate(
            [u[k * padded + a * N1 : k * padded + a * N1 + 16] for k in range(4)], 0
        )
        if a in (0, columns - 1):
            table = side_rim_ref[min(a, 1)]
        else:
            table = own_rim_ref[a - 1]
        found.append((v_ref[a] + dot(table, stacked(rim))) * rec_ref[a])
    return found


def third_back(parts, wbh_ref, wbl_ref):
    high, low = split(jnp.concatenate(parts, 0))
    return dot(high, wbh_ref[...]) + dot(high, wbl_ref[...]) + dot(low, wbh_ref[...])


def faces_kernel(
    far_ref, near_ref, w_ref, v_ref, own_rim_ref, side_rim_ref, rec_ref, wbh_ref, wbl_ref, face_ref,
    out_far_ref, out_near_ref, spectral_ref,
):
    rows = N1
    found = spectral_columns(near_ref, far_ref, w_ref, v_ref, own_rim_ref, side_rim_ref, rec_ref)
    columns = len(found)
    for a in range(columns):
        spectral_ref[a] = found[a]
    parts = [dot(face_ref[a], stacked(found[a])) for a in range(columns)]
    solved = third_back(parts, wbh_ref, wbl_ref)
    row = lax.broadcasted_iota(jnp.int32, (rows, 1), 0)
    up = even(lax.axis_index("cross"))
    for a in range(1, columns - 1):
        sums = []
        for face in range(2):
            base = 16 * a + rows * face
            previous = base - 16 + rows - 1
            after = base + 16
            sums.append(
                solved[base : base + rows]
                + jnp.where(row == 0, solved[previous : previous + 1], 0.0)
                + jnp.where(row == rows - 1, solved[after : after + 1], 0.0)
            )
        here = slice((a - 1) * rows, a * rows)
        out_near_ref[here, :] = jnp.where(up, sums[1], sums[0])
        out_far_ref[here, :] = jnp.where(up, sums[0], sums[1])


def assemble_operator(lp_ref, s_near_ref, s_far_ref, c_near_ref, c_far_ref, out_ref, acc_ref):
    rows = N1
    total_rows, width = lp_ref.shape
    layers = total_rows // rows
    halo = N1 + 2
    padded = c_near_ref.shape[0] // 2
    body = (halo - 1) * rows
    before, after = from_sides(s_near_ref[...], s_far_ref[...], "stream")
    left, right = from_sides(c_near_ref[...], c_far_ref[...], "cross")
    stack = jnp.concatenate([before[body - rows : body], lp_ref[...], after[:rows]], 0)
    acc_ref[...] = stack
    low = acc_ref[pl.ds(0, layers + 2, stride=rows), :]
    high = acc_ref[pl.ds(rows - 1, layers + 2, stride=rows), :]
    acc_ref[pl.ds(0, layers + 2, stride=rows), :] = (
        low + left[padded + halo - 1 : padded + halo + layers + 1]
    )
    acc_ref[pl.ds(rows - 1, layers + 2, stride=rows), :] = (
        high + right[halo - 1 : halo + layers + 1]
    )
    box = N1 * rows
    lane = lax.broadcasted_iota(jnp.int32, (1, width), 1)
    first = (lax.rem(lane, N1) == 0) & (lane > 0)
    final = (lax.rem(lane, N1) == N1 - 1) & (lane < width - 1)
    for a in range(layers // N1):
        base = rows + a * box
        for i in range(N1):
            at = base + i * rows
            value = acc_ref[at : at + rows, :]
            if i == 0:
                value = value + acc_ref[at - rows : at, :]
            if i == N1 - 1:
                value = value + acc_ref[at + rows : at + 2 * rows, :]
            value = (
                value
                + jnp.where(first, pltpu.roll(value, 1, 1), 0.0)
                + jnp.where(final, pltpu.roll(value, width - 1, 1), 0.0)
            )
            out_ref[a * N1 + i] = value


def solve_kernel(
    lp_ref, s_near_ref, s_far_ref, c_far_ref, c_near_ref, spectral_ref, wbh_ref, wbl_ref, pad_ref, back_ref,
    operator_ref, r_ref, out_ref, acc_ref, sem,
):
    assemble_operator(lp_ref, s_near_ref, s_far_ref, c_near_ref, c_far_ref, out_ref, acc_ref)
    copy = pltpu.make_async_copy(out_ref, operator_ref, sem)
    copy.start()
    rows = N1
    box = N1 * rows
    found = [spectral_ref[a] for a in range(spectral_ref.shape[0])]
    columns = len(found)
    pad, pairs = pad_ref.shape[1], spectral_ref.shape[1]
    back_m, back_n = back_tables(pairs, pad, N1 + 2)
    rows_m, rows_n = box_rows(box, pad)
    low = low_back_lanes(pairs)
    body = (N1 + 1) * rows
    sides = from_sides(s_near_ref[...], s_far_ref[...], "stream")
    sides = [jnp.concatenate([side[body:, :pad], side[body:, 16 : 16 + pad]], 0) for side in sides]
    second = jnp.concatenate(split3(pad_ref[columns - 2]), 0)
    parts = [None] * columns
    for a, first, kept in ((0, sides[0], slice(box - 16, box)), (columns - 1, sides[1], slice(0, 16))):
        first = jnp.concatenate(split3(first), 0)
        table = spread_rows(first, back_m, rows_m[kept]) * spread_rows(second, back_n, rows_n[kept])
        parts[a] = dot(halves_by_lane(table, low), stacked(found[a]))
    for a in range(1, columns - 1):
        parts[a] = dot(back_ref[a - 1], stacked(found[a]))
    parts[0] = parts[0][16 - rows :]
    parts[-1] = parts[-1][:rows]
    solved = third_back(parts, wbh_ref, wbl_ref)
    for a in range(columns - 2):
        base = rows + a * box
        top, bottom = solved[base : base + rows], solved[base + box - rows : base + box]
        r_ref[a * box : a * box + rows, :] = top + solved[base - rows : base]
        r_ref[a * box + rows : (a + 1) * box - rows, :] = solved[base + rows : base + box - rows]
        r_ref[(a + 1) * box - rows : (a + 1) * box, :] = bottom + solved[base + box : base + box + rows]
    copy.wait()


def pass_kernel(*refs):
    count = len(refs) // 2
    for source, target in zip(refs[:count], refs[count:]):
        target[...] = source[...]


def add_kernel(r_ref, ahead_ref, far_ref, near_ref, out_ref, acc_ref, sem):
    rows = N1
    near = jnp.where(lax.axis_index("cross") < 2, ahead_ref[...], near_ref[...])
    before, after = from_sides(near, far_ref[...], "cross")
    acc_ref[...] = r_ref[...].reshape(acc_ref.shape)
    acc_ref[:, 0, :] = acc_ref[:, 0, :] + before
    acc_ref[:, rows - 1, :] = acc_ref[:, rows - 1, :] + after
    copy = pltpu.make_async_copy(acc_ref, out_ref, sem)
    copy.start()
    copy.wait()


def shape(*dims, dtype=F32):
    return pltpu.VMEM(dims, dtype)


def call(kernel, name, out, *args, scratch=(), out_specs=None, flops=1000000, place=pltpu.VMEM):
    single = not isinstance(out, list)
    args = [pltpu.with_memory_space_constraint(x, place) for x in args]
    return pl.pallas_call(
        kernel,
        out_shape=out,
        in_specs=[pl.BlockSpec(memory_space=place)] * len(args),
        out_specs=out_specs if out_specs is not None else (VMEM if single else [VMEM] * len(out)),
        scratch_shapes=list(scratch),
        compiler_params=pltpu.CompilerParams(vmem_limit_bytes=VMEM_LIMIT),
        cost_estimate=pl.CostEstimate(flops=flops, bytes_accessed=flops, transcendentals=0),
        name=name,
    )(*args)


def swaps(axis):
    count = lax.axis_size(axis)
    near = [(i, i ^ 1) for i in range(count)]
    far = [(i, (i - 1) % count if i % 2 == 0 else (i + 1) % count) for i in range(count)]
    return near, far


def swap_stream(near, far):
    first, second = swaps("stream")
    near = lax.ppermute(near, "stream", first)
    far = lax.ppermute(far, "stream", second)
    return near, far


def cross_pairs(near, ahead=None):
    count, streams = lax.axis_size("cross"), lax.axis_size("stream")
    pairs = []
    for s in range(streams):
        for i in range(count):
            j = i ^ 1 if near else i - 1 + 2 * (i % 2)
            idle = not 0 <= j < count or (ahead is not None and (i < 2) != ahead)
            pairs.append((s * count + i, (s ^ 1) * count + i if idle else s * count + j))
    return pairs


def swap_cross(near, far):
    axes = ("stream", "cross")
    return lax.ppermute(near, axes, cross_pairs(True)), lax.ppermute(far, axes, cross_pairs(False))


def swap_cross_ahead(near, far):
    axes = ("stream", "cross")
    first = lax.ppermute(near, axes, cross_pairs(True, True))
    far, near = call(pass_kernel, "pass_on", [shape(*far.shape), shape(*near.shape)], far, near)
    return first, lax.ppermute(far, axes, cross_pairs(False)), lax.ppermute(near, axes, cross_pairs(True, False))


def shards(
    pressure, geo_diag, geo_off, modes_first, modes_second, modes_third, eigen_first, eigen_second,
    eigen_third,
):
    layers, rows, width = pressure.shape
    modes = modes_first.shape[1]
    if rows != N1 or modes != N1 + 2 or lax.axis_size("stream") % 2 or lax.axis_size("cross") % 2:
        raise ValueError("unsupported sizes")
    first_blocks, third_blocks = layers // N1, width // N1
    columns = first_blocks + 2
    halo = modes * rows
    box = N1 * rows
    padded = layers + 2 * modes
    wide = third_blocks * modes

    pairs, pad = round_up(modes * modes, 16), round_up(modes, 16)

    mf = jnp.transpose(modes_first, (1, 0, 2))
    ms = jnp.transpose(modes_second, (1, 0, 2))
    mt = jnp.transpose(modes_third, (1, 0, 2)).reshape(modes * third_blocks, modes)

    inputs = [pressure, geo_diag, geo_off, mf, eigen_first, eigen_second]
    lp, s_near, s_far, mf, ef, es = call(
        local_kernel, "local_product",
        [
            shape(layers * rows, width), shape(halo, width), shape(halo, width),
            shape(modes, first_blocks, modes), shape(first_blocks, modes), shape(1, modes),
        ],
        *inputs, place=pltpu.HBM,
        scratch=[pltpu.VMEM(x.shape, x.dtype) for x in inputs[:3]] + [pltpu.SemaphoreType.DMA((len(inputs),))],
    )
    s_near, s_far = swap_stream(s_near, s_far)
    kin, rim_width = 3 * (N1 + 4) * rows, 3 * 64
    w, e3_row, own_columns, own_rim, second_columns, padded_modes, eigen, own_back = call(
        modes_kernel, "mode_tables",
        [
            shape(3 * width, wide, dtype=BF16), shape(1, wide),
            shape(first_blocks, pairs, kin, dtype=BF16), shape(first_blocks, pairs, rim_width, dtype=BF16),
            shape(pairs, kin + rim_width), shape(first_blocks + 1, pad, pad), shape(first_blocks + 1, pad),
            shape(first_blocks, box, 3 * pairs, dtype=BF16),
        ],
        mt, eigen_third, mf, ef, ms, es,
    )
    c_far, c_near = call(
        rows_kernel, "rows_to_send",
        [shape(2 * padded, width), shape(2 * padded, width)],
        lp, s_near, s_far, e3_row,
    )
    c_near, c_far = swap_cross(c_near, c_far)
    v, side_rim, rec, face, wbh, wbl = call(
        columns_kernel, "own_part",
        [
            shape(columns, pairs, wide), shape(2, pairs, rim_width, dtype=BF16), shape(columns, pairs, wide),
            shape(columns, 16, 3 * pairs, dtype=BF16), shape(wide, width, dtype=BF16), shape(wide, width, dtype=BF16),
        ],
        lp, s_near, s_far, w, e3_row, own_columns, second_columns, padded_modes, eigen, mt,
    )
    f_far, f_near, spectral = call(
        faces_kernel, "faces", [shape(layers, width), shape(layers, width), shape(columns, pairs, wide)],
        c_far, c_near, w, v, own_rim, side_rim, rec, wbh, wbl, face,
    )
    f_ahead, f_far, f_near = swap_cross_ahead(f_near, f_far)
    result = pltpu.HBM(pressure.shape, F32)
    in_hbm = pl.BlockSpec(memory_space=pltpu.HBM)
    operator_out, restricted = call(
        solve_kernel, "solve", [result, shape(layers * rows, width)],
        lp, s_near, s_far, c_far, c_near, spectral, wbh, wbl, padded_modes, own_back, out_specs=[in_hbm, VMEM],
        scratch=[
            pltpu.VMEM(pressure.shape, F32), pltpu.VMEM(((layers + 2) * rows, width), F32), pltpu.SemaphoreType.DMA,
        ],
    )
    preconditioned = call(
        add_kernel, "preconditioned", result, restricted, f_ahead, f_far, f_near, out_specs=in_hbm,
        scratch=[pltpu.VMEM(pressure.shape, F32), pltpu.SemaphoreType.DMA],
    )
    return (operator_out, preconditioned)


def solution(mesh):
    in_specs = (
        P("stream", "cross", None),
        P(None, "stream", "cross", None),
        P(None, "stream", "cross", None),
        P("stream", None, None),
        P("cross", None, None),
        P(),
        P("stream", None),
        P("cross", None),
        P(),
    )
    out_specs = (P("stream", "cross", None), P("stream", "cross", None))
    return jax.shard_map(shards, mesh=mesh, in_specs=in_specs, out_specs=out_specs, check_vma=False)
```

```python
import functools

import jax
import jax.numpy as jnp
import numpy as np
from jax import lax
from jax.experimental import pallas as pl
from jax.experimental.pallas import tpu as pltpu
from jax.sharding import PartitionSpec as P

N1 = 8
F32 = jnp.float32
BF16 = jnp.bfloat16
HIGHEST = lax.Precision.HIGHEST
VMEM_LIMIT = 16 * 2**20
VMEM = pl.BlockSpec(memory_space=pltpu.VMEM)


def legendre_values(nodes, degree):
    table = np.zeros((nodes.shape[0], degree + 1))
    table[:, 0] = 1.0
    table[:, 1] = nodes
    for order in range(2, degree + 1):
        table[:, order] = (
            (2 * order - 1) * nodes * table[:, order - 1] - (order - 1) * table[:, order - 2]
        ) / order
    return table


def derivative_table(points):
    degree = points - 1
    nodes = np.cos(np.pi * np.arange(points) / degree)
    for sweep in range(100):
        table = legendre_values(nodes, degree)
        nodes = nodes - (nodes * table[:, degree] - table[:, degree - 1]) / (
            points * table[:, degree]
        )
    gll_nodes = nodes[::-1]
    legendre_at = legendre_values(gll_nodes, degree)[:, degree]
    diff_table = np.zeros((points, points))
    for first_index in range(points):
        for second_index in range(points):
            if first_index != second_index:
                diff_table[first_index, second_index] = legendre_at[first_index] / (
                    legendre_at[second_index] * (gll_nodes[first_index] - gll_nodes[second_index])
                )
    diff_table[0, 0] = -degree * (degree + 1) / 4.0
    diff_table[degree, degree] = degree * (degree + 1) / 4.0
    return diff_table


def round_up(count, unit):
    return -(-count // unit) * unit


def dot(left, right, dims=((1,), (0,)), precision=None):
    return lax.dot_general(
        left, right, (dims, ((), ())), precision=precision, preferred_element_type=F32
    )


def split(value):
    high = value.astype(BF16)
    return high, (value - high.astype(F32)).astype(BF16)


def split3(value):
    high = value.astype(BF16)
    rest = value - high.astype(F32)
    mid = rest.astype(BF16)
    return high, mid, (rest - mid.astype(F32)).astype(BF16)


def stacked(value):
    high, low = split(value)
    return jnp.concatenate([high, low, high], 0)


def abreast(value):
    high, low = split(value)
    return jnp.concatenate([high, high, low], 1)


def even(index):
    return lax.rem(index, 2) == 0


def diff_parts():
    table = derivative_table(N1).astype(np.float32)
    high = table.astype(jnp.bfloat16).astype(np.float32)
    low = (table - high).astype(jnp.bfloat16).astype(np.float32)
    row, column = ramps(N1, N1)
    place = row * N1 + column
    found = []
    for part in (high, low):
        value = jnp.zeros((N1, N1), F32)
        for k, entry in enumerate(part.reshape(-1)):
            if entry:
                value = jnp.where(place == k, float(entry), value)
        found.append(value.astype(BF16))
    return found


def operator_factors(blocks):
    def kron(part, count, inner, turned):
        row, column = ramps(count, N1)
        quotient, rest = over(row, N1)
        pick = mask((rest if inner else quotient) == column)
        value = dot(pick, part, ((1,), (1 if turned else 0,))).astype(BF16)
        value = dot(value, pick, ((1,), (1,)))
        row, column = ramps(count, count)
        row, column = over(row, N1), over(column, N1)
        same = row[0] == column[0] if inner else row[1] == column[1]
        return jnp.where(same, value, 0.0).astype(BF16)

    parts = diff_parts()
    box = N1 * N1
    high, low = [
        jnp.concatenate([kron(part, box, False, False), kron(part, box, True, False)], 0) for part in parts
    ]
    grad = jnp.concatenate([high, high, low], 1)
    high, low = [
        jnp.concatenate([kron(part, box, False, True), kron(part, box, True, True)], 1) for part in parts
    ]
    back = jnp.concatenate([high, high, low], 1)
    high, low = [kron(part, blocks * N1, True, True) for part in parts]
    third = jnp.concatenate([high, low, high], 0)
    high, low = [kron(part, blocks * N1, True, False) for part in parts]
    return grad, third, back, jnp.concatenate([high, low, high], 0)


def local_kernel(*refs):
    count = 6
    sources, outs, scratch = refs[:count], refs[count : count + 6], refs[count + 6 :]
    lp_ref, near_ref, far_ref, mf_ref, ef_ref, es_ref = outs
    p_ref, gd_ref, go_ref, sems = scratch
    targets = (p_ref, gd_ref, go_ref, mf_ref, ef_ref, es_ref)
    copies = [
        pltpu.make_async_copy(source, target, sems.at[k])
        for k, (source, target) in enumerate(zip(sources, targets))
    ]
    for copy in copies:
        copy.start()
    layers, rows, width = p_ref.shape
    grad, third_grad, back, third_back = operator_factors(width // N1)
    copies[0].wait()
    first_blocks = layers // N1
    box = N1 * rows
    modes = mf_ref.shape[0]
    p_all = p_ref[...].reshape(layers * rows, width)
    third = dot(abreast(p_all), third_grad)
    grads = [
        dot(grad, stacked(p_all[a * box : (a + 1) * box])) for a in range(first_blocks)
    ]
    for k in (1, 2):
        copies[k].wait()
    for a in range(first_blocks):
        here = slice(a * box, (a + 1) * box)
        one, two, three = grads[a][:box], grads[a][box:], third[here]
        g = [
            gd_ref[k, a * N1 : (a + 1) * N1].reshape(box, width) for k in range(3)
        ] + [go_ref[k, a * N1 : (a + 1) * N1].reshape(box, width) for k in range(3)]
        flux_one = g[0] * one + g[3] * two + g[4] * three
        flux_two = g[3] * one + g[1] * two + g[5] * three
        flux_three = g[4] * one + g[5] * two + g[2] * three
        lp_ref[here, :] = dot(
            back, stacked(jnp.concatenate([flux_one, flux_two], 0))
        ) + dot(abreast(flux_three), third_back)
    for k in (3, 4, 5):
        copies[k].wait()
    layer = lambda l: slice(l * rows, (l + 1) * rows)
    body = (modes - 1) * rows
    up_layers = [
        (0, rows, lp_ref[layer(layers - modes), :]),
        (rows, 2 * rows, lp_ref[layer(layers - modes + 1), :] + lp_ref[layer(layers - modes + 2), :]),
        (2 * rows, body, lp_ref[(layers - modes + 3) * rows :, :]),
    ]
    down_layers = [
        (0, body - 2 * rows, lp_ref[: (modes - 3) * rows, :]),
        (body - 2 * rows, body - rows, lp_ref[layer(modes - 3), :] + lp_ref[layer(modes - 2), :]),
        (body - rows, body, lp_ref[layer(modes - 1), :]),
    ]
    forward = even(lax.axis_index("stream"))

    def fill(ref, parts, a):
        for begin, end, value in parts:
            ref[begin:end, :] = value
        ref[body:, :] = jnp.zeros((rows, width), F32)
        ref[body:, :modes] = mf_ref[:rows, a, :]
        ref[body : body + modes - rows, 16 : 16 + modes] = mf_ref[rows:, a, :]
        ref[body : body + 1, 32 : 32 + modes] = ef_ref[a : a + 1, :]

    @pl.when(forward)
    def _():
        fill(near_ref, up_layers, first_blocks - 1)
        fill(far_ref, down_layers, 0)

    @pl.when(jnp.logical_not(forward))
    def _():
        fill(near_ref, down_layers, 0)
        fill(far_ref, up_layers, first_blocks - 1)


def from_sides(near, far, axis):
    index = lax.axis_index(axis)
    is_even = even(index)
    before = jnp.where(is_even, far, near)
    after = jnp.where(is_even, near, far)
    before = jnp.where(index == 0, 0.0, before)
    after = jnp.where(index == lax.axis_size(axis) - 1, 0.0, after)
    return before, after


def rows_kernel(lp_ref, near_ref, far_ref, built_ref, out_far_ref, out_near_ref):
    rows = N1
    layers = lp_ref.shape[0] // rows
    count = N1 + 1
    padded = out_near_ref.shape[0] // 2
    width = lp_ref.shape[1]
    found = {}
    for k in (0, 1, rows - 2, rows - 1):
        before, after = from_sides(
            near_ref[pl.ds(k, count, stride=rows), :], far_ref[pl.ds(k, count, stride=rows), :], "stream"
        )
        found[k] = (before, lp_ref[pl.ds(k, layers, stride=rows), :], after)
    up = even(lax.axis_index("cross"))
    for ref, high in ((out_near_ref, up), (out_far_ref, jnp.logical_not(up))):
        for slot in range(2):
            base = slot * padded
            before, own, after = [
                jnp.where(high, one, two) for one, two in zip(found[rows - 2 + slot], found[slot])
            ]
            ref[base : base + count - 1, :] = before[: count - 1]
            base += count - 1
            for l in range(0, layers, N1):
                previous = before[count - 1 :] if l == 0 else own[l - 1 : l]
                ref[base : base + 1, :] = previous + own[l : l + 1]
                ref[base + 1 : base + N1 - 1, :] = own[l + 1 : l + N1 - 1]
                base += N1 - 1
            ref[base : base + 1, :] = own[layers - 1 :] + after[:1]
            ref[base + 1 : base + count, :] = after[1:]
            base += count
            ref[base : (slot + 1) * padded, :] = jnp.zeros(((slot + 1) * padded - base, width), F32)


def spread_columns(parts, lay, pick):
    table = dot(parts, lay, ((0,), (0,)))
    return dot(pick, jnp.concatenate(split3(table), 0))


def spread_rows(parts, pick, rows):
    pad = parts.shape[0] // 3
    table = sum(dot(parts[k * pad : (k + 1) * pad], pick) for k in range(3))
    return dot(rows, jnp.concatenate(split3(table), 0))


def halves_by_lane(value, low):
    high = value.astype(BF16).astype(F32)
    return jnp.where(low, value - high, high).astype(BF16)


def low_lanes(kin, rim):
    lane = lax.broadcasted_iota(jnp.int32, (1, 3 * (kin + rim)), 1)
    return ((lane >= 2 * kin) & (lane < 3 * kin)) | (lane >= 3 * kin + 2 * rim)


def low_back_lanes(pairs):
    return lax.broadcasted_iota(jnp.int32, (1, 3 * pairs), 1) >= 2 * pairs


def ramps(*dims):
    return [lax.broadcasted_iota(jnp.int32, dims, axis) for axis in range(2)]


def over(value, count):
    quotient = ((value.astype(F32) + 0.5) * (1.0 / count)).astype(jnp.int32)
    return quotient, value - quotient * count


def mask(hit):
    return jnp.where(hit, 1.0, 0.0).astype(BF16)


def spread_table(blocks, modes):
    row, column = ramps(modes, blocks * modes)
    return mask(row == over(column, modes)[1])


def gather_table(blocks, modes):
    row, column = ramps(blocks * N1, modes * blocks)
    node, block = over(column, blocks)
    place = row - block * N1
    hit = (place == node - 1) & (node >= 1) & (node <= N1)
    for n, at in ((0, -2), (1, -1), (N1, N1), (N1 + 1, N1 + 1)):
        hit = hit | ((node == n) & (place == at))
    return mask(hit)


def pick_table(pairs, pad, modes, which):
    row, column = ramps(pairs, 3 * pad)
    return mask(over(row, modes)[which] == over(column, pad)[1])


def pick_rows(pairs, pad, modes, which):
    row, column = ramps(pairs, pad)
    return jnp.where(over(row, modes)[which] == column, 1.0, 0.0)


def back_tables(pairs, pad, modes):
    row, column = ramps(pad, 3 * pairs)
    found = over(over(column, pairs)[1], modes)
    return mask(found[0] == row), mask(found[1] == row)


def box_rows(count, pad):
    row, column = ramps(count, 3 * pad)
    first, second = over(row, N1)
    column = over(column, pad)[1]
    return mask(first + 1 == column), mask(second + 1 == column)


def face_rows(pad):
    row, column = ramps(2 * N1, 3 * pad)
    face, first = over(row, N1)
    column = over(column, pad)[1]
    return mask(first + 1 == column), mask(jnp.where(face == 0, 1, N1) == column)


def inner_table(blocks, modes):
    row, column = ramps(modes * blocks, blocks * N1)
    node, block = over(row, blocks)
    place = column - block * N1
    hit = (place == node - 1) & (node >= 1) & (node <= N1)
    return mask(hit | ((node == 1) & (place == -1)) | ((node == N1) & (place == N1)))


def lay_tables(pad, kin, rim):
    layers = kin // N1
    row, column = ramps(3 * pad, 3 * (kin + rim))
    row = over(row, pad)[1]
    own = column < 3 * kin
    l_own, y = over(over(column, kin)[1], N1)
    kind, l_rim = over(over(jnp.maximum(column - 3 * kin, 0), rim)[1], rim // 4)
    node = jnp.where(l_own == 0, 0, jnp.where(l_own == layers - 1, N1 + 1, jnp.clip(l_own - 1, 1, N1)))
    node = jnp.where(own, node, l_rim)
    second = jnp.where(own, y + 1, jnp.where(kind < 2, kind, N1 - 2 + kind))
    inside = own | (l_rim < N1 + 2)
    return mask(inside & (row == node)), mask(inside & (row == second))


def third_parts(mt_ref, spread):
    rows, modes = mt_ref.shape
    blocks = rows // modes
    row, column = ramps(rows, rows)
    own = over(row, blocks)[1] == over(column, modes)[0]
    return [jnp.where(own, dot(part, spread), 0.0).astype(BF16) for part in split3(mt_ref[...])]


def pad_modes(pad_ref, mf_ref, ms_ref):
    modes = ms_ref.shape[0]
    first_blocks = pad_ref.shape[0] - 1
    pad_ref[...] = jnp.zeros_like(pad_ref)
    for a in range(first_blocks):
        pad_ref[a, :modes, :modes] = mf_ref[:, a, :]
    pad_ref[first_blocks, :modes, :modes] = ms_ref[:, 0, :]


def modes_kernel(
    mt_ref, e3_ref, mf_ref, ef_ref, ms_ref, es_ref,
    w_ref, e3_row_ref, own_columns_ref, own_rim_ref, second_columns_ref, pad_ref, eigen_ref, back_ref,
):
    blocks, modes = e3_ref.shape
    spread = spread_table(blocks, modes)
    gather = gather_table(blocks, modes)
    table = sum(dot(gather, part) for part in third_parts(mt_ref, spread))
    high, low = split(table)
    w_ref[...] = jnp.concatenate([high, low, high], 0)
    row, column = ramps(blocks, blocks * modes)
    e3_wide = sum(dot(part, spread) for part in split3(e3_ref[...]))
    e3_row_ref[...] = jnp.sum(
        jnp.where(row == over(column, modes)[0], e3_wide, 0.0), 0, keepdims=True
    )
    first_blocks, pairs, kin = own_columns_ref.shape
    kin, rim, pad = kin // 3, own_rim_ref.shape[2] // 3, pad_ref.shape[1]
    pad_modes(pad_ref, mf_ref, ms_ref)
    eigen_ref[...] = jnp.zeros_like(eigen_ref)
    eigen_ref[:first_blocks, :modes] = ef_ref[...]
    eigen_ref[first_blocks : first_blocks + 1, :modes] = es_ref[...]
    lay_m, lay_n = lay_tables(pad, kin, rim)
    low = low_lanes(kin, rim)
    second = jnp.concatenate(split3(pad_ref[first_blocks]), 0)
    second_columns = spread_columns(second, lay_n, pick_table(pairs, pad, modes, 1))
    second_columns_ref[...] = second_columns
    pick = pick_table(pairs, pad, modes, 0)
    for a in range(first_blocks):
        first = jnp.concatenate(split3(pad_ref[a]), 0)
        columns = halves_by_lane(spread_columns(first, lay_m, pick) * second_columns, low)
        own_columns_ref[a] = columns[:, : 3 * kin]
        own_rim_ref[a] = columns[:, 3 * kin :]
    box = back_ref.shape[1]
    back_m, back_n = back_tables(pairs, pad, modes)
    rows_m, rows_n = box_rows(box, pad)
    second_rows = spread_rows(second, back_n, rows_n)
    for a in range(first_blocks):
        first = jnp.concatenate(split3(pad_ref[a]), 0)
        back_ref[a] = halves_by_lane(spread_rows(first, back_m, rows_m) * second_rows, low_back_lanes(pairs))


def columns_kernel(
    lp_ref, near_ref, far_ref, w_ref, e3_row_ref, own_columns_ref, second_columns_ref, pad_ref,
    eigen_ref, mt_ref, v_ref, side_rim_ref, rec_ref, face_ref, wbh_ref, wbl_ref,
):
    rows = N1
    halo = (N1 + 2) * rows
    first_blocks, pairs, kin = own_columns_ref.shape
    kin, rim, pad, modes = kin // 3, side_rim_ref.shape[2] // 3, pad_ref.shape[1], N1 + 2
    box = N1 * rows
    near, far = near_ref[...], far_ref[...]
    before, after = from_sides(near, far, "stream")
    odd = jnp.logical_not(even(lax.axis_index("stream")))
    body = halo - rows
    zero = jnp.zeros((rows, lp_ref.shape[1]), F32)
    stack = jnp.concatenate(
        [before[:rows], zero, before[rows:body], lp_ref[...], after[: body - rows], zero, after[body - rows : body]], 0
    )
    u = dot(abreast(stack), w_ref[...])
    edge_near, edge_far = near[body : body + 1, 32 : 32 + pad], far[body : body + 1, 32 : 32 + pad]
    low, back_low = low_lanes(kin, rim), low_back_lanes(pairs)
    lay_m, _ = lay_tables(pad, kin, rim)
    pick_p3 = pick_table(pairs, pad, modes, 0)
    pick_p, pick_q = pick_rows(pairs, pad, modes, 0), pick_rows(pairs, pad, modes, 1)
    back_m, back_n = back_tables(pairs, pad, modes)
    face_m, face_n = face_rows(pad)
    own_eigen = eigen_ref[...]
    firsts = [jnp.concatenate([side[body:, :pad], side[body:, 16 : 16 + pad]], 0) for side in (before, after)]
    firsts = [firsts[0]] + [pad_ref[a] for a in range(first_blocks)] + [firsts[1]]
    eigens = [jnp.where(odd, edge_near, edge_far)] + [own_eigen[a : a + 1] for a in range(first_blocks)]
    eigens += [jnp.where(odd, edge_far, edge_near)]
    second = jnp.concatenate(split3(pad_ref[first_blocks]), 0)
    second_faces = spread_rows(second, back_n, face_n)
    second_sum = jnp.sum(pick_q * own_eigen[first_blocks : first_blocks + 1], 1, keepdims=True)
    for a, (first, eigen) in enumerate(zip(firsts, eigens)):
        first = jnp.concatenate(split3(first), 0)
        if a in (0, first_blocks + 1):
            columns = halves_by_lane(
                spread_columns(first, lay_m, pick_p3) * second_columns_ref[...], low
            )
            side_rim_ref[min(a, 1)] = columns[:, 3 * kin :]
            columns = columns[:, : 3 * kin]
        else:
            columns = own_columns_ref[a - 1]
        begin = a * box
        v_ref[a] = dot(columns, stacked(u[begin : begin + kin]))
        face_ref[a] = halves_by_lane(spread_rows(first, back_m, face_m) * second_faces, back_low)
        total = jnp.sum(pick_p * eigen, 1, keepdims=True) + second_sum
        rec_ref[a] = 1.0 / (total + e3_row_ref[...])
    blocks = mt_ref.shape[0] // modes
    inner = inner_table(blocks, modes)
    table = sum(
        dot(part, inner, ((0,), (0,))) for part in third_parts(mt_ref, spread_table(blocks, modes))
    )
    wbh_ref[...], wbl_ref[...] = split(table)


def spectral_columns(near_ref, far_ref, w_ref, v_ref, own_rim_ref, side_rim_ref, rec_ref):
    columns = v_ref.shape[0]
    padded = near_ref.shape[0] // 2
    before, after = from_sides(near_ref[...], far_ref[...], "cross")
    u = dot(abreast(jnp.concatenate([before, after], 0)), w_ref[...])
    u = jnp.concatenate([u, jnp.zeros((8, u.shape[1]), F32)], 0)
    found = []
    for a in range(columns):
        rim = jnp.concatenate(
            [u[k * padded + a * (N1 - 1) : k * padded + a * (N1 - 1) + 16] for k in range(4)], 0
        )
        if a in (0, columns - 1):
            table = side_rim_ref[min(a, 1)]
        else:
            table = own_rim_ref[a - 1]
        found.append((v_ref[a] + dot(table, stacked(rim))) * rec_ref[a])
    return found


def third_back(parts, wbh_ref, wbl_ref):
    high, low = split(jnp.concatenate(parts, 0))
    return dot(high, wbh_ref[...]) + dot(high, wbl_ref[...]) + dot(low, wbh_ref[...])


def faces_kernel(
    far_ref, near_ref, w_ref, v_ref, own_rim_ref, side_rim_ref, rec_ref, wbh_ref, wbl_ref, face_ref,
    out_far_ref, out_near_ref, spectral_ref,
):
    rows = N1
    found = spectral_columns(near_ref, far_ref, w_ref, v_ref, own_rim_ref, side_rim_ref, rec_ref)
    columns = len(found)
    for a in range(columns):
        spectral_ref[a] = found[a]
    parts = [dot(face_ref[a], stacked(found[a])) for a in range(columns)]
    solved = third_back(parts, wbh_ref, wbl_ref)
    row = lax.broadcasted_iota(jnp.int32, (rows, 1), 0)
    up = even(lax.axis_index("cross"))
    for a in range(1, columns - 1):
        sums = []
        for face in range(2):
            base = 16 * a + rows * face
            previous = base - 16 + rows - 1
            after = base + 16
            sums.append(
                solved[base : base + rows]
                + jnp.where(row == 0, solved[previous : previous + 1], 0.0)
                + jnp.where(row == rows - 1, solved[after : after + 1], 0.0)
            )
        here = slice((a - 1) * rows, a * rows)
        out_near_ref[here, :] = jnp.where(up, sums[1], sums[0])
        out_far_ref[here, :] = jnp.where(up, sums[0], sums[1])


def assemble_operator(lp_ref, s_near_ref, s_far_ref, c_near_ref, c_far_ref, out_ref, acc_ref):
    rows = N1
    total_rows, width = lp_ref.shape
    padded = c_near_ref.shape[0] // 2
    body = (N1 + 1) * rows
    box = N1 * rows
    before, after = from_sides(s_near_ref[...], s_far_ref[...], "stream")
    left, right = from_sides(c_near_ref[...], c_far_ref[...], "cross")
    acc_ref[...] = lp_ref[...]
    for base in range(0, total_rows, box):
        last = base + box
        previous = before[body - rows : body] if base == 0 else lp_ref[base - rows : base, :]
        following = after[:rows] if last == total_rows else lp_ref[last : last + rows, :]
        acc_ref[base : base + rows, :] = lp_ref[base : base + rows, :] + previous
        acc_ref[last - rows : last, :] = lp_ref[last - rows : last, :] + following
        node = (N1 - 1) * (base // box + 1) + 1
        low, high = pl.ds(base, N1, stride=rows), pl.ds(base + rows - 1, N1, stride=rows)
        acc_ref[low, :] = acc_ref[low, :] + left[padded + node : padded + node + N1]
        acc_ref[high, :] = acc_ref[high, :] + right[node : node + N1]
    lane = lax.broadcasted_iota(jnp.int32, (1, width), 1)
    first = (lax.rem(lane, N1) == 0) & (lane > 0)
    final = (lax.rem(lane, N1) == N1 - 1) & (lane < width - 1)
    value = acc_ref[...]
    value = (
        value
        + jnp.where(first, pltpu.roll(value, 1, 1), 0.0)
        + jnp.where(final, pltpu.roll(value, width - 1, 1), 0.0)
    )
    out_ref[...] = value.reshape(out_ref.shape)


def solve_kernel(
    lp_ref, s_near_ref, s_far_ref, c_far_ref, c_near_ref, spectral_ref, wbh_ref, wbl_ref, pad_ref, back_ref,
    operator_ref, r_ref, out_ref, acc_ref, sem,
):
    assemble_operator(lp_ref, s_near_ref, s_far_ref, c_near_ref, c_far_ref, out_ref, acc_ref)
    copy = pltpu.make_async_copy(out_ref, operator_ref, sem)
    copy.start()
    rows = N1
    box = N1 * rows
    found = [spectral_ref[a] for a in range(spectral_ref.shape[0])]
    columns = len(found)
    pad, pairs = pad_ref.shape[1], spectral_ref.shape[1]
    back_m, back_n = back_tables(pairs, pad, N1 + 2)
    rows_m, rows_n = box_rows(box, pad)
    low = low_back_lanes(pairs)
    body = (N1 + 1) * rows
    sides = from_sides(s_near_ref[...], s_far_ref[...], "stream")
    sides = [jnp.concatenate([side[body:, :pad], side[body:, 16 : 16 + pad]], 0) for side in sides]
    second = jnp.concatenate(split3(pad_ref[columns - 2]), 0)
    parts = [None] * columns
    for a, first, kept in ((0, sides[0], slice(box - 16, box)), (columns - 1, sides[1], slice(0, 16))):
        first = jnp.concatenate(split3(first), 0)
        table = spread_rows(first, back_m, rows_m[kept]) * spread_rows(second, back_n, rows_n[kept])
        parts[a] = dot(halves_by_lane(table, low), stacked(found[a]))
    for a in range(1, columns - 1):
        parts[a] = dot(back_ref[a - 1], stacked(found[a]))
    parts[0] = parts[0][16 - rows :]
    parts[-1] = parts[-1][:rows]
    solved = third_back(parts, wbh_ref, wbl_ref)
    for a in range(columns - 2):
        base = rows + a * box
        top, bottom = solved[base : base + rows], solved[base + box - rows : base + box]
        r_ref[a * box : a * box + rows, :] = top + solved[base - rows : base]
        r_ref[a * box + rows : (a + 1) * box - rows, :] = solved[base + rows : base + box - rows]
        r_ref[(a + 1) * box - rows : (a + 1) * box, :] = bottom + solved[base + box : base + box + rows]
    copy.wait()


def pass_kernel(*refs):
    count = len(refs) // 2
    for source, target in zip(refs[:count], refs[count:]):
        target[...] = source[...]


def add_kernel(r_ref, ahead_ref, far_ref, near_ref, out_ref, acc_ref, sem):
    rows = N1
    near = jnp.where(lax.axis_index("cross") < 2, ahead_ref[...], near_ref[...])
    before, after = from_sides(near, far_ref[...], "cross")
    acc_ref[...] = r_ref[...].reshape(acc_ref.shape)
    acc_ref[:, 0, :] = acc_ref[:, 0, :] + before
    acc_ref[:, rows - 1, :] = acc_ref[:, rows - 1, :] + after
    copy = pltpu.make_async_copy(acc_ref, out_ref, sem)
    copy.start()
    copy.wait()


def shape(*dims, dtype=F32):
    return pltpu.VMEM(dims, dtype)


def call(kernel, name, out, *args, scratch=(), out_specs=None, flops=1000000, place=pltpu.VMEM):
    single = not isinstance(out, list)
    args = [pltpu.with_memory_space_constraint(x, place) for x in args]
    return pl.pallas_call(
        kernel,
        out_shape=out,
        in_specs=[pl.BlockSpec(memory_space=place)] * len(args),
        out_specs=out_specs if out_specs is not None else (VMEM if single else [VMEM] * len(out)),
        scratch_shapes=list(scratch),
        compiler_params=pltpu.CompilerParams(vmem_limit_bytes=VMEM_LIMIT),
        cost_estimate=pl.CostEstimate(flops=flops, bytes_accessed=flops, transcendentals=0),
        name=name,
    )(*args)


def swaps(axis):
    count = lax.axis_size(axis)
    near = [(i, i ^ 1) for i in range(count)]
    far = [(i, (i - 1) % count if i % 2 == 0 else (i + 1) % count) for i in range(count)]
    return near, far


def swap_stream(near, far):
    first, second = swaps("stream")
    near = lax.ppermute(near, "stream", first)
    far = lax.ppermute(far, "stream", second)
    return near, far


def cross_pairs(near, ahead=None):
    count, streams = lax.axis_size("cross"), lax.axis_size("stream")
    pairs = []
    for s in range(streams):
        for i in range(count):
            j = i ^ 1 if near else i - 1 + 2 * (i % 2)
            idle = not 0 <= j < count or (ahead is not None and (i < 2) != ahead)
            pairs.append((s * count + i, (s ^ 1) * count + i if idle else s * count + j))
    return pairs


def swap_cross(near, far):
    axes = ("stream", "cross")
    return lax.ppermute(near, axes, cross_pairs(True)), lax.ppermute(far, axes, cross_pairs(False))


def swap_cross_ahead(near, far):
    axes = ("stream", "cross")
    first = lax.ppermute(near, axes, cross_pairs(True, True))
    far, near = call(pass_kernel, "pass_on", [shape(*far.shape), shape(*near.shape)], far, near)
    return first, lax.ppermute(far, axes, cross_pairs(False)), lax.ppermute(near, axes, cross_pairs(True, False))


def shards(
    pressure, geo_diag, geo_off, modes_first, modes_second, modes_third, eigen_first, eigen_second,
    eigen_third,
):
    layers, rows, width = pressure.shape
    modes = modes_first.shape[1]
    if rows != N1 or modes != N1 + 2 or lax.axis_size("stream") % 2 or lax.axis_size("cross") % 2:
        raise ValueError("unsupported sizes")
    first_blocks, third_blocks = layers // N1, width // N1
    columns = first_blocks + 2
    halo = modes * rows
    box = N1 * rows
    padded = round_up((first_blocks + 1) * (N1 - 1) + modes, 8)
    wide = third_blocks * modes

    pairs, pad = round_up(modes * modes, 16), round_up(modes, 16)

    mf = jnp.transpose(modes_first, (1, 0, 2))
    ms = jnp.transpose(modes_second, (1, 0, 2))
    mt = jnp.transpose(modes_third, (1, 0, 2)).reshape(modes * third_blocks, modes)

    inputs = [pressure, geo_diag, geo_off, mf, eigen_first, eigen_second]
    lp, s_near, s_far, mf, ef, es = call(
        local_kernel, "local_product",
        [
            shape(layers * rows, width), shape(halo, width), shape(halo, width),
            shape(modes, first_blocks, modes), shape(first_blocks, modes), shape(1, modes),
        ],
        *inputs, place=pltpu.HBM,
        scratch=[pltpu.VMEM(x.shape, x.dtype) for x in inputs[:3]] + [pltpu.SemaphoreType.DMA((len(inputs),))],
    )
    s_near, s_far = swap_stream(s_near, s_far)
    kin, rim_width = 3 * (N1 + 4) * rows, 3 * 64
    w, e3_row, own_columns, own_rim, second_columns, padded_modes, eigen, own_back = call(
        modes_kernel, "mode_tables",
        [
            shape(3 * width, wide, dtype=BF16), shape(1, wide),
            shape(first_blocks, pairs, kin, dtype=BF16), shape(first_blocks, pairs, rim_width, dtype=BF16),
            shape(pairs, kin + rim_width), shape(first_blocks + 1, pad, pad), shape(first_blocks + 1, pad),
            shape(first_blocks, box, 3 * pairs, dtype=BF16),
        ],
        mt, eigen_third, mf, ef, ms, es,
    )
    c_far, c_near = call(
        rows_kernel, "rows_to_send",
        [shape(2 * padded, width), shape(2 * padded, width)],
        lp, s_near, s_far, e3_row,
    )
    c_near, c_far = swap_cross(c_near, c_far)
    v, side_rim, rec, face, wbh, wbl = call(
        columns_kernel, "own_part",
        [
            shape(columns, pairs, wide), shape(2, pairs, rim_width, dtype=BF16), shape(columns, pairs, wide),
            shape(columns, 16, 3 * pairs, dtype=BF16), shape(wide, width, dtype=BF16), shape(wide, width, dtype=BF16),
        ],
        lp, s_near, s_far, w, e3_row, own_columns, second_columns, padded_modes, eigen, mt,
    )
    f_far, f_near, spectral = call(
        faces_kernel, "faces", [shape(layers, width), shape(layers, width), shape(columns, pairs, wide)],
        c_far, c_near, w, v, own_rim, side_rim, rec, wbh, wbl, face,
    )
    f_ahead, f_far, f_near = swap_cross_ahead(f_near, f_far)
    result = pltpu.HBM(pressure.shape, F32)
    in_hbm = pl.BlockSpec(memory_space=pltpu.HBM)
    operator_out, restricted = call(
        solve_kernel, "solve", [result, shape(layers * rows, width)],
        lp, s_near, s_far, c_far, c_near, spectral, wbh, wbl, padded_modes, own_back, out_specs=[in_hbm, VMEM],
        scratch=[
            pltpu.VMEM(pressure.shape, F32), pltpu.VMEM((layers * rows, width), F32), pltpu.SemaphoreType.DMA,
        ],
    )
    preconditioned = call(
        add_kernel, "preconditioned", result, restricted, f_ahead, f_far, f_near, out_specs=in_hbm,
        scratch=[pltpu.VMEM(pressure.shape, F32), pltpu.SemaphoreType.DMA],
    )
    return (operator_out, preconditioned)


def solution(mesh):
    in_specs = (
        P("stream", "cross", None),
        P(None, "stream", "cross", None),
        P(None, "stream", "cross", None),
        P("stream", None, None),
        P("cross", None, None),
        P(),
        P("stream", None),
        P("cross", None),
        P(),
    )
    out_specs = (P("stream", "cross", None), P("stream", "cross", None))
    return jax.shard_map(shards, mesh=mesh, in_specs=in_specs, out_specs=out_specs, check_vma=False)
```

```python
import functools

import jax
import jax.numpy as jnp
import numpy as np
from jax import lax
from jax.experimental import pallas as pl
from jax.experimental.pallas import tpu as pltpu
from jax.sharding import PartitionSpec as P

N1 = 8
F32 = jnp.float32
BF16 = jnp.bfloat16
HIGHEST = lax.Precision.HIGHEST
VMEM_LIMIT = 16 * 2**20
VMEM = pl.BlockSpec(memory_space=pltpu.VMEM)


def legendre_values(nodes, degree):
    table = np.zeros((nodes.shape[0], degree + 1))
    table[:, 0] = 1.0
    table[:, 1] = nodes
    for order in range(2, degree + 1):
        table[:, order] = (
            (2 * order - 1) * nodes * table[:, order - 1] - (order - 1) * table[:, order - 2]
        ) / order
    return table


def derivative_table(points):
    degree = points - 1
    nodes = np.cos(np.pi * np.arange(points) / degree)
    for sweep in range(100):
        table = legendre_values(nodes, degree)
        nodes = nodes - (nodes * table[:, degree] - table[:, degree - 1]) / (
            points * table[:, degree]
        )
    gll_nodes = nodes[::-1]
    legendre_at = legendre_values(gll_nodes, degree)[:, degree]
    diff_table = np.zeros((points, points))
    for first_index in range(points):
        for second_index in range(points):
            if first_index != second_index:
                diff_table[first_index, second_index] = legendre_at[first_index] / (
                    legendre_at[second_index] * (gll_nodes[first_index] - gll_nodes[second_index])
                )
    diff_table[0, 0] = -degree * (degree + 1) / 4.0
    diff_table[degree, degree] = degree * (degree + 1) / 4.0
    return diff_table


def round_up(count, unit):
    return -(-count // unit) * unit


def dot(left, right, dims=((1,), (0,)), precision=None):
    return lax.dot_general(
        left, right, (dims, ((), ())), precision=precision, preferred_element_type=F32
    )


def split(value):
    high = value.astype(BF16)
    return high, (value - high.astype(F32)).astype(BF16)


def split3(value):
    high = value.astype(BF16)
    rest = value - high.astype(F32)
    mid = rest.astype(BF16)
    return high, mid, (rest - mid.astype(F32)).astype(BF16)


def stacked(value):
    high, low = split(value)
    return jnp.concatenate([high, low, high], 0)


def abreast(value):
    high, low = split(value)
    return jnp.concatenate([high, high, low], 1)


def even(index):
    return lax.rem(index, 2) == 0


def diff_parts():
    table = derivative_table(N1).astype(np.float32)
    high = table.astype(jnp.bfloat16).astype(np.float32)
    low = (table - high).astype(jnp.bfloat16).astype(np.float32)
    row, column = ramps(N1, N1)
    place = row * N1 + column
    found = []
    for part in (high, low):
        value = jnp.zeros((N1, N1), F32)
        for k, entry in enumerate(part.reshape(-1)):
            if entry:
                value = jnp.where(place == k, float(entry), value)
        found.append(value.astype(BF16))
    return found


def operator_factors(blocks):
    def kron(part, count, inner, turned):
        row, column = ramps(count, N1)
        quotient, rest = over(row, N1)
        pick = mask((rest if inner else quotient) == column)
        value = dot(pick, part, ((1,), (1 if turned else 0,))).astype(BF16)
        row, column = ramps(N1, count)
        value = dot(value, mask(over(column, N1)[1 if inner else 0] == row))
        row, column = ramps(count, count)
        row, column = over(row, N1), over(column, N1)
        same = row[0] == column[0] if inner else row[1] == column[1]
        return jnp.where(same, value, 0.0).astype(BF16)

    parts = diff_parts()
    box = N1 * N1
    high, low = [
        jnp.concatenate([kron(part, box, False, False), kron(part, box, True, False)], 0) for part in parts
    ]
    grad = jnp.concatenate([high, high, low], 1)
    high, low = [
        jnp.concatenate([kron(part, box, False, True), kron(part, box, True, True)], 1) for part in parts
    ]
    back = jnp.concatenate([high, high, low], 1)
    high, low = [kron(part, blocks * N1, True, True) for part in parts]
    third = jnp.concatenate([high, low, high], 0)
    high, low = [kron(part, blocks * N1, True, False) for part in parts]
    return grad, third, back, jnp.concatenate([high, low, high], 0)


def local_kernel(*refs):
    count = 6
    sources, outs, scratch = refs[:count], refs[count : count + 6], refs[count + 6 :]
    lp_ref, near_ref, far_ref, mf_ref, ef_ref, es_ref = outs
    p_ref, gd_ref, go_ref, sems = scratch
    targets = (p_ref, gd_ref, go_ref, mf_ref, ef_ref, es_ref)
    copies = [
        pltpu.make_async_copy(source, target, sems.at[k])
        for k, (source, target) in enumerate(zip(sources, targets))
    ]
    for copy in copies:
        copy.start()
    layers, rows, width = p_ref.shape
    grad, third_grad, back, third_back = operator_factors(width // N1)
    copies[0].wait()
    first_blocks = layers // N1
    box = N1 * rows
    modes = mf_ref.shape[0]
    p_all = p_ref[...].reshape(layers * rows, width)
    third = dot(abreast(p_all), third_grad)
    grads = [
        dot(grad, stacked(p_all[a * box : (a + 1) * box])) for a in range(first_blocks)
    ]
    for k in (1, 2):
        copies[k].wait()
    for a in range(first_blocks):
        here = slice(a * box, (a + 1) * box)
        one, two, three = grads[a][:box], grads[a][box:], third[here]
        g = [
            gd_ref[k, a * N1 : (a + 1) * N1].reshape(box, width) for k in range(3)
        ] + [go_ref[k, a * N1 : (a + 1) * N1].reshape(box, width) for k in range(3)]
        flux_one = g[0] * one + g[3] * two + g[4] * three
        flux_two = g[3] * one + g[1] * two + g[5] * three
        flux_three = g[4] * one + g[5] * two + g[2] * three
        lp_ref[here, :] = dot(
            back, stacked(jnp.concatenate([flux_one, flux_two], 0))
        ) + dot(abreast(flux_three), third_back)
    for k in (3, 4, 5):
        copies[k].wait()
    layer = lambda l: slice(l * rows, (l + 1) * rows)
    body = (modes - 1) * rows
    up_layers = [
        (0, rows, lp_ref[layer(layers - modes), :]),
        (rows, 2 * rows, lp_ref[layer(layers - modes + 1), :] + lp_ref[layer(layers - modes + 2), :]),
        (2 * rows, body, lp_ref[(layers - modes + 3) * rows :, :]),
    ]
    down_layers = [
        (0, body - 2 * rows, lp_ref[: (modes - 3) * rows, :]),
        (body - 2 * rows, body - rows, lp_ref[layer(modes - 3), :] + lp_ref[layer(modes - 2), :]),
        (body - rows, body, lp_ref[layer(modes - 1), :]),
    ]
    forward = even(lax.axis_index("stream"))

    def fill(ref, parts, a):
        for begin, end, value in parts:
            ref[begin:end, :] = value
        ref[body:, :] = jnp.zeros((rows, width), F32)
        ref[body:, :modes] = mf_ref[:rows, a, :]
        ref[body : body + modes - rows, 16 : 16 + modes] = mf_ref[rows:, a, :]
        ref[body : body + 1, 32 : 32 + modes] = ef_ref[a : a + 1, :]

    @pl.when(forward)
    def _():
        fill(near_ref, up_layers, first_blocks - 1)
        fill(far_ref, down_layers, 0)

    @pl.when(jnp.logical_not(forward))
    def _():
        fill(near_ref, down_layers, 0)
        fill(far_ref, up_layers, first_blocks - 1)


def from_sides(near, far, axis):
    index = lax.axis_index(axis)
    is_even = even(index)
    before = jnp.where(is_even, far, near)
    after = jnp.where(is_even, near, far)
    before = jnp.where(index == 0, 0.0, before)
    after = jnp.where(index == lax.axis_size(axis) - 1, 0.0, after)
    return before, after


def rows_kernel(lp_ref, near_ref, far_ref, built_ref, out_far_ref, out_near_ref):
    rows = N1
    layers = lp_ref.shape[0] // rows
    count = N1 + 1
    padded = out_near_ref.shape[0] // 2
    width = lp_ref.shape[1]
    found = {}
    for k in (0, 1, rows - 2, rows - 1):
        before, after = from_sides(
            near_ref[pl.ds(k, count, stride=rows), :], far_ref[pl.ds(k, count, stride=rows), :], "stream"
        )
        found[k] = (before, lp_ref[pl.ds(k, layers, stride=rows), :], after)
    up = even(lax.axis_index("cross"))
    for ref, high in ((out_near_ref, up), (out_far_ref, jnp.logical_not(up))):
        for slot in range(2):
            base = slot * padded
            before, own, after = [
                jnp.where(high, one, two) for one, two in zip(found[rows - 2 + slot], found[slot])
            ]
            ref[base : base + count - 1, :] = before[: count - 1]
            base += count - 1
            for l in range(0, layers, N1):
                previous = before[count - 1 :] if l == 0 else own[l - 1 : l]
                ref[base : base + 1, :] = previous + own[l : l + 1]
                ref[base + 1 : base + N1 - 1, :] = own[l + 1 : l + N1 - 1]
                base += N1 - 1
            ref[base : base + 1, :] = own[layers - 1 :] + after[:1]
            ref[base + 1 : base + count, :] = after[1:]
            base += count
            ref[base : (slot + 1) * padded, :] = jnp.zeros(((slot + 1) * padded - base, width), F32)


def spread_columns(parts, lay, pick):
    table = dot(parts, lay, ((0,), (0,)))
    return dot(pick, jnp.concatenate(split3(table), 0))


def spread_rows(parts, pick, rows):
    pad = parts.shape[0] // 3
    table = sum(dot(parts[k * pad : (k + 1) * pad], pick) for k in range(3))
    return dot(rows, jnp.concatenate(split3(table), 0))


def halves_by_lane(value, low):
    high = value.astype(BF16).astype(F32)
    return jnp.where(low, value - high, high).astype(BF16)


def low_lanes(kin, rim):
    lane = lax.broadcasted_iota(jnp.int32, (1, 3 * (kin + rim)), 1)
    return ((lane >= 2 * kin) & (lane < 3 * kin)) | (lane >= 3 * kin + 2 * rim)


def low_back_lanes(pairs):
    return lax.broadcasted_iota(jnp.int32, (1, 3 * pairs), 1) >= 2 * pairs


def ramps(*dims):
    return [lax.broadcasted_iota(jnp.int32, dims, axis) for axis in range(2)]


def over(value, count):
    if count & (count - 1) == 0:
        return lax.shift_right_logical(value, count.bit_length() - 1), value & (count - 1)
    quotient = ((value.astype(F32) + 0.5) * (1.0 / count)).astype(jnp.int32)
    return quotient, value - quotient * count


def mask(hit):
    return jnp.where(hit, 1.0, 0.0).astype(BF16)


def spread_table(blocks, modes):
    row, column = ramps(modes, blocks * modes)
    return mask(row == over(column, modes)[1])


def gather_table(blocks, modes):
    row, column = ramps(blocks * N1, modes * blocks)
    node, block = over(column, blocks)
    place = row - block * N1
    hit = (place == node - 1) & (node >= 1) & (node <= N1)
    for n, at in ((0, -2), (1, -1), (N1, N1), (N1 + 1, N1 + 1)):
        hit = hit | ((node == n) & (place == at))
    return mask(hit)


def pick_table(pairs, pad, modes, which):
    row, column = ramps(pairs, 3 * pad)
    return mask(over(row, modes)[which] == over(column, pad)[1])


def pick_rows(pairs, pad, modes, which):
    row, column = ramps(pairs, pad)
    return jnp.where(over(row, modes)[which] == column, 1.0, 0.0)


def back_tables(pairs, pad, modes):
    row, column = ramps(pad, 3 * pairs)
    found = over(over(column, pairs)[1], modes)
    return mask(found[0] == row), mask(found[1] == row)


def box_rows(count, pad):
    row, column = ramps(count, 3 * pad)
    first, second = over(row, N1)
    column = over(column, pad)[1]
    return mask(first + 1 == column), mask(second + 1 == column)


def face_rows(pad):
    row, column = ramps(2 * N1, 3 * pad)
    face, first = over(row, N1)
    column = over(column, pad)[1]
    return mask(first + 1 == column), mask(jnp.where(face == 0, 1, N1) == column)


def inner_table(blocks, modes):
    row, column = ramps(modes * blocks, blocks * N1)
    node, block = over(row, blocks)
    place = column - block * N1
    hit = (place == node - 1) & (node >= 1) & (node <= N1)
    return mask(hit | ((node == 1) & (place == -1)) | ((node == N1) & (place == N1)))


def lay_tables(pad, kin, rim):
    layers = kin // N1
    row, column = ramps(3 * pad, 3 * (kin + rim))
    row = over(row, pad)[1]
    own = column < 3 * kin
    l_own, y = over(over(column, kin)[1], N1)
    kind, l_rim = over(over(jnp.maximum(column - 3 * kin, 0), rim)[1], rim // 4)
    node = jnp.where(l_own == 0, 0, jnp.where(l_own == layers - 1, N1 + 1, jnp.clip(l_own - 1, 1, N1)))
    node = jnp.where(own, node, l_rim)
    second = jnp.where(own, y + 1, jnp.where(kind < 2, kind, N1 - 2 + kind))
    inside = own | (l_rim < N1 + 2)
    return mask(inside & (row == node)), mask(inside & (row == second))


def third_parts(mt_ref, spread):
    rows, modes = mt_ref.shape
    blocks = rows // modes
    row, column = ramps(rows, rows)
    own = over(row, blocks)[1] == over(column, modes)[0]
    return [jnp.where(own, dot(part, spread), 0.0).astype(BF16) for part in split3(mt_ref[...])]


def pad_modes(pad_ref, mf_ref, ms_ref):
    modes = ms_ref.shape[0]
    first_blocks = pad_ref.shape[0] - 1
    pad_ref[...] = jnp.zeros_like(pad_ref)
    for a in range(first_blocks):
        pad_ref[a, :modes, :modes] = mf_ref[:, a, :]
    pad_ref[first_blocks, :modes, :modes] = ms_ref[:, 0, :]


def modes_kernel(
    mt_ref, e3_ref, mf_ref, ef_ref, ms_ref, es_ref,
    w_ref, e3_row_ref, own_columns_ref, own_rim_ref, second_columns_ref, pad_ref, eigen_ref, back_ref,
):
    blocks, modes = e3_ref.shape
    spread = spread_table(blocks, modes)
    gather = gather_table(blocks, modes)
    table = sum(dot(gather, part) for part in third_parts(mt_ref, spread))
    high, low = split(table)
    w_ref[...] = jnp.concatenate([high, low, high], 0)
    row, column = ramps(blocks, blocks * modes)
    e3_wide = sum(dot(part, spread) for part in split3(e3_ref[...]))
    e3_row_ref[...] = jnp.sum(
        jnp.where(row == over(column, modes)[0], e3_wide, 0.0), 0, keepdims=True
    )
    first_blocks, pairs, kin = own_columns_ref.shape
    kin, rim, pad = kin // 3, own_rim_ref.shape[2] // 3, pad_ref.shape[1]
    pad_modes(pad_ref, mf_ref, ms_ref)
    eigen_ref[...] = jnp.zeros_like(eigen_ref)
    eigen_ref[:first_blocks, :modes] = ef_ref[...]
    eigen_ref[first_blocks : first_blocks + 1, :modes] = es_ref[...]
    lay_m, lay_n = lay_tables(pad, kin, rim)
    low = low_lanes(kin, rim)
    second = jnp.concatenate(split3(pad_ref[first_blocks]), 0)
    second_columns = spread_columns(second, lay_n, pick_table(pairs, pad, modes, 1))
    second_columns_ref[...] = second_columns
    pick = pick_table(pairs, pad, modes, 0)
    for a in range(first_blocks):
        first = jnp.concatenate(split3(pad_ref[a]), 0)
        columns = halves_by_lane(spread_columns(first, lay_m, pick) * second_columns, low)
        own_columns_ref[a] = columns[:, : 3 * kin]
        own_rim_ref[a] = columns[:, 3 * kin :]
    box = back_ref.shape[1]
    back_m, back_n = back_tables(pairs, pad, modes)
    rows_m, rows_n = box_rows(box, pad)
    second_rows = spread_rows(second, back_n, rows_n)
    for a in range(first_blocks):
        first = jnp.concatenate(split3(pad_ref[a]), 0)
        back_ref[a] = halves_by_lane(spread_rows(first, back_m, rows_m) * second_rows, low_back_lanes(pairs))


def columns_kernel(
    lp_ref, near_ref, far_ref, w_ref, e3_row_ref, own_columns_ref, second_columns_ref, pad_ref,
    eigen_ref, mt_ref, v_ref, side_rim_ref, rec_ref, face_ref, wbh_ref, wbl_ref,
):
    rows = N1
    halo = (N1 + 2) * rows
    first_blocks, pairs, kin = own_columns_ref.shape
    kin, rim, pad, modes = kin // 3, side_rim_ref.shape[2] // 3, pad_ref.shape[1], N1 + 2
    box = N1 * rows
    near, far = near_ref[...], far_ref[...]
    before, after = from_sides(near, far, "stream")
    odd = jnp.logical_not(even(lax.axis_index("stream")))
    body = halo - rows
    zero = jnp.zeros((rows, lp_ref.shape[1]), F32)
    stack = jnp.concatenate(
        [before[:rows], zero, before[rows:body], lp_ref[...], after[: body - rows], zero, after[body - rows : body]], 0
    )
    u = dot(abreast(stack), w_ref[...])
    edge_near, edge_far = near[body : body + 1, 32 : 32 + pad], far[body : body + 1, 32 : 32 + pad]
    low, back_low = low_lanes(kin, rim), low_back_lanes(pairs)
    lay_m, _ = lay_tables(pad, kin, rim)
    pick_p3 = pick_table(pairs, pad, modes, 0)
    pick_p, pick_q = pick_rows(pairs, pad, modes, 0), pick_rows(pairs, pad, modes, 1)
    back_m, back_n = back_tables(pairs, pad, modes)
    face_m, face_n = face_rows(pad)
    own_eigen = eigen_ref[...]
    firsts = [jnp.concatenate([side[body:, :pad], side[body:, 16 : 16 + pad]], 0) for side in (before, after)]
    firsts = [firsts[0]] + [pad_ref[a] for a in range(first_blocks)] + [firsts[1]]
    eigens = [jnp.where(odd, edge_near, edge_far)] + [own_eigen[a : a + 1] for a in range(first_blocks)]
    eigens += [jnp.where(odd, edge_far, edge_near)]
    second = jnp.concatenate(split3(pad_ref[first_blocks]), 0)
    second_faces = spread_rows(second, back_n, face_n)
    second_sum = jnp.sum(pick_q * own_eigen[first_blocks : first_blocks + 1], 1, keepdims=True)
    for a, (first, eigen) in enumerate(zip(firsts, eigens)):
        first = jnp.concatenate(split3(first), 0)
        if a in (0, first_blocks + 1):
            columns = halves_by_lane(
                spread_columns(first, lay_m, pick_p3) * second_columns_ref[...], low
            )
            side_rim_ref[min(a, 1)] = columns[:, 3 * kin :]
            columns = columns[:, : 3 * kin]
        else:
            columns = own_columns_ref[a - 1]
        begin = a * box
        v_ref[a] = dot(columns, stacked(u[begin : begin + kin]))
        face_ref[a] = halves_by_lane(spread_rows(first, back_m, face_m) * second_faces, back_low)
        total = jnp.sum(pick_p * eigen, 1, keepdims=True) + second_sum
        rec_ref[a] = 1.0 / (total + e3_row_ref[...])
    blocks = mt_ref.shape[0] // modes
    inner = inner_table(blocks, modes)
    table = sum(
        dot(part, inner, ((0,), (0,))) for part in third_parts(mt_ref, spread_table(blocks, modes))
    )
    wbh_ref[...], wbl_ref[...] = split(table)


def spectral_columns(near_ref, far_ref, w_ref, v_ref, own_rim_ref, side_rim_ref, rec_ref):
    columns = v_ref.shape[0]
    padded = near_ref.shape[0] // 2
    before, after = from_sides(near_ref[...], far_ref[...], "cross")
    u = dot(abreast(jnp.concatenate([before, after], 0)), w_ref[...])
    u = jnp.concatenate([u, jnp.zeros((8, u.shape[1]), F32)], 0)
    found = []
    for a in range(columns):
        rim = jnp.concatenate(
            [u[k * padded + a * (N1 - 1) : k * padded + a * (N1 - 1) + 16] for k in range(4)], 0
        )
        if a in (0, columns - 1):
            table = side_rim_ref[min(a, 1)]
        else:
            table = own_rim_ref[a - 1]
        found.append((v_ref[a] + dot(table, stacked(rim))) * rec_ref[a])
    return found


def third_back(parts, wbh_ref, wbl_ref):
    high, low = split(jnp.concatenate(parts, 0))
    return dot(high, wbh_ref[...]) + dot(high, wbl_ref[...]) + dot(low, wbh_ref[...])


def faces_kernel(
    far_ref, near_ref, w_ref, v_ref, own_rim_ref, side_rim_ref, rec_ref, wbh_ref, wbl_ref, face_ref,
    out_far_ref, out_near_ref, spectral_ref,
):
    rows = N1
    found = spectral_columns(near_ref, far_ref, w_ref, v_ref, own_rim_ref, side_rim_ref, rec_ref)
    columns = len(found)
    for a in range(columns):
        spectral_ref[a] = found[a]
    parts = [dot(face_ref[a], stacked(found[a])) for a in range(columns)]
    solved = third_back(parts, wbh_ref, wbl_ref)
    row = lax.broadcasted_iota(jnp.int32, (rows, 1), 0)
    up = even(lax.axis_index("cross"))
    for a in range(1, columns - 1):
        sums = []
        for face in range(2):
            base = 16 * a + rows * face
            previous = base - 16 + rows - 1
            after = base + 16
            sums.append(
                solved[base : base + rows]
                + jnp.where(row == 0, solved[previous : previous + 1], 0.0)
                + jnp.where(row == rows - 1, solved[after : after + 1], 0.0)
            )
        here = slice((a - 1) * rows, a * rows)
        out_near_ref[here, :] = jnp.where(up, sums[1], sums[0])
        out_far_ref[here, :] = jnp.where(up, sums[0], sums[1])


def assemble_operator(lp_ref, s_near_ref, s_far_ref, c_near_ref, c_far_ref, out_ref, acc_ref):
    rows = N1
    total_rows, width = lp_ref.shape
    padded = c_near_ref.shape[0] // 2
    body = (N1 + 1) * rows
    box = N1 * rows
    before, after = from_sides(s_near_ref[...], s_far_ref[...], "stream")
    left, right = from_sides(c_near_ref[...], c_far_ref[...], "cross")
    acc_ref[...] = lp_ref[...]
    for base in range(0, total_rows, box):
        last = base + box
        previous = before[body - rows : body] if base == 0 else lp_ref[base - rows : base, :]
        following = after[:rows] if last == total_rows else lp_ref[last : last + rows, :]
        acc_ref[base : base + rows, :] = lp_ref[base : base + rows, :] + previous
        acc_ref[last - rows : last, :] = lp_ref[last - rows : last, :] + following
        node = (N1 - 1) * (base // box + 1) + 1
        low, high = pl.ds(base, N1, stride=rows), pl.ds(base + rows - 1, N1, stride=rows)
        acc_ref[low, :] = acc_ref[low, :] + left[padded + node : padded + node + N1]
        acc_ref[high, :] = acc_ref[high, :] + right[node : node + N1]
    lane = lax.broadcasted_iota(jnp.int32, (1, width), 1)
    first = (lax.rem(lane, N1) == 0) & (lane > 0)
    final = (lax.rem(lane, N1) == N1 - 1) & (lane < width - 1)
    value = acc_ref[...]
    value = (
        value
        + jnp.where(first, pltpu.roll(value, 1, 1), 0.0)
        + jnp.where(final, pltpu.roll(value, width - 1, 1), 0.0)
    )
    out_ref[...] = value.reshape(out_ref.shape)


def solve_kernel(
    lp_ref, s_near_ref, s_far_ref, c_far_ref, c_near_ref, spectral_ref, wbh_ref, wbl_ref, pad_ref, back_ref,
    operator_ref, r_ref, out_ref, acc_ref, sem,
):
    assemble_operator(lp_ref, s_near_ref, s_far_ref, c_near_ref, c_far_ref, out_ref, acc_ref)
    copy = pltpu.make_async_copy(out_ref, operator_ref, sem)
    copy.start()
    rows = N1
    box = N1 * rows
    found = [spectral_ref[a] for a in range(spectral_ref.shape[0])]
    columns = len(found)
    pad, pairs = pad_ref.shape[1], spectral_ref.shape[1]
    back_m, back_n = back_tables(pairs, pad, N1 + 2)
    rows_m, rows_n = box_rows(box, pad)
    low = low_back_lanes(pairs)
    body = (N1 + 1) * rows
    sides = from_sides(s_near_ref[...], s_far_ref[...], "stream")
    sides = [jnp.concatenate([side[body:, :pad], side[body:, 16 : 16 + pad]], 0) for side in sides]
    second = jnp.concatenate(split3(pad_ref[columns - 2]), 0)
    parts = [None] * columns
    for a, first, kept in ((0, sides[0], slice(box - 16, box)), (columns - 1, sides[1], slice(0, 16))):
        first = jnp.concatenate(split3(first), 0)
        table = spread_rows(first, back_m, rows_m[kept]) * spread_rows(second, back_n, rows_n[kept])
        parts[a] = dot(halves_by_lane(table, low), stacked(found[a]))
    for a in range(1, columns - 1):
        parts[a] = dot(back_ref[a - 1], stacked(found[a]))
    parts[0] = parts[0][16 - rows :]
    parts[-1] = parts[-1][:rows]
    solved = third_back(parts, wbh_ref, wbl_ref)
    for a in range(columns - 2):
        base = rows + a * box
        top, bottom = solved[base : base + rows], solved[base + box - rows : base + box]
        r_ref[a * box : a * box + rows, :] = top + solved[base - rows : base]
        r_ref[a * box + rows : (a + 1) * box - rows, :] = solved[base + rows : base + box - rows]
        r_ref[(a + 1) * box - rows : (a + 1) * box, :] = bottom + solved[base + box : base + box + rows]
    copy.wait()


def pass_kernel(*refs):
    count = len(refs) // 2
    for source, target in zip(refs[:count], refs[count:]):
        target[...] = source[...]


def add_kernel(r_ref, ahead_ref, far_ref, near_ref, out_ref, acc_ref, sem):
    rows = N1
    near = jnp.where(lax.axis_index("cross") < 2, ahead_ref[...], near_ref[...])
    before, after = from_sides(near, far_ref[...], "cross")
    acc_ref[...] = r_ref[...].reshape(acc_ref.shape)
    acc_ref[:, 0, :] = acc_ref[:, 0, :] + before
    acc_ref[:, rows - 1, :] = acc_ref[:, rows - 1, :] + after
    copy = pltpu.make_async_copy(acc_ref, out_ref, sem)
    copy.start()
    copy.wait()


def shape(*dims, dtype=F32):
    return pltpu.VMEM(dims, dtype)


def call(kernel, name, out, *args, scratch=(), out_specs=None, flops=1000000, place=pltpu.VMEM):
    single = not isinstance(out, list)
    args = [pltpu.with_memory_space_constraint(x, place) for x in args]
    return pl.pallas_call(
        kernel,
        out_shape=out,
        in_specs=[pl.BlockSpec(memory_space=place)] * len(args),
        out_specs=out_specs if out_specs is not None else (VMEM if single else [VMEM] * len(out)),
        scratch_shapes=list(scratch),
        compiler_params=pltpu.CompilerParams(vmem_limit_bytes=VMEM_LIMIT),
        cost_estimate=pl.CostEstimate(flops=flops, bytes_accessed=flops, transcendentals=0),
        name=name,
    )(*args)


def swaps(axis):
    count = lax.axis_size(axis)
    near = [(i, i ^ 1) for i in range(count)]
    far = [(i, (i - 1) % count if i % 2 == 0 else (i + 1) % count) for i in range(count)]
    return near, far


def swap_stream(near, far):
    first, second = swaps("stream")
    near = lax.ppermute(near, "stream", first)
    far = lax.ppermute(far, "stream", second)
    return near, far


def cross_pairs(near, ahead=None):
    count, streams = lax.axis_size("cross"), lax.axis_size("stream")
    pairs = []
    for s in range(streams):
        for i in range(count):
            j = i ^ 1 if near else i - 1 + 2 * (i % 2)
            idle = not 0 <= j < count or (ahead is not None and (i < 2) != ahead)
            pairs.append((s * count + i, (s ^ 1) * count + i if idle else s * count + j))
    return pairs


def swap_cross(near, far):
    axes = ("stream", "cross")
    return lax.ppermute(near, axes, cross_pairs(True)), lax.ppermute(far, axes, cross_pairs(False))


def swap_cross_ahead(near, far):
    axes = ("stream", "cross")
    first = lax.ppermute(near, axes, cross_pairs(True, True))
    far, near = call(pass_kernel, "pass_on", [shape(*far.shape), shape(*near.shape)], far, near)
    return first, lax.ppermute(far, axes, cross_pairs(False)), lax.ppermute(near, axes, cross_pairs(True, False))


def shards(
    pressure, geo_diag, geo_off, modes_first, modes_second, modes_third, eigen_first, eigen_second,
    eigen_third,
):
    layers, rows, width = pressure.shape
    modes = modes_first.shape[1]
    if rows != N1 or modes != N1 + 2 or lax.axis_size("stream") % 2 or lax.axis_size("cross") % 2:
        raise ValueError("unsupported sizes")
    first_blocks, third_blocks = layers // N1, width // N1
    columns = first_blocks + 2
    halo = modes * rows
    box = N1 * rows
    padded = round_up((first_blocks + 1) * (N1 - 1) + modes, 8)
    wide = third_blocks * modes

    pairs, pad = round_up(modes * modes, 16), round_up(modes, 16)

    mf = jnp.transpose(modes_first, (1, 0, 2))
    ms = jnp.transpose(modes_second, (1, 0, 2))
    mt = jnp.transpose(modes_third, (1, 0, 2)).reshape(modes * third_blocks, modes)

    inputs = [pressure, geo_diag, geo_off, mf, eigen_first, eigen_second]
    lp, s_near, s_far, mf, ef, es = call(
        local_kernel, "local_product",
        [
            shape(layers * rows, width), shape(halo, width), shape(halo, width),
            shape(modes, first_blocks, modes), shape(first_blocks, modes), shape(1, modes),
        ],
        *inputs, place=pltpu.HBM,
        scratch=[pltpu.VMEM(x.shape, x.dtype) for x in inputs[:3]] + [pltpu.SemaphoreType.DMA((len(inputs),))],
    )
    s_near, s_far = swap_stream(s_near, s_far)
    kin, rim_width = 3 * (N1 + 4) * rows, 3 * 64
    w, e3_row, own_columns, own_rim, second_columns, padded_modes, eigen, own_back = call(
        modes_kernel, "mode_tables",
        [
            shape(3 * width, wide, dtype=BF16), shape(1, wide),
            shape(first_blocks, pairs, kin, dtype=BF16), shape(first_blocks, pairs, rim_width, dtype=BF16),
            shape(pairs, kin + rim_width), shape(first_blocks + 1, pad, pad), shape(first_blocks + 1, pad),
            shape(first_blocks, box, 3 * pairs, dtype=BF16),
        ],
        mt, eigen_third, mf, ef, ms, es,
    )
    c_far, c_near = call(
        rows_kernel, "rows_to_send",
        [shape(2 * padded, width), shape(2 * padded, width)],
        lp, s_near, s_far, e3_row,
    )
    c_near, c_far = swap_cross(c_near, c_far)
    v, side_rim, rec, face, wbh, wbl = call(
        columns_kernel, "own_part",
        [
            shape(columns, pairs, wide), shape(2, pairs, rim_width, dtype=BF16), shape(columns, pairs, wide),
            shape(columns, 16, 3 * pairs, dtype=BF16), shape(wide, width, dtype=BF16), shape(wide, width, dtype=BF16),
        ],
        lp, s_near, s_far, w, e3_row, own_columns, second_columns, padded_modes, eigen, mt,
    )
    f_far, f_near, spectral = call(
        faces_kernel, "faces", [shape(layers, width), shape(layers, width), shape(columns, pairs, wide)],
        c_far, c_near, w, v, own_rim, side_rim, rec, wbh, wbl, face,
    )
    f_ahead, f_far, f_near = swap_cross_ahead(f_near, f_far)
    result = pltpu.HBM(pressure.shape, F32)
    in_hbm = pl.BlockSpec(memory_space=pltpu.HBM)
    operator_out, restricted = call(
        solve_kernel, "solve", [result, shape(layers * rows, width)],
        lp, s_near, s_far, c_far, c_near, spectral, wbh, wbl, padded_modes, own_back, out_specs=[in_hbm, VMEM],
        scratch=[
            pltpu.VMEM(pressure.shape, F32), pltpu.VMEM((layers * rows, width), F32), pltpu.SemaphoreType.DMA,
        ],
    )
    preconditioned = call(
        add_kernel, "preconditioned", result, restricted, f_ahead, f_far, f_near, out_specs=in_hbm,
        scratch=[pltpu.VMEM(pressure.shape, F32), pltpu.SemaphoreType.DMA],
    )
    return (operator_out, preconditioned)


def solution(mesh):
    in_specs = (
        P("stream", "cross", None),
        P(None, "stream", "cross", None),
        P(None, "stream", "cross", None),
        P("stream", None, None),
        P("cross", None, None),
        P(),
        P("stream", None),
        P("cross", None),
        P(),
    )
    out_specs = (P("stream", "cross", None), P("stream", "cross", None))
    return jax.shard_map(shards, mesh=mesh, in_specs=in_specs, out_specs=out_specs, check_vma=False)
```

```python
import functools

import jax
import jax.numpy as jnp
import numpy as np
from jax import lax
from jax.experimental import pallas as pl
from jax.experimental.pallas import tpu as pltpu
from jax.sharding import PartitionSpec as P

N1 = 8
F32 = jnp.float32
BF16 = jnp.bfloat16
HIGHEST = lax.Precision.HIGHEST
VMEM_LIMIT = 16 * 2**20
VMEM = pl.BlockSpec(memory_space=pltpu.VMEM)


def legendre_values(nodes, degree):
    table = np.zeros((nodes.shape[0], degree + 1))
    table[:, 0] = 1.0
    table[:, 1] = nodes
    for order in range(2, degree + 1):
        table[:, order] = (
            (2 * order - 1) * nodes * table[:, order - 1] - (order - 1) * table[:, order - 2]
        ) / order
    return table


def derivative_table(points):
    degree = points - 1
    nodes = np.cos(np.pi * np.arange(points) / degree)
    for sweep in range(100):
        table = legendre_values(nodes, degree)
        nodes = nodes - (nodes * table[:, degree] - table[:, degree - 1]) / (
            points * table[:, degree]
        )
    gll_nodes = nodes[::-1]
    legendre_at = legendre_values(gll_nodes, degree)[:, degree]
    diff_table = np.zeros((points, points))
    for first_index in range(points):
        for second_index in range(points):
            if first_index != second_index:
                diff_table[first_index, second_index] = legendre_at[first_index] / (
                    legendre_at[second_index] * (gll_nodes[first_index] - gll_nodes[second_index])
                )
    diff_table[0, 0] = -degree * (degree + 1) / 4.0
    diff_table[degree, degree] = degree * (degree + 1) / 4.0
    return diff_table


def round_up(count, unit):
    return -(-count // unit) * unit


def dot(left, right, dims=((1,), (0,)), precision=None):
    return lax.dot_general(
        left, right, (dims, ((), ())), precision=precision, preferred_element_type=F32
    )


def split(value):
    high = value.astype(BF16)
    return high, (value - high.astype(F32)).astype(BF16)


def split3(value):
    high = value.astype(BF16)
    rest = value - high.astype(F32)
    mid = rest.astype(BF16)
    return high, mid, (rest - mid.astype(F32)).astype(BF16)


def stacked(value):
    high, low = split(value)
    return jnp.concatenate([high, low, high], 0)


def abreast(value):
    high, low = split(value)
    return jnp.concatenate([high, high, low], 1)


def even(index):
    return lax.rem(index, 2) == 0


def diff_parts():
    table = derivative_table(N1).astype(np.float32)
    high = table.astype(jnp.bfloat16).astype(np.float32)
    low = (table - high).astype(jnp.bfloat16).astype(np.float32)
    row, column = ramps(N1, N1)
    place = row * N1 + column
    found = []
    for part in (high, low):
        value = jnp.zeros((N1, N1), F32)
        for k, entry in enumerate(part.reshape(-1)):
            if entry:
                value = jnp.where(place == k, float(entry), value)
        found.append(value.astype(BF16))
    return found


def operator_factors(blocks):
    def kron(part, count, inner, turned):
        row, column = ramps(count, N1)
        quotient, rest = over(row, N1)
        pick = mask((rest if inner else quotient) == column)
        value = dot(pick, part, ((1,), (1 if turned else 0,))).astype(BF16)
        row, column = ramps(N1, count)
        value = dot(value, mask(over(column, N1)[1 if inner else 0] == row))
        row, column = ramps(count, count)
        row, column = over(row, N1), over(column, N1)
        same = row[0] == column[0] if inner else row[1] == column[1]
        return jnp.where(same, value, 0.0).astype(BF16)

    parts = diff_parts()
    box = N1 * N1
    high, low = [
        jnp.concatenate([kron(part, box, False, False), kron(part, box, True, False)], 0) for part in parts
    ]
    grad = jnp.concatenate([high, high, low], 1)
    high, low = [
        jnp.concatenate([kron(part, box, False, True), kron(part, box, True, True)], 1) for part in parts
    ]
    back = jnp.concatenate([high, high, low], 1)
    high, low = [kron(part, blocks * N1, True, True) for part in parts]
    third = jnp.concatenate([high, low, high], 0)
    high, low = [kron(part, blocks * N1, True, False) for part in parts]
    return grad, third, back, jnp.concatenate([high, low, high], 0)


def local_kernel(*refs):
    count = 6
    sources, outs, scratch = refs[:count], refs[count : count + 6], refs[count + 6 :]
    lp_ref, near_ref, far_ref, mf_ref, ef_ref, es_ref = outs
    p_ref, gd_ref, go_ref, sems = scratch
    targets = (p_ref, gd_ref, go_ref, mf_ref, ef_ref, es_ref)
    copies = [
        pltpu.make_async_copy(source, target, sems.at[k])
        for k, (source, target) in enumerate(zip(sources, targets))
    ]
    for copy in copies:
        copy.start()
    layers, rows, width = p_ref.shape
    grad, third_grad, back, third_back = operator_factors(width // N1)
    copies[0].wait()
    first_blocks = layers // N1
    box = N1 * rows
    modes = mf_ref.shape[0]
    p_all = p_ref[...].reshape(layers * rows, width)
    third = dot(abreast(p_all), third_grad)
    grads = [
        dot(grad, stacked(p_all[a * box : (a + 1) * box])) for a in range(first_blocks)
    ]
    for k in (1, 2):
        copies[k].wait()
    for a in range(first_blocks):
        here = slice(a * box, (a + 1) * box)
        one, two, three = grads[a][:box], grads[a][box:], third[here]
        g = [
            gd_ref[k, a * N1 : (a + 1) * N1].reshape(box, width) for k in range(3)
        ] + [go_ref[k, a * N1 : (a + 1) * N1].reshape(box, width) for k in range(3)]
        flux_one = g[0] * one + g[3] * two + g[4] * three
        flux_two = g[3] * one + g[1] * two + g[5] * three
        flux_three = g[4] * one + g[5] * two + g[2] * three
        lp_ref[here, :] = dot(
            back, stacked(jnp.concatenate([flux_one, flux_two], 0))
        ) + dot(abreast(flux_three), third_back)
    for k in (3, 4, 5):
        copies[k].wait()
    layer = lambda l: slice(l * rows, (l + 1) * rows)
    body = (modes - 1) * rows
    up_layers = [
        (0, rows, lp_ref[layer(layers - modes), :]),
        (rows, 2 * rows, lp_ref[layer(layers - modes + 1), :] + lp_ref[layer(layers - modes + 2), :]),
        (2 * rows, body, lp_ref[(layers - modes + 3) * rows :, :]),
    ]
    down_layers = [
        (0, body - 2 * rows, lp_ref[: (modes - 3) * rows, :]),
        (body - 2 * rows, body - rows, lp_ref[layer(modes - 3), :] + lp_ref[layer(modes - 2), :]),
        (body - rows, body, lp_ref[layer(modes - 1), :]),
    ]
    forward = even(lax.axis_index("stream"))

    def fill(ref, parts, a):
        for begin, end, value in parts:
            ref[begin:end, :] = value
        ref[body:, :] = jnp.zeros((rows, width), F32)
        ref[body:, :modes] = mf_ref[:rows, a, :]
        ref[body : body + modes - rows, 16 : 16 + modes] = mf_ref[rows:, a, :]
        ref[body : body + 1, 32 : 32 + modes] = ef_ref[a : a + 1, :]

    @pl.when(forward)
    def _():
        fill(near_ref, up_layers, first_blocks - 1)
        fill(far_ref, down_layers, 0)

    @pl.when(jnp.logical_not(forward))
    def _():
        fill(near_ref, down_layers, 0)
        fill(far_ref, up_layers, first_blocks - 1)


def from_sides(near, far, axis):
    index = lax.axis_index(axis)
    is_even = even(index)
    before = jnp.where(is_even, far, near)
    after = jnp.where(is_even, near, far)
    before = jnp.where(index == 0, 0.0, before)
    after = jnp.where(index == lax.axis_size(axis) - 1, 0.0, after)
    return before, after


def lane_masks(width):
    lane = lax.broadcasted_iota(jnp.int32, (1, width), 1)
    node = over(lane, N1)[1]
    return lane, node, (node == 0) & (lane > 0)


def pack(upper_ref, lower_ref, spare):
    width = spare.shape[1]
    lane, node, free = lane_masks(width)
    final = (node == N1 - 1) & (lane < width - 1)
    upper = lax.broadcasted_iota(jnp.int32, (N1, 1), 0) < N1 // 2
    hidden = [jnp.where(lane == N1, pltpu.roll(spare, N1, 1), 0.0)]
    hidden += [pltpu.roll(spare, N1 - j, 1) for j in range(1, N1)]
    hidden[N1 - 1] = hidden[N1 - 1] + spare
    last = jnp.zeros_like(spare)
    for j in range(1, N1):
        last = jnp.where(lane == N1 * j, pltpu.roll(spare, N1 + (N1 - 1) * j, 1), last)
    hidden.append(last)
    for ref, mine in ((upper_ref, upper), (lower_ref, jnp.logical_not(upper))):
        value = ref[...]
        value = value + jnp.where(final, pltpu.roll(value, width - 1, 1), 0.0)
        for j in range(ref.shape[0] // N1):
            here = slice(j * N1, (j + 1) * N1)
            ref[here, :] = jnp.where(free & mine, hidden[min(j, N1)], jnp.where(free, 0.0, value[here]))


def unpack(upper_rows, lower_rows, out_upper_ref, out_lower_ref):
    width = upper_rows.shape[1]
    lane, node, free = lane_masks(width)
    upper = lax.broadcasted_iota(jnp.int32, (N1, 1), 0) < N1 // 2
    tiles = []
    for j in range(N1 + 1):
        here = slice(j * N1, (j + 1) * N1)
        tiles.append(jnp.where(upper, upper_rows[here], lower_rows[here]))
    spare = jnp.zeros((N1, width), F32)
    for j in range(N1):
        spare = jnp.where((node == j) & (lane < width - N1), pltpu.roll(tiles[j], width - N1 + j, 1), spare)
    for j in range(1, N1):
        spare = jnp.where(
            lane == width - N1 + j, pltpu.roll(tiles[N1], width - N1 - (N1 - 1) * j, 1), spare
        )
    inner = upper_rows.shape[0] // 2
    padded = out_upper_ref.shape[0] // 2
    for ref, packed, start in ((out_upper_ref, upper_rows, 0), (out_lower_ref, lower_rows, N1 // 2)):
        value = jnp.where(free, 0.0, packed)
        for slot in range(2):
            base, row = slot * padded, start + 2 * slot
            ref[base : base + 1, :] = spare[row : row + 1]
            ref[base + 1 : base + 1 + inner, :] = value[slot * inner : (slot + 1) * inner]
            ref[base + 1 + inner : base + 2 + inner, :] = spare[row + 1 : row + 2]
            ref[base + 2 + inner : base + padded, :] = jnp.zeros((padded - inner - 2, width), F32)


def rows_kernel(lp_ref, near_ref, far_ref, built_ref, out_far_ref, out_near_ref, spare_ref):
    rows = N1
    layers = lp_ref.shape[0] // rows
    count = N1 + 1
    inner = out_near_ref.shape[0] // 2
    found = {}
    for k in (0, 1, rows - 2, rows - 1):
        before, after = from_sides(
            near_ref[pl.ds(k, count, stride=rows), :], far_ref[pl.ds(k, count, stride=rows), :], "stream"
        )
        found[k] = (before, lp_ref[pl.ds(k, layers, stride=rows), :], after)
    up = even(lax.axis_index("cross"))
    messages = ((out_near_ref, up, 0), (out_far_ref, jnp.logical_not(up), N1 // 2))
    for ref, high, start in messages:
        for slot in range(2):
            base = slot * inner
            before, own, after = [
                jnp.where(high, one, two) for one, two in zip(found[rows - 2 + slot], found[slot])
            ]
            place = start + 2 * slot
            spare_ref[place : place + 1, :] = before[:1]
            spare_ref[place + 1 : place + 2, :] = after[count - 1 :]
            ref[base : base + count - 2, :] = before[1 : count - 1]
            base += count - 2
            for l in range(0, layers, N1):
                previous = before[count - 1 :] if l == 0 else own[l - 1 : l]
                ref[base : base + 1, :] = previous + own[l : l + 1]
                ref[base + 1 : base + N1 - 1, :] = own[l + 1 : l + N1 - 1]
                base += N1 - 1
            ref[base : base + 1, :] = own[layers - 1 :] + after[:1]
            ref[base + 1 : base + count - 1, :] = after[1 : count - 1]
    pack(out_near_ref, out_far_ref, spare_ref[...])


def spread_columns(parts, lay, pick):
    table = dot(parts, lay, ((0,), (0,)))
    return dot(pick, jnp.concatenate(split3(table), 0))


def spread_rows(parts, pick, rows):
    pad = parts.shape[0] // 3
    table = sum(dot(parts[k * pad : (k + 1) * pad], pick) for k in range(3))
    return dot(rows, jnp.concatenate(split3(table), 0))


def halves_by_lane(value, low):
    high = value.astype(BF16).astype(F32)
    return jnp.where(low, value - high, high).astype(BF16)


def low_lanes(kin, rim):
    lane = lax.broadcasted_iota(jnp.int32, (1, 3 * (kin + rim)), 1)
    return ((lane >= 2 * kin) & (lane < 3 * kin)) | (lane >= 3 * kin + 2 * rim)


def low_back_lanes(pairs):
    return lax.broadcasted_iota(jnp.int32, (1, 3 * pairs), 1) >= 2 * pairs


def ramps(*dims):
    return [lax.broadcasted_iota(jnp.int32, dims, axis) for axis in range(2)]


def over(value, count):
    if count & (count - 1) == 0:
        return lax.shift_right_logical(value, count.bit_length() - 1), value & (count - 1)
    quotient = ((value.astype(F32) + 0.5) * (1.0 / count)).astype(jnp.int32)
    return quotient, value - quotient * count


def mask(hit):
    return jnp.where(hit, 1.0, 0.0).astype(BF16)


def spread_table(blocks, modes):
    row, column = ramps(modes, blocks * modes)
    return mask(row == over(column, modes)[1])


def gather_table(blocks, modes):
    row, column = ramps(blocks * N1, modes * blocks)
    node, block = over(column, blocks)
    place = row - block * N1
    hit = (place == node - 1) & (node >= 1) & (node <= N1)
    for n, at in ((0, -2), (1, -1), (N1, N1), (N1 + 1, N1 + 1)):
        hit = hit | ((node == n) & (place == at))
    return mask(hit)


def pick_table(pairs, pad, modes, which):
    row, column = ramps(pairs, 3 * pad)
    return mask(over(row, modes)[which] == over(column, pad)[1])


def pick_rows(pairs, pad, modes, which):
    row, column = ramps(pairs, pad)
    return jnp.where(over(row, modes)[which] == column, 1.0, 0.0)


def back_tables(pairs, pad, modes):
    row, column = ramps(pad, 3 * pairs)
    found = over(over(column, pairs)[1], modes)
    return mask(found[0] == row), mask(found[1] == row)


def box_rows(count, pad):
    row, column = ramps(count, 3 * pad)
    first, second = over(row, N1)
    column = over(column, pad)[1]
    return mask(first + 1 == column), mask(second + 1 == column)


def face_rows(pad):
    row, column = ramps(2 * N1, 3 * pad)
    face, first = over(row, N1)
    column = over(column, pad)[1]
    return mask(first + 1 == column), mask(jnp.where(face == 0, 1, N1) == column)


def inner_table(blocks, modes):
    row, column = ramps(modes * blocks, blocks * N1)
    node, block = over(row, blocks)
    place = column - block * N1
    hit = (place == node - 1) & (node >= 1) & (node <= N1)
    return mask(hit | ((node == 1) & (place == -1)) | ((node == N1) & (place == N1)))


def lay_tables(pad, kin, rim):
    layers = kin // N1
    row, column = ramps(3 * pad, 3 * (kin + rim))
    row = over(row, pad)[1]
    own = column < 3 * kin
    l_own, y = over(over(column, kin)[1], N1)
    kind, l_rim = over(over(jnp.maximum(column - 3 * kin, 0), rim)[1], rim // 4)
    node = jnp.where(l_own == 0, 0, jnp.where(l_own == layers - 1, N1 + 1, jnp.clip(l_own - 1, 1, N1)))
    node = jnp.where(own, node, l_rim)
    second = jnp.where(own, y + 1, jnp.where(kind < 2, kind, N1 - 2 + kind))
    inside = own | (l_rim < N1 + 2)
    return mask(inside & (row == node)), mask(inside & (row == second))


def third_parts(mt_ref, spread):
    rows, modes = mt_ref.shape
    blocks = rows // modes
    row, column = ramps(rows, rows)
    own = over(row, blocks)[1] == over(column, modes)[0]
    return [jnp.where(own, dot(part, spread), 0.0).astype(BF16) for part in split3(mt_ref[...])]


def pad_modes(pad_ref, mf_ref, ms_ref):
    modes = ms_ref.shape[0]
    first_blocks = pad_ref.shape[0] - 1
    pad_ref[...] = jnp.zeros_like(pad_ref)
    for a in range(first_blocks):
        pad_ref[a, :modes, :modes] = mf_ref[:, a, :]
    pad_ref[first_blocks, :modes, :modes] = ms_ref[:, 0, :]


def modes_kernel(
    mt_ref, e3_ref, mf_ref, ef_ref, ms_ref, es_ref,
    w_ref, e3_row_ref, own_columns_ref, own_rim_ref, second_columns_ref, pad_ref, eigen_ref, back_ref,
):
    blocks, modes = e3_ref.shape
    spread = spread_table(blocks, modes)
    gather = gather_table(blocks, modes)
    table = sum(dot(gather, part) for part in third_parts(mt_ref, spread))
    high, low = split(table)
    w_ref[...] = jnp.concatenate([high, low, high], 0)
    row, column = ramps(blocks, blocks * modes)
    e3_wide = sum(dot(part, spread) for part in split3(e3_ref[...]))
    e3_row_ref[...] = jnp.sum(
        jnp.where(row == over(column, modes)[0], e3_wide, 0.0), 0, keepdims=True
    )
    first_blocks, pairs, kin = own_columns_ref.shape
    kin, rim, pad = kin // 3, own_rim_ref.shape[2] // 3, pad_ref.shape[1]
    pad_modes(pad_ref, mf_ref, ms_ref)
    eigen_ref[...] = jnp.zeros_like(eigen_ref)
    eigen_ref[:first_blocks, :modes] = ef_ref[...]
    eigen_ref[first_blocks : first_blocks + 1, :modes] = es_ref[...]
    lay_m, lay_n = lay_tables(pad, kin, rim)
    low = low_lanes(kin, rim)
    second = jnp.concatenate(split3(pad_ref[first_blocks]), 0)
    second_columns = spread_columns(second, lay_n, pick_table(pairs, pad, modes, 1))
    second_columns_ref[...] = second_columns
    pick = pick_table(pairs, pad, modes, 0)
    for a in range(first_blocks):
        first = jnp.concatenate(split3(pad_ref[a]), 0)
        columns = halves_by_lane(spread_columns(first, lay_m, pick) * second_columns, low)
        own_columns_ref[a] = columns[:, : 3 * kin]
        own_rim_ref[a] = columns[:, 3 * kin :]
    box = back_ref.shape[1]
    back_m, back_n = back_tables(pairs, pad, modes)
    rows_m, rows_n = box_rows(box, pad)
    second_rows = spread_rows(second, back_n, rows_n)
    for a in range(first_blocks):
        first = jnp.concatenate(split3(pad_ref[a]), 0)
        back_ref[a] = halves_by_lane(spread_rows(first, back_m, rows_m) * second_rows, low_back_lanes(pairs))


def columns_kernel(
    lp_ref, near_ref, far_ref, w_ref, e3_row_ref, own_columns_ref, second_columns_ref, pad_ref,
    eigen_ref, mt_ref, v_ref, side_rim_ref, rec_ref, face_ref, wbh_ref, wbl_ref,
):
    rows = N1
    halo = (N1 + 2) * rows
    first_blocks, pairs, kin = own_columns_ref.shape
    kin, rim, pad, modes = kin // 3, side_rim_ref.shape[2] // 3, pad_ref.shape[1], N1 + 2
    box = N1 * rows
    near, far = near_ref[...], far_ref[...]
    before, after = from_sides(near, far, "stream")
    odd = jnp.logical_not(even(lax.axis_index("stream")))
    body = halo - rows
    zero = jnp.zeros((rows, lp_ref.shape[1]), F32)
    stack = jnp.concatenate(
        [before[:rows], zero, before[rows:body], lp_ref[...], after[: body - rows], zero, after[body - rows : body]], 0
    )
    u = dot(abreast(stack), w_ref[...])
    edge_near, edge_far = near[body : body + 1, 32 : 32 + pad], far[body : body + 1, 32 : 32 + pad]
    low, back_low = low_lanes(kin, rim), low_back_lanes(pairs)
    lay_m, _ = lay_tables(pad, kin, rim)
    pick_p3 = pick_table(pairs, pad, modes, 0)
    pick_p, pick_q = pick_rows(pairs, pad, modes, 0), pick_rows(pairs, pad, modes, 1)
    back_m, back_n = back_tables(pairs, pad, modes)
    face_m, face_n = face_rows(pad)
    own_eigen = eigen_ref[...]
    firsts = [jnp.concatenate([side[body:, :pad], side[body:, 16 : 16 + pad]], 0) for side in (before, after)]
    firsts = [firsts[0]] + [pad_ref[a] for a in range(first_blocks)] + [firsts[1]]
    eigens = [jnp.where(odd, edge_near, edge_far)] + [own_eigen[a : a + 1] for a in range(first_blocks)]
    eigens += [jnp.where(odd, edge_far, edge_near)]
    second = jnp.concatenate(split3(pad_ref[first_blocks]), 0)
    second_faces = spread_rows(second, back_n, face_n)
    second_sum = jnp.sum(pick_q * own_eigen[first_blocks : first_blocks + 1], 1, keepdims=True)
    for a, (first, eigen) in enumerate(zip(firsts, eigens)):
        first = jnp.concatenate(split3(first), 0)
        if a in (0, first_blocks + 1):
            columns = halves_by_lane(
                spread_columns(first, lay_m, pick_p3) * second_columns_ref[...], low
            )
            side_rim_ref[min(a, 1)] = columns[:, 3 * kin :]
            columns = columns[:, : 3 * kin]
        else:
            columns = own_columns_ref[a - 1]
        begin = a * box
        v_ref[a] = dot(columns, stacked(u[begin : begin + kin]))
        face_ref[a] = halves_by_lane(spread_rows(first, back_m, face_m) * second_faces, back_low)
        total = jnp.sum(pick_p * eigen, 1, keepdims=True) + second_sum
        rec_ref[a] = 1.0 / (total + e3_row_ref[...])
    blocks = mt_ref.shape[0] // modes
    inner = inner_table(blocks, modes)
    table = sum(
        dot(part, inner, ((0,), (0,))) for part in third_parts(mt_ref, spread_table(blocks, modes))
    )
    wbh_ref[...], wbl_ref[...] = split(table)


def spectral_columns(near_ref, far_ref, w_ref, v_ref, own_rim_ref, side_rim_ref, rec_ref):
    columns = v_ref.shape[0]
    padded = near_ref.shape[0] // 2
    before, after = from_sides(near_ref[...], far_ref[...], "cross")
    u = dot(abreast(jnp.concatenate([before, after], 0)), w_ref[...])
    u = jnp.concatenate([u, jnp.zeros((8, u.shape[1]), F32)], 0)
    found = []
    for a in range(columns):
        rim = jnp.concatenate(
            [u[k * padded + a * (N1 - 1) : k * padded + a * (N1 - 1) + 16] for k in range(4)], 0
        )
        if a in (0, columns - 1):
            table = side_rim_ref[min(a, 1)]
        else:
            table = own_rim_ref[a - 1]
        found.append((v_ref[a] + dot(table, stacked(rim))) * rec_ref[a])
    return found


def third_back(parts, wbh_ref, wbl_ref):
    high, low = split(jnp.concatenate(parts, 0))
    return dot(high, wbh_ref[...]) + dot(high, wbl_ref[...]) + dot(low, wbh_ref[...])


def faces_kernel(
    far_ref, near_ref, w_ref, v_ref, own_rim_ref, side_rim_ref, rec_ref, wbh_ref, wbl_ref, face_ref,
    out_far_ref, out_near_ref, spectral_ref, all_far_ref, all_near_ref,
):
    rows = N1
    unpack(near_ref[...], far_ref[...], all_near_ref, all_far_ref)
    found = spectral_columns(all_near_ref, all_far_ref, w_ref, v_ref, own_rim_ref, side_rim_ref, rec_ref)
    columns = len(found)
    for a in range(columns):
        spectral_ref[a] = found[a]
    parts = [dot(face_ref[a], stacked(found[a])) for a in range(columns)]
    solved = third_back(parts, wbh_ref, wbl_ref)
    row = lax.broadcasted_iota(jnp.int32, (rows, 1), 0)
    up = even(lax.axis_index("cross"))
    for a in range(1, columns - 1):
        sums = []
        for face in range(2):
            base = 16 * a + rows * face
            previous = base - 16 + rows - 1
            after = base + 16
            sums.append(
                solved[base : base + rows]
                + jnp.where(row == 0, solved[previous : previous + 1], 0.0)
                + jnp.where(row == rows - 1, solved[after : after + 1], 0.0)
            )
        here = slice((a - 1) * rows, a * rows)
        out_near_ref[here, :] = jnp.where(up, sums[1], sums[0])
        out_far_ref[here, :] = jnp.where(up, sums[0], sums[1])


def assemble_operator(lp_ref, s_near_ref, s_far_ref, c_near_ref, c_far_ref, out_ref, acc_ref):
    rows = N1
    total_rows, width = lp_ref.shape
    padded = c_near_ref.shape[0] // 2
    body = (N1 + 1) * rows
    box = N1 * rows
    before, after = from_sides(s_near_ref[...], s_far_ref[...], "stream")
    left, right = from_sides(c_near_ref[...], c_far_ref[...], "cross")
    acc_ref[...] = lp_ref[...]
    for base in range(0, total_rows, box):
        last = base + box
        previous = before[body - rows : body] if base == 0 else lp_ref[base - rows : base, :]
        following = after[:rows] if last == total_rows else lp_ref[last : last + rows, :]
        acc_ref[base : base + rows, :] = lp_ref[base : base + rows, :] + previous
        acc_ref[last - rows : last, :] = lp_ref[last - rows : last, :] + following
        node = (N1 - 1) * (base // box + 1) + 1
        low, high = pl.ds(base, N1, stride=rows), pl.ds(base + rows - 1, N1, stride=rows)
        acc_ref[low, :] = acc_ref[low, :] + left[padded + node : padded + node + N1]
        acc_ref[high, :] = acc_ref[high, :] + right[node : node + N1]
    lane = lax.broadcasted_iota(jnp.int32, (1, width), 1)
    first = (lax.rem(lane, N1) == 0) & (lane > 0)
    final = (lax.rem(lane, N1) == N1 - 1) & (lane < width - 1)
    value = acc_ref[...]
    value = (
        value
        + jnp.where(first, pltpu.roll(value, 1, 1), 0.0)
        + jnp.where(final, pltpu.roll(value, width - 1, 1), 0.0)
    )
    out_ref[...] = value.reshape(out_ref.shape)


def solve_kernel(
    lp_ref, s_near_ref, s_far_ref, c_far_ref, c_near_ref, spectral_ref, wbh_ref, wbl_ref, pad_ref, back_ref,
    operator_ref, r_ref, out_ref, acc_ref, sem,
):
    assemble_operator(lp_ref, s_near_ref, s_far_ref, c_near_ref, c_far_ref, out_ref, acc_ref)
    copy = pltpu.make_async_copy(out_ref, operator_ref, sem)
    copy.start()
    rows = N1
    box = N1 * rows
    found = [spectral_ref[a] for a in range(spectral_ref.shape[0])]
    columns = len(found)
    pad, pairs = pad_ref.shape[1], spectral_ref.shape[1]
    back_m, back_n = back_tables(pairs, pad, N1 + 2)
    rows_m, rows_n = box_rows(box, pad)
    low = low_back_lanes(pairs)
    body = (N1 + 1) * rows
    sides = from_sides(s_near_ref[...], s_far_ref[...], "stream")
    sides = [jnp.concatenate([side[body:, :pad], side[body:, 16 : 16 + pad]], 0) for side in sides]
    second = jnp.concatenate(split3(pad_ref[columns - 2]), 0)
    parts = [None] * columns
    for a, first, kept in ((0, sides[0], slice(box - 16, box)), (columns - 1, sides[1], slice(0, 16))):
        first = jnp.concatenate(split3(first), 0)
        table = spread_rows(first, back_m, rows_m[kept]) * spread_rows(second, back_n, rows_n[kept])
        parts[a] = dot(halves_by_lane(table, low), stacked(found[a]))
    for a in range(1, columns - 1):
        parts[a] = dot(back_ref[a - 1], stacked(found[a]))
    parts[0] = parts[0][16 - rows :]
    parts[-1] = parts[-1][:rows]
    solved = third_back(parts, wbh_ref, wbl_ref)
    for a in range(columns - 2):
        base = rows + a * box
        top, bottom = solved[base : base + rows], solved[base + box - rows : base + box]
        r_ref[a * box : a * box + rows, :] = top + solved[base - rows : base]
        r_ref[a * box + rows : (a + 1) * box - rows, :] = solved[base + rows : base + box - rows]
        r_ref[(a + 1) * box - rows : (a + 1) * box, :] = bottom + solved[base + box : base + box + rows]
    copy.wait()


def pass_kernel(*refs):
    count = len(refs) // 2
    for source, target in zip(refs[:count], refs[count:]):
        target[...] = source[...]


def add_kernel(r_ref, ahead_ref, far_ref, near_ref, out_ref, acc_ref, sem):
    rows = N1
    near = jnp.where(lax.axis_index("cross") < 2, ahead_ref[...], near_ref[...])
    before, after = from_sides(near, far_ref[...], "cross")
    acc_ref[...] = r_ref[...].reshape(acc_ref.shape)
    acc_ref[:, 0, :] = acc_ref[:, 0, :] + before
    acc_ref[:, rows - 1, :] = acc_ref[:, rows - 1, :] + after
    copy = pltpu.make_async_copy(acc_ref, out_ref, sem)
    copy.start()
    copy.wait()


def shape(*dims, dtype=F32):
    return pltpu.VMEM(dims, dtype)


def call(kernel, name, out, *args, scratch=(), out_specs=None, flops=1000000, place=pltpu.VMEM):
    single = not isinstance(out, list)
    args = [pltpu.with_memory_space_constraint(x, place) for x in args]
    return pl.pallas_call(
        kernel,
        out_shape=out,
        in_specs=[pl.BlockSpec(memory_space=place)] * len(args),
        out_specs=out_specs if out_specs is not None else (VMEM if single else [VMEM] * len(out)),
        scratch_shapes=list(scratch),
        compiler_params=pltpu.CompilerParams(vmem_limit_bytes=VMEM_LIMIT),
        cost_estimate=pl.CostEstimate(flops=flops, bytes_accessed=flops, transcendentals=0),
        name=name,
    )(*args)


def swaps(axis):
    count = lax.axis_size(axis)
    near = [(i, i ^ 1) for i in range(count)]
    far = [(i, (i - 1) % count if i % 2 == 0 else (i + 1) % count) for i in range(count)]
    return near, far


def swap_stream(near, far):
    first, second = swaps("stream")
    near = lax.ppermute(near, "stream", first)
    far = lax.ppermute(far, "stream", second)
    return near, far


def cross_pairs(near, ahead=None):
    count, streams = lax.axis_size("cross"), lax.axis_size("stream")
    pairs = []
    for s in range(streams):
        for i in range(count):
            j = i ^ 1 if near else i - 1 + 2 * (i % 2)
            idle = not 0 <= j < count or (ahead is not None and (i < 2) != ahead)
            pairs.append((s * count + i, (s ^ 1) * count + i if idle else s * count + j))
    return pairs


def swap_cross(near, far):
    axes = ("stream", "cross")
    return lax.ppermute(near, axes, cross_pairs(True)), lax.ppermute(far, axes, cross_pairs(False))


def swap_cross_ahead(near, far):
    axes = ("stream", "cross")
    first = lax.ppermute(near, axes, cross_pairs(True, True))
    far, near = call(pass_kernel, "pass_on", [shape(*far.shape), shape(*near.shape)], far, near)
    return first, lax.ppermute(far, axes, cross_pairs(False)), lax.ppermute(near, axes, cross_pairs(True, False))


def shards(
    pressure, geo_diag, geo_off, modes_first, modes_second, modes_third, eigen_first, eigen_second,
    eigen_third,
):
    layers, rows, width = pressure.shape
    modes = modes_first.shape[1]
    if layers < 3 * N1 or rows != N1 or modes != N1 + 2 or lax.axis_size("stream") % 2 or lax.axis_size("cross") % 2:
        raise ValueError("unsupported sizes")
    first_blocks, third_blocks = layers // N1, width // N1
    columns = first_blocks + 2
    halo = modes * rows
    box = N1 * rows
    nodes = (first_blocks + 1) * (N1 - 1) + modes
    padded = round_up(nodes, 8)
    wide = third_blocks * modes

    pairs, pad = round_up(modes * modes, 16), round_up(modes, 16)

    mf = jnp.transpose(modes_first, (1, 0, 2))
    ms = jnp.transpose(modes_second, (1, 0, 2))
    mt = jnp.transpose(modes_third, (1, 0, 2)).reshape(modes * third_blocks, modes)

    inputs = [pressure, geo_diag, geo_off, mf, eigen_first, eigen_second]
    lp, s_near, s_far, mf, ef, es = call(
        local_kernel, "local_product",
        [
            shape(layers * rows, width), shape(halo, width), shape(halo, width),
            shape(modes, first_blocks, modes), shape(first_blocks, modes), shape(1, modes),
        ],
        *inputs, place=pltpu.HBM,
        scratch=[pltpu.VMEM(x.shape, x.dtype) for x in inputs[:3]] + [pltpu.SemaphoreType.DMA((len(inputs),))],
    )
    s_near, s_far = swap_stream(s_near, s_far)
    kin, rim_width = 3 * (N1 + 4) * rows, 3 * 64
    w, e3_row, own_columns, own_rim, second_columns, padded_modes, eigen, own_back = call(
        modes_kernel, "mode_tables",
        [
            shape(3 * width, wide, dtype=BF16), shape(1, wide),
            shape(first_blocks, pairs, kin, dtype=BF16), shape(first_blocks, pairs, rim_width, dtype=BF16),
            shape(pairs, kin + rim_width), shape(first_blocks + 1, pad, pad), shape(first_blocks + 1, pad),
            shape(first_blocks, box, 3 * pairs, dtype=BF16),
        ],
        mt, eigen_third, mf, ef, ms, es,
    )
    c_far, c_near = call(
        rows_kernel, "rows_to_send",
        [shape(2 * nodes - 4, width), shape(2 * nodes - 4, width)],
        lp, s_near, s_far, e3_row, scratch=[pltpu.VMEM((N1, width), F32)],
    )
    c_near, c_far = swap_cross(c_near, c_far)
    v, side_rim, rec, face, wbh, wbl = call(
        columns_kernel, "own_part",
        [
            shape(columns, pairs, wide), shape(2, pairs, rim_width, dtype=BF16), shape(columns, pairs, wide),
            shape(columns, 16, 3 * pairs, dtype=BF16), shape(wide, width, dtype=BF16), shape(wide, width, dtype=BF16),
        ],
        lp, s_near, s_far, w, e3_row, own_columns, second_columns, padded_modes, eigen, mt,
    )
    f_far, f_near, spectral, c_far, c_near = call(
        faces_kernel, "faces",
        [
            shape(layers, width), shape(layers, width), shape(columns, pairs, wide), shape(2 * padded, width),
            shape(2 * padded, width),
        ],
        c_far, c_near, w, v, own_rim, side_rim, rec, wbh, wbl, face,
    )
    f_ahead, f_far, f_near = swap_cross_ahead(f_near, f_far)
    result = pltpu.HBM(pressure.shape, F32)
    in_hbm = pl.BlockSpec(memory_space=pltpu.HBM)
    operator_out, restricted = call(
        solve_kernel, "solve", [result, shape(layers * rows, width)],
        lp, s_near, s_far, c_far, c_near, spectral, wbh, wbl, padded_modes, own_back, out_specs=[in_hbm, VMEM],
        scratch=[
            pltpu.VMEM(pressure.shape, F32), pltpu.VMEM((layers * rows, width), F32), pltpu.SemaphoreType.DMA,
        ],
    )
    preconditioned = call(
        add_kernel, "preconditioned", result, restricted, f_ahead, f_far, f_near, out_specs=in_hbm,
        scratch=[pltpu.VMEM(pressure.shape, F32), pltpu.SemaphoreType.DMA],
    )
    return (operator_out, preconditioned)


def solution(mesh):
    in_specs = (
        P("stream", "cross", None),
        P(None, "stream", "cross", None),
        P(None, "stream", "cross", None),
        P("stream", None, None),
        P("cross", None, None),
        P(),
        P("stream", None),
        P("cross", None),
        P(),
    )
    out_specs = (P("stream", "cross", None), P("stream", "cross", None))
    return jax.shard_map(shards, mesh=mesh, in_specs=in_specs, out_specs=out_specs, check_vma=False)
```

```python
import functools

import jax
import jax.numpy as jnp
import numpy as np
from jax import lax
from jax.experimental import pallas as pl
from jax.experimental.pallas import tpu as pltpu
from jax.sharding import PartitionSpec as P

N1 = 8
F32 = jnp.float32
BF16 = jnp.bfloat16
HIGHEST = lax.Precision.HIGHEST
VMEM_LIMIT = 16 * 2**20
VMEM = pl.BlockSpec(memory_space=pltpu.VMEM)


def legendre_values(nodes, degree):
    table = np.zeros((nodes.shape[0], degree + 1))
    table[:, 0] = 1.0
    table[:, 1] = nodes
    for order in range(2, degree + 1):
        table[:, order] = (
            (2 * order - 1) * nodes * table[:, order - 1] - (order - 1) * table[:, order - 2]
        ) / order
    return table


def derivative_table(points):
    degree = points - 1
    nodes = np.cos(np.pi * np.arange(points) / degree)
    for sweep in range(100):
        table = legendre_values(nodes, degree)
        nodes = nodes - (nodes * table[:, degree] - table[:, degree - 1]) / (
            points * table[:, degree]
        )
    gll_nodes = nodes[::-1]
    legendre_at = legendre_values(gll_nodes, degree)[:, degree]
    diff_table = np.zeros((points, points))
    for first_index in range(points):
        for second_index in range(points):
            if first_index != second_index:
                diff_table[first_index, second_index] = legendre_at[first_index] / (
                    legendre_at[second_index] * (gll_nodes[first_index] - gll_nodes[second_index])
                )
    diff_table[0, 0] = -degree * (degree + 1) / 4.0
    diff_table[degree, degree] = degree * (degree + 1) / 4.0
    return diff_table


def round_up(count, unit):
    return -(-count // unit) * unit


def dot(left, right, dims=((1,), (0,)), precision=None):
    return lax.dot_general(
        left, right, (dims, ((), ())), precision=precision, preferred_element_type=F32
    )


def split(value):
    high = value.astype(BF16)
    return high, (value - high.astype(F32)).astype(BF16)


def split3(value):
    high = value.astype(BF16)
    rest = value - high.astype(F32)
    mid = rest.astype(BF16)
    return high, mid, (rest - mid.astype(F32)).astype(BF16)


def stacked(value):
    high, low = split(value)
    return jnp.concatenate([high, low, high], 0)


def abreast(value):
    high, low = split(value)
    return jnp.concatenate([high, high, low], 1)


def even(index):
    return lax.rem(index, 2) == 0


def diff_parts():
    table = derivative_table(N1).astype(np.float32)
    high = table.astype(jnp.bfloat16).astype(np.float32)
    low = (table - high).astype(jnp.bfloat16).astype(np.float32)
    row, column = ramps(N1, N1)
    place = row * N1 + column
    found = []
    for part in (high, low):
        value = jnp.zeros((N1, N1), F32)
        for k, entry in enumerate(part.reshape(-1)):
            if entry:
                value = jnp.where(place == k, float(entry), value)
        found.append(value.astype(BF16))
    return found


def operator_factors(blocks):
    def kron(part, count, inner, turned):
        row, column = ramps(count, N1)
        quotient, rest = over(row, N1)
        pick = mask((rest if inner else quotient) == column)
        value = dot(pick, part, ((1,), (1 if turned else 0,))).astype(BF16)
        row, column = ramps(N1, count)
        value = dot(value, mask(over(column, N1)[1 if inner else 0] == row))
        row, column = ramps(count, count)
        row, column = over(row, N1), over(column, N1)
        same = row[0] == column[0] if inner else row[1] == column[1]
        return jnp.where(same, value, 0.0).astype(BF16)

    parts = diff_parts()
    box = N1 * N1
    high, low = [
        jnp.concatenate([kron(part, box, False, False), kron(part, box, True, False)], 0) for part in parts
    ]
    grad = jnp.concatenate([high, high, low], 1)
    high, low = [
        jnp.concatenate([kron(part, box, False, True), kron(part, box, True, True)], 1) for part in parts
    ]
    back = jnp.concatenate([high, high, low], 1)
    high, low = [kron(part, blocks * N1, True, True) for part in parts]
    third = jnp.concatenate([high, low, high], 0)
    high, low = [kron(part, blocks * N1, True, False) for part in parts]
    return grad, third, back, jnp.concatenate([high, low, high], 0)


def local_kernel(*refs):
    count = 6
    sources, outs, scratch = refs[:count], refs[count : count + 6], refs[count + 6 :]
    lp_ref, near_ref, far_ref, mf_ref, ef_ref, es_ref = outs
    p_ref, gd_ref, go_ref, sems = scratch
    targets = (p_ref, gd_ref, go_ref, mf_ref, ef_ref, es_ref)
    copies = [
        pltpu.make_async_copy(source, target, sems.at[k])
        for k, (source, target) in enumerate(zip(sources, targets))
    ]
    for copy in copies:
        copy.start()
    layers, rows, width = p_ref.shape
    grad, third_grad, back, third_back = operator_factors(width // N1)
    copies[0].wait()
    first_blocks = layers // N1
    box = N1 * rows
    modes = mf_ref.shape[0]
    p_all = p_ref[...].reshape(layers * rows, width)
    third = dot(abreast(p_all), third_grad)
    grads = [
        dot(grad, stacked(p_all[a * box : (a + 1) * box])) for a in range(first_blocks)
    ]
    for k in (1, 2):
        copies[k].wait()
    for a in range(first_blocks):
        here = slice(a * box, (a + 1) * box)
        one, two, three = grads[a][:box], grads[a][box:], third[here]
        g = [
            gd_ref[k, a * N1 : (a + 1) * N1].reshape(box, width) for k in range(3)
        ] + [go_ref[k, a * N1 : (a + 1) * N1].reshape(box, width) for k in range(3)]
        flux_one = g[0] * one + g[3] * two + g[4] * three
        flux_two = g[3] * one + g[1] * two + g[5] * three
        flux_three = g[4] * one + g[5] * two + g[2] * three
        lp_ref[here, :] = dot(
            back, stacked(jnp.concatenate([flux_one, flux_two], 0))
        ) + dot(abreast(flux_three), third_back)
    for k in (3, 4, 5):
        copies[k].wait()
    layer = lambda l: slice(l * rows, (l + 1) * rows)
    body = (modes - 1) * rows
    up_layers = [
        (0, rows, lp_ref[layer(layers - modes), :]),
        (rows, 2 * rows, lp_ref[layer(layers - modes + 1), :] + lp_ref[layer(layers - modes + 2), :]),
        (2 * rows, body, lp_ref[(layers - modes + 3) * rows :, :]),
    ]
    down_layers = [
        (0, body - 2 * rows, lp_ref[: (modes - 3) * rows, :]),
        (body - 2 * rows, body - rows, lp_ref[layer(modes - 3), :] + lp_ref[layer(modes - 2), :]),
        (body - rows, body, lp_ref[layer(modes - 1), :]),
    ]
    forward = even(lax.axis_index("stream"))

    def fill(ref, parts, a):
        for begin, end, value in parts:
            ref[begin:end, :] = value
        ref[body:, :] = jnp.zeros((rows, width), F32)
        ref[body:, :modes] = mf_ref[:rows, a, :]
        ref[body : body + modes - rows, 16 : 16 + modes] = mf_ref[rows:, a, :]
        ref[body : body + 1, 32 : 32 + modes] = ef_ref[a : a + 1, :]

    @pl.when(forward)
    def _():
        fill(near_ref, up_layers, first_blocks - 1)
        fill(far_ref, down_layers, 0)

    @pl.when(jnp.logical_not(forward))
    def _():
        fill(near_ref, down_layers, 0)
        fill(far_ref, up_layers, first_blocks - 1)


def from_sides(near, far, axis):
    index = lax.axis_index(axis)
    is_even = even(index)
    before = jnp.where(is_even, far, near)
    after = jnp.where(is_even, near, far)
    before = jnp.where(index == 0, 0.0, before)
    after = jnp.where(index == lax.axis_size(axis) - 1, 0.0, after)
    return before, after


def lane_masks(width):
    lane = lax.broadcasted_iota(jnp.int32, (1, width), 1)
    node = over(lane, N1)[1]
    return lane, node, (node == 0) & (lane > 0)


def pack(upper_ref, lower_ref, spare):
    width = spare.shape[1]
    lane, node, free = lane_masks(width)
    final = (node == N1 - 1) & (lane < width - 1)
    upper = lax.broadcasted_iota(jnp.int32, (N1, 1), 0) < N1 // 2
    hidden = [jnp.where(lane == N1, pltpu.roll(spare, N1, 1), 0.0)]
    hidden += [pltpu.roll(spare, N1 - j, 1) for j in range(1, N1)]
    hidden[N1 - 1] = hidden[N1 - 1] + spare
    last = jnp.zeros_like(spare)
    for j in range(1, N1):
        last = jnp.where(lane == N1 * j, pltpu.roll(spare, N1 + (N1 - 1) * j, 1), last)
    hidden.append(last)
    for ref, mine in ((upper_ref, upper), (lower_ref, jnp.logical_not(upper))):
        value = ref[...]
        value = value + jnp.where(final, pltpu.roll(value, width - 1, 1), 0.0)
        for j in range(ref.shape[0] // N1):
            here = slice(j * N1, (j + 1) * N1)
            ref[here, :] = jnp.where(free & mine, hidden[min(j, N1)], jnp.where(free, 0.0, value[here]))


def unpack_spare(upper_rows, lower_rows):
    width = upper_rows.shape[1]
    lane, node, _ = lane_masks(width)
    upper = lax.broadcasted_iota(jnp.int32, (N1, 1), 0) < N1 // 2
    tiles = []
    for j in range(N1 + 1):
        here = slice(j * N1, (j + 1) * N1)
        tiles.append(jnp.where(upper, upper_rows[here], lower_rows[here]))
    spare = jnp.zeros((N1, width), F32)
    for j in range(N1):
        spare = jnp.where((node == j) & (lane < width - N1), pltpu.roll(tiles[j], width - N1 + j, 1), spare)
    for j in range(1, N1):
        spare = jnp.where(
            lane == width - N1 + j, pltpu.roll(tiles[N1], width - N1 - (N1 - 1) * j, 1), spare
        )
    return spare


def unpack(upper_rows, lower_rows, out_upper_ref, out_lower_ref):
    width = upper_rows.shape[1]
    free = lane_masks(width)[2]
    spare = unpack_spare(upper_rows, lower_rows)
    inner = upper_rows.shape[0] // 2
    padded = out_upper_ref.shape[0] // 2
    for ref, packed, start in ((out_upper_ref, upper_rows, 0), (out_lower_ref, lower_rows, N1 // 2)):
        value = jnp.where(free, 0.0, packed)
        for slot in range(2):
            base, row = slot * padded, start + 2 * slot
            ref[base : base + 1, :] = spare[row : row + 1]
            ref[base + 1 : base + 1 + inner, :] = value[slot * inner : (slot + 1) * inner]
            ref[base + 1 + inner : base + 2 + inner, :] = spare[row + 1 : row + 2]
            ref[base + 2 + inner : base + padded, :] = jnp.zeros((padded - inner - 2, width), F32)


def rows_kernel(lp_ref, near_ref, far_ref, built_ref, out_far_ref, out_near_ref, spare_ref):
    rows = N1
    layers = lp_ref.shape[0] // rows
    count = N1 + 1
    inner = out_near_ref.shape[0] // 2
    found = {}
    for k in (0, 1, rows - 2, rows - 1):
        before, after = from_sides(
            near_ref[pl.ds(k, count, stride=rows), :], far_ref[pl.ds(k, count, stride=rows), :], "stream"
        )
        found[k] = (before, lp_ref[pl.ds(k, layers, stride=rows), :], after)
    up = even(lax.axis_index("cross"))
    messages = ((out_near_ref, up, 0), (out_far_ref, jnp.logical_not(up), N1 // 2))
    for ref, high, start in messages:
        for slot in range(2):
            base = slot * inner
            before, own, after = [
                jnp.where(high, one, two) for one, two in zip(found[rows - 2 + slot], found[slot])
            ]
            place = start + 2 * slot
            spare_ref[place : place + 1, :] = before[:1]
            spare_ref[place + 1 : place + 2, :] = after[count - 1 :]
            ref[base : base + count - 2, :] = before[1 : count - 1]
            base += count - 2
            for l in range(0, layers, N1):
                previous = before[count - 1 :] if l == 0 else own[l - 1 : l]
                ref[base : base + 1, :] = previous + own[l : l + 1]
                ref[base + 1 : base + N1 - 1, :] = own[l + 1 : l + N1 - 1]
                base += N1 - 1
            ref[base : base + 1, :] = own[layers - 1 :] + after[:1]
            ref[base + 1 : base + count - 1, :] = after[1 : count - 1]
    pack(out_near_ref, out_far_ref, spare_ref[...])


def spread_columns(parts, lay, pick):
    table = dot(parts, lay, ((0,), (0,)))
    return dot(pick, jnp.concatenate(split3(table), 0))


def spread_rows(parts, pick, rows):
    pad = parts.shape[0] // 3
    table = sum(dot(parts[k * pad : (k + 1) * pad], pick) for k in range(3))
    return dot(rows, jnp.concatenate(split3(table), 0))


def halves_by_lane(value, low):
    high = value.astype(BF16).astype(F32)
    return jnp.where(low, value - high, high).astype(BF16)


def low_lanes(kin, rim):
    lane = lax.broadcasted_iota(jnp.int32, (1, 3 * (kin + rim)), 1)
    return ((lane >= 2 * kin) & (lane < 3 * kin)) | (lane >= 3 * kin + 2 * rim)


def low_back_lanes(pairs):
    return lax.broadcasted_iota(jnp.int32, (1, 3 * pairs), 1) >= 2 * pairs


def ramps(*dims):
    return [lax.broadcasted_iota(jnp.int32, dims, axis) for axis in range(2)]


def over(value, count):
    if count & (count - 1) == 0:
        return lax.shift_right_logical(value, count.bit_length() - 1), value & (count - 1)
    quotient = ((value.astype(F32) + 0.5) * (1.0 / count)).astype(jnp.int32)
    return quotient, value - quotient * count


def mask(hit):
    return jnp.where(hit, 1.0, 0.0).astype(BF16)


def spread_table(blocks, modes):
    row, column = ramps(modes, blocks * modes)
    return mask(row == over(column, modes)[1])


def gather_table(blocks, modes):
    row, column = ramps(blocks * N1, modes * blocks)
    node, block = over(column, blocks)
    place = row - block * N1
    hit = (place == node - 1) & (node >= 1) & (node <= N1)
    for n, at in ((0, -2), (1, -1), (N1, N1), (N1 + 1, N1 + 1)):
        hit = hit | ((node == n) & (place == at))
    return mask(hit)


def pick_table(pairs, pad, modes, which):
    row, column = ramps(pairs, 3 * pad)
    return mask(over(row, modes)[which] == over(column, pad)[1])


def pick_rows(pairs, pad, modes, which):
    row, column = ramps(pairs, pad)
    return jnp.where(over(row, modes)[which] == column, 1.0, 0.0)


def back_tables(pairs, pad, modes):
    row, column = ramps(pad, 3 * pairs)
    found = over(over(column, pairs)[1], modes)
    return mask(found[0] == row), mask(found[1] == row)


def box_rows(count, pad):
    row, column = ramps(count, 3 * pad)
    first, second = over(row, N1)
    column = over(column, pad)[1]
    return mask(first + 1 == column), mask(second + 1 == column)


def face_rows(pad):
    row, column = ramps(2 * N1, 3 * pad)
    face, first = over(row, N1)
    column = over(column, pad)[1]
    return mask(first + 1 == column), mask(jnp.where(face == 0, 1, N1) == column)


def inner_table(blocks, modes):
    row, column = ramps(modes * blocks, blocks * N1)
    node, block = over(row, blocks)
    place = column - block * N1
    hit = (place == node - 1) & (node >= 1) & (node <= N1)
    return mask(hit | ((node == 1) & (place == -1)) | ((node == N1) & (place == N1)))


def lay_tables(pad, kin, rim):
    layers = kin // N1
    row, column = ramps(3 * pad, 3 * (kin + rim))
    row = over(row, pad)[1]
    own = column < 3 * kin
    l_own, y = over(over(column, kin)[1], N1)
    kind, l_rim = over(over(jnp.maximum(column - 3 * kin, 0), rim)[1], rim // 4)
    node = jnp.where(l_own == 0, 0, jnp.where(l_own == layers - 1, N1 + 1, jnp.clip(l_own - 1, 1, N1)))
    node = jnp.where(own, node, l_rim)
    second = jnp.where(own, y + 1, jnp.where(kind < 2, kind, N1 - 2 + kind))
    inside = own | (l_rim < N1 + 2)
    return mask(inside & (row == node)), mask(inside & (row == second))


def third_parts(mt_ref, spread):
    rows, modes = mt_ref.shape
    blocks = rows // modes
    row, column = ramps(rows, rows)
    own = over(row, blocks)[1] == over(column, modes)[0]
    return [jnp.where(own, dot(part, spread), 0.0).astype(BF16) for part in split3(mt_ref[...])]


def pad_modes(pad_ref, mf_ref, ms_ref):
    modes = ms_ref.shape[0]
    first_blocks = pad_ref.shape[0] - 1
    pad_ref[...] = jnp.zeros_like(pad_ref)
    for a in range(first_blocks):
        pad_ref[a, :modes, :modes] = mf_ref[:, a, :]
    pad_ref[first_blocks, :modes, :modes] = ms_ref[:, 0, :]


def modes_kernel(
    mt_ref, e3_ref, mf_ref, ef_ref, ms_ref, es_ref,
    w_ref, e3_row_ref, own_columns_ref, own_rim_ref, second_columns_ref, pad_ref, eigen_ref, back_ref,
):
    blocks, modes = e3_ref.shape
    spread = spread_table(blocks, modes)
    gather = gather_table(blocks, modes)
    table = sum(dot(gather, part) for part in third_parts(mt_ref, spread))
    high, low = split(table)
    w_ref[...] = jnp.concatenate([high, low, high], 0)
    row, column = ramps(blocks, blocks * modes)
    e3_wide = sum(dot(part, spread) for part in split3(e3_ref[...]))
    e3_row_ref[...] = jnp.sum(
        jnp.where(row == over(column, modes)[0], e3_wide, 0.0), 0, keepdims=True
    )
    first_blocks, pairs, kin = own_columns_ref.shape
    kin, rim, pad = kin // 3, own_rim_ref.shape[2] // 3, pad_ref.shape[1]
    pad_modes(pad_ref, mf_ref, ms_ref)
    eigen_ref[...] = jnp.zeros_like(eigen_ref)
    eigen_ref[:first_blocks, :modes] = ef_ref[...]
    eigen_ref[first_blocks : first_blocks + 1, :modes] = es_ref[...]
    lay_m, lay_n = lay_tables(pad, kin, rim)
    low = low_lanes(kin, rim)
    second = jnp.concatenate(split3(pad_ref[first_blocks]), 0)
    second_columns = spread_columns(second, lay_n, pick_table(pairs, pad, modes, 1))
    second_columns_ref[...] = second_columns
    pick = pick_table(pairs, pad, modes, 0)
    for a in range(first_blocks):
        first = jnp.concatenate(split3(pad_ref[a]), 0)
        columns = halves_by_lane(spread_columns(first, lay_m, pick) * second_columns, low)
        own_columns_ref[a] = columns[:, : 3 * kin]
        own_rim_ref[a] = columns[:, 3 * kin :]
    box = back_ref.shape[1]
    back_m, back_n = back_tables(pairs, pad, modes)
    rows_m, rows_n = box_rows(box, pad)
    second_rows = spread_rows(second, back_n, rows_n)
    for a in range(first_blocks):
        first = jnp.concatenate(split3(pad_ref[a]), 0)
        back_ref[a] = halves_by_lane(spread_rows(first, back_m, rows_m) * second_rows, low_back_lanes(pairs))


def columns_kernel(
    lp_ref, near_ref, far_ref, w_ref, e3_row_ref, own_columns_ref, second_columns_ref, pad_ref,
    eigen_ref, mt_ref, v_ref, side_rim_ref, rec_ref, face_ref, wbh_ref, wbl_ref,
):
    rows = N1
    halo = (N1 + 2) * rows
    first_blocks, pairs, kin = own_columns_ref.shape
    kin, rim, pad, modes = kin // 3, side_rim_ref.shape[2] // 3, pad_ref.shape[1], N1 + 2
    box = N1 * rows
    near, far = near_ref[...], far_ref[...]
    before, after = from_sides(near, far, "stream")
    odd = jnp.logical_not(even(lax.axis_index("stream")))
    body = halo - rows
    zero = jnp.zeros((rows, lp_ref.shape[1]), F32)
    stack = jnp.concatenate(
        [before[:rows], zero, before[rows:body], lp_ref[...], after[: body - rows], zero, after[body - rows : body]], 0
    )
    u = dot(abreast(stack), w_ref[...])
    edge_near, edge_far = near[body : body + 1, 32 : 32 + pad], far[body : body + 1, 32 : 32 + pad]
    low, back_low = low_lanes(kin, rim), low_back_lanes(pairs)
    lay_m, _ = lay_tables(pad, kin, rim)
    pick_p3 = pick_table(pairs, pad, modes, 0)
    pick_p, pick_q = pick_rows(pairs, pad, modes, 0), pick_rows(pairs, pad, modes, 1)
    back_m, back_n = back_tables(pairs, pad, modes)
    face_m, face_n = face_rows(pad)
    own_eigen = eigen_ref[...]
    firsts = [jnp.concatenate([side[body:, :pad], side[body:, 16 : 16 + pad]], 0) for side in (before, after)]
    firsts = [firsts[0]] + [pad_ref[a] for a in range(first_blocks)] + [firsts[1]]
    eigens = [jnp.where(odd, edge_near, edge_far)] + [own_eigen[a : a + 1] for a in range(first_blocks)]
    eigens += [jnp.where(odd, edge_far, edge_near)]
    second = jnp.concatenate(split3(pad_ref[first_blocks]), 0)
    second_faces = spread_rows(second, back_n, face_n)
    second_sum = jnp.sum(pick_q * own_eigen[first_blocks : first_blocks + 1], 1, keepdims=True)
    for a, (first, eigen) in enumerate(zip(firsts, eigens)):
        first = jnp.concatenate(split3(first), 0)
        if a in (0, first_blocks + 1):
            columns = halves_by_lane(
                spread_columns(first, lay_m, pick_p3) * second_columns_ref[...], low
            )
            side_rim_ref[min(a, 1)] = columns[:, 3 * kin :]
            columns = columns[:, : 3 * kin]
        else:
            columns = own_columns_ref[a - 1]
        begin = a * box
        v_ref[a] = dot(columns, stacked(u[begin : begin + kin]))
        face_ref[a] = halves_by_lane(spread_rows(first, back_m, face_m) * second_faces, back_low)
        total = jnp.sum(pick_p * eigen, 1, keepdims=True) + second_sum
        rec_ref[a] = 1.0 / (total + e3_row_ref[...])
    blocks = mt_ref.shape[0] // modes
    inner = inner_table(blocks, modes)
    table = sum(
        dot(part, inner, ((0,), (0,))) for part in third_parts(mt_ref, spread_table(blocks, modes))
    )
    wbh_ref[...], wbl_ref[...] = split(table)


def spectral_columns(near, far, w_ref, v_ref, own_rim_ref, side_rim_ref, rec_ref):
    columns = v_ref.shape[0]
    inner = near.shape[0] // 2
    half = N1 // 2
    free = lane_masks(near.shape[1])[2]
    spare = unpack_spare(near, far)
    before, after = from_sides(jnp.where(free, 0.0, near), jnp.where(free, 0.0, far), "cross")
    ends = jnp.concatenate(from_sides(spare[:half], spare[half:], "cross"), 0)
    u = dot(abreast(jnp.concatenate([before, after, ends], 0)), w_ref[...])
    found = []
    for a in range(columns):
        rim = []
        for k in range(4):
            base, end = k * inner, 4 * inner + 2 * k
            start = a * (N1 - 1) - 1
            if a == 0:
                rim += [u[end : end + 1], u[base : base + 15]]
            elif a == columns - 1:
                count = inner - start
                rim += [u[base + start : base + inner], u[end + 1 : end + 2]]
                rim += [jnp.zeros((15 - count, u.shape[1]), F32)]
            else:
                rim += [u[base + start : base + start + 16]]
        rim = jnp.concatenate(rim, 0)
        table = side_rim_ref[min(a, 1)] if a in (0, columns - 1) else own_rim_ref[a - 1]
        found.append((v_ref[a] + dot(table, stacked(rim))) * rec_ref[a])
    return found


def third_back(parts, wbh_ref, wbl_ref):
    high, low = split(jnp.concatenate(parts, 0))
    return dot(high, wbh_ref[...]) + dot(high, wbl_ref[...]) + dot(low, wbh_ref[...])


def faces_kernel(
    far_ref, near_ref, w_ref, v_ref, own_rim_ref, side_rim_ref, rec_ref, wbh_ref, wbl_ref, face_ref,
    out_far_ref, out_near_ref, spectral_ref,
):
    rows = N1
    found = spectral_columns(near_ref[...], far_ref[...], w_ref, v_ref, own_rim_ref, side_rim_ref, rec_ref)
    columns = len(found)
    for a in range(columns):
        spectral_ref[a] = found[a]
    parts = [dot(face_ref[a], stacked(found[a])) for a in range(columns)]
    solved = third_back(parts, wbh_ref, wbl_ref)
    row = lax.broadcasted_iota(jnp.int32, (rows, 1), 0)
    up = even(lax.axis_index("cross"))
    for a in range(1, columns - 1):
        sums = []
        for face in range(2):
            base = 16 * a + rows * face
            previous = base - 16 + rows - 1
            after = base + 16
            sums.append(
                solved[base : base + rows]
                + jnp.where(row == 0, solved[previous : previous + 1], 0.0)
                + jnp.where(row == rows - 1, solved[after : after + 1], 0.0)
            )
        here = slice((a - 1) * rows, a * rows)
        out_near_ref[here, :] = jnp.where(up, sums[1], sums[0])
        out_far_ref[here, :] = jnp.where(up, sums[0], sums[1])


def assemble_operator(lp_ref, s_near_ref, s_far_ref, c_near_ref, c_far_ref, out_ref, acc_ref):
    rows = N1
    total_rows, width = lp_ref.shape
    padded = c_near_ref.shape[0] // 2
    body = (N1 + 1) * rows
    box = N1 * rows
    before, after = from_sides(s_near_ref[...], s_far_ref[...], "stream")
    left, right = from_sides(c_near_ref[...], c_far_ref[...], "cross")
    acc_ref[...] = lp_ref[...]
    for base in range(0, total_rows, box):
        last = base + box
        previous = before[body - rows : body] if base == 0 else lp_ref[base - rows : base, :]
        following = after[:rows] if last == total_rows else lp_ref[last : last + rows, :]
        acc_ref[base : base + rows, :] = lp_ref[base : base + rows, :] + previous
        acc_ref[last - rows : last, :] = lp_ref[last - rows : last, :] + following
        node = (N1 - 1) * (base // box + 1) + 1
        low, high = pl.ds(base, N1, stride=rows), pl.ds(base + rows - 1, N1, stride=rows)
        acc_ref[low, :] = acc_ref[low, :] + left[padded + node : padded + node + N1]
        acc_ref[high, :] = acc_ref[high, :] + right[node : node + N1]
    lane = lax.broadcasted_iota(jnp.int32, (1, width), 1)
    first = (lax.rem(lane, N1) == 0) & (lane > 0)
    final = (lax.rem(lane, N1) == N1 - 1) & (lane < width - 1)
    value = acc_ref[...]
    value = (
        value
        + jnp.where(first, pltpu.roll(value, 1, 1), 0.0)
        + jnp.where(final, pltpu.roll(value, width - 1, 1), 0.0)
    )
    out_ref[...] = value.reshape(out_ref.shape)


def solve_kernel(
    lp_ref, s_near_ref, s_far_ref, c_far_ref, c_near_ref, spectral_ref, wbh_ref, wbl_ref, pad_ref, back_ref,
    operator_ref, r_ref, out_ref, acc_ref, all_near_ref, all_far_ref, sem,
):
    unpack(c_near_ref[...], c_far_ref[...], all_near_ref, all_far_ref)
    assemble_operator(lp_ref, s_near_ref, s_far_ref, all_near_ref, all_far_ref, out_ref, acc_ref)
    copy = pltpu.make_async_copy(out_ref, operator_ref, sem)
    copy.start()
    rows = N1
    box = N1 * rows
    found = [spectral_ref[a] for a in range(spectral_ref.shape[0])]
    columns = len(found)
    pad, pairs = pad_ref.shape[1], spectral_ref.shape[1]
    back_m, back_n = back_tables(pairs, pad, N1 + 2)
    rows_m, rows_n = box_rows(box, pad)
    low = low_back_lanes(pairs)
    body = (N1 + 1) * rows
    sides = from_sides(s_near_ref[...], s_far_ref[...], "stream")
    sides = [jnp.concatenate([side[body:, :pad], side[body:, 16 : 16 + pad]], 0) for side in sides]
    second = jnp.concatenate(split3(pad_ref[columns - 2]), 0)
    parts = [None] * columns
    for a, first, kept in ((0, sides[0], slice(box - 16, box)), (columns - 1, sides[1], slice(0, 16))):
        first = jnp.concatenate(split3(first), 0)
        table = spread_rows(first, back_m, rows_m[kept]) * spread_rows(second, back_n, rows_n[kept])
        parts[a] = dot(halves_by_lane(table, low), stacked(found[a]))
    for a in range(1, columns - 1):
        parts[a] = dot(back_ref[a - 1], stacked(found[a]))
    parts[0] = parts[0][16 - rows :]
    parts[-1] = parts[-1][:rows]
    solved = third_back(parts, wbh_ref, wbl_ref)
    for a in range(columns - 2):
        base = rows + a * box
        top, bottom = solved[base : base + rows], solved[base + box - rows : base + box]
        r_ref[a * box : a * box + rows, :] = top + solved[base - rows : base]
        r_ref[a * box + rows : (a + 1) * box - rows, :] = solved[base + rows : base + box - rows]
        r_ref[(a + 1) * box - rows : (a + 1) * box, :] = bottom + solved[base + box : base + box + rows]
    copy.wait()


def pass_kernel(*refs):
    count = len(refs) // 2
    for source, target in zip(refs[:count], refs[count:]):
        target[...] = source[...]


def add_kernel(r_ref, ahead_ref, far_ref, near_ref, out_ref, acc_ref, sem):
    rows = N1
    near = jnp.where(lax.axis_index("cross") < 2, ahead_ref[...], near_ref[...])
    before, after = from_sides(near, far_ref[...], "cross")
    acc_ref[...] = r_ref[...].reshape(acc_ref.shape)
    acc_ref[:, 0, :] = acc_ref[:, 0, :] + before
    acc_ref[:, rows - 1, :] = acc_ref[:, rows - 1, :] + after
    copy = pltpu.make_async_copy(acc_ref, out_ref, sem)
    copy.start()
    copy.wait()


def shape(*dims, dtype=F32):
    return pltpu.VMEM(dims, dtype)


def call(kernel, name, out, *args, scratch=(), out_specs=None, flops=1000000, place=pltpu.VMEM):
    single = not isinstance(out, list)
    args = [pltpu.with_memory_space_constraint(x, place) for x in args]
    return pl.pallas_call(
        kernel,
        out_shape=out,
        in_specs=[pl.BlockSpec(memory_space=place)] * len(args),
        out_specs=out_specs if out_specs is not None else (VMEM if single else [VMEM] * len(out)),
        scratch_shapes=list(scratch),
        compiler_params=pltpu.CompilerParams(vmem_limit_bytes=VMEM_LIMIT),
        cost_estimate=pl.CostEstimate(flops=flops, bytes_accessed=flops, transcendentals=0),
        name=name,
    )(*args)


def swaps(axis):
    count = lax.axis_size(axis)
    near = [(i, i ^ 1) for i in range(count)]
    far = [(i, (i - 1) % count if i % 2 == 0 else (i + 1) % count) for i in range(count)]
    return near, far


def swap_stream(near, far):
    first, second = swaps("stream")
    near = lax.ppermute(near, "stream", first)
    far = lax.ppermute(far, "stream", second)
    return near, far


def cross_pairs(near, ahead=None):
    count, streams = lax.axis_size("cross"), lax.axis_size("stream")
    pairs = []
    for s in range(streams):
        for i in range(count):
            j = i ^ 1 if near else i - 1 + 2 * (i % 2)
            idle = not 0 <= j < count or (ahead is not None and (i < 2) != ahead)
            pairs.append((s * count + i, (s ^ 1) * count + i if idle else s * count + j))
    return pairs


def swap_cross(near, far):
    axes = ("stream", "cross")
    return lax.ppermute(near, axes, cross_pairs(True)), lax.ppermute(far, axes, cross_pairs(False))


def swap_cross_ahead(near, far):
    axes = ("stream", "cross")
    first = lax.ppermute(near, axes, cross_pairs(True, True))
    far, near = call(pass_kernel, "pass_on", [shape(*far.shape), shape(*near.shape)], far, near)
    return first, lax.ppermute(far, axes, cross_pairs(False)), lax.ppermute(near, axes, cross_pairs(True, False))


def shards(
    pressure, geo_diag, geo_off, modes_first, modes_second, modes_third, eigen_first, eigen_second,
    eigen_third,
):
    layers, rows, width = pressure.shape
    modes = modes_first.shape[1]
    if layers < 3 * N1 or rows != N1 or modes != N1 + 2 or lax.axis_size("stream") % 2 or lax.axis_size("cross") % 2:
        raise ValueError("unsupported sizes")
    first_blocks, third_blocks = layers // N1, width // N1
    columns = first_blocks + 2
    halo = modes * rows
    box = N1 * rows
    nodes = (first_blocks + 1) * (N1 - 1) + modes
    padded = round_up(nodes, 8)
    wide = third_blocks * modes

    pairs, pad = round_up(modes * modes, 16), round_up(modes, 16)

    mf = jnp.transpose(modes_first, (1, 0, 2))
    ms = jnp.transpose(modes_second, (1, 0, 2))
    mt = jnp.transpose(modes_third, (1, 0, 2)).reshape(modes * third_blocks, modes)

    inputs = [pressure, geo_diag, geo_off, mf, eigen_first, eigen_second]
    lp, s_near, s_far, mf, ef, es = call(
        local_kernel, "local_product",
        [
            shape(layers * rows, width), shape(halo, width), shape(halo, width),
            shape(modes, first_blocks, modes), shape(first_blocks, modes), shape(1, modes),
        ],
        *inputs, place=pltpu.HBM,
        scratch=[pltpu.VMEM(x.shape, x.dtype) for x in inputs[:3]] + [pltpu.SemaphoreType.DMA((len(inputs),))],
    )
    s_near, s_far = swap_stream(s_near, s_far)
    kin, rim_width = 3 * (N1 + 4) * rows, 3 * 64
    w, e3_row, own_columns, own_rim, second_columns, padded_modes, eigen, own_back = call(
        modes_kernel, "mode_tables",
        [
            shape(3 * width, wide, dtype=BF16), shape(1, wide),
            shape(first_blocks, pairs, kin, dtype=BF16), shape(first_blocks, pairs, rim_width, dtype=BF16),
            shape(pairs, kin + rim_width), shape(first_blocks + 1, pad, pad), shape(first_blocks + 1, pad),
            shape(first_blocks, box, 3 * pairs, dtype=BF16),
        ],
        mt, eigen_third, mf, ef, ms, es,
    )
    c_far, c_near = call(
        rows_kernel, "rows_to_send",
        [shape(2 * nodes - 4, width), shape(2 * nodes - 4, width)],
        lp, s_near, s_far, e3_row, scratch=[pltpu.VMEM((N1, width), F32)],
    )
    c_near, c_far = swap_cross(c_near, c_far)
    v, side_rim, rec, face, wbh, wbl = call(
        columns_kernel, "own_part",
        [
            shape(columns, pairs, wide), shape(2, pairs, rim_width, dtype=BF16), shape(columns, pairs, wide),
            shape(columns, 16, 3 * pairs, dtype=BF16), shape(wide, width, dtype=BF16), shape(wide, width, dtype=BF16),
        ],
        lp, s_near, s_far, w, e3_row, own_columns, second_columns, padded_modes, eigen, mt,
    )
    f_far, f_near, spectral = call(
        faces_kernel, "faces",
        [
            shape(layers, width), shape(layers, width), shape(columns, pairs, wide),
        ],
        c_far, c_near, w, v, own_rim, side_rim, rec, wbh, wbl, face,
    )
    f_ahead, f_far, f_near = swap_cross_ahead(f_near, f_far)
    result = pltpu.HBM(pressure.shape, F32)
    in_hbm = pl.BlockSpec(memory_space=pltpu.HBM)
    operator_out, restricted = call(
        solve_kernel, "solve", [result, shape(layers * rows, width)],
        lp, s_near, s_far, c_far, c_near, spectral, wbh, wbl, padded_modes, own_back, out_specs=[in_hbm, VMEM],
        scratch=[
            pltpu.VMEM(pressure.shape, F32), pltpu.VMEM((layers * rows, width), F32),
            pltpu.VMEM((2 * padded, width), F32), pltpu.VMEM((2 * padded, width), F32), pltpu.SemaphoreType.DMA,
        ],
    )
    preconditioned = call(
        add_kernel, "preconditioned", result, restricted, f_ahead, f_far, f_near, out_specs=in_hbm,
        scratch=[pltpu.VMEM(pressure.shape, F32), pltpu.SemaphoreType.DMA],
    )
    return (operator_out, preconditioned)


def solution(mesh):
    in_specs = (
        P("stream", "cross", None),
        P(None, "stream", "cross", None),
        P(None, "stream", "cross", None),
        P("stream", None, None),
        P("cross", None, None),
        P(),
        P("stream", None),
        P("cross", None),
        P(),
    )
    out_specs = (P("stream", "cross", None), P("stream", "cross", None))
    return jax.shard_map(shards, mesh=mesh, in_specs=in_specs, out_specs=out_specs, check_vma=False)
```

```python
import functools

import jax
import jax.numpy as jnp
import numpy as np
from jax import lax
from jax.experimental import pallas as pl
from jax.experimental.pallas import tpu as pltpu
from jax.sharding import PartitionSpec as P

N1 = 8
F32 = jnp.float32
BF16 = jnp.bfloat16
HIGHEST = lax.Precision.HIGHEST
VMEM_LIMIT = 16 * 2**20
VMEM = pl.BlockSpec(memory_space=pltpu.VMEM)


def legendre_values(nodes, degree):
    table = np.zeros((nodes.shape[0], degree + 1))
    table[:, 0] = 1.0
    table[:, 1] = nodes
    for order in range(2, degree + 1):
        table[:, order] = (
            (2 * order - 1) * nodes * table[:, order - 1] - (order - 1) * table[:, order - 2]
        ) / order
    return table


def derivative_table(points):
    degree = points - 1
    nodes = np.cos(np.pi * np.arange(points) / degree)
    for sweep in range(100):
        table = legendre_values(nodes, degree)
        nodes = nodes - (nodes * table[:, degree] - table[:, degree - 1]) / (
            points * table[:, degree]
        )
    gll_nodes = nodes[::-1]
    legendre_at = legendre_values(gll_nodes, degree)[:, degree]
    diff_table = np.zeros((points, points))
    for first_index in range(points):
        for second_index in range(points):
            if first_index != second_index:
                diff_table[first_index, second_index] = legendre_at[first_index] / (
                    legendre_at[second_index] * (gll_nodes[first_index] - gll_nodes[second_index])
                )
    diff_table[0, 0] = -degree * (degree + 1) / 4.0
    diff_table[degree, degree] = degree * (degree + 1) / 4.0
    return diff_table


def round_up(count, unit):
    return -(-count // unit) * unit


def dot(left, right, dims=((1,), (0,)), precision=None):
    return lax.dot_general(
        left, right, (dims, ((), ())), precision=precision, preferred_element_type=F32
    )


def split(value):
    high = value.astype(BF16)
    return high, (value - high.astype(F32)).astype(BF16)


def split3(value):
    high = value.astype(BF16)
    rest = value - high.astype(F32)
    mid = rest.astype(BF16)
    return high, mid, (rest - mid.astype(F32)).astype(BF16)


def stacked(value):
    high, low = split(value)
    return jnp.concatenate([high, low, high], 0)


def abreast(value):
    high, low = split(value)
    return jnp.concatenate([high, high, low], 1)


def even(index):
    return lax.rem(index, 2) == 0


def diff_parts():
    table = derivative_table(N1).astype(np.float32)
    high = table.astype(jnp.bfloat16).astype(np.float32)
    low = (table - high).astype(jnp.bfloat16).astype(np.float32)
    row, column = ramps(N1, N1)
    place = row * N1 + column
    found = []
    for part in (high, low):
        value = jnp.zeros((N1, N1), F32)
        for k, entry in enumerate(part.reshape(-1)):
            if entry:
                value = jnp.where(place == k, float(entry), value)
        found.append(value.astype(BF16))
    return found


def operator_factors(blocks):
    def kron(part, count, inner, turned):
        row, column = ramps(count, N1)
        quotient, rest = over(row, N1)
        pick = mask((rest if inner else quotient) == column)
        value = dot(pick, part, ((1,), (1 if turned else 0,))).astype(BF16)
        row, column = ramps(N1, count)
        value = dot(value, mask(over(column, N1)[1 if inner else 0] == row))
        row, column = ramps(count, count)
        row, column = over(row, N1), over(column, N1)
        same = row[0] == column[0] if inner else row[1] == column[1]
        return jnp.where(same, value, 0.0).astype(BF16)

    parts = diff_parts()
    box = N1 * N1
    high, low = [
        jnp.concatenate([kron(part, box, False, False), kron(part, box, True, False)], 0) for part in parts
    ]
    grad = jnp.concatenate([high, high, low], 1)
    high, low = [
        jnp.concatenate([kron(part, box, False, True), kron(part, box, True, True)], 1) for part in parts
    ]
    back = jnp.concatenate([high, high, low], 1)
    high, low = [kron(part, blocks * N1, True, True) for part in parts]
    third = jnp.concatenate([high, low, high], 0)
    high, low = [kron(part, blocks * N1, True, False) for part in parts]
    return grad, third, back, jnp.concatenate([high, low, high], 0)


def local_kernel(*refs):
    count = 6
    sources, outs, scratch = refs[:count], refs[count : count + 6], refs[count + 6 :]
    lp_ref, near_ref, far_ref, mf_ref, ef_ref, es_ref = outs
    p_ref, gd_ref, go_ref, sems = scratch
    targets = (p_ref, gd_ref, go_ref, mf_ref, ef_ref, es_ref)
    copies = [
        pltpu.make_async_copy(source, target, sems.at[k])
        for k, (source, target) in enumerate(zip(sources, targets))
    ]
    for copy in copies:
        copy.start()
    layers, rows, width = p_ref.shape
    grad, third_grad, back, third_back = operator_factors(width // N1)
    copies[0].wait()
    first_blocks = layers // N1
    box = N1 * rows
    modes = mf_ref.shape[0]
    p_all = p_ref[...].reshape(layers * rows, width)
    third = dot(abreast(p_all), third_grad)
    grads = [
        dot(grad, stacked(p_all[a * box : (a + 1) * box])) for a in range(first_blocks)
    ]
    for k in (1, 2):
        copies[k].wait()
    for a in range(first_blocks):
        here = slice(a * box, (a + 1) * box)
        one, two, three = grads[a][:box], grads[a][box:], third[here]
        g = [
            gd_ref[k, a * N1 : (a + 1) * N1].reshape(box, width) for k in range(3)
        ] + [go_ref[k, a * N1 : (a + 1) * N1].reshape(box, width) for k in range(3)]
        flux_one = g[0] * one + g[3] * two + g[4] * three
        flux_two = g[3] * one + g[1] * two + g[5] * three
        flux_three = g[4] * one + g[5] * two + g[2] * three
        lp_ref[here, :] = dot(
            back, stacked(jnp.concatenate([flux_one, flux_two], 0))
        ) + dot(abreast(flux_three), third_back)
    for k in (3, 4, 5):
        copies[k].wait()
    layer = lambda l: slice(l * rows, (l + 1) * rows)
    body = (modes - 1) * rows
    up_layers = [
        (0, rows, lp_ref[layer(layers - modes), :]),
        (rows, 2 * rows, lp_ref[layer(layers - modes + 1), :] + lp_ref[layer(layers - modes + 2), :]),
        (2 * rows, body, lp_ref[(layers - modes + 3) * rows :, :]),
    ]
    down_layers = [
        (0, body - 2 * rows, lp_ref[: (modes - 3) * rows, :]),
        (body - 2 * rows, body - rows, lp_ref[layer(modes - 3), :] + lp_ref[layer(modes - 2), :]),
        (body - rows, body, lp_ref[layer(modes - 1), :]),
    ]
    forward = even(lax.axis_index("stream"))

    def fill(ref, parts, a):
        for begin, end, value in parts:
            ref[begin:end, :] = value
        ref[body:, :] = jnp.zeros((rows, width), F32)
        ref[body:, :modes] = mf_ref[:rows, a, :]
        ref[body : body + modes - rows, 16 : 16 + modes] = mf_ref[rows:, a, :]
        ref[body : body + 1, 32 : 32 + modes] = ef_ref[a : a + 1, :]

    @pl.when(forward)
    def _():
        fill(near_ref, up_layers, first_blocks - 1)
        fill(far_ref, down_layers, 0)

    @pl.when(jnp.logical_not(forward))
    def _():
        fill(near_ref, down_layers, 0)
        fill(far_ref, up_layers, first_blocks - 1)


def from_sides(near, far, axis):
    index = lax.axis_index(axis)
    is_even = even(index)
    before = jnp.where(is_even, far, near)
    after = jnp.where(is_even, near, far)
    before = jnp.where(index == 0, 0.0, before)
    after = jnp.where(index == lax.axis_size(axis) - 1, 0.0, after)
    return before, after


def lane_masks(width):
    lane = lax.broadcasted_iota(jnp.int32, (1, width), 1)
    node = over(lane, N1)[1]
    return lane, node, (node == 0) & (lane > 0)


def pack(upper_ref, lower_ref, spare):
    width = spare.shape[1]
    lane, node, free = lane_masks(width)
    final = (node == N1 - 1) & (lane < width - 1)
    upper = lax.broadcasted_iota(jnp.int32, (N1, 1), 0) < N1 // 2
    hidden = [jnp.where(lane == N1, pltpu.roll(spare, N1, 1), 0.0)]
    hidden += [pltpu.roll(spare, N1 - j, 1) for j in range(1, N1)]
    hidden[N1 - 1] = hidden[N1 - 1] + spare
    last = jnp.zeros_like(spare)
    for j in range(1, N1):
        last = jnp.where(lane == N1 * j, pltpu.roll(spare, N1 + (N1 - 1) * j, 1), last)
    hidden.append(last)
    for ref, mine in ((upper_ref, upper), (lower_ref, jnp.logical_not(upper))):
        value = ref[...]
        value = value + jnp.where(final, pltpu.roll(value, width - 1, 1), 0.0)
        for j in range(ref.shape[0] // N1):
            here = slice(j * N1, (j + 1) * N1)
            ref[here, :] = jnp.where(free & mine, hidden[min(j, N1)], jnp.where(free, 0.0, value[here]))


def unpack_spare(upper_rows, lower_rows):
    width = upper_rows.shape[1]
    lane, node, _ = lane_masks(width)
    upper = lax.broadcasted_iota(jnp.int32, (N1, 1), 0) < N1 // 2
    tiles = []
    for j in range(N1 + 1):
        here = slice(j * N1, (j + 1) * N1)
        tiles.append(jnp.where(upper, upper_rows[here], lower_rows[here]))
    spare = jnp.zeros((N1, width), F32)
    for j in range(N1):
        spare = jnp.where((node == j) & (lane < width - N1), pltpu.roll(tiles[j], width - N1 + j, 1), spare)
    for j in range(1, N1):
        spare = jnp.where(
            lane == width - N1 + j, pltpu.roll(tiles[N1], width - N1 - (N1 - 1) * j, 1), spare
        )
    return spare


def unpack(upper_rows, lower_rows, out_upper_ref, out_lower_ref):
    width = upper_rows.shape[1]
    free = lane_masks(width)[2]
    spare = unpack_spare(upper_rows, lower_rows)
    inner = upper_rows.shape[0] // 2
    padded = out_upper_ref.shape[0] // 2
    for ref, packed, start in ((out_upper_ref, upper_rows, 0), (out_lower_ref, lower_rows, N1 // 2)):
        value = jnp.where(free, 0.0, packed)
        for slot in range(2):
            base, row = slot * padded, start + 2 * slot
            ref[base : base + 1, :] = spare[row : row + 1]
            ref[base + 1 : base + 1 + inner, :] = value[slot * inner : (slot + 1) * inner]
            ref[base + 1 + inner : base + 2 + inner, :] = spare[row + 1 : row + 2]
            ref[base + 2 + inner : base + padded, :] = jnp.zeros((padded - inner - 2, width), F32)


def rows_kernel(lp_ref, near_ref, far_ref, built_ref, out_far_ref, out_near_ref, spare_ref):
    rows = N1
    layers = lp_ref.shape[0] // rows
    count = N1 + 1
    inner = out_near_ref.shape[0] // 2
    found = {}
    for k in (0, 1, rows - 2, rows - 1):
        before, after = from_sides(
            near_ref[pl.ds(k, count, stride=rows), :], far_ref[pl.ds(k, count, stride=rows), :], "stream"
        )
        found[k] = (before, lp_ref[pl.ds(k, layers, stride=rows), :], after)
    up = even(lax.axis_index("cross"))
    messages = ((out_near_ref, up, 0), (out_far_ref, jnp.logical_not(up), N1 // 2))
    for ref, high, start in messages:
        for slot in range(2):
            base = slot * inner
            before, own, after = [
                jnp.where(high, one, two) for one, two in zip(found[rows - 2 + slot], found[slot])
            ]
            place = start + 2 * slot
            spare_ref[place : place + 1, :] = before[:1]
            spare_ref[place + 1 : place + 2, :] = after[count - 1 :]
            ref[base : base + count - 2, :] = before[1 : count - 1]
            base += count - 2
            for l in range(0, layers, N1):
                previous = before[count - 1 :] if l == 0 else own[l - 1 : l]
                ref[base : base + 1, :] = previous + own[l : l + 1]
                ref[base + 1 : base + N1 - 1, :] = own[l + 1 : l + N1 - 1]
                base += N1 - 1
            ref[base : base + 1, :] = own[layers - 1 :] + after[:1]
            ref[base + 1 : base + count - 1, :] = after[1 : count - 1]
    pack(out_near_ref, out_far_ref, spare_ref[...])


def spread_columns(parts, lay, pick):
    table = dot(parts, lay, ((0,), (0,)))
    return dot(pick, jnp.concatenate(split3(table), 0))


def spread_rows(parts, pick, rows):
    pad = parts.shape[0] // 3
    table = sum(dot(parts[k * pad : (k + 1) * pad], pick) for k in range(3))
    return dot(rows, jnp.concatenate(split3(table), 0))


def halves_by_lane(value, low):
    high = value.astype(BF16).astype(F32)
    return jnp.where(low, value - high, high).astype(BF16)


def low_lanes(kin, rim):
    lane = lax.broadcasted_iota(jnp.int32, (1, 3 * (kin + rim)), 1)
    return ((lane >= 2 * kin) & (lane < 3 * kin)) | (lane >= 3 * kin + 2 * rim)


def low_back_lanes(pairs):
    return lax.broadcasted_iota(jnp.int32, (1, 3 * pairs), 1) >= 2 * pairs


def ramps(*dims):
    return [lax.broadcasted_iota(jnp.int32, dims, axis) for axis in range(2)]


def over(value, count):
    if count & (count - 1) == 0:
        return lax.shift_right_logical(value, count.bit_length() - 1), value & (count - 1)
    quotient = ((value.astype(F32) + 0.5) * (1.0 / count)).astype(jnp.int32)
    return quotient, value - quotient * count


def mask(hit):
    return jnp.where(hit, 1.0, 0.0).astype(BF16)


def spread_table(blocks, modes):
    row, column = ramps(modes, blocks * modes)
    return mask(row == over(column, modes)[1])


def gather_table(blocks, modes):
    row, column = ramps(blocks * N1, modes * blocks)
    node, block = over(column, blocks)
    place = row - block * N1
    hit = (place == node - 1) & (node >= 1) & (node <= N1)
    for n, at in ((0, -2), (1, -1), (N1, N1), (N1 + 1, N1 + 1)):
        hit = hit | ((node == n) & (place == at))
    return mask(hit)


def pick_table(pairs, pad, modes, which):
    row, column = ramps(pairs, 3 * pad)
    return mask(over(row, modes)[which] == over(column, pad)[1])


def pick_rows(pairs, pad, modes, which):
    row, column = ramps(pairs, pad)
    return jnp.where(over(row, modes)[which] == column, 1.0, 0.0)


def back_tables(pairs, pad, modes):
    row, column = ramps(pad, 3 * pairs)
    found = over(over(column, pairs)[1], modes)
    return mask(found[0] == row), mask(found[1] == row)


def box_rows(count, pad):
    row, column = ramps(count, 3 * pad)
    first, second = over(row, N1)
    column = over(column, pad)[1]
    return mask(first + 1 == column), mask(second + 1 == column)


def face_rows(pad):
    row, column = ramps(2 * N1, 3 * pad)
    face, first = over(row, N1)
    column = over(column, pad)[1]
    return mask(first + 1 == column), mask(jnp.where(face == 0, 1, N1) == column)


def inner_table(blocks, modes):
    row, column = ramps(modes * blocks, blocks * N1)
    node, block = over(row, blocks)
    place = column - block * N1
    hit = (place == node - 1) & (node >= 1) & (node <= N1)
    return mask(hit | ((node == 1) & (place == -1)) | ((node == N1) & (place == N1)))


def lay_tables(pad, kin, rim):
    layers = kin // N1
    row, column = ramps(3 * pad, 3 * (kin + rim))
    row = over(row, pad)[1]
    own = column < 3 * kin
    l_own, y = over(over(column, kin)[1], N1)
    kind, l_rim = over(over(jnp.maximum(column - 3 * kin, 0), rim)[1], rim // 4)
    node = jnp.where(l_own == 0, 0, jnp.where(l_own == layers - 1, N1 + 1, jnp.clip(l_own - 1, 1, N1)))
    node = jnp.where(own, node, l_rim)
    second = jnp.where(own, y + 1, jnp.where(kind < 2, kind, N1 - 2 + kind))
    inside = own | (l_rim < N1 + 2)
    return mask(inside & (row == node)), mask(inside & (row == second))


def third_parts(mt_ref, spread):
    rows, modes = mt_ref.shape
    blocks = rows // modes
    row, column = ramps(rows, rows)
    own = over(row, blocks)[1] == over(column, modes)[0]
    return [jnp.where(own, dot(part, spread), 0.0).astype(BF16) for part in split3(mt_ref[...])]


def pad_modes(pad_ref, mf_ref, ms_ref):
    modes = ms_ref.shape[0]
    first_blocks = pad_ref.shape[0] - 1
    pad_ref[...] = jnp.zeros_like(pad_ref)
    for a in range(first_blocks):
        pad_ref[a, :modes, :modes] = mf_ref[:, a, :]
    pad_ref[first_blocks, :modes, :modes] = ms_ref[:, 0, :]


def modes_kernel(
    mt_ref, e3_ref, mf_ref, ef_ref, ms_ref, es_ref,
    w_ref, e3_row_ref, own_columns_ref, own_rim_ref, second_columns_ref, pad_ref, eigen_ref, back_ref,
):
    blocks, modes = e3_ref.shape
    spread = spread_table(blocks, modes)
    gather = gather_table(blocks, modes)
    table = sum(dot(gather, part) for part in third_parts(mt_ref, spread))
    high, low = split(table)
    w_ref[...] = jnp.concatenate([high, low, high], 0)
    row, column = ramps(blocks, blocks * modes)
    e3_wide = sum(dot(part, spread) for part in split3(e3_ref[...]))
    e3_row_ref[...] = jnp.sum(
        jnp.where(row == over(column, modes)[0], e3_wide, 0.0), 0, keepdims=True
    )
    first_blocks, pairs, kin = own_columns_ref.shape
    kin, rim, pad = kin // 3, own_rim_ref.shape[2] // 3, pad_ref.shape[1]
    pad_modes(pad_ref, mf_ref, ms_ref)
    eigen_ref[...] = jnp.zeros_like(eigen_ref)
    eigen_ref[:first_blocks, :modes] = ef_ref[...]
    eigen_ref[first_blocks : first_blocks + 1, :modes] = es_ref[...]
    lay_m, lay_n = lay_tables(pad, kin, rim)
    low = low_lanes(kin, rim)
    second = jnp.concatenate(split3(pad_ref[first_blocks]), 0)
    second_columns = spread_columns(second, lay_n, pick_table(pairs, pad, modes, 1))
    second_columns_ref[...] = second_columns
    pick = pick_table(pairs, pad, modes, 0)
    for a in range(first_blocks):
        first = jnp.concatenate(split3(pad_ref[a]), 0)
        columns = halves_by_lane(spread_columns(first, lay_m, pick) * second_columns, low)
        own_columns_ref[a] = columns[:, : 3 * kin]
        own_rim_ref[a] = columns[:, 3 * kin :]
    box = back_ref.shape[1]
    back_m, back_n = back_tables(pairs, pad, modes)
    rows_m, rows_n = box_rows(box, pad)
    second_rows = spread_rows(second, back_n, rows_n)
    for a in range(first_blocks):
        first = jnp.concatenate(split3(pad_ref[a]), 0)
        back_ref[a] = halves_by_lane(spread_rows(first, back_m, rows_m) * second_rows, low_back_lanes(pairs))


def columns_kernel(
    lp_ref, near_ref, far_ref, w_ref, e3_row_ref, own_columns_ref, second_columns_ref, pad_ref,
    eigen_ref, mt_ref, v_ref, side_rim_ref, rec_ref, face_ref, wbh_ref, wbl_ref,
):
    rows = N1
    halo = (N1 + 2) * rows
    first_blocks, pairs, kin = own_columns_ref.shape
    kin, rim, pad, modes = kin // 3, side_rim_ref.shape[2] // 3, pad_ref.shape[1], N1 + 2
    box = N1 * rows
    near, far = near_ref[...], far_ref[...]
    before, after = from_sides(near, far, "stream")
    odd = jnp.logical_not(even(lax.axis_index("stream")))
    body = halo - rows
    zero = jnp.zeros((rows, lp_ref.shape[1]), F32)
    stack = jnp.concatenate(
        [before[:rows], zero, before[rows:body], lp_ref[...], after[: body - rows], zero, after[body - rows : body]], 0
    )
    u = dot(abreast(stack), w_ref[...])
    edge_near, edge_far = near[body : body + 1, 32 : 32 + pad], far[body : body + 1, 32 : 32 + pad]
    low, back_low = low_lanes(kin, rim), low_back_lanes(pairs)
    lay_m, _ = lay_tables(pad, kin, rim)
    pick_p3 = pick_table(pairs, pad, modes, 0)
    pick_p, pick_q = pick_rows(pairs, pad, modes, 0), pick_rows(pairs, pad, modes, 1)
    back_m, back_n = back_tables(pairs, pad, modes)
    face_m, face_n = face_rows(pad)
    own_eigen = eigen_ref[...]
    firsts = [jnp.concatenate([side[body:, :pad], side[body:, 16 : 16 + pad]], 0) for side in (before, after)]
    firsts = [firsts[0]] + [pad_ref[a] for a in range(first_blocks)] + [firsts[1]]
    eigens = [jnp.where(odd, edge_near, edge_far)] + [own_eigen[a : a + 1] for a in range(first_blocks)]
    eigens += [jnp.where(odd, edge_far, edge_near)]
    second = jnp.concatenate(split3(pad_ref[first_blocks]), 0)
    second_faces = spread_rows(second, back_n, face_n)
    second_sum = jnp.sum(pick_q * own_eigen[first_blocks : first_blocks + 1], 1, keepdims=True)
    for a, (first, eigen) in enumerate(zip(firsts, eigens)):
        first = jnp.concatenate(split3(first), 0)
        if a in (0, first_blocks + 1):
            columns = halves_by_lane(
                spread_columns(first, lay_m, pick_p3) * second_columns_ref[...], low
            )
            side_rim_ref[min(a, 1)] = columns[:, 3 * kin :]
            columns = columns[:, : 3 * kin]
        else:
            columns = own_columns_ref[a - 1]
        begin = a * box
        v_ref[a] = dot(columns, stacked(u[begin : begin + kin]))
        face_ref[a] = halves_by_lane(spread_rows(first, back_m, face_m) * second_faces, back_low)
        total = jnp.sum(pick_p * eigen, 1, keepdims=True) + second_sum
        rec_ref[a] = 1.0 / (total + e3_row_ref[...])
    blocks = mt_ref.shape[0] // modes
    inner = inner_table(blocks, modes)
    table = sum(
        dot(part, inner, ((0,), (0,))) for part in third_parts(mt_ref, spread_table(blocks, modes))
    )
    wbh_ref[...], wbl_ref[...] = split(table)


def spectral_columns(near, far, w_ref, v_ref, own_rim_ref, side_rim_ref, rec_ref):
    columns = v_ref.shape[0]
    inner = near.shape[0] // 2
    half = N1 // 2
    free = lane_masks(near.shape[1])[2]
    spare = unpack_spare(near, far)
    before, after = from_sides(jnp.where(free, 0.0, near), jnp.where(free, 0.0, far), "cross")
    ends = jnp.concatenate(from_sides(spare[:half], spare[half:], "cross"), 0)
    u = dot(abreast(jnp.concatenate([before, after, ends], 0)), w_ref[...])
    found = []
    for a in range(columns):
        rim = []
        for k in range(4):
            base, end = k * inner, 4 * inner + 2 * k
            start = a * (N1 - 1) - 1
            if a == 0:
                rim += [u[end : end + 1], u[base : base + 15]]
            elif a == columns - 1:
                count = inner - start
                rim += [u[base + start : base + inner], u[end + 1 : end + 2]]
                rim += [jnp.zeros((15 - count, u.shape[1]), F32)]
            else:
                rim += [u[base + start : base + start + 16]]
        rim = jnp.concatenate(rim, 0)
        table = side_rim_ref[min(a, 1)] if a in (0, columns - 1) else own_rim_ref[a - 1]
        found.append((v_ref[a] + dot(table, stacked(rim))) * rec_ref[a])
    return found


def third_back(parts, wbh_ref, wbl_ref):
    high, low = split(jnp.concatenate(parts, 0))
    count, width = high.shape[0], wbh_ref.shape[1]
    both = dot(jnp.concatenate([high, low], 0), jnp.concatenate([wbh_ref[...], wbl_ref[...]], 1))
    return both[:count, :width] + both[count:, :width] + both[:count, width:]


def faces_kernel(
    far_ref, near_ref, w_ref, v_ref, own_rim_ref, side_rim_ref, rec_ref, wbh_ref, wbl_ref, face_ref,
    out_far_ref, out_near_ref, spectral_ref,
):
    rows = N1
    found = spectral_columns(near_ref[...], far_ref[...], w_ref, v_ref, own_rim_ref, side_rim_ref, rec_ref)
    columns = len(found)
    for a in range(columns):
        spectral_ref[a] = found[a]
    parts = [dot(face_ref[a], stacked(found[a])) for a in range(columns)]
    solved = third_back(parts, wbh_ref, wbl_ref)
    row = lax.broadcasted_iota(jnp.int32, (rows, 1), 0)
    up = even(lax.axis_index("cross"))
    for a in range(1, columns - 1):
        sums = []
        for face in range(2):
            base = 16 * a + rows * face
            previous = base - 16 + rows - 1
            after = base + 16
            sums.append(
                solved[base : base + rows]
                + jnp.where(row == 0, solved[previous : previous + 1], 0.0)
                + jnp.where(row == rows - 1, solved[after : after + 1], 0.0)
            )
        here = slice((a - 1) * rows, a * rows)
        out_near_ref[here, :] = jnp.where(up, sums[1], sums[0])
        out_far_ref[here, :] = jnp.where(up, sums[0], sums[1])


def assemble_operator(lp_ref, s_near_ref, s_far_ref, c_near_ref, c_far_ref, out_ref, acc_ref):
    rows = N1
    total_rows, width = lp_ref.shape
    padded = c_near_ref.shape[0] // 2
    body = (N1 + 1) * rows
    box = N1 * rows
    before, after = from_sides(s_near_ref[...], s_far_ref[...], "stream")
    left, right = from_sides(c_near_ref[...], c_far_ref[...], "cross")
    acc_ref[...] = lp_ref[...]
    for base in range(0, total_rows, box):
        last = base + box
        previous = before[body - rows : body] if base == 0 else lp_ref[base - rows : base, :]
        following = after[:rows] if last == total_rows else lp_ref[last : last + rows, :]
        acc_ref[base : base + rows, :] = lp_ref[base : base + rows, :] + previous
        acc_ref[last - rows : last, :] = lp_ref[last - rows : last, :] + following
        node = (N1 - 1) * (base // box + 1) + 1
        low, high = pl.ds(base, N1, stride=rows), pl.ds(base + rows - 1, N1, stride=rows)
        acc_ref[low, :] = acc_ref[low, :] + left[padded + node : padded + node + N1]
        acc_ref[high, :] = acc_ref[high, :] + right[node : node + N1]
    lane = lax.broadcasted_iota(jnp.int32, (1, width), 1)
    first = (lax.rem(lane, N1) == 0) & (lane > 0)
    final = (lax.rem(lane, N1) == N1 - 1) & (lane < width - 1)
    value = acc_ref[...]
    value = (
        value
        + jnp.where(first, pltpu.roll(value, 1, 1), 0.0)
        + jnp.where(final, pltpu.roll(value, width - 1, 1), 0.0)
    )
    out_ref[...] = value.reshape(out_ref.shape)


def solve_kernel(
    lp_ref, s_near_ref, s_far_ref, c_far_ref, c_near_ref, spectral_ref, wbh_ref, wbl_ref, pad_ref, back_ref,
    operator_ref, r_ref, out_ref, acc_ref, all_near_ref, all_far_ref, sem,
):
    unpack(c_near_ref[...], c_far_ref[...], all_near_ref, all_far_ref)
    assemble_operator(lp_ref, s_near_ref, s_far_ref, all_near_ref, all_far_ref, out_ref, acc_ref)
    copy = pltpu.make_async_copy(out_ref, operator_ref, sem)
    copy.start()
    rows = N1
    box = N1 * rows
    found = [spectral_ref[a] for a in range(spectral_ref.shape[0])]
    columns = len(found)
    pad, pairs = pad_ref.shape[1], spectral_ref.shape[1]
    back_m, back_n = back_tables(pairs, pad, N1 + 2)
    rows_m, rows_n = box_rows(box, pad)
    low = low_back_lanes(pairs)
    body = (N1 + 1) * rows
    sides = from_sides(s_near_ref[...], s_far_ref[...], "stream")
    sides = [jnp.concatenate([side[body:, :pad], side[body:, 16 : 16 + pad]], 0) for side in sides]
    second = jnp.concatenate(split3(pad_ref[columns - 2]), 0)
    parts = [None] * columns
    for a, first, kept in ((0, sides[0], slice(box - 16, box)), (columns - 1, sides[1], slice(0, 16))):
        first = jnp.concatenate(split3(first), 0)
        table = spread_rows(first, back_m, rows_m[kept]) * spread_rows(second, back_n, rows_n[kept])
        parts[a] = dot(halves_by_lane(table, low), stacked(found[a]))
    for a in range(1, columns - 1):
        parts[a] = dot(back_ref[a - 1], stacked(found[a]))
    parts[0] = parts[0][16 - rows :]
    parts[-1] = parts[-1][:rows]
    solved = third_back(parts, wbh_ref, wbl_ref)
    for a in range(columns - 2):
        base = rows + a * box
        top, bottom = solved[base : base + rows], solved[base + box - rows : base + box]
        r_ref[a * box : a * box + rows, :] = top + solved[base - rows : base]
        r_ref[a * box + rows : (a + 1) * box - rows, :] = solved[base + rows : base + box - rows]
        r_ref[(a + 1) * box - rows : (a + 1) * box, :] = bottom + solved[base + box : base + box + rows]
    copy.wait()


def pass_kernel(*refs):
    count = len(refs) // 2
    for source, target in zip(refs[:count], refs[count:]):
        target[...] = source[...]


def add_kernel(r_ref, ahead_ref, far_ref, near_ref, out_ref, acc_ref, sem):
    rows = N1
    near = jnp.where(lax.axis_index("cross") < 2, ahead_ref[...], near_ref[...])
    before, after = from_sides(near, far_ref[...], "cross")
    row = lax.broadcasted_iota(jnp.int32, (rows, 1), 0)
    for l in range(acc_ref.shape[0]):
        value = r_ref[l * rows : (l + 1) * rows, :] + jnp.where(row == 0, before[l : l + 1], 0.0)
        acc_ref[l] = value + jnp.where(row == rows - 1, after[l : l + 1], 0.0)
    copy = pltpu.make_async_copy(acc_ref, out_ref, sem)
    copy.start()
    copy.wait()


def shape(*dims, dtype=F32):
    return pltpu.VMEM(dims, dtype)


def call(kernel, name, out, *args, scratch=(), out_specs=None, flops=1000000, place=pltpu.VMEM):
    single = not isinstance(out, list)
    args = [pltpu.with_memory_space_constraint(x, place) for x in args]
    return pl.pallas_call(
        kernel,
        out_shape=out,
        in_specs=[pl.BlockSpec(memory_space=place)] * len(args),
        out_specs=out_specs if out_specs is not None else (VMEM if single else [VMEM] * len(out)),
        scratch_shapes=list(scratch),
        compiler_params=pltpu.CompilerParams(vmem_limit_bytes=VMEM_LIMIT),
        cost_estimate=pl.CostEstimate(flops=flops, bytes_accessed=flops, transcendentals=0),
        name=name,
    )(*args)


def swaps(axis):
    count = lax.axis_size(axis)
    near = [(i, i ^ 1) for i in range(count)]
    far = [(i, (i - 1) % count if i % 2 == 0 else (i + 1) % count) for i in range(count)]
    return near, far


def swap_stream(near, far):
    first, second = swaps("stream")
    near = lax.ppermute(near, "stream", first)
    far = lax.ppermute(far, "stream", second)
    return near, far


def cross_pairs(near, ahead=None):
    count, streams = lax.axis_size("cross"), lax.axis_size("stream")
    pairs = []
    for s in range(streams):
        for i in range(count):
            j = i ^ 1 if near else i - 1 + 2 * (i % 2)
            idle = not 0 <= j < count or (ahead is not None and (i < 2) != ahead)
            pairs.append((s * count + i, (s ^ 1) * count + i if idle else s * count + j))
    return pairs


def swap_cross(near, far):
    axes = ("stream", "cross")
    return lax.ppermute(near, axes, cross_pairs(True)), lax.ppermute(far, axes, cross_pairs(False))


def swap_cross_ahead(near, far):
    axes = ("stream", "cross")
    first = lax.ppermute(near, axes, cross_pairs(True, True))
    far, near = call(pass_kernel, "pass_on", [shape(*far.shape), shape(*near.shape)], far, near)
    return first, lax.ppermute(far, axes, cross_pairs(False)), lax.ppermute(near, axes, cross_pairs(True, False))


def shards(
    pressure, geo_diag, geo_off, modes_first, modes_second, modes_third, eigen_first, eigen_second,
    eigen_third,
):
    layers, rows, width = pressure.shape
    modes = modes_first.shape[1]
    if layers < 3 * N1 or rows != N1 or modes != N1 + 2 or lax.axis_size("stream") % 2 or lax.axis_size("cross") % 2:
        raise ValueError("unsupported sizes")
    first_blocks, third_blocks = layers // N1, width // N1
    columns = first_blocks + 2
    halo = modes * rows
    box = N1 * rows
    nodes = (first_blocks + 1) * (N1 - 1) + modes
    padded = round_up(nodes, 8)
    wide = third_blocks * modes

    pairs, pad = round_up(modes * modes, 16), round_up(modes, 16)

    mf = jnp.transpose(modes_first, (1, 0, 2))
    ms = jnp.transpose(modes_second, (1, 0, 2))
    mt = jnp.transpose(modes_third, (1, 0, 2)).reshape(modes * third_blocks, modes)

    inputs = [pressure, geo_diag, geo_off, mf, eigen_first, eigen_second]
    lp, s_near, s_far, mf, ef, es = call(
        local_kernel, "local_product",
        [
            shape(layers * rows, width), shape(halo, width), shape(halo, width),
            shape(modes, first_blocks, modes), shape(first_blocks, modes), shape(1, modes),
        ],
        *inputs, place=pltpu.HBM,
        scratch=[pltpu.VMEM(x.shape, x.dtype) for x in inputs[:3]] + [pltpu.SemaphoreType.DMA((len(inputs),))],
    )
    s_near, s_far = swap_stream(s_near, s_far)
    kin, rim_width = 3 * (N1 + 4) * rows, 3 * 64
    w, e3_row, own_columns, own_rim, second_columns, padded_modes, eigen, own_back = call(
        modes_kernel, "mode_tables",
        [
            shape(3 * width, wide, dtype=BF16), shape(1, wide),
            shape(first_blocks, pairs, kin, dtype=BF16), shape(first_blocks, pairs, rim_width, dtype=BF16),
            shape(pairs, kin + rim_width), shape(first_blocks + 1, pad, pad), shape(first_blocks + 1, pad),
            shape(first_blocks, box, 3 * pairs, dtype=BF16),
        ],
        mt, eigen_third, mf, ef, ms, es,
    )
    c_far, c_near = call(
        rows_kernel, "rows_to_send",
        [shape(2 * nodes - 4, width), shape(2 * nodes - 4, width)],
        lp, s_near, s_far, e3_row, scratch=[pltpu.VMEM((N1, width), F32)],
    )
    c_near, c_far = swap_cross(c_near, c_far)
    v, side_rim, rec, face, wbh, wbl = call(
        columns_kernel, "own_part",
        [
            shape(columns, pairs, wide), shape(2, pairs, rim_width, dtype=BF16), shape(columns, pairs, wide),
            shape(columns, 16, 3 * pairs, dtype=BF16), shape(wide, width, dtype=BF16), shape(wide, width, dtype=BF16),
        ],
        lp, s_near, s_far, w, e3_row, own_columns, second_columns, padded_modes, eigen, mt,
    )
    f_far, f_near, spectral = call(
        faces_kernel, "faces",
        [
            shape(layers, width), shape(layers, width), shape(columns, pairs, wide),
        ],
        c_far, c_near, w, v, own_rim, side_rim, rec, wbh, wbl, face,
    )
    f_ahead, f_far, f_near = swap_cross_ahead(f_near, f_far)
    result = pltpu.HBM(pressure.shape, F32)
    in_hbm = pl.BlockSpec(memory_space=pltpu.HBM)
    operator_out, restricted = call(
        solve_kernel, "solve", [result, shape(layers * rows, width)],
        lp, s_near, s_far, c_far, c_near, spectral, wbh, wbl, padded_modes, own_back, out_specs=[in_hbm, VMEM],
        scratch=[
            pltpu.VMEM(pressure.shape, F32), pltpu.VMEM((layers * rows, width), F32),
            pltpu.VMEM((2 * padded, width), F32), pltpu.VMEM((2 * padded, width), F32), pltpu.SemaphoreType.DMA,
        ],
    )
    preconditioned = call(
        add_kernel, "preconditioned", result, restricted, f_ahead, f_far, f_near, out_specs=in_hbm,
        scratch=[pltpu.VMEM(pressure.shape, F32), pltpu.SemaphoreType.DMA],
    )
    return (operator_out, preconditioned)


def solution(mesh):
    in_specs = (
        P("stream", "cross", None),
        P(None, "stream", "cross", None),
        P(None, "stream", "cross", None),
        P("stream", None, None),
        P("cross", None, None),
        P(),
        P("stream", None),
        P("cross", None),
        P(),
    )
    out_specs = (P("stream", "cross", None), P("stream", "cross", None))
    return jax.shard_map(shards, mesh=mesh, in_specs=in_specs, out_specs=out_specs, check_vma=False)
```

```python
import functools

import jax
import jax.numpy as jnp
import numpy as np
from jax import lax
from jax.experimental import pallas as pl
from jax.experimental.pallas import tpu as pltpu
from jax.sharding import PartitionSpec as P

N1 = 8
F32 = jnp.float32
BF16 = jnp.bfloat16
HIGHEST = lax.Precision.HIGHEST
VMEM_LIMIT = 16 * 2**20
VMEM = pl.BlockSpec(memory_space=pltpu.VMEM)


def legendre_values(nodes, degree):
    table = np.zeros((nodes.shape[0], degree + 1))
    table[:, 0] = 1.0
    table[:, 1] = nodes
    for order in range(2, degree + 1):
        table[:, order] = (
            (2 * order - 1) * nodes * table[:, order - 1] - (order - 1) * table[:, order - 2]
        ) / order
    return table


def derivative_table(points):
    degree = points - 1
    nodes = np.cos(np.pi * np.arange(points) / degree)
    for sweep in range(100):
        table = legendre_values(nodes, degree)
        nodes = nodes - (nodes * table[:, degree] - table[:, degree - 1]) / (
            points * table[:, degree]
        )
    gll_nodes = nodes[::-1]
    legendre_at = legendre_values(gll_nodes, degree)[:, degree]
    diff_table = np.zeros((points, points))
    for first_index in range(points):
        for second_index in range(points):
            if first_index != second_index:
                diff_table[first_index, second_index] = legendre_at[first_index] / (
                    legendre_at[second_index] * (gll_nodes[first_index] - gll_nodes[second_index])
                )
    diff_table[0, 0] = -degree * (degree + 1) / 4.0
    diff_table[degree, degree] = degree * (degree + 1) / 4.0
    return diff_table


def round_up(count, unit):
    return -(-count // unit) * unit


def dot(left, right, dims=((1,), (0,)), precision=None):
    return lax.dot_general(
        left, right, (dims, ((), ())), precision=precision, preferred_element_type=F32
    )


def split(value):
    high = value.astype(BF16)
    return high, (value - high.astype(F32)).astype(BF16)


def split3(value):
    high = value.astype(BF16)
    rest = value - high.astype(F32)
    mid = rest.astype(BF16)
    return high, mid, (rest - mid.astype(F32)).astype(BF16)


def stacked(value):
    high, low = split(value)
    return jnp.concatenate([high, low, high], 0)


def abreast(value):
    high, low = split(value)
    return jnp.concatenate([high, high, low], 1)


def even(index):
    return lax.rem(index, 2) == 0


def diff_parts():
    table = derivative_table(N1).astype(np.float32)
    high = table.astype(jnp.bfloat16).astype(np.float32)
    low = (table - high).astype(jnp.bfloat16).astype(np.float32)
    row, column = ramps(N1, N1)
    place = row * N1 + column
    found = []
    for part in (high, low):
        value = jnp.zeros((N1, N1), F32)
        for k, entry in enumerate(part.reshape(-1)):
            if entry:
                value = jnp.where(place == k, float(entry), value)
        found.append(value.astype(BF16))
    return found


def operator_factors(blocks):
    def kron(part, count, inner, turned):
        row, column = ramps(count, N1)
        quotient, rest = over(row, N1)
        pick = mask((rest if inner else quotient) == column)
        value = dot(pick, part, ((1,), (1 if turned else 0,))).astype(BF16)
        row, column = ramps(N1, count)
        value = dot(value, mask(over(column, N1)[1 if inner else 0] == row))
        row, column = ramps(count, count)
        row, column = over(row, N1), over(column, N1)
        same = row[0] == column[0] if inner else row[1] == column[1]
        return jnp.where(same, value, 0.0).astype(BF16)

    parts = diff_parts()
    box = N1 * N1
    high, low = [
        jnp.concatenate([kron(part, box, False, False), kron(part, box, True, False)], 0) for part in parts
    ]
    grad = jnp.concatenate([high, high, low], 1)
    high, low = [
        jnp.concatenate([kron(part, box, False, True), kron(part, box, True, True)], 1) for part in parts
    ]
    back = jnp.concatenate([high, high, low], 1)
    high, low = [kron(part, blocks * N1, True, True) for part in parts]
    third = jnp.concatenate([high, low, high], 0)
    high, low = [kron(part, blocks * N1, True, False) for part in parts]
    return grad, third, back, jnp.concatenate([high, low, high], 0)


def local_kernel(*refs):
    count = 6
    sources, outs, scratch = refs[:count], refs[count : count + 6], refs[count + 6 :]
    lp_ref, near_ref, far_ref, mf_ref, ef_ref, es_ref = outs
    p_ref, gd_ref, go_ref, sems = scratch
    targets = (p_ref, gd_ref, go_ref, mf_ref, ef_ref, es_ref)
    copies = [
        pltpu.make_async_copy(source, target, sems.at[k])
        for k, (source, target) in enumerate(zip(sources, targets))
    ]
    for copy in copies:
        copy.start()
    layers, rows, width = p_ref.shape
    grad, third_grad, back, third_back = operator_factors(width // N1)
    copies[0].wait()
    first_blocks = layers // N1
    box = N1 * rows
    modes = mf_ref.shape[0]
    p_all = p_ref[...].reshape(layers * rows, width)
    third = dot(abreast(p_all), third_grad)
    grads = [
        dot(grad, stacked(p_all[a * box : (a + 1) * box])) for a in range(first_blocks)
    ]
    for k in (1, 2):
        copies[k].wait()
    for a in range(first_blocks):
        here = slice(a * box, (a + 1) * box)
        one, two, three = grads[a][:box], grads[a][box:], third[here]
        g = [
            gd_ref[k, a * N1 : (a + 1) * N1].reshape(box, width) for k in range(3)
        ] + [go_ref[k, a * N1 : (a + 1) * N1].reshape(box, width) for k in range(3)]
        flux_one = g[0] * one + g[3] * two + g[4] * three
        flux_two = g[3] * one + g[1] * two + g[5] * three
        flux_three = g[4] * one + g[5] * two + g[2] * three
        lp_ref[here, :] = dot(
            back, stacked(jnp.concatenate([flux_one, flux_two], 0))
        ) + dot(abreast(flux_three), third_back)
    for k in (3, 4, 5):
        copies[k].wait()
    layer = lambda l: slice(l * rows, (l + 1) * rows)
    body = (modes - 1) * rows
    up_layers = [
        (0, rows, lp_ref[layer(layers - modes), :]),
        (rows, 2 * rows, lp_ref[layer(layers - modes + 1), :] + lp_ref[layer(layers - modes + 2), :]),
        (2 * rows, body, lp_ref[(layers - modes + 3) * rows :, :]),
    ]
    down_layers = [
        (0, body - 2 * rows, lp_ref[: (modes - 3) * rows, :]),
        (body - 2 * rows, body - rows, lp_ref[layer(modes - 3), :] + lp_ref[layer(modes - 2), :]),
        (body - rows, body, lp_ref[layer(modes - 1), :]),
    ]
    forward = even(lax.axis_index("stream"))

    def fill(ref, parts, a):
        for begin, end, value in parts:
            ref[begin:end, :] = value
        ref[body:, :] = jnp.zeros((rows, width), F32)
        ref[body:, :modes] = mf_ref[:rows, a, :]
        ref[body : body + modes - rows, 16 : 16 + modes] = mf_ref[rows:, a, :]
        ref[body : body + 1, 32 : 32 + modes] = ef_ref[a : a + 1, :]

    @pl.when(forward)
    def _():
        fill(near_ref, up_layers, first_blocks - 1)
        fill(far_ref, down_layers, 0)

    @pl.when(jnp.logical_not(forward))
    def _():
        fill(near_ref, down_layers, 0)
        fill(far_ref, up_layers, first_blocks - 1)


def from_sides(near, far, axis):
    index = lax.axis_index(axis)
    is_even = even(index)
    before = jnp.where(is_even, far, near)
    after = jnp.where(is_even, near, far)
    before = jnp.where(index == 0, 0.0, before)
    after = jnp.where(index == lax.axis_size(axis) - 1, 0.0, after)
    return before, after


def lane_masks(width):
    lane = lax.broadcasted_iota(jnp.int32, (1, width), 1)
    node = over(lane, N1)[1]
    return lane, node, (node == 0) & (lane > 0)


def pack(upper_ref, lower_ref, spare):
    width = spare.shape[1]
    lane, node, free = lane_masks(width)
    final = (node == N1 - 1) & (lane < width - 1)
    upper = lax.broadcasted_iota(jnp.int32, (N1, 1), 0) < N1 // 2
    hidden = [jnp.where(lane == N1, pltpu.roll(spare, N1, 1), 0.0)]
    hidden += [pltpu.roll(spare, N1 - j, 1) for j in range(1, N1)]
    hidden[N1 - 1] = hidden[N1 - 1] + spare
    last = jnp.zeros_like(spare)
    for j in range(1, N1):
        last = jnp.where(lane == N1 * j, pltpu.roll(spare, N1 + (N1 - 1) * j, 1), last)
    hidden.append(last)
    for ref, mine in ((upper_ref, upper), (lower_ref, jnp.logical_not(upper))):
        value = ref[...]
        value = value + jnp.where(final, pltpu.roll(value, width - 1, 1), 0.0)
        for j in range(ref.shape[0] // N1):
            here = slice(j * N1, (j + 1) * N1)
            ref[here, :] = jnp.where(free & mine, hidden[min(j, N1)], jnp.where(free, 0.0, value[here]))


def unpack_spare(upper_rows, lower_rows):
    width = upper_rows.shape[1]
    lane, node, _ = lane_masks(width)
    upper = lax.broadcasted_iota(jnp.int32, (N1, 1), 0) < N1 // 2
    tiles = []
    for j in range(N1 + 1):
        here = slice(j * N1, (j + 1) * N1)
        tiles.append(jnp.where(upper, upper_rows[here], lower_rows[here]))
    spare = jnp.zeros((N1, width), F32)
    for j in range(N1):
        spare = jnp.where((node == j) & (lane < width - N1), pltpu.roll(tiles[j], width - N1 + j, 1), spare)
    for j in range(1, N1):
        spare = jnp.where(
            lane == width - N1 + j, pltpu.roll(tiles[N1], width - N1 - (N1 - 1) * j, 1), spare
        )
    return spare


def unpack(upper_rows, lower_rows, out_upper_ref, out_lower_ref):
    width = upper_rows.shape[1]
    free = lane_masks(width)[2]
    spare = unpack_spare(upper_rows, lower_rows)
    inner = upper_rows.shape[0] // 2
    padded = out_upper_ref.shape[0] // 2
    for ref, packed, start in ((out_upper_ref, upper_rows, 0), (out_lower_ref, lower_rows, N1 // 2)):
        value = jnp.where(free, 0.0, packed)
        for slot in range(2):
            base, row = slot * padded, start + 2 * slot
            ref[base : base + 1, :] = spare[row : row + 1]
            ref[base + 1 : base + 1 + inner, :] = value[slot * inner : (slot + 1) * inner]
            ref[base + 1 + inner : base + 2 + inner, :] = spare[row + 1 : row + 2]
            ref[base + 2 + inner : base + padded, :] = jnp.zeros((padded - inner - 2, width), F32)


def rows_kernel(lp_ref, near_ref, far_ref, built_ref, out_far_ref, out_near_ref):
    rows = N1
    layers = lp_ref.shape[0] // rows
    count = N1 + 1
    inner = out_near_ref.shape[0] // 2
    found = {}
    for k in (0, 1, rows - 2, rows - 1):
        before, after = from_sides(
            near_ref[pl.ds(k, count, stride=rows), :], far_ref[pl.ds(k, count, stride=rows), :], "stream"
        )
        found[k] = (before, lp_ref[pl.ds(k, layers, stride=rows), :], after)
    up = even(lax.axis_index("cross"))
    spare = []
    for ref, high in ((out_near_ref, up), (out_far_ref, jnp.logical_not(up))):
        for slot in range(2):
            base = slot * inner
            before, own, after = [
                jnp.where(high, one, two) for one, two in zip(found[rows - 2 + slot], found[slot])
            ]
            spare += [before[:1], after[count - 1 :]]
            ref[base : base + count - 2, :] = before[1 : count - 1]
            base += count - 2
            for l in range(0, layers, N1):
                previous = before[count - 1 :] if l == 0 else own[l - 1 : l]
                ref[base : base + 1, :] = previous + own[l : l + 1]
                ref[base + 1 : base + N1 - 1, :] = own[l + 1 : l + N1 - 1]
                base += N1 - 1
            ref[base : base + 1, :] = own[layers - 1 :] + after[:1]
            ref[base + 1 : base + count - 1, :] = after[1 : count - 1]
    pack(out_near_ref, out_far_ref, jnp.concatenate(spare, 0))


def spread_columns(parts, lay, pick):
    table = dot(parts, lay, ((0,), (0,)))
    return dot(pick, jnp.concatenate(split3(table), 0))


def spread_rows(parts, pick, rows):
    pad = parts.shape[0] // 3
    table = sum(dot(parts[k * pad : (k + 1) * pad], pick) for k in range(3))
    return dot(rows, jnp.concatenate(split3(table), 0))


def halves_by_lane(value, low):
    high = value.astype(BF16).astype(F32)
    return jnp.where(low, value - high, high).astype(BF16)


def low_lanes(kin, rim):
    lane = lax.broadcasted_iota(jnp.int32, (1, 3 * (kin + rim)), 1)
    return ((lane >= 2 * kin) & (lane < 3 * kin)) | (lane >= 3 * kin + 2 * rim)


def low_back_lanes(pairs):
    return lax.broadcasted_iota(jnp.int32, (1, 3 * pairs), 1) >= 2 * pairs


def ramps(*dims):
    return [lax.broadcasted_iota(jnp.int32, dims, axis) for axis in range(2)]


def over(value, count):
    if count & (count - 1) == 0:
        return lax.shift_right_logical(value, count.bit_length() - 1), value & (count - 1)
    quotient = ((value.astype(F32) + 0.5) * (1.0 / count)).astype(jnp.int32)
    return quotient, value - quotient * count


def mask(hit):
    return jnp.where(hit, 1.0, 0.0).astype(BF16)


def spread_table(blocks, modes):
    row, column = ramps(modes, blocks * modes)
    return mask(row == over(column, modes)[1])


def gather_table(blocks, modes):
    row, column = ramps(blocks * N1, modes * blocks)
    node, block = over(column, blocks)
    place = row - block * N1
    hit = (place == node - 1) & (node >= 1) & (node <= N1)
    for n, at in ((0, -2), (1, -1), (N1, N1), (N1 + 1, N1 + 1)):
        hit = hit | ((node == n) & (place == at))
    return mask(hit)


def pick_table(pairs, pad, modes, which):
    row, column = ramps(pairs, 3 * pad)
    return mask(over(row, modes)[which] == over(column, pad)[1])


def pick_rows(pairs, pad, modes, which):
    row, column = ramps(pairs, pad)
    return jnp.where(over(row, modes)[which] == column, 1.0, 0.0)


def back_tables(pairs, pad, modes):
    row, column = ramps(pad, 3 * pairs)
    found = over(over(column, pairs)[1], modes)
    return mask(found[0] == row), mask(found[1] == row)


def box_rows(count, pad):
    row, column = ramps(count, 3 * pad)
    first, second = over(row, N1)
    column = over(column, pad)[1]
    return mask(first + 1 == column), mask(second + 1 == column)


def face_rows(pad):
    row, column = ramps(2 * N1, 3 * pad)
    face, first = over(row, N1)
    column = over(column, pad)[1]
    return mask(first + 1 == column), mask(jnp.where(face == 0, 1, N1) == column)


def inner_table(blocks, modes):
    row, column = ramps(modes * blocks, blocks * N1)
    node, block = over(row, blocks)
    place = column - block * N1
    hit = (place == node - 1) & (node >= 1) & (node <= N1)
    return mask(hit | ((node == 1) & (place == -1)) | ((node == N1) & (place == N1)))


def lay_tables(pad, kin, rim):
    layers = kin // N1
    row, column = ramps(3 * pad, 3 * (kin + rim))
    row = over(row, pad)[1]
    own = column < 3 * kin
    l_own, y = over(over(column, kin)[1], N1)
    kind, l_rim = over(over(jnp.maximum(column - 3 * kin, 0), rim)[1], rim // 4)
    node = jnp.where(l_own == 0, 0, jnp.where(l_own == layers - 1, N1 + 1, jnp.clip(l_own - 1, 1, N1)))
    node = jnp.where(own, node, l_rim)
    second = jnp.where(own, y + 1, jnp.where(kind < 2, kind, N1 - 2 + kind))
    inside = own | (l_rim < N1 + 2)
    return mask(inside & (row == node)), mask(inside & (row == second))


def third_parts(mt_ref, spread):
    rows, modes = mt_ref.shape
    blocks = rows // modes
    row, column = ramps(rows, rows)
    own = over(row, blocks)[1] == over(column, modes)[0]
    return [jnp.where(own, dot(part, spread), 0.0).astype(BF16) for part in split3(mt_ref[...])]


def pad_modes(pad_ref, mf_ref, ms_ref):
    modes = ms_ref.shape[0]
    first_blocks = pad_ref.shape[0] - 1
    pad_ref[...] = jnp.zeros_like(pad_ref)
    for a in range(first_blocks):
        pad_ref[a, :modes, :modes] = mf_ref[:, a, :]
    pad_ref[first_blocks, :modes, :modes] = ms_ref[:, 0, :]


def modes_kernel(
    mt_ref, e3_ref, mf_ref, ef_ref, ms_ref, es_ref,
    w_ref, e3_row_ref, own_columns_ref, own_rim_ref, second_columns_ref, pad_ref, eigen_ref, back_ref,
):
    blocks, modes = e3_ref.shape
    spread = spread_table(blocks, modes)
    gather = gather_table(blocks, modes)
    table = sum(dot(gather, part) for part in third_parts(mt_ref, spread))
    high, low = split(table)
    w_ref[...] = jnp.concatenate([high, low, high], 0)
    row, column = ramps(blocks, blocks * modes)
    e3_wide = sum(dot(part, spread) for part in split3(e3_ref[...]))
    e3_row_ref[...] = jnp.sum(
        jnp.where(row == over(column, modes)[0], e3_wide, 0.0), 0, keepdims=True
    )
    first_blocks, pairs, kin = own_columns_ref.shape
    kin, rim, pad = kin // 3, own_rim_ref.shape[2] // 3, pad_ref.shape[1]
    pad_modes(pad_ref, mf_ref, ms_ref)
    eigen_ref[...] = jnp.zeros_like(eigen_ref)
    eigen_ref[:first_blocks, :modes] = ef_ref[...]
    eigen_ref[first_blocks : first_blocks + 1, :modes] = es_ref[...]
    lay_m, lay_n = lay_tables(pad, kin, rim)
    low = low_lanes(kin, rim)
    second = jnp.concatenate(split3(pad_ref[first_blocks]), 0)
    second_columns = spread_columns(second, lay_n, pick_table(pairs, pad, modes, 1))
    second_columns_ref[...] = second_columns
    pick = pick_table(pairs, pad, modes, 0)
    for a in range(first_blocks):
        first = jnp.concatenate(split3(pad_ref[a]), 0)
        columns = halves_by_lane(spread_columns(first, lay_m, pick) * second_columns, low)
        own_columns_ref[a] = columns[:, : 3 * kin]
        own_rim_ref[a] = columns[:, 3 * kin :]
    box = back_ref.shape[1]
    back_m, back_n = back_tables(pairs, pad, modes)
    rows_m, rows_n = box_rows(box, pad)
    second_rows = spread_rows(second, back_n, rows_n)
    for a in range(first_blocks):
        first = jnp.concatenate(split3(pad_ref[a]), 0)
        back_ref[a] = halves_by_lane(spread_rows(first, back_m, rows_m) * second_rows, low_back_lanes(pairs))


def columns_kernel(
    lp_ref, near_ref, far_ref, w_ref, e3_row_ref, own_columns_ref, second_columns_ref, pad_ref,
    eigen_ref, mt_ref, v_ref, side_rim_ref, rec_ref, face_ref, wbh_ref, wbl_ref,
):
    rows = N1
    halo = (N1 + 2) * rows
    first_blocks, pairs, kin = own_columns_ref.shape
    kin, rim, pad, modes = kin // 3, side_rim_ref.shape[2] // 3, pad_ref.shape[1], N1 + 2
    box = N1 * rows
    near, far = near_ref[...], far_ref[...]
    before, after = from_sides(near, far, "stream")
    odd = jnp.logical_not(even(lax.axis_index("stream")))
    body = halo - rows
    zero = jnp.zeros((rows, lp_ref.shape[1]), F32)
    stack = jnp.concatenate(
        [before[:rows], zero, before[rows:body], lp_ref[...], after[: body - rows], zero, after[body - rows : body]], 0
    )
    u = dot(abreast(stack), w_ref[...])
    edge_near, edge_far = near[body : body + 1, 32 : 32 + pad], far[body : body + 1, 32 : 32 + pad]
    low = low_lanes(kin, rim)
    lay_m, _ = lay_tables(pad, kin, rim)
    pick_p3 = pick_table(pairs, pad, modes, 0)
    pick_p, pick_q = pick_rows(pairs, pad, modes, 0), pick_rows(pairs, pad, modes, 1)
    back_m, back_n = back_tables(pairs, pad, modes)
    face_m, face_n = face_rows(pad)
    own_eigen = eigen_ref[...]
    firsts = [jnp.concatenate([side[body:, :pad], side[body:, 16 : 16 + pad]], 0) for side in (before, after)]
    firsts = [firsts[0]] + [pad_ref[a] for a in range(first_blocks)] + [firsts[1]]
    eigens = [jnp.where(odd, edge_near, edge_far)] + [own_eigen[a : a + 1] for a in range(first_blocks)]
    eigens += [jnp.where(odd, edge_far, edge_near)]
    second = jnp.concatenate(split3(pad_ref[first_blocks]), 0)
    second_faces = spread_rows(second, back_n, face_n)
    second_sum = jnp.sum(pick_q * own_eigen[first_blocks : first_blocks + 1], 1, keepdims=True)
    for a, (first, eigen) in enumerate(zip(firsts, eigens)):
        first = jnp.concatenate(split3(first), 0)
        if a in (0, first_blocks + 1):
            columns = halves_by_lane(
                spread_columns(first, lay_m, pick_p3) * second_columns_ref[...], low
            )
            side_rim_ref[min(a, 1)] = columns[:, 3 * kin :]
            columns = columns[:, : 3 * kin]
        else:
            columns = own_columns_ref[a - 1]
        begin = a * box
        v_ref[a] = dot(columns, stacked(u[begin : begin + kin]))
        high, low_half = split((spread_rows(first, back_m, face_m) * second_faces)[:, :pairs])
        face_ref[a] = jnp.concatenate([high, low_half], 0)
        total = jnp.sum(pick_p * eigen, 1, keepdims=True) + second_sum
        rec_ref[a] = 1.0 / (total + e3_row_ref[...])
    blocks = mt_ref.shape[0] // modes
    inner = inner_table(blocks, modes)
    table = sum(
        dot(part, inner, ((0,), (0,))) for part in third_parts(mt_ref, spread_table(blocks, modes))
    )
    wbh_ref[...], wbl_ref[...] = split(table)


def spectral_columns(near, far, w_ref, v_ref, own_rim_ref, side_rim_ref, rec_ref):
    columns = v_ref.shape[0]
    inner = near.shape[0] // 2
    half = N1 // 2
    free = lane_masks(near.shape[1])[2]
    spare = unpack_spare(near, far)
    before, after = from_sides(jnp.where(free, 0.0, near), jnp.where(free, 0.0, far), "cross")
    ends = jnp.concatenate(from_sides(spare[:half], spare[half:], "cross"), 0)
    u = dot(abreast(jnp.concatenate([before, after, ends], 0)), w_ref[...])
    found = []
    for a in range(columns):
        rim = []
        for k in range(4):
            base, end = k * inner, 4 * inner + 2 * k
            start = a * (N1 - 1) - 1
            if a == 0:
                rim += [u[end : end + 1], u[base : base + 15]]
            elif a == columns - 1:
                count = inner - start
                rim += [u[base + start : base + inner], u[end + 1 : end + 2]]
                rim += [jnp.zeros((15 - count, u.shape[1]), F32)]
            else:
                rim += [u[base + start : base + start + 16]]
        rim = jnp.concatenate(rim, 0)
        table = side_rim_ref[min(a, 1)] if a in (0, columns - 1) else own_rim_ref[a - 1]
        found.append((v_ref[a] + dot(table, stacked(rim))) * rec_ref[a])
    return found


def third_back(parts, wbh_ref, wbl_ref):
    high, low = split(jnp.concatenate(parts, 0))
    count, width = high.shape[0], wbh_ref.shape[1]
    both = dot(jnp.concatenate([high, low], 0), jnp.concatenate([wbh_ref[...], wbl_ref[...]], 1))
    return both[:count, :width] + both[count:, :width] + both[:count, width:]


def faces_kernel(
    far_ref, near_ref, w_ref, v_ref, own_rim_ref, side_rim_ref, rec_ref, wbh_ref, wbl_ref, face_ref,
    out_far_ref, out_near_ref, spectral_ref,
):
    rows = N1
    found = spectral_columns(near_ref[...], far_ref[...], w_ref, v_ref, own_rim_ref, side_rim_ref, rec_ref)
    columns = len(found)
    for a in range(columns):
        spectral_ref[a] = found[a]
    parts = []
    for a in range(columns):
        high, low = split(found[a])
        both = dot(face_ref[a], high)
        parts.append(both[: 2 * N1] + both[2 * N1 :] + dot(face_ref[a, : 2 * N1], low))
    solved = third_back(parts, wbh_ref, wbl_ref)
    row = lax.broadcasted_iota(jnp.int32, (rows, 1), 0)
    up = even(lax.axis_index("cross"))
    for a in range(1, columns - 1):
        sums = []
        for face in range(2):
            base = 16 * a + rows * face
            previous = base - 16 + rows - 1
            after = base + 16
            sums.append(
                solved[base : base + rows]
                + jnp.where(row == 0, solved[previous : previous + 1], 0.0)
                + jnp.where(row == rows - 1, solved[after : after + 1], 0.0)
            )
        here = slice((a - 1) * rows, a * rows)
        out_near_ref[here, :] = jnp.where(up, sums[1], sums[0])
        out_far_ref[here, :] = jnp.where(up, sums[0], sums[1])


def assemble_operator(lp_ref, s_near_ref, s_far_ref, c_near_ref, c_far_ref, out_ref, acc_ref):
    rows = N1
    total_rows, width = lp_ref.shape
    padded = c_near_ref.shape[0] // 2
    body = (N1 + 1) * rows
    box = N1 * rows
    before, after = from_sides(s_near_ref[...], s_far_ref[...], "stream")
    left, right = from_sides(c_near_ref[...], c_far_ref[...], "cross")
    acc_ref[...] = lp_ref[...]
    for base in range(0, total_rows, box):
        last = base + box
        previous = before[body - rows : body] if base == 0 else lp_ref[base - rows : base, :]
        following = after[:rows] if last == total_rows else lp_ref[last : last + rows, :]
        acc_ref[base : base + rows, :] = lp_ref[base : base + rows, :] + previous
        acc_ref[last - rows : last, :] = lp_ref[last - rows : last, :] + following
        node = (N1 - 1) * (base // box + 1) + 1
        low, high = pl.ds(base, N1, stride=rows), pl.ds(base + rows - 1, N1, stride=rows)
        acc_ref[low, :] = acc_ref[low, :] + left[padded + node : padded + node + N1]
        acc_ref[high, :] = acc_ref[high, :] + right[node : node + N1]
    lane = lax.broadcasted_iota(jnp.int32, (1, width), 1)
    first = (lax.rem(lane, N1) == 0) & (lane > 0)
    final = (lax.rem(lane, N1) == N1 - 1) & (lane < width - 1)
    value = acc_ref[...]
    value = (
        value
        + jnp.where(first, pltpu.roll(value, 1, 1), 0.0)
        + jnp.where(final, pltpu.roll(value, width - 1, 1), 0.0)
    )
    out_ref[...] = value.reshape(out_ref.shape)


def solve_kernel(
    lp_ref, s_near_ref, s_far_ref, c_far_ref, c_near_ref, spectral_ref, wbh_ref, wbl_ref, pad_ref, back_ref,
    operator_ref, r_ref, out_ref, acc_ref, all_near_ref, all_far_ref, sem,
):
    unpack(c_near_ref[...], c_far_ref[...], all_near_ref, all_far_ref)
    assemble_operator(lp_ref, s_near_ref, s_far_ref, all_near_ref, all_far_ref, out_ref, acc_ref)
    copy = pltpu.make_async_copy(out_ref, operator_ref, sem)
    copy.start()
    rows = N1
    box = N1 * rows
    found = [spectral_ref[a] for a in range(spectral_ref.shape[0])]
    columns = len(found)
    pad, pairs = pad_ref.shape[1], spectral_ref.shape[1]
    back_m, back_n = back_tables(pairs, pad, N1 + 2)
    rows_m, rows_n = box_rows(box, pad)
    low = low_back_lanes(pairs)
    body = (N1 + 1) * rows
    sides = from_sides(s_near_ref[...], s_far_ref[...], "stream")
    sides = [jnp.concatenate([side[body:, :pad], side[body:, 16 : 16 + pad]], 0) for side in sides]
    second = jnp.concatenate(split3(pad_ref[columns - 2]), 0)
    parts = [None] * columns
    for a, first, kept in ((0, sides[0], slice(box - 16, box)), (columns - 1, sides[1], slice(0, 16))):
        first = jnp.concatenate(split3(first), 0)
        table = spread_rows(first, back_m, rows_m[kept]) * spread_rows(second, back_n, rows_n[kept])
        parts[a] = dot(halves_by_lane(table, low), stacked(found[a]))
    for a in range(1, columns - 1):
        parts[a] = dot(back_ref[a - 1], stacked(found[a]))
    parts[0] = parts[0][16 - rows :]
    parts[-1] = parts[-1][:rows]
    solved = third_back(parts, wbh_ref, wbl_ref)
    for a in range(columns - 2):
        base = rows + a * box
        top, bottom = solved[base : base + rows], solved[base + box - rows : base + box]
        r_ref[a * box : a * box + rows, :] = top + solved[base - rows : base]
        r_ref[a * box + rows : (a + 1) * box - rows, :] = solved[base + rows : base + box - rows]
        r_ref[(a + 1) * box - rows : (a + 1) * box, :] = bottom + solved[base + box : base + box + rows]
    copy.wait()


def pass_kernel(*refs):
    count = len(refs) // 2
    for source, target in zip(refs[:count], refs[count:]):
        target[...] = source[...]


def add_kernel(r_ref, ahead_ref, far_ref, near_ref, out_ref, acc_ref, sem):
    rows = N1
    near = jnp.where(lax.axis_index("cross") < 2, ahead_ref[...], near_ref[...])
    before, after = from_sides(near, far_ref[...], "cross")
    row = lax.broadcasted_iota(jnp.int32, (rows, 1), 0)
    for l in range(acc_ref.shape[0]):
        value = r_ref[l * rows : (l + 1) * rows, :] + jnp.where(row == 0, before[l : l + 1], 0.0)
        acc_ref[l] = value + jnp.where(row == rows - 1, after[l : l + 1], 0.0)
    copy = pltpu.make_async_copy(acc_ref, out_ref, sem)
    copy.start()
    copy.wait()


def shape(*dims, dtype=F32):
    return pltpu.VMEM(dims, dtype)


def call(kernel, name, out, *args, scratch=(), out_specs=None, flops=1000000, place=pltpu.VMEM):
    single = not isinstance(out, list)
    args = [pltpu.with_memory_space_constraint(x, place) for x in args]
    return pl.pallas_call(
        kernel,
        out_shape=out,
        in_specs=[pl.BlockSpec(memory_space=place)] * len(args),
        out_specs=out_specs if out_specs is not None else (VMEM if single else [VMEM] * len(out)),
        scratch_shapes=list(scratch),
        compiler_params=pltpu.CompilerParams(vmem_limit_bytes=VMEM_LIMIT),
        cost_estimate=pl.CostEstimate(flops=flops, bytes_accessed=flops, transcendentals=0),
        name=name,
    )(*args)


def swaps(axis):
    count = lax.axis_size(axis)
    near = [(i, i ^ 1) for i in range(count)]
    far = [(i, (i - 1) % count if i % 2 == 0 else (i + 1) % count) for i in range(count)]
    return near, far


def swap_stream(near, far):
    first, second = swaps("stream")
    near = lax.ppermute(near, "stream", first)
    far = lax.ppermute(far, "stream", second)
    return near, far


def cross_pairs(near, ahead=None):
    count, streams = lax.axis_size("cross"), lax.axis_size("stream")
    pairs = []
    for s in range(streams):
        for i in range(count):
            j = i ^ 1 if near else i - 1 + 2 * (i % 2)
            idle = not 0 <= j < count or (ahead is not None and (i < 2) != ahead)
            pairs.append((s * count + i, (s ^ 1) * count + i if idle else s * count + j))
    return pairs


def swap_cross(near, far):
    axes = ("stream", "cross")
    return lax.ppermute(near, axes, cross_pairs(True)), lax.ppermute(far, axes, cross_pairs(False))


def swap_cross_ahead(near, far):
    axes = ("stream", "cross")
    first = lax.ppermute(near, axes, cross_pairs(True, True))
    far, near = call(pass_kernel, "pass_on", [shape(*far.shape), shape(*near.shape)], far, near)
    return first, lax.ppermute(far, axes, cross_pairs(False)), lax.ppermute(near, axes, cross_pairs(True, False))


def shards(
    pressure, geo_diag, geo_off, modes_first, modes_second, modes_third, eigen_first, eigen_second,
    eigen_third,
):
    layers, rows, width = pressure.shape
    modes = modes_first.shape[1]
    if layers < 3 * N1 or rows != N1 or modes != N1 + 2 or lax.axis_size("stream") % 2 or lax.axis_size("cross") % 2:
        raise ValueError("unsupported sizes")
    first_blocks, third_blocks = layers // N1, width // N1
    columns = first_blocks + 2
    halo = modes * rows
    box = N1 * rows
    nodes = (first_blocks + 1) * (N1 - 1) + modes
    padded = round_up(nodes, 8)
    wide = third_blocks * modes

    pairs, pad = round_up(modes * modes, 16), round_up(modes, 16)

    mf = jnp.transpose(modes_first, (1, 0, 2))
    ms = jnp.transpose(modes_second, (1, 0, 2))
    mt = jnp.transpose(modes_third, (1, 0, 2)).reshape(modes * third_blocks, modes)

    inputs = [pressure, geo_diag, geo_off, mf, eigen_first, eigen_second]
    lp, s_near, s_far, mf, ef, es = call(
        local_kernel, "local_product",
        [
            shape(layers * rows, width), shape(halo, width), shape(halo, width),
            shape(modes, first_blocks, modes), shape(first_blocks, modes), shape(1, modes),
        ],
        *inputs, place=pltpu.HBM,
        scratch=[pltpu.VMEM(x.shape, x.dtype) for x in inputs[:3]] + [pltpu.SemaphoreType.DMA((len(inputs),))],
    )
    s_near, s_far = swap_stream(s_near, s_far)
    kin, rim_width = 3 * (N1 + 4) * rows, 3 * 64
    w, e3_row, own_columns, own_rim, second_columns, padded_modes, eigen, own_back = call(
        modes_kernel, "mode_tables",
        [
            shape(3 * width, wide, dtype=BF16), shape(1, wide),
            shape(first_blocks, pairs, kin, dtype=BF16), shape(first_blocks, pairs, rim_width, dtype=BF16),
            shape(pairs, kin + rim_width), shape(first_blocks + 1, pad, pad), shape(first_blocks + 1, pad),
            shape(first_blocks, box, 3 * pairs, dtype=BF16),
        ],
        mt, eigen_third, mf, ef, ms, es,
    )
    c_far, c_near = call(
        rows_kernel, "rows_to_send",
        [shape(2 * nodes - 4, width), shape(2 * nodes - 4, width)],
        lp, s_near, s_far, e3_row,
    )
    c_near, c_far = swap_cross(c_near, c_far)
    v, side_rim, rec, face, wbh, wbl = call(
        columns_kernel, "own_part",
        [
            shape(columns, pairs, wide), shape(2, pairs, rim_width, dtype=BF16), shape(columns, pairs, wide),
            shape(columns, 4 * N1, pairs, dtype=BF16), shape(wide, width, dtype=BF16), shape(wide, width, dtype=BF16),
        ],
        lp, s_near, s_far, w, e3_row, own_columns, second_columns, padded_modes, eigen, mt,
    )
    f_far, f_near, spectral = call(
        faces_kernel, "faces",
        [
            shape(layers, width), shape(layers, width), shape(columns, pairs, wide),
        ],
        c_far, c_near, w, v, own_rim, side_rim, rec, wbh, wbl, face,
    )
    f_ahead, f_far, f_near = swap_cross_ahead(f_near, f_far)
    result = pltpu.HBM(pressure.shape, F32)
    in_hbm = pl.BlockSpec(memory_space=pltpu.HBM)
    operator_out, restricted = call(
        solve_kernel, "solve", [result, shape(layers * rows, width)],
        lp, s_near, s_far, c_far, c_near, spectral, wbh, wbl, padded_modes, own_back, out_specs=[in_hbm, VMEM],
        scratch=[
            pltpu.VMEM(pressure.shape, F32), pltpu.VMEM((layers * rows, width), F32),
            pltpu.VMEM((2 * padded, width), F32), pltpu.VMEM((2 * padded, width), F32), pltpu.SemaphoreType.DMA,
        ],
    )
    preconditioned = call(
        add_kernel, "preconditioned", result, restricted, f_ahead, f_far, f_near, out_specs=in_hbm,
        scratch=[pltpu.VMEM(pressure.shape, F32), pltpu.SemaphoreType.DMA],
    )
    return (operator_out, preconditioned)


def solution(mesh):
    in_specs = (
        P("stream", "cross", None),
        P(None, "stream", "cross", None),
        P(None, "stream", "cross", None),
        P("stream", None, None),
        P("cross", None, None),
        P(),
        P("stream", None),
        P("cross", None),
        P(),
    )
    out_specs = (P("stream", "cross", None), P("stream", "cross", None))
    return jax.shard_map(shards, mesh=mesh, in_specs=in_specs, out_specs=out_specs, check_vma=False)
```

```python
import functools

import jax
import jax.numpy as jnp
import numpy as np
from jax import lax
from jax.experimental import pallas as pl
from jax.experimental.pallas import tpu as pltpu
from jax.sharding import PartitionSpec as P

N1 = 8
F32 = jnp.float32
BF16 = jnp.bfloat16
HIGHEST = lax.Precision.HIGHEST
VMEM_LIMIT = 16 * 2**20
VMEM = pl.BlockSpec(memory_space=pltpu.VMEM)


def legendre_values(nodes, degree):
    table = np.zeros((nodes.shape[0], degree + 1))
    table[:, 0] = 1.0
    table[:, 1] = nodes
    for order in range(2, degree + 1):
        table[:, order] = (
            (2 * order - 1) * nodes * table[:, order - 1] - (order - 1) * table[:, order - 2]
        ) / order
    return table


def derivative_table(points):
    degree = points - 1
    nodes = np.cos(np.pi * np.arange(points) / degree)
    for sweep in range(100):
        table = legendre_values(nodes, degree)
        nodes = nodes - (nodes * table[:, degree] - table[:, degree - 1]) / (
            points * table[:, degree]
        )
    gll_nodes = nodes[::-1]
    legendre_at = legendre_values(gll_nodes, degree)[:, degree]
    diff_table = np.zeros((points, points))
    for first_index in range(points):
        for second_index in range(points):
            if first_index != second_index:
                diff_table[first_index, second_index] = legendre_at[first_index] / (
                    legendre_at[second_index] * (gll_nodes[first_index] - gll_nodes[second_index])
                )
    diff_table[0, 0] = -degree * (degree + 1) / 4.0
    diff_table[degree, degree] = degree * (degree + 1) / 4.0
    return diff_table


def round_up(count, unit):
    return -(-count // unit) * unit


def dot(left, right, dims=((1,), (0,)), precision=None):
    return lax.dot_general(
        left, right, (dims, ((), ())), precision=precision, preferred_element_type=F32
    )


def split(value):
    high = value.astype(BF16)
    return high, (value - high.astype(F32)).astype(BF16)


def split3(value):
    high = value.astype(BF16)
    rest = value - high.astype(F32)
    mid = rest.astype(BF16)
    return high, mid, (rest - mid.astype(F32)).astype(BF16)


def stacked(value):
    high, low = split(value)
    return jnp.concatenate([high, low, high], 0)


def abreast(value):
    high, low = split(value)
    return jnp.concatenate([high, high, low], 1)


def even(index):
    return lax.rem(index, 2) == 0


def diff_parts():
    table = derivative_table(N1).astype(np.float32)
    high = table.astype(jnp.bfloat16).astype(np.float32)
    low = (table - high).astype(jnp.bfloat16).astype(np.float32)
    row, column = ramps(N1, N1)
    place = row * N1 + column
    found = []
    for part in (high, low):
        value = jnp.zeros((N1, N1), F32)
        for k, entry in enumerate(part.reshape(-1)):
            if entry:
                value = jnp.where(place == k, float(entry), value)
        found.append(value.astype(BF16))
    return found


def operator_factors(blocks):
    def kron(part, count, inner, turned):
        row, column = ramps(count, N1)
        quotient, rest = over(row, N1)
        pick = mask((rest if inner else quotient) == column)
        value = dot(pick, part, ((1,), (1 if turned else 0,))).astype(BF16)
        row, column = ramps(N1, count)
        value = dot(value, mask(over(column, N1)[1 if inner else 0] == row))
        row, column = ramps(count, count)
        row, column = over(row, N1), over(column, N1)
        same = row[0] == column[0] if inner else row[1] == column[1]
        return jnp.where(same, value, 0.0).astype(BF16)

    parts = diff_parts()
    box = N1 * N1
    high, low = [
        jnp.concatenate([kron(part, box, False, False), kron(part, box, True, False)], 0) for part in parts
    ]
    grad = jnp.concatenate([high, high, low], 1)
    high, low = [
        jnp.concatenate([kron(part, box, False, True), kron(part, box, True, True)], 1) for part in parts
    ]
    back = jnp.concatenate([high, high, low], 1)
    high, low = [kron(part, blocks * N1, True, True) for part in parts]
    third = jnp.concatenate([high, low, high], 0)
    high, low = [kron(part, blocks * N1, True, False) for part in parts]
    return grad, third, back, jnp.concatenate([high, low, high], 0)


def local_kernel(*refs):
    count = 6
    sources, outs, scratch = refs[:count], refs[count : count + 6], refs[count + 6 :]
    lp_ref, near_ref, far_ref, mf_ref, ef_ref, es_ref = outs
    p_ref, gd_ref, go_ref, sems = scratch
    targets = (p_ref, gd_ref, go_ref, mf_ref, ef_ref, es_ref)
    copies = [
        pltpu.make_async_copy(source, target, sems.at[k])
        for k, (source, target) in enumerate(zip(sources, targets))
    ]
    for copy in copies:
        copy.start()
    layers, rows, width = p_ref.shape
    grad, third_grad, back, third_back = operator_factors(width // N1)
    copies[0].wait()
    first_blocks = layers // N1
    box = N1 * rows
    modes = mf_ref.shape[0]
    p_all = p_ref[...].reshape(layers * rows, width)
    third = dot(abreast(p_all), third_grad)
    grads = [
        dot(grad, stacked(p_all[a * box : (a + 1) * box])) for a in range(first_blocks)
    ]
    for k in (1, 2):
        copies[k].wait()
    for a in range(first_blocks):
        here = slice(a * box, (a + 1) * box)
        one, two, three = grads[a][:box], grads[a][box:], third[here]
        g = [
            gd_ref[k, a * N1 : (a + 1) * N1].reshape(box, width) for k in range(3)
        ] + [go_ref[k, a * N1 : (a + 1) * N1].reshape(box, width) for k in range(3)]
        flux_one = g[0] * one + g[3] * two + g[4] * three
        flux_two = g[3] * one + g[1] * two + g[5] * three
        flux_three = g[4] * one + g[5] * two + g[2] * three
        lp_ref[here, :] = dot(
            back, stacked(jnp.concatenate([flux_one, flux_two], 0))
        ) + dot(abreast(flux_three), third_back)
    for k in (3, 4, 5):
        copies[k].wait()
    layer = lambda l: slice(l * rows, (l + 1) * rows)
    body = (modes - 1) * rows
    up_layers = [
        (0, rows, lp_ref[layer(layers - modes), :]),
        (rows, 2 * rows, lp_ref[layer(layers - modes + 1), :] + lp_ref[layer(layers - modes + 2), :]),
        (2 * rows, body, lp_ref[(layers - modes + 3) * rows :, :]),
    ]
    down_layers = [
        (0, body - 2 * rows, lp_ref[: (modes - 3) * rows, :]),
        (body - 2 * rows, body - rows, lp_ref[layer(modes - 3), :] + lp_ref[layer(modes - 2), :]),
        (body - rows, body, lp_ref[layer(modes - 1), :]),
    ]
    forward = even(lax.axis_index("stream"))

    def fill(ref, parts, a):
        for begin, end, value in parts:
            ref[begin:end, :] = value
        ref[body:, :] = jnp.zeros((rows, width), F32)
        ref[body:, :modes] = mf_ref[:rows, a, :]
        ref[body : body + modes - rows, 16 : 16 + modes] = mf_ref[rows:, a, :]
        ref[body : body + 1, 32 : 32 + modes] = ef_ref[a : a + 1, :]

    @pl.when(forward)
    def _():
        fill(near_ref, up_layers, first_blocks - 1)
        fill(far_ref, down_layers, 0)

    @pl.when(jnp.logical_not(forward))
    def _():
        fill(near_ref, down_layers, 0)
        fill(far_ref, up_layers, first_blocks - 1)


def from_sides(near, far, axis):
    index = lax.axis_index(axis)
    is_even = even(index)
    before = jnp.where(is_even, far, near)
    after = jnp.where(is_even, near, far)
    before = jnp.where(index == 0, 0.0, before)
    after = jnp.where(index == lax.axis_size(axis) - 1, 0.0, after)
    return before, after


def lane_masks(width):
    lane = lax.broadcasted_iota(jnp.int32, (1, width), 1)
    node = over(lane, N1)[1]
    return lane, node, (node == 0) & (lane > 0)


def pack(upper_ref, lower_ref, spare):
    width = spare.shape[1]
    lane, node, free = lane_masks(width)
    final = (node == N1 - 1) & (lane < width - 1)
    upper = lax.broadcasted_iota(jnp.int32, (N1, 1), 0) < N1 // 2
    hidden = [jnp.where(lane == N1, pltpu.roll(spare, N1, 1), 0.0)]
    hidden += [pltpu.roll(spare, N1 - j, 1) for j in range(1, N1)]
    hidden[N1 - 1] = hidden[N1 - 1] + spare
    last = jnp.zeros_like(spare)
    for j in range(1, N1):
        last = jnp.where(lane == N1 * j, pltpu.roll(spare, N1 + (N1 - 1) * j, 1), last)
    hidden.append(last)
    for ref, mine in ((upper_ref, upper), (lower_ref, jnp.logical_not(upper))):
        value = ref[...]
        value = value + jnp.where(final, pltpu.roll(value, width - 1, 1), 0.0)
        for j in range(ref.shape[0] // N1):
            here = slice(j * N1, (j + 1) * N1)
            ref[here, :] = jnp.where(free & mine, hidden[min(j, N1)], jnp.where(free, 0.0, value[here]))


def unpack_spare(upper_rows, lower_rows):
    width = upper_rows.shape[1]
    lane, node, _ = lane_masks(width)
    upper = lax.broadcasted_iota(jnp.int32, (N1, 1), 0) < N1 // 2
    tiles = []
    for j in range(N1 + 1):
        here = slice(j * N1, (j + 1) * N1)
        tiles.append(jnp.where(upper, upper_rows[here], lower_rows[here]))
    spare = jnp.zeros((N1, width), F32)
    for j in range(N1):
        spare = jnp.where((node == j) & (lane < width - N1), pltpu.roll(tiles[j], width - N1 + j, 1), spare)
    for j in range(1, N1):
        spare = jnp.where(
            lane == width - N1 + j, pltpu.roll(tiles[N1], width - N1 - (N1 - 1) * j, 1), spare
        )
    return spare


def unpack(upper_rows, lower_rows, out_upper_ref, out_lower_ref):
    width = upper_rows.shape[1]
    free = lane_masks(width)[2]
    spare = unpack_spare(upper_rows, lower_rows)
    inner = upper_rows.shape[0] // 2
    padded = out_upper_ref.shape[0] // 2
    for ref, packed, start in ((out_upper_ref, upper_rows, 0), (out_lower_ref, lower_rows, N1 // 2)):
        value = jnp.where(free, 0.0, packed)
        for slot in range(2):
            base, row = slot * padded, start + 2 * slot
            ref[base : base + 1, :] = spare[row : row + 1]
            ref[base + 1 : base + 1 + inner, :] = value[slot * inner : (slot + 1) * inner]
            ref[base + 1 + inner : base + 2 + inner, :] = spare[row + 1 : row + 2]
            ref[base + 2 + inner : base + padded, :] = jnp.zeros((padded - inner - 2, width), F32)


def rows_kernel(lp_ref, near_ref, far_ref, built_ref, out_far_ref, out_near_ref):
    rows = N1
    layers = lp_ref.shape[0] // rows
    count = N1 + 1
    inner = out_near_ref.shape[0] // 2
    found = {}
    for k in (0, 1, rows - 2, rows - 1):
        before, after = from_sides(
            near_ref[pl.ds(k, count, stride=rows), :], far_ref[pl.ds(k, count, stride=rows), :], "stream"
        )
        found[k] = (before, lp_ref[pl.ds(k, layers, stride=rows), :], after)
    up = even(lax.axis_index("cross"))
    spare = []
    for ref, high in ((out_near_ref, up), (out_far_ref, jnp.logical_not(up))):
        for slot in range(2):
            base = slot * inner
            before, own, after = [
                jnp.where(high, one, two) for one, two in zip(found[rows - 2 + slot], found[slot])
            ]
            spare += [before[:1], after[count - 1 :]]
            ref[base : base + count - 2, :] = before[1 : count - 1]
            base += count - 2
            for l in range(0, layers, N1):
                previous = before[count - 1 :] if l == 0 else own[l - 1 : l]
                ref[base : base + 1, :] = previous + own[l : l + 1]
                ref[base + 1 : base + N1 - 1, :] = own[l + 1 : l + N1 - 1]
                base += N1 - 1
            ref[base : base + 1, :] = own[layers - 1 :] + after[:1]
            ref[base + 1 : base + count - 1, :] = after[1 : count - 1]
    pack(out_near_ref, out_far_ref, jnp.concatenate(spare, 0))


def spread_columns(parts, lay, pick):
    table = dot(parts, lay, ((0,), (0,)))
    return dot(pick, jnp.concatenate(split3(table), 0))


def spread_rows(parts, pick, rows):
    pad = parts.shape[0] // 3
    table = sum(dot(parts[k * pad : (k + 1) * pad], pick) for k in range(3))
    return dot(rows, jnp.concatenate(split3(table), 0))


def halves_by_lane(value, low):
    high = value.astype(BF16).astype(F32)
    return jnp.where(low, value - high, high).astype(BF16)


def low_lanes(kin, rim):
    lane = lax.broadcasted_iota(jnp.int32, (1, 3 * (kin + rim)), 1)
    return ((lane >= 2 * kin) & (lane < 3 * kin)) | (lane >= 3 * kin + 2 * rim)


def low_back_lanes(pairs):
    return lax.broadcasted_iota(jnp.int32, (1, 3 * pairs), 1) >= 2 * pairs


def ramps(*dims):
    return [lax.broadcasted_iota(jnp.int32, dims, axis) for axis in range(2)]


def over(value, count):
    if count & (count - 1) == 0:
        return lax.shift_right_logical(value, count.bit_length() - 1), value & (count - 1)
    quotient = ((value.astype(F32) + 0.5) * (1.0 / count)).astype(jnp.int32)
    return quotient, value - quotient * count


def mask(hit):
    return jnp.where(hit, 1.0, 0.0).astype(BF16)


def spread_table(blocks, modes):
    row, column = ramps(modes, blocks * modes)
    return mask(row == over(column, modes)[1])


def gather_table(blocks, modes):
    row, column = ramps(blocks * N1, modes * blocks)
    node, block = over(column, blocks)
    place = row - block * N1
    hit = (place == node - 1) & (node >= 1) & (node <= N1)
    for n, at in ((0, -2), (1, -1), (N1, N1), (N1 + 1, N1 + 1)):
        hit = hit | ((node == n) & (place == at))
    return mask(hit)


def pick_table(pairs, pad, modes, which):
    row, column = ramps(pairs, 3 * pad)
    return mask(over(row, modes)[which] == over(column, pad)[1])


def pick_rows(pairs, pad, modes, which):
    row, column = ramps(pairs, pad)
    return jnp.where(over(row, modes)[which] == column, 1.0, 0.0)


def back_tables(pairs, pad, modes):
    row, column = ramps(pad, 3 * pairs)
    found = over(over(column, pairs)[1], modes)
    return mask(found[0] == row), mask(found[1] == row)


def box_rows(count, pad):
    row, column = ramps(count, 3 * pad)
    first, second = over(row, N1)
    column = over(column, pad)[1]
    return mask(first + 1 == column), mask(second + 1 == column)


def face_rows(pad):
    row, column = ramps(2 * N1, 3 * pad)
    face, first = over(row, N1)
    column = over(column, pad)[1]
    return mask(first + 1 == column), mask(jnp.where(face == 0, 1, N1) == column)


def inner_table(blocks, modes):
    row, column = ramps(modes * blocks, blocks * N1)
    node, block = over(row, blocks)
    place = column - block * N1
    hit = (place == node - 1) & (node >= 1) & (node <= N1)
    return mask(hit | ((node == 1) & (place == -1)) | ((node == N1) & (place == N1)))


def lay_tables(pad, kin, rim):
    layers = kin // N1
    row, column = ramps(3 * pad, 3 * (kin + rim))
    row = over(row, pad)[1]
    own = column < 3 * kin
    l_own, y = over(over(column, kin)[1], N1)
    kind, l_rim = over(over(jnp.maximum(column - 3 * kin, 0), rim)[1], rim // 4)
    node = jnp.where(l_own == 0, 0, jnp.where(l_own == layers - 1, N1 + 1, jnp.clip(l_own - 1, 1, N1)))
    node = jnp.where(own, node, l_rim)
    second = jnp.where(own, y + 1, jnp.where(kind < 2, kind, N1 - 2 + kind))
    inside = own | (l_rim < N1 + 2)
    return mask(inside & (row == node)), mask(inside & (row == second))


def third_parts(mt_ref, spread):
    rows, modes = mt_ref.shape
    blocks = rows // modes
    row, column = ramps(rows, rows)
    own = over(row, blocks)[1] == over(column, modes)[0]
    return [jnp.where(own, dot(part, spread), 0.0).astype(BF16) for part in split3(mt_ref[...])]


def pad_modes(pad_ref, mf_ref, ms_ref):
    modes = ms_ref.shape[0]
    first_blocks = pad_ref.shape[0] - 1
    pad_ref[...] = jnp.zeros_like(pad_ref)
    for a in range(first_blocks):
        pad_ref[a, :modes, :modes] = mf_ref[:, a, :]
    pad_ref[first_blocks, :modes, :modes] = ms_ref[:, 0, :]


def modes_kernel(
    mt_ref, e3_ref, mf_ref, ef_ref, ms_ref, es_ref,
    w_ref, e3_row_ref, own_columns_ref, own_rim_ref, second_columns_ref, pad_ref, eigen_ref, back_ref,
):
    blocks, modes = e3_ref.shape
    spread = spread_table(blocks, modes)
    gather = gather_table(blocks, modes)
    table = sum(dot(gather, part) for part in third_parts(mt_ref, spread))
    high, low = split(table)
    w_ref[...] = jnp.concatenate([high, low, high], 0)
    row, column = ramps(blocks, blocks * modes)
    e3_wide = sum(dot(part, spread) for part in split3(e3_ref[...]))
    e3_row_ref[...] = jnp.sum(
        jnp.where(row == over(column, modes)[0], e3_wide, 0.0), 0, keepdims=True
    )
    first_blocks, pairs, kin = own_columns_ref.shape
    kin, rim, pad = kin // 3, own_rim_ref.shape[2] // 3, pad_ref.shape[1]
    pad_modes(pad_ref, mf_ref, ms_ref)
    eigen_ref[...] = jnp.zeros_like(eigen_ref)
    eigen_ref[:first_blocks, :modes] = ef_ref[...]
    eigen_ref[first_blocks : first_blocks + 1, :modes] = es_ref[...]
    lay_m, lay_n = lay_tables(pad, kin, rim)
    low = low_lanes(kin, rim)
    second = jnp.concatenate(split3(pad_ref[first_blocks]), 0)
    second_columns = spread_columns(second, lay_n, pick_table(pairs, pad, modes, 1))
    second_columns_ref[...] = second_columns
    pick = pick_table(pairs, pad, modes, 0)
    for a in range(first_blocks):
        first = jnp.concatenate(split3(pad_ref[a]), 0)
        columns = halves_by_lane(spread_columns(first, lay_m, pick) * second_columns, low)
        own_columns_ref[a] = columns[:, : 3 * kin]
        own_rim_ref[a] = columns[:, 3 * kin :]
    box = back_ref.shape[1]
    back_m, back_n = back_tables(pairs, pad, modes)
    rows_m, rows_n = box_rows(box, pad)
    second_rows = spread_rows(second, back_n, rows_n)
    for a in range(first_blocks):
        first = jnp.concatenate(split3(pad_ref[a]), 0)
        back_ref[a] = halves_by_lane(spread_rows(first, back_m, rows_m) * second_rows, low_back_lanes(pairs))


def columns_kernel(
    lp_ref, near_ref, far_ref, w_ref, e3_row_ref, own_columns_ref, second_columns_ref, pad_ref,
    eigen_ref, mt_ref, v_ref, side_rim_ref, rec_ref, face_ref, wbh_ref, wbl_ref,
):
    rows = N1
    halo = (N1 + 2) * rows
    first_blocks, pairs, kin = own_columns_ref.shape
    kin, rim, pad, modes = kin // 3, side_rim_ref.shape[2] // 3, pad_ref.shape[1], N1 + 2
    box = N1 * rows
    near, far = near_ref[...], far_ref[...]
    before, after = from_sides(near, far, "stream")
    odd = jnp.logical_not(even(lax.axis_index("stream")))
    body = halo - rows
    zero = jnp.zeros((rows, lp_ref.shape[1]), F32)
    stack = jnp.concatenate(
        [before[:rows], zero, before[rows:body], lp_ref[...], after[: body - rows], zero, after[body - rows : body]], 0
    )
    u = dot(abreast(stack), w_ref[...])
    edge_near, edge_far = near[body : body + 1, 32 : 32 + pad], far[body : body + 1, 32 : 32 + pad]
    low = low_lanes(kin, rim)
    lay_m, _ = lay_tables(pad, kin, rim)
    pick_p3 = pick_table(pairs, pad, modes, 0)
    pick_p, pick_q = pick_rows(pairs, pad, modes, 0), pick_rows(pairs, pad, modes, 1)
    back_m, back_n = back_tables(pairs, pad, modes)
    face_m, face_n = face_rows(pad)
    own_eigen = eigen_ref[...]
    firsts = [jnp.concatenate([side[body:, :pad], side[body:, 16 : 16 + pad]], 0) for side in (before, after)]
    firsts = [firsts[0]] + [pad_ref[a] for a in range(first_blocks)] + [firsts[1]]
    eigens = [jnp.where(odd, edge_near, edge_far)] + [own_eigen[a : a + 1] for a in range(first_blocks)]
    eigens += [jnp.where(odd, edge_far, edge_near)]
    second = jnp.concatenate(split3(pad_ref[first_blocks]), 0)
    second_faces = spread_rows(second, back_n, face_n)
    second_sum = jnp.sum(pick_q * own_eigen[first_blocks : first_blocks + 1], 1, keepdims=True)
    for a, (first, eigen) in enumerate(zip(firsts, eigens)):
        first = jnp.concatenate(split3(first), 0)
        if a in (0, first_blocks + 1):
            columns = halves_by_lane(
                spread_columns(first, lay_m, pick_p3) * second_columns_ref[...], low
            )
            side_rim_ref[min(a, 1)] = columns[:, 3 * kin :]
            columns = columns[:, : 3 * kin]
        else:
            columns = own_columns_ref[a - 1]
        begin = a * box
        high, low_half = split((spread_rows(first, back_m, face_m) * second_faces)[:, :pairs])
        face_ref[a] = jnp.concatenate([high, low_half], 0)
        total = jnp.sum(pick_p * eigen, 1, keepdims=True) + second_sum
        reciprocal = 1.0 / (total + e3_row_ref[...])
        rec_ref[a] = reciprocal
        v_ref[a] = dot(columns, stacked(u[begin : begin + kin])) * reciprocal
    blocks = mt_ref.shape[0] // modes
    inner = inner_table(blocks, modes)
    table = sum(
        dot(part, inner, ((0,), (0,))) for part in third_parts(mt_ref, spread_table(blocks, modes))
    )
    wbh_ref[...], wbl_ref[...] = split(table)


def spectral_columns(near, far, w_ref, v_ref, own_rim_ref, side_rim_ref, rec_ref):
    columns = v_ref.shape[0]
    inner = near.shape[0] // 2
    half = N1 // 2
    free = lane_masks(near.shape[1])[2]
    spare = unpack_spare(near, far)
    before, after = from_sides(jnp.where(free, 0.0, near), jnp.where(free, 0.0, far), "cross")
    ends = jnp.concatenate(from_sides(spare[:half], spare[half:], "cross"), 0)
    u = dot(abreast(jnp.concatenate([before, after, ends], 0)), w_ref[...])
    found = []
    for a in range(columns):
        rim = []
        for k in range(4):
            base, end = k * inner, 4 * inner + 2 * k
            start = a * (N1 - 1) - 1
            if a == 0:
                rim += [u[end : end + 1], u[base : base + 15]]
            elif a == columns - 1:
                count = inner - start
                rim += [u[base + start : base + inner], u[end + 1 : end + 2]]
                rim += [jnp.zeros((15 - count, u.shape[1]), F32)]
            else:
                rim += [u[base + start : base + start + 16]]
        rim = jnp.concatenate(rim, 0)
        table = side_rim_ref[min(a, 1)] if a in (0, columns - 1) else own_rim_ref[a - 1]
        found.append(v_ref[a] + dot(table, stacked(rim)) * rec_ref[a])
    return found


def third_back(parts, wbh_ref, wbl_ref):
    high, low = split(jnp.concatenate(parts, 0))
    count, width = high.shape[0], wbh_ref.shape[1]
    both = dot(jnp.concatenate([high, low], 0), jnp.concatenate([wbh_ref[...], wbl_ref[...]], 1))
    return both[:count, :width] + both[count:, :width] + both[:count, width:]


def faces_kernel(
    far_ref, near_ref, w_ref, v_ref, own_rim_ref, side_rim_ref, rec_ref, wbh_ref, wbl_ref, face_ref,
    out_far_ref, out_near_ref, spectral_ref,
):
    rows = N1
    found = spectral_columns(near_ref[...], far_ref[...], w_ref, v_ref, own_rim_ref, side_rim_ref, rec_ref)
    columns = len(found)
    for a in range(columns):
        spectral_ref[a] = found[a]
    parts = []
    for a in range(columns):
        high, low = split(found[a])
        both = dot(face_ref[a], high)
        parts.append(both[: 2 * N1] + both[2 * N1 :] + dot(face_ref[a, : 2 * N1], low))
    solved = third_back(parts, wbh_ref, wbl_ref)
    row = lax.broadcasted_iota(jnp.int32, (rows, 1), 0)
    up = even(lax.axis_index("cross"))
    for a in range(1, columns - 1):
        sums = []
        for face in range(2):
            base = 16 * a + rows * face
            previous = base - 16 + rows - 1
            after = base + 16
            sums.append(
                solved[base : base + rows]
                + jnp.where(row == 0, solved[previous : previous + 1], 0.0)
                + jnp.where(row == rows - 1, solved[after : after + 1], 0.0)
            )
        here = slice((a - 1) * rows, a * rows)
        out_near_ref[here, :] = jnp.where(up, sums[1], sums[0])
        out_far_ref[here, :] = jnp.where(up, sums[0], sums[1])


def assemble_operator(lp_ref, s_near_ref, s_far_ref, c_near_ref, c_far_ref, out_ref, acc_ref):
    rows = N1
    total_rows, width = lp_ref.shape
    padded = c_near_ref.shape[0] // 2
    body = (N1 + 1) * rows
    box = N1 * rows
    before, after = from_sides(s_near_ref[...], s_far_ref[...], "stream")
    left, right = from_sides(c_near_ref[...], c_far_ref[...], "cross")
    acc_ref[...] = lp_ref[...]
    for base in range(0, total_rows, box):
        last = base + box
        previous = before[body - rows : body] if base == 0 else lp_ref[base - rows : base, :]
        following = after[:rows] if last == total_rows else lp_ref[last : last + rows, :]
        acc_ref[base : base + rows, :] = lp_ref[base : base + rows, :] + previous
        acc_ref[last - rows : last, :] = lp_ref[last - rows : last, :] + following
        node = (N1 - 1) * (base // box + 1) + 1
        low, high = pl.ds(base, N1, stride=rows), pl.ds(base + rows - 1, N1, stride=rows)
        acc_ref[low, :] = acc_ref[low, :] + left[padded + node : padded + node + N1]
        acc_ref[high, :] = acc_ref[high, :] + right[node : node + N1]
    lane = lax.broadcasted_iota(jnp.int32, (1, width), 1)
    first = (lax.rem(lane, N1) == 0) & (lane > 0)
    final = (lax.rem(lane, N1) == N1 - 1) & (lane < width - 1)
    value = acc_ref[...]
    value = (
        value
        + jnp.where(first, pltpu.roll(value, 1, 1), 0.0)
        + jnp.where(final, pltpu.roll(value, width - 1, 1), 0.0)
    )
    out_ref[...] = value.reshape(out_ref.shape)


def solve_kernel(
    lp_ref, s_near_ref, s_far_ref, c_far_ref, c_near_ref, spectral_ref, wbh_ref, wbl_ref, pad_ref, back_ref,
    operator_ref, r_ref, out_ref, acc_ref, all_near_ref, all_far_ref, sem,
):
    unpack(c_near_ref[...], c_far_ref[...], all_near_ref, all_far_ref)
    assemble_operator(lp_ref, s_near_ref, s_far_ref, all_near_ref, all_far_ref, out_ref, acc_ref)
    copy = pltpu.make_async_copy(out_ref, operator_ref, sem)
    copy.start()
    rows = N1
    box = N1 * rows
    found = [spectral_ref[a] for a in range(spectral_ref.shape[0])]
    columns = len(found)
    pad, pairs = pad_ref.shape[1], spectral_ref.shape[1]
    back_m, back_n = back_tables(pairs, pad, N1 + 2)
    rows_m, rows_n = box_rows(box, pad)
    low = low_back_lanes(pairs)
    body = (N1 + 1) * rows
    sides = from_sides(s_near_ref[...], s_far_ref[...], "stream")
    sides = [jnp.concatenate([side[body:, :pad], side[body:, 16 : 16 + pad]], 0) for side in sides]
    second = jnp.concatenate(split3(pad_ref[columns - 2]), 0)
    parts = [None] * columns
    for a, first, kept in ((0, sides[0], slice(box - 16, box)), (columns - 1, sides[1], slice(0, 16))):
        first = jnp.concatenate(split3(first), 0)
        table = spread_rows(first, back_m, rows_m[kept]) * spread_rows(second, back_n, rows_n[kept])
        parts[a] = dot(halves_by_lane(table, low), stacked(found[a]))
    for a in range(1, columns - 1):
        parts[a] = dot(back_ref[a - 1], stacked(found[a]))
    parts[0] = parts[0][16 - rows :]
    parts[-1] = parts[-1][:rows]
    solved = third_back(parts, wbh_ref, wbl_ref)
    for a in range(columns - 2):
        base = rows + a * box
        top, bottom = solved[base : base + rows], solved[base + box - rows : base + box]
        r_ref[a * box : a * box + rows, :] = top + solved[base - rows : base]
        r_ref[a * box + rows : (a + 1) * box - rows, :] = solved[base + rows : base + box - rows]
        r_ref[(a + 1) * box - rows : (a + 1) * box, :] = bottom + solved[base + box : base + box + rows]
    copy.wait()


def pass_kernel(*refs):
    count = len(refs) // 2
    for source, target in zip(refs[:count], refs[count:]):
        target[...] = source[...]


def add_kernel(r_ref, ahead_ref, far_ref, near_ref, out_ref, acc_ref, sem):
    rows = N1
    near = jnp.where(lax.axis_index("cross") < 2, ahead_ref[...], near_ref[...])
    before, after = from_sides(near, far_ref[...], "cross")
    row = lax.broadcasted_iota(jnp.int32, (rows, 1), 0)
    for l in range(acc_ref.shape[0]):
        value = r_ref[l * rows : (l + 1) * rows, :] + jnp.where(row == 0, before[l : l + 1], 0.0)
        acc_ref[l] = value + jnp.where(row == rows - 1, after[l : l + 1], 0.0)
    copy = pltpu.make_async_copy(acc_ref, out_ref, sem)
    copy.start()
    copy.wait()


def shape(*dims, dtype=F32):
    return pltpu.VMEM(dims, dtype)


def call(kernel, name, out, *args, scratch=(), out_specs=None, flops=1000000, place=pltpu.VMEM):
    single = not isinstance(out, list)
    args = [pltpu.with_memory_space_constraint(x, place) for x in args]
    return pl.pallas_call(
        kernel,
        out_shape=out,
        in_specs=[pl.BlockSpec(memory_space=place)] * len(args),
        out_specs=out_specs if out_specs is not None else (VMEM if single else [VMEM] * len(out)),
        scratch_shapes=list(scratch),
        compiler_params=pltpu.CompilerParams(vmem_limit_bytes=VMEM_LIMIT),
        cost_estimate=pl.CostEstimate(flops=flops, bytes_accessed=flops, transcendentals=0),
        name=name,
    )(*args)


def swaps(axis):
    count = lax.axis_size(axis)
    near = [(i, i ^ 1) for i in range(count)]
    far = [(i, (i - 1) % count if i % 2 == 0 else (i + 1) % count) for i in range(count)]
    return near, far


def swap_stream(near, far):
    first, second = swaps("stream")
    near = lax.ppermute(near, "stream", first)
    far = lax.ppermute(far, "stream", second)
    return near, far


def cross_pairs(near, ahead=None):
    count, streams = lax.axis_size("cross"), lax.axis_size("stream")
    pairs = []
    for s in range(streams):
        for i in range(count):
            j = i ^ 1 if near else i - 1 + 2 * (i % 2)
            idle = not 0 <= j < count or (ahead is not None and (i < 2) != ahead)
            pairs.append((s * count + i, (s ^ 1) * count + i if idle else s * count + j))
    return pairs


def swap_cross(near, far):
    axes = ("stream", "cross")
    return lax.ppermute(near, axes, cross_pairs(True)), lax.ppermute(far, axes, cross_pairs(False))


def swap_cross_ahead(near, far):
    axes = ("stream", "cross")
    first = lax.ppermute(near, axes, cross_pairs(True, True))
    far, near = call(pass_kernel, "pass_on", [shape(*far.shape), shape(*near.shape)], far, near)
    return first, lax.ppermute(far, axes, cross_pairs(False)), lax.ppermute(near, axes, cross_pairs(True, False))


def shards(
    pressure, geo_diag, geo_off, modes_first, modes_second, modes_third, eigen_first, eigen_second,
    eigen_third,
):
    layers, rows, width = pressure.shape
    modes = modes_first.shape[1]
    if layers < 3 * N1 or rows != N1 or modes != N1 + 2 or lax.axis_size("stream") % 2 or lax.axis_size("cross") % 2:
        raise ValueError("unsupported sizes")
    first_blocks, third_blocks = layers // N1, width // N1
    columns = first_blocks + 2
    halo = modes * rows
    box = N1 * rows
    nodes = (first_blocks + 1) * (N1 - 1) + modes
    padded = round_up(nodes, 8)
    wide = third_blocks * modes

    pairs, pad = round_up(modes * modes, 16), round_up(modes, 16)

    mf = jnp.transpose(modes_first, (1, 0, 2))
    ms = jnp.transpose(modes_second, (1, 0, 2))
    mt = jnp.transpose(modes_third, (1, 0, 2)).reshape(modes * third_blocks, modes)

    inputs = [pressure, geo_diag, geo_off, mf, eigen_first, eigen_second]
    lp, s_near, s_far, mf, ef, es = call(
        local_kernel, "local_product",
        [
            shape(layers * rows, width), shape(halo, width), shape(halo, width),
            shape(modes, first_blocks, modes), shape(first_blocks, modes), shape(1, modes),
        ],
        *inputs, place=pltpu.HBM,
        scratch=[pltpu.VMEM(x.shape, x.dtype) for x in inputs[:3]] + [pltpu.SemaphoreType.DMA((len(inputs),))],
    )
    s_near, s_far = swap_stream(s_near, s_far)
    kin, rim_width = 3 * (N1 + 4) * rows, 3 * 64
    w, e3_row, own_columns, own_rim, second_columns, padded_modes, eigen, own_back = call(
        modes_kernel, "mode_tables",
        [
            shape(3 * width, wide, dtype=BF16), shape(1, wide),
            shape(first_blocks, pairs, kin, dtype=BF16), shape(first_blocks, pairs, rim_width, dtype=BF16),
            shape(pairs, kin + rim_width), shape(first_blocks + 1, pad, pad), shape(first_blocks + 1, pad),
            shape(first_blocks, box, 3 * pairs, dtype=BF16),
        ],
        mt, eigen_third, mf, ef, ms, es,
    )
    c_far, c_near = call(
        rows_kernel, "rows_to_send",
        [shape(2 * nodes - 4, width), shape(2 * nodes - 4, width)],
        lp, s_near, s_far, e3_row,
    )
    c_near, c_far = swap_cross(c_near, c_far)
    v, side_rim, rec, face, wbh, wbl = call(
        columns_kernel, "own_part",
        [
            shape(columns, pairs, wide), shape(2, pairs, rim_width, dtype=BF16), shape(columns, pairs, wide),
            shape(columns, 4 * N1, pairs, dtype=BF16), shape(wide, width, dtype=BF16), shape(wide, width, dtype=BF16),
        ],
        lp, s_near, s_far, w, e3_row, own_columns, second_columns, padded_modes, eigen, mt,
    )
    f_far, f_near, spectral = call(
        faces_kernel, "faces",
        [
            shape(layers, width), shape(layers, width), shape(columns, pairs, wide),
        ],
        c_far, c_near, w, v, own_rim, side_rim, rec, wbh, wbl, face,
    )
    f_ahead, f_far, f_near = swap_cross_ahead(f_near, f_far)
    result = pltpu.HBM(pressure.shape, F32)
    in_hbm = pl.BlockSpec(memory_space=pltpu.HBM)
    operator_out, restricted = call(
        solve_kernel, "solve", [result, shape(layers * rows, width)],
        lp, s_near, s_far, c_far, c_near, spectral, wbh, wbl, padded_modes, own_back, out_specs=[in_hbm, VMEM],
        scratch=[
            pltpu.VMEM(pressure.shape, F32), pltpu.VMEM((layers * rows, width), F32),
            pltpu.VMEM((2 * padded, width), F32), pltpu.VMEM((2 * padded, width), F32), pltpu.SemaphoreType.DMA,
        ],
    )
    preconditioned = call(
        add_kernel, "preconditioned", result, restricted, f_ahead, f_far, f_near, out_specs=in_hbm,
        scratch=[pltpu.VMEM(pressure.shape, F32), pltpu.SemaphoreType.DMA],
    )
    return (operator_out, preconditioned)


def solution(mesh):
    in_specs = (
        P("stream", "cross", None),
        P(None, "stream", "cross", None),
        P(None, "stream", "cross", None),
        P("stream", None, None),
        P("cross", None, None),
        P(),
        P("stream", None),
        P("cross", None),
        P(),
    )
    out_specs = (P("stream", "cross", None), P("stream", "cross", None))
    return jax.shard_map(shards, mesh=mesh, in_specs=in_specs, out_specs=out_specs, check_vma=False)
```
